32 devices in a mesh: inner: 4 (over y, x), outer: 8 (over z, core).
Axes of the slice: x: 2, y: 2, z: 4, core: 2. Of those that a mesh axis runs over, the one named last changes fastest.
Arguments:
- tokens: int32 [512], P('outer'), may hold values from 0 to 16383
- step_index: int32 [1], replicated, may hold values from 0 to 31
- embed_table: bfloat16 [16384, 2048], P(None, 'inner'), may hold values from -6 to 6
- gain_one: float32 [2048], replicated, may hold values from 0.5 to 1.5
- gate_weight: bfloat16 [2048, 5632], P(None, 'inner'), may hold values from -0.125 to 0.125
- up_weight: bfloat16 [2048, 5632], P(None, 'inner'), may hold values from -0.125 to 0.125
- down_weight: bfloat16 [5632, 2048], P('inner'), may hold values from -0.078125 to 0.078125
- gain_two: float32 [2048], replicated, may hold values from 0.5 to 1.5
- query_weight: bfloat16 [2048, 2048], P(None, 'inner'), may hold values from -0.125 to 0.125
- key_weight: bfloat16 [2048, 2048], P(None, 'inner'), may hold values from -0.125 to 0.125
- value_weight: bfloat16 [2048, 4096], P(None, 'inner'), may hold values from -0.125 to 0.125
- decay_weight: bfloat16 [2048, 16], P(None, 'inner'), may hold values from -0.125 to 0.125
- beta_weight: bfloat16 [2048, 16], P(None, 'inner'), may hold values from -0.125 to 0.125
- rate_log: float32 [16], P('inner'), may hold values from -12 to -2
- decay_bias: float32 [16], P('inner'), may hold values from -1 to 1
- beta_bias: float32 [16], P('inner'), may hold values from -6 to -2
- cotangent: bfloat16 [512, 4096], P('outer', 'inner'), may hold values from -192 to 192
Outputs:
- attribution: float32 [512, 5632], P('outer', 'inner')
The draws below stay inside these ranges and needn't reach their ends.
All inputs are finite; a program needn't handle non-finite values.
Results may differ from the reference program's by a relative error of at most 0.029.
Values may be sent and summed in bfloat16 or wider, within the bound.
No kernel may reach another device: no remote copies, remote signals or barrier semaphores. Data moves between devices by JAX's collectives and lax.ppermute only.
A program may use at most 128 MiB of HBM per device.

```python
import functools
import math
import jax
import jax.numpy as jnp
import numpy as np
from jax import lax

D = 2048
FF = 5632
H = 16
KD = 128
VD = 256
VOCAB = 16384
STEPS = 32
TOKENS = 512
N_INNER = 4


def with_ends(values, stream_key, smallest, top_value):
    shape = values.shape
    spot = [jax.random.randint(jax.random.fold_in(stream_key, axis), (), 0, shape[axis]) for axis in range(len(shape))]
    values = values.at[tuple(spot)].set(smallest)
    longest = shape.index(max(shape))
    spot[longest] = (spot[longest] + 1) % shape[longest]
    return values.at[tuple(spot)].set(top_value)


def steps_of(key, dims, shards, smallest, largest):
    level, own = 1.0, jax.random.fold_in(key, 6)
    for position, parts in shards:
        heights = jnp.exp(jax.random.uniform(jax.random.fold_in(own, position), (parts,), jnp.float32, smallest / len(shards), largest / len(shards)))
        level = level * jnp.repeat(heights, dims[position] // parts).reshape([-1 if axis == position else 1 for axis in range(len(dims))])
    return level


def rank_bounds(count, lean):
    loads = [(1 << 20) // math.isqrt(grade ** lean) + 1 for grade in range(1, count + 1)]
    scale = 1 + sum(loads) // (1 << 30)
    return np.cumsum(np.array([max(1, weight // scale) for weight in loads]))


def skewed_ids(key, shape, number_of, skew):
    grid = rank_bounds(number_of, skew)
    lot = jax.random.randint(jax.random.fold_in(key, 1), shape, 0, int(grid[number_of - 1]))
    grade = jnp.searchsorted(jnp.asarray(grid, jnp.int32), lot, side="right")
    return jax.random.permutation(jax.random.fold_in(key, 2), number_of)[grade].astype(jnp.int32)


def noise(rng, extent, deviation, reach, cuts=(), kind=jnp.bfloat16):
    entries = jax.random.normal(rng, extent, jnp.float32) * deviation
    if len(cuts) > 0:
        entries = steps_of(rng, extent, cuts, -0.22, 0.18) * entries
    return jnp.clip(entries, min=-reach, max=reach).astype(kind)


def setup_inputs(seed: int = 0) -> dict:
    arg_keys = jax.random.split(jax.random.key(seed), 18)
    return {
        "tokens": with_ends(skewed_ids(arg_keys[0], (TOKENS,), VOCAB, 2), jax.random.fold_in(arg_keys[0], 3), 0, VOCAB - 1).astype(jnp.int32),
        "step_index": jax.random.randint(arg_keys[1], (1,), 0, STEPS).astype(jnp.int32),
        "embed_table": noise(arg_keys[2], (VOCAB, D), 1.0, 6.0, ((1, 4),)),
        "gain_one": jnp.clip(1.0 + 0.1 * jax.random.normal(arg_keys[3], (D,), jnp.float32), 0.5, 1.5),
        "gate_weight": noise(arg_keys[4], (D, FF), D ** -0.5, 0.125, ((1, 4),)),
        "up_weight": noise(arg_keys[5], (D, FF), D ** -0.5, 0.125, ((1, 4),)),
        "down_weight": noise(arg_keys[6], (FF, D), FF ** -0.5, 0.078125, ((0, 4),)),
        "gain_two": jnp.clip(1.0 + 0.1 * jax.random.normal(arg_keys[7], (D,), jnp.float32), 0.5, 1.5),
        "query_weight": noise(arg_keys[8], (D, H * KD), D ** -0.5, 0.125, ((1, 4),)),
        "key_weight": noise(arg_keys[9], (D, H * KD), D ** -0.5, 0.125, ((1, 4),)),
        "value_weight": noise(arg_keys[10], (D, H * VD), D ** -0.5, 0.125, ((1, 4),)),
        "decay_weight": noise(arg_keys[11], (D, H), D ** -0.5, 0.125, ((1, 4),)),
        "beta_weight": noise(arg_keys[12], (D, H), D ** -0.5, 0.125, ((1, 4),)),
        "rate_log": jnp.clip(-12.0 + 10.0 * jax.random.uniform(arg_keys[13], (H,), jnp.float32) ** steps_of(arg_keys[13], (H,), ((0, 4),), -0.2, 0.2), -12.0, -2.0),
        "decay_bias": jnp.clip(jax.random.uniform(arg_keys[14], (H,), jnp.float32, -1.0, 1.0) * steps_of(arg_keys[14], (H,), ((0, 4),), -0.4, 0.0), -1.0, 1.0),
        "beta_bias": jnp.clip(-6.0 + 4.0 * jax.random.uniform(arg_keys[15], (H,), jnp.float32) ** steps_of(arg_keys[15], (H,), ((0, 4),), -0.2, 0.2), -6.0, -2.0),
        "cotangent": noise(arg_keys[16], (TOKENS, H * VD), 32.0, 192.0, ((0, 8), (1, 4))),
    }


def unit_rows(values):
    return values * lax.rsqrt(lax.optimization_barrier(jnp.sum(values * values, axis=-1, keepdims=True)) + 1e-06)

def head_inputs(query_rows, key_rows, decay_rows, beta_rows, log_rate, rate_shift, beta_shift):
    queries = unit_rows(query_rows) * query_rows.shape[-1] ** (-0.5)
    keys_unit = unit_rows(key_rows)
    log_decay = -jnp.exp(log_rate) * jax.nn.softplus(decay_rows + rate_shift)
    betas = jax.nn.sigmoid(beta_rows + beta_shift)
    return (queries, keys_unit, log_decay, betas)

def block_step(with_out, state, pieces):
    queries, keys_unit, values, log_decay, betas = pieces
    block_len = keys_unit.shape[0]
    highest = lax.Precision.HIGHEST
    cum_decay = jnp.cumsum(log_decay)
    row_ids = jnp.arange(block_len)[:, None]
    col_ids = jnp.arange(block_len)[None, :]
    lower_mask = row_ids >= col_ids
    decay_mat = jnp.where(lower_mask, jnp.exp(jnp.where(lower_mask, cum_decay[:, None] - cum_decay[None, :], 0.0)), 0.0)
    key_gram = jnp.dot(keys_unit, keys_unit.T, precision=highest)
    strict = jnp.where(row_ids > col_ids, betas[:, None] * decay_mat * key_gram, 0.0)
    system = strict + jnp.eye(block_len, dtype=jnp.float32)
    start_scale = jnp.exp(cum_decay)[:, None]
    target = betas[:, None] * (values - start_scale * jnp.dot(keys_unit, state, precision=highest))
    fresh_vals = lax.linalg.triangular_solve(system, target, left_side=True, lower=True, unit_diagonal=True)
    tail_keys = jnp.exp(cum_decay[-1] - cum_decay)[:, None] * keys_unit
    new_state = jnp.exp(cum_decay[-1]) * state + jnp.dot(tail_keys.T, fresh_vals, precision=highest)
    if with_out:
        scores = decay_mat * jnp.dot(queries, keys_unit.T, precision=highest)
        output = start_scale * jnp.dot(queries, state, precision=highest) + jnp.dot(scores, fresh_vals, precision=highest)
        return (new_state, output)
    return (new_state, None)

def run_blocks(queries, keys_unit, values, log_decay, betas, state, with_out):
    length = keys_unit.shape[0]
    block_len = math.gcd(64, length)
    block_count = length // block_len

    def blocked(array):
        return array.reshape((block_count, block_len) + array.shape[1:])
    step_fn = functools.partial(block_step, with_out)
    final_state, outputs = lax.scan(step_fn, state, (blocked(queries), blocked(keys_unit), blocked(values), blocked(log_decay), blocked(betas)))
    if with_out:
        outputs = outputs.reshape((length,) + outputs.shape[2:])
    return (final_state, outputs)

def rms_scaled(values, gain):
    return values * lax.rsqrt(lax.optimization_barrier(jnp.mean(values * values, axis=-1, keepdims=True)) + 1e-06) * gain

def to_wire(values):
    return lax.optimization_barrier(values.astype(jnp.bfloat16)).astype(jnp.float32)

def head_grads(items):
    query_rows, key_rows, value_rows, decay_rows, beta_rows, cot_rows, log_rate, rate_shift, beta_shift = items

    def target_of(query_in, key_in, value_in, decay_in, beta_in):
        queries, keys_unit, log_decay, betas = head_inputs(query_in, key_in, decay_in, beta_in, log_rate, rate_shift, beta_shift)
        start_state = jnp.zeros((key_in.shape[1], value_in.shape[1]), jnp.float32)
        final_state, outputs = run_blocks(queries, keys_unit, value_in, log_decay, betas, start_state, True)
        return jnp.sum(outputs * cot_rows)
    score_value, pull_back = jax.vjp(target_of, query_rows, key_rows, value_rows, decay_rows, beta_rows)
    return pull_back(jnp.ones_like(score_value))

def reference(tokens, step_index, embed_table, gain_one, gate_weight, up_weight, down_weight, gain_two, query_weight, key_weight, value_weight, decay_weight, beta_weight, rate_log, decay_bias, beta_bias, cotangent):
    embedded = jnp.take(embed_table, tokens, axis=0)
    emb_float = embedded.astype(jnp.float32)
    normed_one = rms_scaled(emb_float, gain_one).astype(jnp.bfloat16)
    gate_rows = jnp.dot(normed_one.astype(jnp.float32), gate_weight.astype(jnp.float32), preferred_element_type=jnp.float32)
    up_rows = jnp.dot(normed_one.astype(jnp.float32), up_weight.astype(jnp.float32), preferred_element_type=jnp.float32)
    hidden = jax.nn.silu(gate_rows) * up_rows
    path_scale = (step_index[0].astype(jnp.float32) + 0.5) / STEPS
    scaled = (path_scale * hidden).astype(jnp.bfloat16)
    group_units = FF // N_INNER
    mixed_rows = emb_float
    for member in range(N_INNER):
        first_unit = member * group_units
        last_unit = first_unit + group_units
        mixed_rows = mixed_rows + to_wire(jnp.dot(scaled[:, first_unit:last_unit].astype(jnp.float32), down_weight[first_unit:last_unit].astype(jnp.float32), preferred_element_type=jnp.float32))

    def normalize(values):
        return rms_scaled(values, gain_two)
    normed_float, norm_pull = jax.vjp(normalize, mixed_rows)
    normed_two = normed_float.astype(jnp.bfloat16)
    query_pre = jnp.dot(normed_two.astype(jnp.float32), query_weight.astype(jnp.float32), preferred_element_type=jnp.float32)
    key_pre = jnp.dot(normed_two.astype(jnp.float32), key_weight.astype(jnp.float32), preferred_element_type=jnp.float32)
    value_pre = jnp.dot(normed_two.astype(jnp.float32), value_weight.astype(jnp.float32), preferred_element_type=jnp.float32)
    decay_pre = jnp.dot(normed_two.astype(jnp.float32), decay_weight.astype(jnp.float32), preferred_element_type=jnp.float32)
    beta_pre = jnp.dot(normed_two.astype(jnp.float32), beta_weight.astype(jnp.float32), preferred_element_type=jnp.float32)

    def by_head(columns_block, width):
        return columns_block.reshape(TOKENS, H, width).transpose(1, 0, 2)
    cot_heads = by_head(cotangent.astype(jnp.float32), VD)
    gradients = lax.map(head_grads, (by_head(query_pre, KD), by_head(key_pre, KD), by_head(value_pre, VD), decay_pre.T, beta_pre.T, cot_heads, rate_log, decay_bias, beta_bias))

    def by_rows(head_block):
        return head_block.transpose(1, 0, 2).reshape(TOKENS, -1).astype(jnp.bfloat16)
    grad_query = by_rows(gradients[0])
    grad_key = by_rows(gradients[1])
    grad_value = by_rows(gradients[2])
    grad_decay = gradients[3].T.astype(jnp.bfloat16)
    grad_beta = gradients[4].T.astype(jnp.bfloat16)
    heads_dev = H // N_INNER
    back = jnp.zeros((TOKENS, D), jnp.float32)
    for member in range(N_INNER):
        key_lo = member * heads_dev * KD
        key_hi = key_lo + heads_dev * KD
        val_lo = member * heads_dev * VD
        val_hi = val_lo + heads_dev * VD
        head_lo = member * heads_dev
        head_hi = head_lo + heads_dev
        partial_sum = jnp.dot(grad_query[:, key_lo:key_hi].astype(jnp.float32), query_weight[:, key_lo:key_hi].T.astype(jnp.float32), preferred_element_type=jnp.float32)
        partial_sum = partial_sum + jnp.dot(grad_key[:, key_lo:key_hi].astype(jnp.float32), key_weight[:, key_lo:key_hi].T.astype(jnp.float32), preferred_element_type=jnp.float32)
        partial_sum = partial_sum + jnp.dot(grad_value[:, val_lo:val_hi].astype(jnp.float32), value_weight[:, val_lo:val_hi].T.astype(jnp.float32), preferred_element_type=jnp.float32)
        partial_sum = partial_sum + jnp.dot(grad_decay[:, head_lo:head_hi].astype(jnp.float32), decay_weight[:, head_lo:head_hi].T.astype(jnp.float32), preferred_element_type=jnp.float32)
        partial_sum = partial_sum + jnp.dot(grad_beta[:, head_lo:head_hi].astype(jnp.float32), beta_weight[:, head_lo:head_hi].T.astype(jnp.float32), preferred_element_type=jnp.float32)
        back = back + to_wire(partial_sum)
    grad_mixed = norm_pull(back)[0].astype(jnp.bfloat16)
    return hidden * jnp.dot(grad_mixed.astype(jnp.float32), down_weight.T.astype(jnp.float32), preferred_element_type=jnp.float32)
```

```python
import functools
import math

import jax
import jax.numpy as jnp
from jax import lax
from jax.experimental import pallas as pl
from jax.experimental.pallas import tpu as pltpu
from jax.sharding import PartitionSpec as P

STEPS = 32


def from_behind(array, axis, by):
    devices = lax.axis_size(axis)
    pairs = [(i, i + by) for i in range(devices) if 0 <= i + by < devices]
    return lax.ppermute(array, axis, pairs)


def unit_rows(values):
    return values * lax.rsqrt(jnp.sum(values * values, axis=-1, keepdims=True) + 1e-06)


def head_inputs(query_rows, key_rows, decay_rows, beta_rows, log_rate, rate_shift, beta_shift):
    queries = unit_rows(query_rows) * query_rows.shape[-1] ** (-0.5)
    keys_unit = unit_rows(key_rows)
    log_decay = -jnp.exp(log_rate) * jax.nn.softplus(decay_rows + rate_shift)
    betas = jax.nn.sigmoid(beta_rows + beta_shift)
    return (queries, keys_unit, log_decay, betas)


def block_step(with_out, state, pieces):
    queries, keys_unit, values, log_decay, betas = pieces
    block_len = keys_unit.shape[0]
    highest = lax.Precision.HIGHEST
    cum_decay = jnp.cumsum(log_decay)
    row_ids = jnp.arange(block_len)[:, None]
    col_ids = jnp.arange(block_len)[None, :]
    lower_mask = row_ids >= col_ids
    decay_mat = jnp.where(
        lower_mask,
        jnp.exp(jnp.where(lower_mask, cum_decay[:, None] - cum_decay[None, :], 0.0)),
        0.0,
    )
    key_gram = jnp.dot(keys_unit, keys_unit.T, precision=highest)
    strict = jnp.where(row_ids > col_ids, betas[:, None] * decay_mat * key_gram, 0.0)
    system = strict + jnp.eye(block_len, dtype=jnp.float32)
    start_scale = jnp.exp(cum_decay)[:, None]
    target = betas[:, None] * (values - start_scale * jnp.dot(keys_unit, state, precision=highest))
    fresh_vals = lax.linalg.triangular_solve(
        system, target, left_side=True, lower=True, unit_diagonal=True
    )
    tail_keys = jnp.exp(cum_decay[-1] - cum_decay)[:, None] * keys_unit
    new_state = jnp.exp(cum_decay[-1]) * state + jnp.dot(tail_keys.T, fresh_vals, precision=highest)
    if with_out:
        scores = decay_mat * jnp.dot(queries, keys_unit.T, precision=highest)
        output = start_scale * jnp.dot(queries, state, precision=highest) + jnp.dot(
            scores, fresh_vals, precision=highest
        )
        return (new_state, output)
    return (new_state, None)


def run_blocks(queries, keys_unit, values, log_decay, betas, state, with_out):
    length = keys_unit.shape[0]
    block_len = math.gcd(64, length)
    block_count = length // block_len

    def blocked(array):
        return array.reshape((block_count, block_len) + array.shape[1:])

    step_fn = functools.partial(block_step, with_out)
    final_state, outputs = lax.scan(
        step_fn,
        state,
        (blocked(queries), blocked(keys_unit), blocked(values), blocked(log_decay), blocked(betas)),
    )
    if with_out:
        outputs = outputs.reshape((length,) + outputs.shape[2:])
    return (final_state, outputs)


def rms_scaled(values, gain):
    return values * lax.rsqrt(jnp.mean(values * values, axis=-1, keepdims=True) + 1e-06) * gain


def apply_map(matrix, state):
    return jnp.einsum("hij,hjv->hiv", matrix, state, precision=lax.Precision.HIGHEST)


def shards(
    tokens,
    step_index,
    embed_table,
    gain_one,
    gate_weight,
    up_weight,
    down_weight,
    gain_two,
    query_weight,
    key_weight,
    value_weight,
    decay_weight,
    beta_weight,
    rate_log,
    decay_bias,
    beta_bias,
    cotangent,
):
    columns = jnp.take(embed_table, tokens, axis=0)
    embedded = lax.all_gather(columns, "inner", axis=1, tiled=True)
    emb_float = embedded.astype(jnp.float32)
    normed_one = rms_scaled(emb_float, gain_one).astype(jnp.bfloat16)
    gate_rows = jnp.dot(normed_one, gate_weight, preferred_element_type=jnp.float32)
    up_rows = jnp.dot(normed_one, up_weight, preferred_element_type=jnp.float32)
    hidden = jax.nn.silu(gate_rows) * up_rows
    path_scale = (step_index[0].astype(jnp.float32) + 0.5) / STEPS
    scaled = (path_scale * hidden).astype(jnp.bfloat16)
    group_rows = tokens.shape[0]
    row_share = group_rows // lax.axis_size("inner")
    head_count = rate_log.shape[0]
    key_dim = query_weight.shape[1] // head_count
    value_dim = value_weight.shape[1] // head_count
    main_weight = jnp.concatenate([query_weight, key_weight, value_weight], axis=1)
    gate_pair = jnp.concatenate([decay_weight, beta_weight], axis=1)

    def normalize(values):
        return rms_scaled(values, gain_two)

    mixed_share = lax.psum_scatter(
        jnp.dot(scaled, down_weight, preferred_element_type=jnp.float32).astype(jnp.bfloat16),
        "inner",
        scatter_dimension=0,
        tiled=True,
    ).astype(jnp.float32)
    own_rows = lax.dynamic_slice_in_dim(
        emb_float, lax.axis_index("inner") * row_share, row_share, 0
    )
    normed_float, norm_pull = jax.vjp(normalize, own_rows + mixed_share)
    block_piece = lax.all_gather(normed_float.astype(jnp.bfloat16), "inner", axis=0, tiled=True)
    main_part = jnp.dot(block_piece, main_weight, preferred_element_type=jnp.float32)
    gate_part = jnp.dot(block_piece, gate_pair, preferred_element_type=jnp.float32)
    projected = jnp.concatenate([main_part, gate_part], axis=1)
    key_span = head_count * key_dim
    value_span = head_count * value_dim

    def by_head(columns_block, width):
        return columns_block.reshape(group_rows, head_count, width).transpose(1, 0, 2)

    query_pre = by_head(projected[:, :key_span], key_dim)
    key_pre = by_head(projected[:, key_span : 2 * key_span], key_dim)
    value_pre = by_head(projected[:, 2 * key_span : 2 * key_span + value_span], value_dim)
    gate_start = 2 * key_span + value_span
    decay_pre = projected[:, gate_start : gate_start + head_count].T
    beta_pre = projected[:, gate_start + head_count : gate_start + 2 * head_count].T
    cot_heads = by_head(cotangent.astype(jnp.float32), value_dim)

    def carry_map(key_rows, value_rows, decay_rows, beta_rows, log_rate, rate_shift, beta_shift):
        unused_query, keys_unit, log_decay, betas = head_inputs(
            key_rows, key_rows, decay_rows, beta_rows, log_rate, rate_shift, beta_shift
        )
        padded_vals = jnp.concatenate(
            [value_rows, jnp.zeros((key_rows.shape[0], key_dim), jnp.float32)], axis=1
        )
        start_state = jnp.concatenate(
            [jnp.zeros((key_dim, value_dim), jnp.float32), jnp.eye(key_dim, dtype=jnp.float32)],
            axis=1,
        )
        final_state, unused_out = run_blocks(
            keys_unit, keys_unit, padded_vals, log_decay, betas, start_state, False
        )
        return final_state

    joined_state = jax.vmap(carry_map)(
        key_pre, value_pre, decay_pre, beta_pre, rate_log, decay_bias, beta_bias
    )
    offset_state = joined_state[:, :, :value_dim]
    transition = joined_state[:, :, value_dim:]

    def forward_step(turn_index, carried):
        incoming = from_behind(carried[1].astype(jnp.bfloat16), "outer", 1).astype(jnp.float32)
        return (incoming, apply_map(transition, incoming) + offset_state)

    state_in, unused_end = lax.fori_loop(
        0, lax.axis_size("outer") - 1, forward_step, (jnp.zeros_like(offset_state), offset_state)
    )

    def local_score(query_in, key_in, value_in, decay_in, beta_in, start_in):

        def one_head(
            query_rows,
            key_rows,
            value_rows,
            decay_rows,
            beta_rows,
            start_state,
            cot_rows,
            log_rate,
            rate_shift,
            beta_shift,
        ):
            queries, keys_unit, log_decay, betas = head_inputs(
                query_rows, key_rows, decay_rows, beta_rows, log_rate, rate_shift, beta_shift
            )
            final_state, outputs = run_blocks(
                queries, keys_unit, value_rows, log_decay, betas, start_state, True
            )
            return (jnp.sum(outputs * cot_rows), final_state)

        head_scores, final_states = jax.vmap(one_head)(
            query_in,
            key_in,
            value_in,
            decay_in,
            beta_in,
            start_in,
            cot_heads,
            rate_log,
            decay_bias,
            beta_bias,
        )
        return (jnp.sum(head_scores), final_states)

    score_pair, pull_back = jax.vjp(
        local_score, query_pre, key_pre, value_pre, decay_pre, beta_pre, state_in
    )
    first_pull = pull_back((jnp.ones_like(score_pair[0]), jnp.zeros_like(score_pair[1])))
    grad_local = first_pull[5]
    grad_trans = jnp.swapaxes(transition, 1, 2)

    def backward_step(turn_index, carried):
        incoming = from_behind(carried[1].astype(jnp.bfloat16), "outer", -1).astype(jnp.float32)
        return (incoming, apply_map(grad_trans, incoming) + grad_local)

    state_grad, unused_start = lax.fori_loop(
        0, lax.axis_size("outer") - 1, backward_step, (jnp.zeros_like(grad_local), grad_local)
    )
    second_pull = pull_back((jnp.zeros_like(score_pair[0]), state_grad))
    summed = [first_pull[which] + second_pull[which] for which in range(5)]

    def by_rows(head_block):
        return head_block.transpose(1, 0, 2).reshape(group_rows, -1).astype(jnp.bfloat16)

    grad_main = jnp.concatenate(
        [by_rows(summed[0]), by_rows(summed[1]), by_rows(summed[2])], axis=1
    )
    grad_gates = jnp.concatenate(
        [summed[3].T.astype(jnp.bfloat16), summed[4].T.astype(jnp.bfloat16)], axis=1
    )
    main_part = jnp.dot(grad_main, main_weight.T, preferred_element_type=jnp.float32)
    back_share = lax.psum_scatter(
        (main_part + jnp.dot(grad_gates, gate_pair.T, preferred_element_type=jnp.float32)).astype(
            jnp.bfloat16
        ),
        "inner",
        scatter_dimension=0,
        tiled=True,
    ).astype(jnp.float32)
    grad_mixed = norm_pull(back_share)[0].astype(jnp.bfloat16)
    return hidden * jnp.dot(
        lax.all_gather(grad_mixed, "inner", axis=0, tiled=True),
        down_weight.T,
        preferred_element_type=jnp.float32,
    )


BF16 = jnp.bfloat16
F32 = jnp.float32
MIB = 1 << 20
VMEM = pl.BlockSpec(memory_space=pltpu.VMEM)
SMEM = pl.BlockSpec(memory_space=pltpu.SMEM)
HBM = pl.BlockSpec(memory_space=pl.ANY)


def call(kernel, out_shape, in_specs, scratch=(), limit=16 * MIB, flops=0, moved=0):
    return pl.pallas_call(
        kernel,
        out_shape=out_shape,
        in_specs=in_specs,
        out_specs=jax.tree.map(lambda _: VMEM, out_shape),
        scratch_shapes=list(scratch),
        compiler_params=pltpu.CompilerParams(vmem_limit_bytes=limit),
        cost_estimate=pl.CostEstimate(flops=flops, bytes_accessed=moved, transcendentals=0),
    )


def like(shape, dtype):
    return jax.ShapeDtypeStruct(shape, dtype)


def dot(a, b, transposed=False):
    dims = (((1,), (1 if transposed else 0,)), ((), ()))
    return lax.dot_general(a, b, dims, preferred_element_type=F32)


def mm(a, b, transposed=False):
    return dot(a.astype(BF16), b.astype(BF16), transposed)


def mm3(a, b):
    a_hi, b_hi = a.astype(BF16), b.astype(BF16)
    a_lo = (a - a_hi.astype(F32)).astype(BF16)
    b_lo = (b - b_hi.astype(F32)).astype(BF16)
    return dot(a_hi, b_hi) + (dot(a_hi, b_lo) + dot(a_lo, b_hi))


def row_sum(values):
    return jnp.sum(values, axis=-1, keepdims=True)


def spans(total, step):
    return [(at, min(step, total - at)) for at in range(0, total, step)]


def stream(pairs, sems):
    copies = [
        pltpu.make_async_copy(source, target, sems.at[which])
        for which, (source, target) in enumerate(pairs)
    ]
    for copy in copies:
        copy.start()
    return copies


def grid_ids(size):
    shape = (size, size)
    return lax.broadcasted_iota(jnp.int32, shape, 0), lax.broadcasted_iota(jnp.int32, shape, 1)


def in_order(pieces, target, rows_each):
    me = lax.axis_index("inner")
    for which, piece in enumerate(pieces):
        at = pl.multiple_of((me ^ which) * rows_each, rows_each)
        target[pl.ds(at, rows_each), :] = piece[...]


def embed_kernel(ids, id_row, table, out, blocks, sem):
    count = out.shape[0]

    @pl.loop(0, count)
    def _(which):
        base = pl.multiple_of((ids[which] // 16) * 16, 16)
        pltpu.make_async_copy(
            table.at[pl.ds(base, 16)], blocks.at[pl.ds(pl.multiple_of(which * 16, 16), 16)], sem
        ).start()

    row_ids, col_ids = grid_ids(count)
    low_bits = jnp.broadcast_to(id_row[...] & 15, (count, count))
    inside = row_sum(jnp.where(row_ids == col_ids, low_bits, 0).astype(F32)).astype(jnp.int32)
    wide = (count, 16 * count)
    wanted = lax.broadcasted_iota(jnp.int32, wide, 0) * 16 + inside
    pick = jnp.where(lax.broadcasted_iota(jnp.int32, wide, 1) == wanted, 1.0, 0.0).astype(BF16)
    pltpu.make_async_copy(table.at[pl.ds(0, 16 * count)], blocks, sem).wait()
    out[...] = dot(pick, blocks[...]).astype(BF16)


def feed_kernel(
    step, piece0, piece1, piece2, piece3, gain, gate, up, down,
    hidden, own_rows, part0, part1, part2, part3,
    gate_buf, up_buf, down_buf, emb, scaled, partial, sems,
):
    width = hidden.shape[1]
    cuts = spans(width, 512)
    outs = spans(down.shape[1], 512)
    pairs = []
    for at, size in cuts:
        pairs.append((gate.at[:, pl.ds(at, size)], gate_buf.at[:, pl.ds(at, size)]))
        pairs.append((up.at[:, pl.ds(at, size)], up_buf.at[:, pl.ds(at, size)]))
    for at, size in outs:
        pairs.append((down.at[:, pl.ds(at, size)], down_buf.at[:, pl.ds(at, size)]))
    copies = stream(pairs, sems)
    me = lax.axis_index("inner")
    share = piece0.shape[1]
    for which, piece in enumerate((piece0, piece1, piece2, piece3)):
        emb[:, pl.ds(pl.multiple_of((me ^ which) * share, share), share)] = piece[...]
    emb_float = emb[...].astype(F32)
    mean = jnp.mean(emb_float * emb_float, axis=-1, keepdims=True)
    normed = (emb_float * lax.rsqrt(mean + 1e-06) * gain[...]).astype(BF16)
    path_scale = (step[0].astype(F32) + 0.5) / STEPS
    for which, (at, size) in enumerate(cuts):
        copies[2 * which].wait()
        gate_rows = dot(normed, gate_buf[:, at : at + size])
        copies[2 * which + 1].wait()
        up_rows = dot(normed, up_buf[:, at : at + size])
        units = gate_rows / (1.0 + jnp.exp(-gate_rows)) * up_rows
        hidden[:, at : at + size] = units
        scaled[:, at : at + size] = (path_scale * units).astype(BF16)
    for which, (at, size) in enumerate(outs):
        copies[2 * len(cuts) + which].wait()
        partial[:, at : at + size] = dot(scaled[...], down_buf[:, at : at + size])
    rows = own_rows.shape[0]
    own_rows[...] = emb[pl.ds(pl.multiple_of(me * rows, rows), rows), :]
    for which, part in enumerate((part0, part1, part2, part3)):
        at = pl.multiple_of((me ^ which) * rows, rows)
        part[...] = partial[pl.ds(at, rows), :].astype(BF16)


def norm_kernel(own_rows, part0, part1, part2, part3, gain, mixed, normed):
    total = own_rows[...].astype(F32)
    for part in (part0, part1, part2, part3):
        total = total + part[...].astype(F32)
    mixed[...] = total
    mean = jnp.mean(total * total, axis=-1, keepdims=True)
    normed[...] = (total * lax.rsqrt(mean + 1e-06) * gain[...]).astype(BF16)


def project_kernel(
    piece0, piece1, piece2, piece3, query, key, value, decay, beta,
    own, send,
    query_buf, key_buf, value_buf, decay_buf, beta_buf, rows, sems,
):
    half_key = query.shape[1] // 2
    half_value = value.shape[1] // 2
    pairs = [(decay, decay_buf), (beta, beta_buf), (query, query_buf), (key, key_buf)]
    for side in range(2):
        span = pl.ds(side * half_value, half_value)
        pairs.append((value.at[:, span], value_buf.at[:, span]))
    copies = stream(pairs, sems)
    first = lax.axis_index("outer") % 2 == 0
    in_order((piece0, piece1, piece2, piece3), rows, piece0.shape[0])

    def put(at, low, high):
        size = low.shape[1]
        own[:, at : at + size] = jnp.where(first, low, high).astype(BF16)
        send[:, at : at + size] = jnp.where(first, high, low).astype(BF16)

    taken = rows[...]
    copies[0].wait()
    copies[1].wait()
    gates = (dot(taken, decay_buf[...]), dot(taken, beta_buf[...]))
    heads = decay.shape[1] // 2
    lanes = lax.broadcasted_iota(jnp.int32, (taken.shape[0], 128), 1)
    packed = []
    for side in range(2):
        lane, pack = 0, jnp.zeros((taken.shape[0], 128), F32)
        for values in gates:
            for head in range(side * heads, (side + 1) * heads):
                column = values[:, head : head + 1]
                top = column.astype(BF16).astype(F32)
                pack = jnp.where(lanes == lane, top, pack)
                pack = jnp.where(lanes == lane + 1, column - top, pack)
                lane += 2
        packed.append(pack)
    copies[2].wait()
    out = dot(taken, query_buf[...])
    put(0, out[:, :half_key], out[:, half_key:])
    copies[3].wait()
    out = dot(taken, key_buf[...])
    put(half_key, out[:, :half_key], out[:, half_key:])
    copies[4].wait()
    low = dot(taken, value_buf[:, :half_value])
    copies[5].wait()
    put(2 * half_key, low, dot(taken, value_buf[:, half_value:]))
    put(2 * half_key + half_value, *packed)


def both_blocks(own, other, target):
    core = lax.axis_index("outer") % 2
    size = own.shape[0]
    target[pl.ds(pl.multiple_of(core * size, size), size), :] = own[...]
    target[pl.ds(pl.multiple_of((1 - core) * size, size), size), :] = other[...]


def cumulate(chosen, column):
    top = column.astype(BF16)
    rest = column - top.astype(F32)
    middle = rest.astype(BF16)
    low = (rest - middle.astype(F32)).astype(BF16)
    picked = jnp.where(chosen, 1.0, 0.0).astype(BF16)

    def part(values):
        return dot(picked, jnp.broadcast_to(values, (values.shape[0], 128)))

    return part(top) + (part(middle) + part(low))


def unit_inverse(strict):
    size = strict.shape[0]
    row_ids, col_ids = grid_ids(size)
    inverse = jnp.where(row_ids == col_ids, 1.0, 0.0)
    inverse = inverse - jnp.where(row_ids // 2 == col_ids // 2, strict, 0.0)
    block = 2
    while block < size:
        below = (row_ids // (2 * block) == col_ids // (2 * block)) & (
            row_ids // block != col_ids // block
        )
        inverse = inverse - mm3(mm3(inverse, jnp.where(below, strict, 0.0)), inverse)
        block *= 2
    return inverse


def front_kernel(
    own, other, cot_own, cot_other, rate_log, decay_bias, beta_bias,
    packs, cots, sent, kept_offset, kept_map,
    decay_mats, grams, inverses, scores, maps, fresh, pulled, columns,
):
    both_blocks(own, other, packs)
    both_blocks(cot_own, cot_other, cots)
    heads, length, _ = decay_mats.shape
    key_dim, value_dim = maps.shape[2], fresh.shape[2]
    place = lax.axis_index("outer")
    even = (place // 2) % 2 == 0
    first_head = (place % 2) * heads
    row_ids, col_ids = grid_ids(length)
    lower, strictly = row_ids >= col_ids, row_ids > col_ids
    lanes = lax.broadcasted_iota(jnp.int32, (length, 128), 1)
    gate_at = heads * (2 * key_dim + value_dim)
    gates = packs[:, gate_at : gate_at + 128].astype(F32)
    for head in range(heads):
        at = head * key_dim
        query_rows = packs[:, at : at + key_dim].astype(F32)
        at += heads * key_dim
        key_rows = packs[:, at : at + key_dim].astype(F32)
        at = 2 * heads * key_dim + head * value_dim
        values = packs[:, at : at + value_dim].astype(F32)
        cot = cots[:, head * value_dim : (head + 1) * value_dim]
        lane = 2 * head
        decay_in = gates[:, lane : lane + 1] + gates[:, lane + 1 : lane + 2]
        decay_in = decay_in + decay_bias[first_head + head]
        lane += 2 * heads
        beta_in = gates[:, lane : lane + 1] + gates[:, lane + 1 : lane + 2]
        beta_in = beta_in + beta_bias[first_head + head]
        rate = jnp.exp(jnp.full((length, 1), rate_log[first_head + head], F32))
        query_scale = lax.rsqrt(row_sum(query_rows * query_rows) + 1e-06) * key_dim ** (-0.5)
        key_scale = lax.rsqrt(row_sum(key_rows * key_rows) + 1e-06)
        queries, keys_unit = query_rows * query_scale, key_rows * key_scale
        log_decay = -rate * (jnp.maximum(decay_in, 0.0) + jnp.log1p(jnp.exp(-jnp.abs(decay_in))))
        betas = 1.0 / (1.0 + jnp.exp(-beta_in))
        cum = cumulate(lower, log_decay)
        decay_mat = jnp.where(
            lower, jnp.exp(jnp.where(lower, cum - jnp.transpose(cum), 0.0)), 0.0
        )
        total = cum[:, :1]
        start_scale = jnp.exp(total)
        tail_scale = jnp.exp(total[length - 1 :] - total)
        gram = jnp.where(strictly, decay_mat * mm(keys_unit, keys_unit, True), 0.0)
        inverse = unit_inverse(betas * gram)
        score = decay_mat * mm(queries, keys_unit, True)
        state_map = mm(inverse, (betas * start_scale) * keys_unit)
        fresh_vals = mm(inverse, betas * values)
        tail_t = jnp.transpose(tail_scale * keys_unit)
        transition = jnp.where(row_ids == col_ids, start_scale[length - 1 :], 0.0) - mm(
            tail_t, state_map
        )
        offset = mm(tail_t, fresh_vals)
        score_pull = mm(jnp.transpose(score), cot)
        grad_local = mm(jnp.transpose(start_scale * queries), cot) - mm(
            jnp.transpose(state_map), score_pull
        )
        flipped = jnp.transpose(transition)
        sent[head, :, :value_dim] = jnp.where(even, offset, grad_local).astype(BF16)
        sent[head, :, value_dim:] = jnp.where(even, transition, flipped).astype(BF16)
        kept_offset[head] = jnp.where(even, grad_local, offset)
        kept_map[head] = jnp.where(even, flipped, transition).astype(BF16)
        decay_mats[head] = decay_mat
        grams[head] = gram
        inverses[head] = jnp.transpose(inverse).astype(BF16)
        scores[head] = score
        maps[head] = state_map.astype(BF16)
        fresh[head] = fresh_vals
        pulled[head] = score_pull
        pack = jnp.zeros((length, 128), F32)
        for lane, column in enumerate(
            (query_scale, key_scale, betas, start_scale, tail_scale, decay_in, rate)
        ):
            pack = jnp.where(lanes == lane, column, pack)
        columns[head] = pack


def combine_kernel(kept_map, kept_offset, got, out):
    value_dim = out.shape[2]
    for head in range(out.shape[0]):
        joined = dot(kept_map[head], got[head, :, :value_dim]) + kept_offset[head]
        out[head] = joined.astype(BF16)


def back_kernel(
    near, far_one, far_two, packs, cots,
    decay_mats, grams, inverses, scores, maps, fresh, pulled, columns,
    own, send, grads,
):
    heads, length, _ = decay_mats.shape
    key_dim, value_dim = maps.shape[2], fresh.shape[2]
    place = lax.axis_index("outer")
    core, chip = place % 2, place // 2
    outer_chip = (chip == 0) | (chip == 3)
    odd = chip % 2 == 1
    row_ids, col_ids = grid_ids(length)
    strictly, upper = row_ids > col_ids, row_ids <= col_ids
    lanes = lax.broadcasted_iota(jnp.int32, (length, 128), 1)
    gate_at = heads * (2 * key_dim + value_dim)
    gate_grads = jnp.zeros((length, 128), F32)
    for head in range(heads):
        at = head * key_dim
        query_rows = packs[:, at : at + key_dim].astype(F32)
        key_at = at + heads * key_dim
        key_rows = packs[:, key_at : key_at + key_dim].astype(F32)
        value_at = 2 * heads * key_dim + head * value_dim
        values = packs[:, value_at : value_at + value_dim].astype(F32)
        cot = cots[:, head * value_dim : (head + 1) * value_dim]
        pack = columns[head]
        query_scale, key_scale, betas = pack[:, 0:1], pack[:, 1:2], pack[:, 2:3]
        start_scale, tail_scale = pack[:, 3:4], pack[:, 4:5]
        decay_in, rate = pack[:, 5:6], pack[:, 6:7]
        end_scale = start_scale[length - 1 :]
        queries, keys_unit = query_rows * query_scale, key_rows * key_scale
        decay_mat, gram, score = decay_mats[head], grams[head], scores[head]
        far = far_one[head] + far_two[head]
        close = near[head, :, :value_dim].astype(F32)
        reached = dot(near[head, :, value_dim:], far) + close
        first = jnp.where(outer_chip, reached, close)
        second = jnp.where(outer_chip, 0.0, far.astype(F32))
        state = jnp.where(odd, first, second)
        state_grad = jnp.where(odd, second, first)
        state_half, state_grad_half = state.astype(BF16), state_grad.astype(BF16)
        new_vals = fresh[head] - dot(maps[head], state_half)
        new_half = new_vals.astype(BF16)
        grad_new = pulled[head] + mm(tail_scale * keys_unit, state_grad_half)
        grad_target = mm(inverses[head], grad_new)
        target_half = grad_target.astype(BF16)
        grad_score = dot(cot, new_half, True)
        grad_sys = jnp.where(strictly, -dot(target_half, new_half, True), 0.0)
        cot_state = dot(cot, state_half, True)
        target_state = dot(target_half, state_half, True)
        new_state = dot(new_half, state_grad_half, True)
        weighted = decay_mat * grad_score
        grad_gram = grad_sys * decay_mat * betas
        grad_query = mm(weighted, keys_unit) + start_scale * cot_state
        grad_key = (
            mm(jnp.transpose(weighted), queries)
            + mm(grad_gram + jnp.transpose(grad_gram), keys_unit)
            + tail_scale * new_state
            - (betas * start_scale) * target_state
        )
        key_target = row_sum(keys_unit * target_state)
        sys_gram = grad_sys * gram
        grad_beta = row_sum(grad_target * values) - start_scale * key_target + row_sum(sys_gram)
        both = score * grad_score + betas * sys_gram
        tails = tail_scale * row_sum(keys_unit * new_state)
        grad_cum = (
            row_sum(both - jnp.transpose(both))
            + start_scale * row_sum(queries * cot_state)
            - (betas * start_scale) * key_target
            - tails
        )
        ending = jnp.sum(tails, axis=0, keepdims=True) + end_scale * jnp.sum(
            row_sum(state * state_grad), axis=0, keepdims=True
        )
        grad_log = cumulate(upper, grad_cum)[:, :1] + ending
        grad_decay = grad_log * -rate / (1.0 + jnp.exp(-decay_in))
        grad_beta = grad_beta * betas * (1.0 - betas)
        units = queries * key_dim**0.5
        grad_query = query_scale * (grad_query - units * row_sum(units * grad_query))
        grad_key = key_scale * (grad_key - keys_unit * row_sum(keys_unit * grad_key))
        grads[:, at : at + key_dim] = grad_query.astype(BF16)
        grads[:, key_at : key_at + key_dim] = grad_key.astype(BF16)
        grads[:, value_at : value_at + value_dim] = (betas * grad_target).astype(BF16)
        gate_grads = jnp.where(lanes == head, grad_decay, gate_grads)
        gate_grads = jnp.where(lanes == heads + head, grad_beta, gate_grads)
    grads[:, gate_at : gate_at + 128] = gate_grads.astype(BF16)
    size = own.shape[0]
    own[...] = grads[pl.ds(pl.multiple_of(core * size, size), size), :]
    send[...] = grads[pl.ds(pl.multiple_of((1 - core) * size, size), size), :]


def return_kernel(
    own, other, query, key, value, decay, beta,
    part0, part1, part2, part3,
    query_buf, key_buf, value_buf, decay_buf, beta_buf, total, sems,
):
    half_key = query.shape[1] // 2
    half_value = value.shape[1] // 2
    pairs = [(query, query_buf), (key, key_buf), (value, value_buf)]
    pairs += [(decay, decay_buf), (beta, beta_buf)]
    copies = stream(pairs, sems)
    first = lax.axis_index("outer") % 2 == 0

    def sides(at, size):
        mine, yours = own[:, at : at + size], other[:, at : at + size]
        return jnp.concatenate(
            [jnp.where(first, mine, yours), jnp.where(first, yours, mine)], axis=1
        )

    gate_at = 2 * half_key + half_value
    heads = decay.shape[1] // 2
    copies[0].wait()
    sums = dot(sides(0, half_key), query_buf[...], True)
    copies[1].wait()
    sums = sums + dot(sides(half_key, half_key), key_buf[...], True)
    copies[2].wait()
    sums = sums + dot(sides(2 * half_key, half_value), value_buf[...], True)
    copies[3].wait()
    sums = sums + dot(sides(gate_at, heads), decay_buf[...], True)
    copies[4].wait()
    sums = sums + dot(sides(gate_at + heads, heads), beta_buf[...], True)
    total[...] = sums
    rows = part0.shape[0]
    me = lax.axis_index("inner")
    for which, part in enumerate((part0, part1, part2, part3)):
        at = pl.multiple_of((me ^ which) * rows, rows)
        part[...] = total[pl.ds(at, rows), :].astype(BF16)


def pull_kernel(part0, part1, part2, part3, mixed, gain, out):
    total = part0[...].astype(F32)
    for part in (part1, part2, part3):
        total = total + part[...].astype(F32)
    rows = mixed[...]
    scale = lax.rsqrt(jnp.mean(rows * rows, axis=-1, keepdims=True) + 1e-06)
    gained = total * gain[...]
    along = jnp.mean(rows * gained, axis=-1, keepdims=True)
    out[...] = (scale * gained - rows * (scale * scale * scale * along)).astype(BF16)


def final_kernel(piece0, piece1, piece2, piece3, hidden, down, out, down_buf, rows, sems):
    cuts = spans(down.shape[0], 512)
    copies = stream(
        [(down.at[pl.ds(at, size)], down_buf.at[pl.ds(at, size)]) for at, size in cuts], sems
    )
    in_order((piece0, piece1, piece2, piece3), rows, piece0.shape[0])
    taken = rows[...]
    for which, (at, size) in enumerate(cuts):
        copies[which].wait()
        product = dot(taken, down_buf[at : at + size, :], True)
        out[:, at : at + size] = hidden[:, at : at + size] * product


def swap(array, axis, bit):
    return lax.ppermute(array, axis, [(i, i ^ bit) for i in range(lax.axis_size(axis))])


def swap_inner(arrays):
    return [swap(array, "inner", which + 1) for which, array in enumerate(arrays)]


def four_chips(
    tokens, step_index, embed_table, gain_one, gate_weight, up_weight, down_weight, gain_two,
    query_weight, key_weight, value_weight, decay_weight, beta_weight,
    rate_log, decay_bias, beta_bias, cotangent,
):
    count, model = tokens.shape[0], gain_one.shape[0]
    width = gate_weight.shape[1]
    share = count // 4
    head_count = rate_log.shape[0]
    heads = head_count // 2
    key_dim = query_weight.shape[1] // head_count
    value_dim = value_weight.shape[1] // head_count
    pack_width = heads * (2 * key_dim + value_dim) + 128
    length = 2 * count
    rows_shape = like((share, model), BF16)
    dma = pltpu.SemaphoreType.DMA

    def weight_scratch():
        return [
            pltpu.VMEM(weight.shape, BF16)
            for weight in (query_weight, key_weight, value_weight, decay_weight, beta_weight)
        ]

    weight_args = (query_weight, key_weight, value_weight, decay_weight, beta_weight)
    cot_half = heads * value_dim
    core = lax.axis_index("outer") % 2
    cot_own = lax.dynamic_slice_in_dim(cotangent, core * cot_half, cot_half, 1)
    cot_send = lax.dynamic_slice_in_dim(cotangent, (1 - core) * cot_half, cot_half, 1)
    cot_other = swap(cot_send, "outer", 1)

    columns = call(
        embed_kernel,
        like((count, embed_table.shape[1]), BF16),
        [SMEM, VMEM, HBM],
        [pltpu.VMEM((16 * count, embed_table.shape[1]), BF16), dma],
    )(tokens, tokens.reshape(1, count), embed_table)
    pieces = [columns] + swap_inner([columns] * 3)
    hidden, own_rows, *parts = call(
        feed_kernel,
        [like((count, width), F32)] + [rows_shape] * 5,
        [SMEM] + [VMEM] * 5 + [HBM] * 3,
        [
            pltpu.VMEM((model, width), BF16),
            pltpu.VMEM((model, width), BF16),
            pltpu.VMEM((width, model), BF16),
            pltpu.VMEM((count, model), BF16),
            pltpu.VMEM((count, width), BF16),
            pltpu.VMEM((count, model), F32),
            dma((2 * len(spans(width, 512)) + len(spans(model, 512)),)),
        ],
        limit=32 * MIB,
    )(step_index, *pieces, gain_one.reshape(1, model), gate_weight, up_weight, down_weight)
    parts = [parts[0]] + swap_inner(parts[1:])
    mixed, normed = call(
        norm_kernel, [like((share, model), F32), rows_shape], [VMEM] * 6
    )(own_rows, *parts, gain_two.reshape(1, model))
    pieces = [normed] + swap_inner([normed] * 3)
    own, send = call(
        project_kernel,
        [like((count, pack_width), BF16)] * 2,
        [VMEM] * 4 + [HBM] * 5,
        weight_scratch() + [pltpu.VMEM((count, model), BF16), dma((6,))],
        limit=24 * MIB,
    )(*pieces, *weight_args)
    other = swap(send, "outer", 1)
    square = (heads, length, length)
    valued = (heads, length, value_dim)
    packs, cots, sent, kept_offset, kept_map, *saved = call(
        front_kernel,
        [
            like((length, pack_width), BF16),
            like((length, cot_half), BF16),
            like((heads, key_dim, value_dim + key_dim), BF16),
            like((heads, key_dim, value_dim), F32),
            like((heads, key_dim, key_dim), BF16),
            like(square, F32),
            like(square, F32),
            like(square, BF16),
            like(square, F32),
            like((heads, length, key_dim), BF16),
            like(valued, F32),
            like(valued, F32),
            like((heads, length, 128), F32),
        ],
        [VMEM] * 4 + [SMEM] * 3,
    )(own, other, cot_own, cot_other, rate_log, decay_bias, beta_bias)
    near = swap(sent, "outer", 2)
    joined = call(
        combine_kernel, like((heads, key_dim, value_dim), BF16), [VMEM] * 3
    )(kept_map, kept_offset, near)
    far_one = lax.ppermute(joined, "outer", [(2, 4), (3, 5), (4, 2), (5, 3)])
    far_two = lax.ppermute(joined, "outer", [(2, 6), (3, 7), (4, 0), (5, 1)])
    own, send = call(
        back_kernel,
        [like((count, pack_width), BF16)] * 2,
        [VMEM] * 13,
        [pltpu.VMEM((length, pack_width), BF16)],
    )(near, far_one, far_two, packs, cots, *saved)
    other = swap(send, "outer", 1)
    parts = call(
        return_kernel,
        [rows_shape] * 4,
        [VMEM] * 2 + [HBM] * 5,
        weight_scratch() + [pltpu.VMEM((count, model), F32), dma((5,))],
        limit=24 * MIB,
    )(own, other, *weight_args)
    parts = [parts[0]] + swap_inner(parts[1:])
    grad = call(pull_kernel, rows_shape, [VMEM] * 6)(*parts, mixed, gain_two.reshape(1, model))
    pieces = [grad] + swap_inner([grad] * 3)
    return call(
        final_kernel,
        like((count, width), F32),
        [VMEM] * 5 + [HBM],
        [
            pltpu.VMEM((width, model), BF16),
            pltpu.VMEM((count, model), BF16),
            dma((len(spans(width, 512)),)),
        ],
        limit=16 * MIB,
    )(*pieces, hidden, down_weight)


def local_part(*args):
    fits = (
        lax.axis_size("inner") == 4
        and lax.axis_size("outer") == 8
        and args[0].shape[0] == 64
        and args[13].shape[0] % 2 == 0
    )
    return four_chips(*args) if fits else shards(*args)


def solution(mesh):
    placed = (
        P("outer"),
        P(),
        P(None, "inner"),
        P(),
        P(None, "inner"),
        P(None, "inner"),
        P("inner", None),
        P(),
        P(None, "inner"),
        P(None, "inner"),
        P(None, "inner"),
        P(None, "inner"),
        P(None, "inner"),
        P("inner"),
        P("inner"),
        P("inner"),
        P("outer", "inner"),
    )
    return jax.shard_map(
        local_part, mesh=mesh, in_specs=placed, out_specs=P("outer", "inner"), check_vma=False
    )
```

```python
import functools
import math

import jax
import jax.numpy as jnp
from jax import lax
from jax.experimental import pallas as pl
from jax.experimental.pallas import tpu as pltpu
from jax.sharding import PartitionSpec as P

STEPS = 32


def from_behind(array, axis, by):
    devices = lax.axis_size(axis)
    pairs = [(i, i + by) for i in range(devices) if 0 <= i + by < devices]
    return lax.ppermute(array, axis, pairs)


def unit_rows(values):
    return values * lax.rsqrt(jnp.sum(values * values, axis=-1, keepdims=True) + 1e-06)


def head_inputs(query_rows, key_rows, decay_rows, beta_rows, log_rate, rate_shift, beta_shift):
    queries = unit_rows(query_rows) * query_rows.shape[-1] ** (-0.5)
    keys_unit = unit_rows(key_rows)
    log_decay = -jnp.exp(log_rate) * jax.nn.softplus(decay_rows + rate_shift)
    betas = jax.nn.sigmoid(beta_rows + beta_shift)
    return (queries, keys_unit, log_decay, betas)


def block_step(with_out, state, pieces):
    queries, keys_unit, values, log_decay, betas = pieces
    block_len = keys_unit.shape[0]
    highest = lax.Precision.HIGHEST
    cum_decay = jnp.cumsum(log_decay)
    row_ids = jnp.arange(block_len)[:, None]
    col_ids = jnp.arange(block_len)[None, :]
    lower_mask = row_ids >= col_ids
    decay_mat = jnp.where(
        lower_mask,
        jnp.exp(jnp.where(lower_mask, cum_decay[:, None] - cum_decay[None, :], 0.0)),
        0.0,
    )
    key_gram = jnp.dot(keys_unit, keys_unit.T, precision=highest)
    strict = jnp.where(row_ids > col_ids, betas[:, None] * decay_mat * key_gram, 0.0)
    system = strict + jnp.eye(block_len, dtype=jnp.float32)
    start_scale = jnp.exp(cum_decay)[:, None]
    target = betas[:, None] * (values - start_scale * jnp.dot(keys_unit, state, precision=highest))
    fresh_vals = lax.linalg.triangular_solve(
        system, target, left_side=True, lower=True, unit_diagonal=True
    )
    tail_keys = jnp.exp(cum_decay[-1] - cum_decay)[:, None] * keys_unit
    new_state = jnp.exp(cum_decay[-1]) * state + jnp.dot(tail_keys.T, fresh_vals, precision=highest)
    if with_out:
        scores = decay_mat * jnp.dot(queries, keys_unit.T, precision=highest)
        output = start_scale * jnp.dot(queries, state, precision=highest) + jnp.dot(
            scores, fresh_vals, precision=highest
        )
        return (new_state, output)
    return (new_state, None)


def run_blocks(queries, keys_unit, values, log_decay, betas, state, with_out):
    length = keys_unit.shape[0]
    block_len = math.gcd(64, length)
    block_count = length // block_len

    def blocked(array):
        return array.reshape((block_count, block_len) + array.shape[1:])

    step_fn = functools.partial(block_step, with_out)
    final_state, outputs = lax.scan(
        step_fn,
        state,
        (blocked(queries), blocked(keys_unit), blocked(values), blocked(log_decay), blocked(betas)),
    )
    if with_out:
        outputs = outputs.reshape((length,) + outputs.shape[2:])
    return (final_state, outputs)


def rms_scaled(values, gain):
    return values * lax.rsqrt(jnp.mean(values * values, axis=-1, keepdims=True) + 1e-06) * gain


def apply_map(matrix, state):
    return jnp.einsum("hij,hjv->hiv", matrix, state, precision=lax.Precision.HIGHEST)


def shards(
    tokens,
    step_index,
    embed_table,
    gain_one,
    gate_weight,
    up_weight,
    down_weight,
    gain_two,
    query_weight,
    key_weight,
    value_weight,
    decay_weight,
    beta_weight,
    rate_log,
    decay_bias,
    beta_bias,
    cotangent,
):
    columns = jnp.take(embed_table, tokens, axis=0)
    embedded = lax.all_gather(columns, "inner", axis=1, tiled=True)
    emb_float = embedded.astype(jnp.float32)
    normed_one = rms_scaled(emb_float, gain_one).astype(jnp.bfloat16)
    gate_rows = jnp.dot(normed_one, gate_weight, preferred_element_type=jnp.float32)
    up_rows = jnp.dot(normed_one, up_weight, preferred_element_type=jnp.float32)
    hidden = jax.nn.silu(gate_rows) * up_rows
    path_scale = (step_index[0].astype(jnp.float32) + 0.5) / STEPS
    scaled = (path_scale * hidden).astype(jnp.bfloat16)
    group_rows = tokens.shape[0]
    row_share = group_rows // lax.axis_size("inner")
    head_count = rate_log.shape[0]
    key_dim = query_weight.shape[1] // head_count
    value_dim = value_weight.shape[1] // head_count
    main_weight = jnp.concatenate([query_weight, key_weight, value_weight], axis=1)
    gate_pair = jnp.concatenate([decay_weight, beta_weight], axis=1)

    def normalize(values):
        return rms_scaled(values, gain_two)

    mixed_share = lax.psum_scatter(
        jnp.dot(scaled, down_weight, preferred_element_type=jnp.float32).astype(jnp.bfloat16),
        "inner",
        scatter_dimension=0,
        tiled=True,
    ).astype(jnp.float32)
    own_rows = lax.dynamic_slice_in_dim(
        emb_float, lax.axis_index("inner") * row_share, row_share, 0
    )
    normed_float, norm_pull = jax.vjp(normalize, own_rows + mixed_share)
    block_piece = lax.all_gather(normed_float.astype(jnp.bfloat16), "inner", axis=0, tiled=True)
    main_part = jnp.dot(block_piece, main_weight, preferred_element_type=jnp.float32)
    gate_part = jnp.dot(block_piece, gate_pair, preferred_element_type=jnp.float32)
    projected = jnp.concatenate([main_part, gate_part], axis=1)
    key_span = head_count * key_dim
    value_span = head_count * value_dim

    def by_head(columns_block, width):
        return columns_block.reshape(group_rows, head_count, width).transpose(1, 0, 2)

    query_pre = by_head(projected[:, :key_span], key_dim)
    key_pre = by_head(projected[:, key_span : 2 * key_span], key_dim)
    value_pre = by_head(projected[:, 2 * key_span : 2 * key_span + value_span], value_dim)
    gate_start = 2 * key_span + value_span
    decay_pre = projected[:, gate_start : gate_start + head_count].T
    beta_pre = projected[:, gate_start + head_count : gate_start + 2 * head_count].T
    cot_heads = by_head(cotangent.astype(jnp.float32), value_dim)

    def carry_map(key_rows, value_rows, decay_rows, beta_rows, log_rate, rate_shift, beta_shift):
        unused_query, keys_unit, log_decay, betas = head_inputs(
            key_rows, key_rows, decay_rows, beta_rows, log_rate, rate_shift, beta_shift
        )
        padded_vals = jnp.concatenate(
            [value_rows, jnp.zeros((key_rows.shape[0], key_dim), jnp.float32)], axis=1
        )
        start_state = jnp.concatenate(
            [jnp.zeros((key_dim, value_dim), jnp.float32), jnp.eye(key_dim, dtype=jnp.float32)],
            axis=1,
        )
        final_state, unused_out = run_blocks(
            keys_unit, keys_unit, padded_vals, log_decay, betas, start_state, False
        )
        return final_state

    joined_state = jax.vmap(carry_map)(
        key_pre, value_pre, decay_pre, beta_pre, rate_log, decay_bias, beta_bias
    )
    offset_state = joined_state[:, :, :value_dim]
    transition = joined_state[:, :, value_dim:]

    def forward_step(turn_index, carried):
        incoming = from_behind(carried[1].astype(jnp.bfloat16), "outer", 1).astype(jnp.float32)
        return (incoming, apply_map(transition, incoming) + offset_state)

    state_in, unused_end = lax.fori_loop(
        0, lax.axis_size("outer") - 1, forward_step, (jnp.zeros_like(offset_state), offset_state)
    )

    def local_score(query_in, key_in, value_in, decay_in, beta_in, start_in):

        def one_head(
            query_rows,
            key_rows,
            value_rows,
            decay_rows,
            beta_rows,
            start_state,
            cot_rows,
            log_rate,
            rate_shift,
            beta_shift,
        ):
            queries, keys_unit, log_decay, betas = head_inputs(
                query_rows, key_rows, decay_rows, beta_rows, log_rate, rate_shift, beta_shift
            )
            final_state, outputs = run_blocks(
                queries, keys_unit, value_rows, log_decay, betas, start_state, True
            )
            return (jnp.sum(outputs * cot_rows), final_state)

        head_scores, final_states = jax.vmap(one_head)(
            query_in,
            key_in,
            value_in,
            decay_in,
            beta_in,
            start_in,
            cot_heads,
            rate_log,
            decay_bias,
            beta_bias,
        )
        return (jnp.sum(head_scores), final_states)

    score_pair, pull_back = jax.vjp(
        local_score, query_pre, key_pre, value_pre, decay_pre, beta_pre, state_in
    )
    first_pull = pull_back((jnp.ones_like(score_pair[0]), jnp.zeros_like(score_pair[1])))
    grad_local = first_pull[5]
    grad_trans = jnp.swapaxes(transition, 1, 2)

    def backward_step(turn_index, carried):
        incoming = from_behind(carried[1].astype(jnp.bfloat16), "outer", -1).astype(jnp.float32)
        return (incoming, apply_map(grad_trans, incoming) + grad_local)

    state_grad, unused_start = lax.fori_loop(
        0, lax.axis_size("outer") - 1, backward_step, (jnp.zeros_like(grad_local), grad_local)
    )
    second_pull = pull_back((jnp.zeros_like(score_pair[0]), state_grad))
    summed = [first_pull[which] + second_pull[which] for which in range(5)]

    def by_rows(head_block):
        return head_block.transpose(1, 0, 2).reshape(group_rows, -1).astype(jnp.bfloat16)

    grad_main = jnp.concatenate(
        [by_rows(summed[0]), by_rows(summed[1]), by_rows(summed[2])], axis=1
    )
    grad_gates = jnp.concatenate(
        [summed[3].T.astype(jnp.bfloat16), summed[4].T.astype(jnp.bfloat16)], axis=1
    )
    main_part = jnp.dot(grad_main, main_weight.T, preferred_element_type=jnp.float32)
    back_share = lax.psum_scatter(
        (main_part + jnp.dot(grad_gates, gate_pair.T, preferred_element_type=jnp.float32)).astype(
            jnp.bfloat16
        ),
        "inner",
        scatter_dimension=0,
        tiled=True,
    ).astype(jnp.float32)
    grad_mixed = norm_pull(back_share)[0].astype(jnp.bfloat16)
    return hidden * jnp.dot(
        lax.all_gather(grad_mixed, "inner", axis=0, tiled=True),
        down_weight.T,
        preferred_element_type=jnp.float32,
    )


BF16 = jnp.bfloat16
F32 = jnp.float32
MIB = 1 << 20
FETCH_PARTS = 4
TURN_ROWS = 128
VMEM = pl.BlockSpec(memory_space=pltpu.VMEM)
SMEM = pl.BlockSpec(memory_space=pltpu.SMEM)
HBM = pl.BlockSpec(memory_space=pl.ANY)


def pinned(array):
    return pltpu.with_memory_space_constraint(array, pltpu.HBM)


def call(kernel, out_shape, in_specs, scratch=(), limit=16 * MIB, flops=0, moved=0):
    return pl.pallas_call(
        kernel,
        out_shape=out_shape,
        in_specs=in_specs,
        out_specs=jax.tree.map(lambda _: VMEM, out_shape),
        scratch_shapes=list(scratch),
        compiler_params=pltpu.CompilerParams(vmem_limit_bytes=limit),
        cost_estimate=pl.CostEstimate(flops=flops, bytes_accessed=moved, transcendentals=0),
    )


def like(shape, dtype):
    return jax.ShapeDtypeStruct(shape, dtype)


def dot(a, b, transposed=False):
    dims = (((1,), (1 if transposed else 0,)), ((), ()))
    return lax.dot_general(a, b, dims, preferred_element_type=F32)


def mm(a, b, transposed=False):
    return dot(a.astype(BF16), b.astype(BF16), transposed)


def mm3(a, b):
    a_hi, b_hi = a.astype(BF16), b.astype(BF16)
    a_lo = (a - a_hi.astype(F32)).astype(BF16)
    b_lo = (b - b_hi.astype(F32)).astype(BF16)
    return dot(a_hi, b_hi) + (dot(a_hi, b_lo) + dot(a_lo, b_hi))


def row_sum(values):
    return jnp.sum(values, axis=-1, keepdims=True)


def spans(total, step):
    return [(at, min(step, total - at)) for at in range(0, total, step)]


def stream(pairs, sems):
    copies = [
        pltpu.make_async_copy(source, target, sems.at[which])
        for which, (source, target) in enumerate(pairs)
    ]
    for copy in copies:
        copy.start()
    return copies


def grid_ids(size):
    shape = (size, size)
    return lax.broadcasted_iota(jnp.int32, shape, 0), lax.broadcasted_iota(jnp.int32, shape, 1)


def quarters(source, target):
    cuts = spans(source.shape[0], source.shape[0] // FETCH_PARTS)
    return [(source.at[pl.ds(at, size)], target.at[pl.ds(at, size)]) for at, size in cuts]


def embed_kernel(
    ids_in, table, cot, out, cot_own, cot_send,
    ids, id_row, blocks, id_sems, sem, cot_sems,
):
    count = out.shape[0]
    copies = stream([(ids_in, ids), (ids_in, id_row)], id_sems)
    copies[0].wait()
    for which in range(count):
        base = pl.multiple_of((ids[0, which] // 16) * 16, 16)
        pltpu.make_async_copy(
            table.at[pl.ds(base, 16)], blocks.at[pl.ds(which * 16, 16)], sem
        ).start()
    core, half = lax.axis_index("outer") % 2, cot_own.shape[1]
    mine = pl.ds(pl.multiple_of(core * half, half), half)
    yours = pl.ds(pl.multiple_of((1 - core) * half, half), half)
    halves = stream([(cot.at[:, mine], cot_own), (cot.at[:, yours], cot_send)], cot_sems)
    copies[1].wait()
    row_ids, col_ids = grid_ids(count)
    low_bits = jnp.broadcast_to(id_row[...] & 15, (count, count))
    inside = row_sum(jnp.where(row_ids == col_ids, low_bits, 0).astype(F32)).astype(jnp.int32)
    wide = (count, 16 * count)
    wanted = lax.broadcasted_iota(jnp.int32, wide, 0) * 16 + inside
    pick = jnp.where(lax.broadcasted_iota(jnp.int32, wide, 1) == wanted, 1.0, 0.0).astype(BF16)
    pltpu.make_async_copy(table.at[pl.ds(0, 16 * count)], blocks, sem).wait()
    out[...] = dot(pick, blocks[...]).astype(BF16)
    for copy in halves:
        copy.wait()


def fetch_kernel(count, *refs):
    sources, targets, sems = refs[-1 - 2 * count : -1 - count], refs[-1 - count : -1], refs[-1]
    pairs = []
    for source, target in zip(sources, targets):
        pairs += quarters(source, target)
    for copy in stream(pairs, sems):
        copy.wait()


def fetch(after, arrays, beside=()):
    moved = sum(2 * array.size for array in arrays)
    return call(
        functools.partial(fetch_kernel, len(arrays)),
        [like(array.shape, BF16) for array in arrays],
        [HBM] * (1 + len(beside) + len(arrays)),
        [pltpu.SemaphoreType.DMA((FETCH_PARTS * len(arrays),))],
        limit=MIB,
        moved=0,
    )(after, *beside, *[pinned(array) for array in arrays])


def turn(source, target):
    for at, size in spans(source.shape[0], TURN_ROWS):
        target[:, at : at + size] = jnp.transpose(source[at : at + size, :])


def turn_kernel(count, *refs):
    for source, target in zip(refs[1 : 1 + count], refs[1 + count :]):
        turn(source, target)


def turned(after, arrays):
    return call(
        functools.partial(turn_kernel, len(arrays)),
        [like(array.shape[::-1], BF16) for array in arrays],
        [HBM] + [VMEM] * len(arrays),
        limit=4 * MIB,
        moved=0,
    )(after, *arrays)


def feed_kernel(
    step, piece0, piece1, piece2, piece3, gain, gate, up, down,
    hidden, emb, part_low, part_high,
    scaled,
):
    width = hidden.shape[1]
    cuts = spans(width, 512)
    outs = spans(down.shape[1], 512)
    me = lax.axis_index("inner")
    share = piece0.shape[1]
    for which, piece in enumerate((piece0, piece1, piece2, piece3)):
        emb[:, pl.ds(pl.multiple_of((me ^ which) * share, share), share)] = piece[...]
    emb_float = emb[...].astype(F32)
    mean = jnp.mean(emb_float * emb_float, axis=-1, keepdims=True)
    normed = (emb_float * lax.rsqrt(mean + 1e-06) * gain[...]).astype(BF16)
    path_scale = (step[0].astype(F32) + 0.5) / STEPS
    for at, size in cuts:
        gate_rows = dot(normed, gate[:, at : at + size])
        up_rows = dot(normed, up[:, at : at + size])
        units = gate_rows / (1.0 + jnp.exp(-gate_rows)) * up_rows
        hidden[:, at : at + size] = units
        scaled[:, at : at + size] = (path_scale * units).astype(BF16)
    half = part_low.shape[0]
    for at, size in outs:
        sums = dot(scaled[...], down[:, at : at + size]).astype(BF16)
        part_low[:, at : at + size] = sums[:half]
        part_high[:, at : at + size] = sums[half:]


def pair_kernel(mine, other, *refs):
    refs[-1][...] = (mine[...].astype(F32) + other[...].astype(F32)).astype(BF16)


def pair_sums(low, high, before):
    shape = like(low.shape, BF16)
    low_other, high_other = swap(low, "inner", 1), swap(high, "inner", 2)
    low = call(pair_kernel, shape, [VMEM] * 2 + [HBM] * len(before))(low, low_other, *before)
    low_other = swap(low, "inner", 2)
    high = call(pair_kernel, shape, [VMEM] * 2)(high, high_other)
    return low, low_other, high, swap(high, "inner", 1)


def whole(low, low_other, high, high_other):
    return jnp.concatenate(
        [
            low[...].astype(F32) + low_other[...].astype(F32),
            high[...].astype(F32) + high_other[...].astype(F32),
        ],
        axis=0,
    )


def project_kernel(
    emb, low, low_other, high, high_other, gain, query, key, value, decay, beta,
    mixed, own, send,
):
    half_key = query.shape[1] // 2
    half_value = value.shape[1] // 2
    first = lax.axis_index("outer") % 2 == 0
    total = emb[...].astype(F32) + whole(low, low_other, high, high_other)
    mixed[...] = total
    mean = jnp.mean(total * total, axis=-1, keepdims=True)
    taken = (total * lax.rsqrt(mean + 1e-06) * gain[...]).astype(BF16)

    def put(at, low, high):
        size = low.shape[1]
        own[:, at : at + size] = jnp.where(first, low, high).astype(BF16)
        send[:, at : at + size] = jnp.where(first, high, low).astype(BF16)

    gates = (dot(taken, decay[...], True), dot(taken, beta[...], True))
    heads = decay.shape[0] // 2
    lanes = lax.broadcasted_iota(jnp.int32, (taken.shape[0], 128), 1)
    packed = []
    for side in range(2):
        lane, pack = 0, jnp.zeros((taken.shape[0], 128), F32)
        for values in gates:
            for head in range(side * heads, (side + 1) * heads):
                column = values[:, head : head + 1]
                top = column.astype(BF16).astype(F32)
                pack = jnp.where(lanes == lane, top, pack)
                pack = jnp.where(lanes == lane + 1, column - top, pack)
                lane += 2
        packed.append(pack)
    out = dot(taken, query[...])
    put(0, out[:, :half_key], out[:, half_key:])
    out = dot(taken, key[...])
    put(half_key, out[:, :half_key], out[:, half_key:])
    low = dot(taken, value[:, :half_value])
    put(2 * half_key, low, dot(taken, value[:, half_value:]))
    put(2 * half_key + half_value, *packed)


def both_blocks(own, other, target):
    core = lax.axis_index("outer") % 2
    size = own.shape[0]
    target[pl.ds(pl.multiple_of(core * size, size), size), :] = own[...]
    target[pl.ds(pl.multiple_of((1 - core) * size, size), size), :] = other[...]


def cumulate(chosen, column):
    top = column.astype(BF16)
    rest = column - top.astype(F32)
    middle = rest.astype(BF16)
    low = (rest - middle.astype(F32)).astype(BF16)
    picked = jnp.where(chosen, 1.0, 0.0).astype(BF16)

    def part(values):
        return dot(picked, jnp.broadcast_to(values, (values.shape[0], 128)))

    return part(top) + (part(middle) + part(low))


def unit_inverse(strict):
    size = strict.shape[0]
    row_ids, col_ids = grid_ids(size)
    inverse = jnp.where(row_ids == col_ids, 1.0, 0.0)
    inverse = inverse - jnp.where(row_ids // 2 == col_ids // 2, strict, 0.0)
    block = 2
    while block < size:
        below = (row_ids // (2 * block) == col_ids // (2 * block)) & (
            row_ids // block != col_ids // block
        )
        inverse = inverse - mm3(mm3(inverse, jnp.where(below, strict, 0.0)), inverse)
        block *= 2
    return inverse


def front_kernel(
    own, other, cot_own, cot_other, rate_log, decay_bias, beta_bias,
    packs, cots, sent, sent_map, kept_offset, kept_map,
    decay_mats, grams, inverses, scores, maps, fresh, pulled, columns,
):
    both_blocks(own, other, packs)
    both_blocks(cot_own, cot_other, cots)
    heads, length, _ = decay_mats.shape
    key_dim, value_dim = maps.shape[2], fresh.shape[2]
    place = lax.axis_index("outer")
    even = (place // 2) % 2 == 0
    first_head = (place % 2) * heads
    row_ids, col_ids = grid_ids(length)
    lower, strictly = row_ids >= col_ids, row_ids > col_ids
    lanes = lax.broadcasted_iota(jnp.int32, (length, 128), 1)
    gate_at = heads * (2 * key_dim + value_dim)
    gates = packs[:, gate_at : gate_at + 128].astype(F32)
    for head in range(heads):
        at = head * key_dim
        query_rows = packs[:, at : at + key_dim].astype(F32)
        at += heads * key_dim
        key_rows = packs[:, at : at + key_dim].astype(F32)
        at = 2 * heads * key_dim + head * value_dim
        values = packs[:, at : at + value_dim].astype(F32)
        cot = cots[:, head * value_dim : (head + 1) * value_dim]
        lane = 2 * head
        decay_in = gates[:, lane : lane + 1] + gates[:, lane + 1 : lane + 2]
        decay_in = decay_in + decay_bias[first_head + head]
        lane += 2 * heads
        beta_in = gates[:, lane : lane + 1] + gates[:, lane + 1 : lane + 2]
        beta_in = beta_in + beta_bias[first_head + head]
        rate = jnp.exp(jnp.full((length, 1), rate_log[first_head + head], F32))
        query_scale = lax.rsqrt(row_sum(query_rows * query_rows) + 1e-06) * key_dim ** (-0.5)
        key_scale = lax.rsqrt(row_sum(key_rows * key_rows) + 1e-06)
        queries, keys_unit = query_rows * query_scale, key_rows * key_scale
        log_decay = -rate * (jnp.maximum(decay_in, 0.0) + jnp.log1p(jnp.exp(-jnp.abs(decay_in))))
        betas = 1.0 / (1.0 + jnp.exp(-beta_in))
        cum = cumulate(lower, log_decay)
        decay_mat = jnp.where(
            lower, jnp.exp(jnp.where(lower, cum - jnp.transpose(cum), 0.0)), 0.0
        )
        total = cum[:, :1]
        start_scale = jnp.exp(total)
        tail_scale = jnp.exp(total[length - 1 :] - total)
        gram = jnp.where(strictly, decay_mat * mm(keys_unit, keys_unit, True), 0.0)
        inverse = unit_inverse(betas * gram)
        score = decay_mat * mm(queries, keys_unit, True)
        state_map = mm(inverse, (betas * start_scale) * keys_unit)
        fresh_vals = mm(inverse, betas * values)
        tail_t = jnp.transpose(tail_scale * keys_unit)
        transition = jnp.where(row_ids == col_ids, start_scale[length - 1 :], 0.0) - mm(
            tail_t, state_map
        )
        offset = mm(tail_t, fresh_vals)
        score_pull = mm(jnp.transpose(score), cot)
        grad_local = mm(jnp.transpose(start_scale * queries), cot) - mm(
            jnp.transpose(state_map), score_pull
        )
        flipped = jnp.transpose(transition)
        sent[head] = jnp.where(even, offset, grad_local).astype(BF16)
        sent_map[head] = jnp.where(even, transition, flipped).astype(BF16)
        kept_offset[head] = jnp.where(even, grad_local, offset)
        kept_map[head] = jnp.where(even, flipped, transition).astype(BF16)
        decay_mats[head] = decay_mat
        grams[head] = gram
        inverses[head] = jnp.transpose(inverse).astype(BF16)
        scores[head] = score
        maps[head] = state_map.astype(BF16)
        fresh[head] = fresh_vals
        pulled[head] = score_pull
        pack = jnp.zeros((length, 128), F32)
        for lane, column in enumerate(
            (query_scale, key_scale, betas, start_scale, tail_scale, decay_in, rate)
        ):
            pack = jnp.where(lanes == lane, column, pack)
        columns[head] = pack


def combine_kernel(kept_map, kept_offset, got, after, out):
    for head in range(out.shape[0]):
        joined = dot(kept_map[head], got[head]) + kept_offset[head]
        out[head] = joined.astype(BF16)


def back_kernel(
    near, near_map, far_one, far_two, packs, cots,
    decay_mats, grams, inverses, scores, maps, fresh, pulled, columns, after,
    own, send, grads,
):
    heads, length, _ = decay_mats.shape
    key_dim, value_dim = maps.shape[2], fresh.shape[2]
    place = lax.axis_index("outer")
    core, chip = place % 2, place // 2
    outer_chip = (chip == 0) | (chip == 3)
    odd = chip % 2 == 1
    row_ids, col_ids = grid_ids(length)
    strictly, upper = row_ids > col_ids, row_ids <= col_ids
    lanes = lax.broadcasted_iota(jnp.int32, (length, 128), 1)
    gate_at = heads * (2 * key_dim + value_dim)
    gate_grads = jnp.zeros((length, 128), F32)
    for head in range(heads):
        at = head * key_dim
        query_rows = packs[:, at : at + key_dim].astype(F32)
        key_at = at + heads * key_dim
        key_rows = packs[:, key_at : key_at + key_dim].astype(F32)
        value_at = 2 * heads * key_dim + head * value_dim
        values = packs[:, value_at : value_at + value_dim].astype(F32)
        cot = cots[:, head * value_dim : (head + 1) * value_dim]
        pack = columns[head]
        query_scale, key_scale, betas = pack[:, 0:1], pack[:, 1:2], pack[:, 2:3]
        start_scale, tail_scale = pack[:, 3:4], pack[:, 4:5]
        decay_in, rate = pack[:, 5:6], pack[:, 6:7]
        end_scale = start_scale[length - 1 :]
        queries, keys_unit = query_rows * query_scale, key_rows * key_scale
        decay_mat, gram, score = decay_mats[head], grams[head], scores[head]
        far = far_one[head] + far_two[head]
        close = near[head].astype(F32)
        reached = dot(near_map[head], far) + close
        first = jnp.where(outer_chip, reached, close)
        second = jnp.where(outer_chip, 0.0, far.astype(F32))
        state = jnp.where(odd, first, second)
        state_grad = jnp.where(odd, second, first)
        state_half, state_grad_half = state.astype(BF16), state_grad.astype(BF16)
        new_vals = fresh[head] - dot(maps[head], state_half)
        new_half = new_vals.astype(BF16)
        grad_new = pulled[head] + mm(tail_scale * keys_unit, state_grad_half)
        grad_target = mm(inverses[head], grad_new)
        target_half = grad_target.astype(BF16)
        grad_score = dot(cot, new_half, True)
        grad_sys = jnp.where(strictly, -dot(target_half, new_half, True), 0.0)
        cot_state = dot(cot, state_half, True)
        target_state = dot(target_half, state_half, True)
        new_state = dot(new_half, state_grad_half, True)
        weighted = decay_mat * grad_score
        grad_gram = grad_sys * decay_mat * betas
        grad_query = mm(weighted, keys_unit) + start_scale * cot_state
        grad_key = (
            mm(jnp.transpose(weighted), queries)
            + mm(grad_gram + jnp.transpose(grad_gram), keys_unit)
            + tail_scale * new_state
            - (betas * start_scale) * target_state
        )
        key_target = row_sum(keys_unit * target_state)
        sys_gram = grad_sys * gram
        grad_beta = row_sum(grad_target * values) - start_scale * key_target + row_sum(sys_gram)
        both = score * grad_score + betas * sys_gram
        tails = tail_scale * row_sum(keys_unit * new_state)
        grad_cum = (
            row_sum(both - jnp.transpose(both))
            + start_scale * row_sum(queries * cot_state)
            - (betas * start_scale) * key_target
            - tails
        )
        ending = jnp.sum(tails, axis=0, keepdims=True) + end_scale * jnp.sum(
            row_sum(state * state_grad), axis=0, keepdims=True
        )
        grad_log = cumulate(upper, grad_cum)[:, :1] + ending
        grad_decay = grad_log * -rate / (1.0 + jnp.exp(-decay_in))
        grad_beta = grad_beta * betas * (1.0 - betas)
        units = queries * key_dim**0.5
        grad_query = query_scale * (grad_query - units * row_sum(units * grad_query))
        grad_key = key_scale * (grad_key - keys_unit * row_sum(keys_unit * grad_key))
        grads[:, at : at + key_dim] = grad_query.astype(BF16)
        grads[:, key_at : key_at + key_dim] = grad_key.astype(BF16)
        grads[:, value_at : value_at + value_dim] = (betas * grad_target).astype(BF16)
        gate_grads = jnp.where(lanes == head, grad_decay, gate_grads)
        gate_grads = jnp.where(lanes == heads + head, grad_beta, gate_grads)
    grads[:, gate_at : gate_at + 128] = gate_grads.astype(BF16)
    size = own.shape[0]
    own[...] = grads[pl.ds(pl.multiple_of(core * size, size), size), :]
    send[...] = grads[pl.ds(pl.multiple_of((1 - core) * size, size), size), :]


def return_kernel(own, other, query, key, value, decay, beta, part_low, part_high):
    half_key = query.shape[0] // 2
    half_value = value.shape[0] // 2
    first = lax.axis_index("outer") % 2 == 0

    def sides(at, size):
        mine, yours = own[:, at : at + size], other[:, at : at + size]
        return jnp.concatenate(
            [jnp.where(first, mine, yours), jnp.where(first, yours, mine)], axis=1
        )

    gate_at = 2 * half_key + half_value
    heads = decay.shape[0] // 2
    sums = dot(sides(0, half_key), query[...])
    sums = sums + dot(sides(half_key, half_key), key[...])
    sums = sums + dot(sides(2 * half_key, half_value), value[...])
    sums = sums + dot(sides(gate_at, heads), decay[...])
    sums = sums + dot(sides(gate_at + heads, heads), beta[...])
    half = part_low.shape[0]
    part_low[...] = sums[:half].astype(BF16)
    part_high[...] = sums[half:].astype(BF16)


def final_kernel(low, low_other, high, high_other, mixed, gain, hidden, down, out):
    total = whole(low, low_other, high, high_other)
    rows = mixed[...]
    scale = lax.rsqrt(jnp.mean(rows * rows, axis=-1, keepdims=True) + 1e-06)
    gained = total * gain[...]
    along = jnp.mean(rows * gained, axis=-1, keepdims=True)
    taken = (scale * gained - rows * (scale * scale * scale * along)).astype(BF16)
    for at, size in spans(down.shape[1], 512):
        product = dot(taken, down[:, at : at + size])
        out[:, at : at + size] = hidden[:, at : at + size] * product


def swap(array, axis, bit):
    return lax.ppermute(array, axis, [(i, i ^ bit) for i in range(lax.axis_size(axis))])


def swap_inner(arrays):
    return [swap(array, "inner", which + 1) for which, array in enumerate(arrays)]


def four_chips(
    tokens, step_index, embed_table, gain_one, gate_weight, up_weight, down_weight, gain_two,
    query_weight, key_weight, value_weight, decay_weight, beta_weight,
    rate_log, decay_bias, beta_bias, cotangent,
):
    count, model = tokens.shape[0], gain_one.shape[0]
    width = gate_weight.shape[1]
    head_count = rate_log.shape[0]
    heads = head_count // 2
    key_dim = query_weight.shape[1] // head_count
    value_dim = value_weight.shape[1] // head_count
    pack_width = heads * (2 * key_dim + value_dim) + 128
    length = 2 * count
    half_shape = like((count // 2, model), BF16)
    rows_shape = like((count, model), BF16)
    dma = pltpu.SemaphoreType.DMA
    cot_half = heads * value_dim
    columns, cot_own, cot_send = call(
        embed_kernel,
        [like((count, embed_table.shape[1]), BF16)]
        + [like((count, cot_half), BF16)] * 2,
        [HBM] * 3,
        [
            pltpu.SMEM((1, count), jnp.int32),
            pltpu.VMEM((1, count), jnp.int32),
            pltpu.VMEM((16 * count, embed_table.shape[1]), BF16),
            dma((2,)),
            dma,
            dma((2,)),
        ],
    )(pinned(tokens.reshape(1, count)), pinned(embed_table), pinned(cotangent))
    cot_other = swap(cot_send, "outer", 1)
    pieces = [columns] + swap_inner([columns] * 3)
    (down_kept,) = fetch(columns, [down_weight], [gate_weight, up_weight])
    hidden, emb, part_low, part_high = call(
        feed_kernel,
        [like((count, width), F32), rows_shape] + [half_shape] * 2,
        [SMEM] + [VMEM] * 8,
        [
            pltpu.VMEM((count, width), BF16),
        ],
    )(
        step_index, *pieces, gain_one.reshape(1, model), gate_weight, up_weight, down_kept
    )
    weights = fetch(part_low, [query_weight, key_weight])
    sums = pair_sums(part_low, part_high, [weights[0], cot_other])
    weights += fetch(sums[0], [value_weight])
    weights = (*weights, decay_weight.T, beta_weight.T)
    mixed, own, send = call(
        project_kernel,
        [like((count, model), F32)] + [like((count, pack_width), BF16)] * 2,
        [VMEM] * 11,
    )(emb, *sums, gain_two.reshape(1, model), *weights)
    other = swap(send, "outer", 1)
    square = (heads, length, length)
    valued = (heads, length, value_dim)
    packs, cots, sent, sent_map, kept_offset, kept_map, *saved = call(
        front_kernel,
        [
            like((length, pack_width), BF16),
            like((length, cot_half), BF16),
            like((heads, key_dim, value_dim), BF16),
            like((heads, key_dim, key_dim), BF16),
            like((heads, key_dim, value_dim), F32),
            like((heads, key_dim, key_dim), BF16),
            like(square, F32),
            like(square, F32),
            like(square, BF16),
            like(square, F32),
            like((heads, length, key_dim), BF16),
            like(valued, F32),
            like(valued, F32),
            like((heads, length, 128), F32),
        ],
        [VMEM] * 4 + [SMEM] * 3,
    )(own, other, cot_own, cot_other, rate_log, decay_bias, beta_bias)
    near = swap(sent, "outer", 2)
    query_turned, key_turned = turned(sent, weights[:2])
    near_map = swap(sent_map, "outer", 2)
    joined = call(combine_kernel, like((heads, key_dim, value_dim), BF16), [VMEM] * 3 + [HBM])(
        kept_map, kept_offset, near, query_turned
    )
    (value_turned,) = turned(joined, weights[2:3])
    far_two = lax.ppermute(joined, "outer", [(2, 6), (3, 7), (4, 0), (5, 1)])
    far_one = lax.ppermute(joined, "outer", [(2, 4), (3, 5), (4, 2), (5, 3)])
    own, send = call(
        back_kernel,
        [like((count, pack_width), BF16)] * 2,
        [VMEM] * 14 + [HBM],
        [pltpu.VMEM((length, pack_width), BF16)],
    )(near, near_map, far_one, far_two, packs, cots, *saved, value_turned)
    other = swap(send, "outer", 1)
    part_low, part_high = call(return_kernel, [half_shape] * 2, [VMEM] * 7)(
        own, other, query_turned, key_turned, value_turned, *weights[3:]
    )
    (down_turned,) = turned(part_low, [down_kept])
    sums = pair_sums(part_low, part_high, [down_turned])
    return call(final_kernel, jax.ShapeDtypeStruct((count, width), F32), [VMEM] * 8)(
        *sums, mixed, gain_two.reshape(1, model), hidden, down_turned
    )


def local_part(*args):
    fits = (
        lax.axis_size("inner") == 4
        and lax.axis_size("outer") == 8
        and args[0].shape[0] == 64
        and args[13].shape[0] % 2 == 0
    )
    return four_chips(*args) if fits else shards(*args)


def solution(mesh):
    placed = (
        P("outer"),
        P(),
        P(None, "inner"),
        P(),
        P(None, "inner"),
        P(None, "inner"),
        P("inner", None),
        P(),
        P(None, "inner"),
        P(None, "inner"),
        P(None, "inner"),
        P(None, "inner"),
        P(None, "inner"),
        P("inner"),
        P("inner"),
        P("inner"),
        P("outer", "inner"),
    )
    return jax.shard_map(
        local_part, mesh=mesh, in_specs=placed, out_specs=P("outer", "inner"), check_vma=False
    )
```

```python
import functools
import math

import jax
import jax.numpy as jnp
from jax import lax
from jax.experimental import pallas as pl
from jax.experimental.pallas import tpu as pltpu
from jax.sharding import PartitionSpec as P

STEPS = 32


def from_behind(array, axis, by):
    devices = lax.axis_size(axis)
    pairs = [(i, i + by) for i in range(devices) if 0 <= i + by < devices]
    return lax.ppermute(array, axis, pairs)


def unit_rows(values):
    return values * lax.rsqrt(jnp.sum(values * values, axis=-1, keepdims=True) + 1e-06)


def head_inputs(query_rows, key_rows, decay_rows, beta_rows, log_rate, rate_shift, beta_shift):
    queries = unit_rows(query_rows) * query_rows.shape[-1] ** (-0.5)
    keys_unit = unit_rows(key_rows)
    log_decay = -jnp.exp(log_rate) * jax.nn.softplus(decay_rows + rate_shift)
    betas = jax.nn.sigmoid(beta_rows + beta_shift)
    return (queries, keys_unit, log_decay, betas)


def block_step(with_out, state, pieces):
    queries, keys_unit, values, log_decay, betas = pieces
    block_len = keys_unit.shape[0]
    highest = lax.Precision.HIGHEST
    cum_decay = jnp.cumsum(log_decay)
    row_ids = jnp.arange(block_len)[:, None]
    col_ids = jnp.arange(block_len)[None, :]
    lower_mask = row_ids >= col_ids
    decay_mat = jnp.where(
        lower_mask,
        jnp.exp(jnp.where(lower_mask, cum_decay[:, None] - cum_decay[None, :], 0.0)),
        0.0,
    )
    key_gram = jnp.dot(keys_unit, keys_unit.T, precision=highest)
    strict = jnp.where(row_ids > col_ids, betas[:, None] * decay_mat * key_gram, 0.0)
    system = strict + jnp.eye(block_len, dtype=jnp.float32)
    start_scale = jnp.exp(cum_decay)[:, None]
    target = betas[:, None] * (values - start_scale * jnp.dot(keys_unit, state, precision=highest))
    fresh_vals = lax.linalg.triangular_solve(
        system, target, left_side=True, lower=True, unit_diagonal=True
    )
    tail_keys = jnp.exp(cum_decay[-1] - cum_decay)[:, None] * keys_unit
    new_state = jnp.exp(cum_decay[-1]) * state + jnp.dot(tail_keys.T, fresh_vals, precision=highest)
    if with_out:
        scores = decay_mat * jnp.dot(queries, keys_unit.T, precision=highest)
        output = start_scale * jnp.dot(queries, state, precision=highest) + jnp.dot(
            scores, fresh_vals, precision=highest
        )
        return (new_state, output)
    return (new_state, None)


def run_blocks(queries, keys_unit, values, log_decay, betas, state, with_out):
    length = keys_unit.shape[0]
    block_len = math.gcd(64, length)
    block_count = length // block_len

    def blocked(array):
        return array.reshape((block_count, block_len) + array.shape[1:])

    step_fn = functools.partial(block_step, with_out)
    final_state, outputs = lax.scan(
        step_fn,
        state,
        (blocked(queries), blocked(keys_unit), blocked(values), blocked(log_decay), blocked(betas)),
    )
    if with_out:
        outputs = outputs.reshape((length,) + outputs.shape[2:])
    return (final_state, outputs)


def rms_scaled(values, gain):
    return values * lax.rsqrt(jnp.mean(values * values, axis=-1, keepdims=True) + 1e-06) * gain


def apply_map(matrix, state):
    return jnp.einsum("hij,hjv->hiv", matrix, state, precision=lax.Precision.HIGHEST)


def shards(
    tokens,
    step_index,
    embed_table,
    gain_one,
    gate_weight,
    up_weight,
    down_weight,
    gain_two,
    query_weight,
    key_weight,
    value_weight,
    decay_weight,
    beta_weight,
    rate_log,
    decay_bias,
    beta_bias,
    cotangent,
):
    columns = jnp.take(embed_table, tokens, axis=0)
    embedded = lax.all_gather(columns, "inner", axis=1, tiled=True)
    emb_float = embedded.astype(jnp.float32)
    normed_one = rms_scaled(emb_float, gain_one).astype(jnp.bfloat16)
    gate_rows = jnp.dot(normed_one, gate_weight, preferred_element_type=jnp.float32)
    up_rows = jnp.dot(normed_one, up_weight, preferred_element_type=jnp.float32)
    hidden = jax.nn.silu(gate_rows) * up_rows
    path_scale = (step_index[0].astype(jnp.float32) + 0.5) / STEPS
    scaled = (path_scale * hidden).astype(jnp.bfloat16)
    group_rows = tokens.shape[0]
    row_share = group_rows // lax.axis_size("inner")
    head_count = rate_log.shape[0]
    key_dim = query_weight.shape[1] // head_count
    value_dim = value_weight.shape[1] // head_count
    main_weight = jnp.concatenate([query_weight, key_weight, value_weight], axis=1)
    gate_pair = jnp.concatenate([decay_weight, beta_weight], axis=1)

    def normalize(values):
        return rms_scaled(values, gain_two)

    mixed_share = lax.psum_scatter(
        jnp.dot(scaled, down_weight, preferred_element_type=jnp.float32).astype(jnp.bfloat16),
        "inner",
        scatter_dimension=0,
        tiled=True,
    ).astype(jnp.float32)
    own_rows = lax.dynamic_slice_in_dim(
        emb_float, lax.axis_index("inner") * row_share, row_share, 0
    )
    normed_float, norm_pull = jax.vjp(normalize, own_rows + mixed_share)
    block_piece = lax.all_gather(normed_float.astype(jnp.bfloat16), "inner", axis=0, tiled=True)
    main_part = jnp.dot(block_piece, main_weight, preferred_element_type=jnp.float32)
    gate_part = jnp.dot(block_piece, gate_pair, preferred_element_type=jnp.float32)
    projected = jnp.concatenate([main_part, gate_part], axis=1)
    key_span = head_count * key_dim
    value_span = head_count * value_dim

    def by_head(columns_block, width):
        return columns_block.reshape(group_rows, head_count, width).transpose(1, 0, 2)

    query_pre = by_head(projected[:, :key_span], key_dim)
    key_pre = by_head(projected[:, key_span : 2 * key_span], key_dim)
    value_pre = by_head(projected[:, 2 * key_span : 2 * key_span + value_span], value_dim)
    gate_start = 2 * key_span + value_span
    decay_pre = projected[:, gate_start : gate_start + head_count].T
    beta_pre = projected[:, gate_start + head_count : gate_start + 2 * head_count].T
    cot_heads = by_head(cotangent.astype(jnp.float32), value_dim)

    def carry_map(key_rows, value_rows, decay_rows, beta_rows, log_rate, rate_shift, beta_shift):
        unused_query, keys_unit, log_decay, betas = head_inputs(
            key_rows, key_rows, decay_rows, beta_rows, log_rate, rate_shift, beta_shift
        )
        padded_vals = jnp.concatenate(
            [value_rows, jnp.zeros((key_rows.shape[0], key_dim), jnp.float32)], axis=1
        )
        start_state = jnp.concatenate(
            [jnp.zeros((key_dim, value_dim), jnp.float32), jnp.eye(key_dim, dtype=jnp.float32)],
            axis=1,
        )
        final_state, unused_out = run_blocks(
            keys_unit, keys_unit, padded_vals, log_decay, betas, start_state, False
        )
        return final_state

    joined_state = jax.vmap(carry_map)(
        key_pre, value_pre, decay_pre, beta_pre, rate_log, decay_bias, beta_bias
    )
    offset_state = joined_state[:, :, :value_dim]
    transition = joined_state[:, :, value_dim:]

    def forward_step(turn_index, carried):
        incoming = from_behind(carried[1].astype(jnp.bfloat16), "outer", 1).astype(jnp.float32)
        return (incoming, apply_map(transition, incoming) + offset_state)

    state_in, unused_end = lax.fori_loop(
        0, lax.axis_size("outer") - 1, forward_step, (jnp.zeros_like(offset_state), offset_state)
    )

    def local_score(query_in, key_in, value_in, decay_in, beta_in, start_in):

        def one_head(
            query_rows,
            key_rows,
            value_rows,
            decay_rows,
            beta_rows,
            start_state,
            cot_rows,
            log_rate,
            rate_shift,
            beta_shift,
        ):
            queries, keys_unit, log_decay, betas = head_inputs(
                query_rows, key_rows, decay_rows, beta_rows, log_rate, rate_shift, beta_shift
            )
            final_state, outputs = run_blocks(
                queries, keys_unit, value_rows, log_decay, betas, start_state, True
            )
            return (jnp.sum(outputs * cot_rows), final_state)

        head_scores, final_states = jax.vmap(one_head)(
            query_in,
            key_in,
            value_in,
            decay_in,
            beta_in,
            start_in,
            cot_heads,
            rate_log,
            decay_bias,
            beta_bias,
        )
        return (jnp.sum(head_scores), final_states)

    score_pair, pull_back = jax.vjp(
        local_score, query_pre, key_pre, value_pre, decay_pre, beta_pre, state_in
    )
    first_pull = pull_back((jnp.ones_like(score_pair[0]), jnp.zeros_like(score_pair[1])))
    grad_local = first_pull[5]
    grad_trans = jnp.swapaxes(transition, 1, 2)

    def backward_step(turn_index, carried):
        incoming = from_behind(carried[1].astype(jnp.bfloat16), "outer", -1).astype(jnp.float32)
        return (incoming, apply_map(grad_trans, incoming) + grad_local)

    state_grad, unused_start = lax.fori_loop(
        0, lax.axis_size("outer") - 1, backward_step, (jnp.zeros_like(grad_local), grad_local)
    )
    second_pull = pull_back((jnp.zeros_like(score_pair[0]), state_grad))
    summed = [first_pull[which] + second_pull[which] for which in range(5)]

    def by_rows(head_block):
        return head_block.transpose(1, 0, 2).reshape(group_rows, -1).astype(jnp.bfloat16)

    grad_main = jnp.concatenate(
        [by_rows(summed[0]), by_rows(summed[1]), by_rows(summed[2])], axis=1
    )
    grad_gates = jnp.concatenate(
        [summed[3].T.astype(jnp.bfloat16), summed[4].T.astype(jnp.bfloat16)], axis=1
    )
    main_part = jnp.dot(grad_main, main_weight.T, preferred_element_type=jnp.float32)
    back_share = lax.psum_scatter(
        (main_part + jnp.dot(grad_gates, gate_pair.T, preferred_element_type=jnp.float32)).astype(
            jnp.bfloat16
        ),
        "inner",
        scatter_dimension=0,
        tiled=True,
    ).astype(jnp.float32)
    grad_mixed = norm_pull(back_share)[0].astype(jnp.bfloat16)
    return hidden * jnp.dot(
        lax.all_gather(grad_mixed, "inner", axis=0, tiled=True),
        down_weight.T,
        preferred_element_type=jnp.float32,
    )


BF16 = jnp.bfloat16
F32 = jnp.float32
MIB = 1 << 20
FETCH_PARTS = 4
TURN_ROWS = 128
BASE = 16
VMEM = pl.BlockSpec(memory_space=pltpu.VMEM)
SMEM = pl.BlockSpec(memory_space=pltpu.SMEM)
HBM = pl.BlockSpec(memory_space=pl.ANY)


def pinned(array):
    return pltpu.with_memory_space_constraint(array, pltpu.HBM)


def call(kernel, out_shape, in_specs, scratch=(), limit=16 * MIB, flops=0, moved=0):
    return pl.pallas_call(
        kernel,
        out_shape=out_shape,
        in_specs=in_specs,
        out_specs=jax.tree.map(lambda _: VMEM, out_shape),
        scratch_shapes=list(scratch),
        compiler_params=pltpu.CompilerParams(vmem_limit_bytes=limit),
        cost_estimate=pl.CostEstimate(flops=flops, bytes_accessed=moved, transcendentals=0),
    )


def like(shape, dtype):
    return jax.ShapeDtypeStruct(shape, dtype)


def dot(a, b, transposed=False):
    dims = (((1,), (1 if transposed else 0,)), ((), ()))
    return lax.dot_general(a, b, dims, preferred_element_type=F32)


def mm(a, b, transposed=False):
    return dot(a.astype(BF16), b.astype(BF16), transposed)


def row_sum(values):
    return jnp.sum(values, axis=-1, keepdims=True)


def spans(total, step):
    return [(at, min(step, total - at)) for at in range(0, total, step)]


def stream(pairs, sems):
    copies = [
        pltpu.make_async_copy(source, target, sems.at[which])
        for which, (source, target) in enumerate(pairs)
    ]
    for copy in copies:
        copy.start()
    return copies


def grid_ids(size):
    shape = (size, size)
    return lax.broadcasted_iota(jnp.int32, shape, 0), lax.broadcasted_iota(jnp.int32, shape, 1)


def quarters(source, target):
    cuts = spans(source.shape[0], source.shape[0] // FETCH_PARTS)
    return [(source.at[pl.ds(at, size)], target.at[pl.ds(at, size)]) for at, size in cuts]


def embed_kernel(
    ids_in, table, cot, out, cot_own, cot_send,
    ids, id_row, blocks, id_sems, sem, cot_sems,
):
    count = out.shape[0]
    copies = stream([(ids_in, ids), (ids_in, id_row)], id_sems)
    copies[0].wait()
    for which in range(count):
        base = pl.multiple_of((ids[0, which] // 16) * 16, 16)
        pltpu.make_async_copy(
            table.at[pl.ds(base, 16)], blocks.at[pl.ds(which * 16, 16)], sem
        ).start()
    core, half = lax.axis_index("outer") % 2, cot_own.shape[1]
    mine = pl.ds(pl.multiple_of(core * half, half), half)
    yours = pl.ds(pl.multiple_of((1 - core) * half, half), half)
    halves = stream([(cot.at[:, mine], cot_own), (cot.at[:, yours], cot_send)], cot_sems)
    copies[1].wait()
    row_ids, col_ids = grid_ids(count)
    low_bits = jnp.broadcast_to(id_row[...] & 15, (count, count))
    inside = row_sum(jnp.where(row_ids == col_ids, low_bits, 0).astype(F32)).astype(jnp.int32)
    wide = (count, 16 * count)
    wanted = lax.broadcasted_iota(jnp.int32, wide, 0) * 16 + inside
    pick = jnp.where(lax.broadcasted_iota(jnp.int32, wide, 1) == wanted, 1.0, 0.0).astype(BF16)
    pltpu.make_async_copy(table.at[pl.ds(0, 16 * count)], blocks, sem).wait()
    out[...] = dot(pick, blocks[...]).astype(BF16)
    for copy in halves:
        copy.wait()


def fetch_kernel(count, *refs):
    sources, targets, sems = refs[-1 - 2 * count : -1 - count], refs[-1 - count : -1], refs[-1]
    pairs = []
    for source, target in zip(sources, targets):
        pairs += quarters(source, target)
    for copy in stream(pairs, sems):
        copy.wait()


def fetch(after, arrays, beside=()):
    moved = sum(2 * array.size for array in arrays)
    return call(
        functools.partial(fetch_kernel, len(arrays)),
        [like(array.shape, BF16) for array in arrays],
        [HBM] * (1 + len(beside) + len(arrays)),
        [pltpu.SemaphoreType.DMA((FETCH_PARTS * len(arrays),))],
        limit=MIB,
        moved=0,
    )(after, *beside, *[pinned(array) for array in arrays])


def turn(source, target):
    for at, size in spans(source.shape[0], TURN_ROWS):
        target[:, at : at + size] = jnp.transpose(source[at : at + size, :])


def turn_kernel(count, *refs):
    for source, target in zip(refs[1 : 1 + count], refs[1 + count :]):
        turn(source, target)


def turned(after, arrays):
    return call(
        functools.partial(turn_kernel, len(arrays)),
        [like(array.shape[::-1], BF16) for array in arrays],
        [HBM] + [VMEM] * len(arrays),
        limit=4 * MIB,
        moved=0,
    )(after, *arrays)


def feed_kernel(
    step, piece0, piece1, piece2, piece3, gain, gate, up, down,
    hidden, emb, part_low, part_high,
    scaled,
):
    width = hidden.shape[1]
    cuts = spans(width, 512)
    outs = spans(down.shape[1], 512)
    me = lax.axis_index("inner")
    share = piece0.shape[1]
    for which, piece in enumerate((piece0, piece1, piece2, piece3)):
        emb[:, pl.ds(pl.multiple_of((me ^ which) * share, share), share)] = piece[...]
    emb_float = emb[...].astype(F32)
    mean = jnp.mean(emb_float * emb_float, axis=-1, keepdims=True)
    normed = (emb_float * lax.rsqrt(mean + 1e-06) * gain[...]).astype(BF16)
    path_scale = (step[0].astype(F32) + 0.5) / STEPS
    for at, size in cuts:
        gate_rows = dot(normed, gate[:, at : at + size])
        up_rows = dot(normed, up[:, at : at + size])
        units = gate_rows / (1.0 + jnp.exp(-gate_rows)) * up_rows
        hidden[:, at : at + size] = units
        scaled[:, at : at + size] = (path_scale * units).astype(BF16)
    half = part_low.shape[0]
    for at, size in outs:
        sums = dot(scaled[...], down[:, at : at + size]).astype(BF16)
        part_low[:, at : at + size] = sums[:half]
        part_high[:, at : at + size] = sums[half:]


def pair_kernel(mine, other, *refs):
    refs[-1][...] = (mine[...].astype(F32) + other[...].astype(F32)).astype(BF16)


def pair_sums(low, high, before):
    shape = like(low.shape, BF16)
    low_other, high_other = swap(low, "inner", 1), swap(high, "inner", 2)
    low = call(pair_kernel, shape, [VMEM] * 2 + [HBM] * len(before))(low, low_other, *before)
    low_other = swap(low, "inner", 2)
    high = call(pair_kernel, shape, [VMEM] * 2)(high, high_other)
    return low, low_other, high, swap(high, "inner", 1)


def whole(low, low_other, high, high_other):
    return jnp.concatenate(
        [
            low[...].astype(F32) + low_other[...].astype(F32),
            high[...].astype(F32) + high_other[...].astype(F32),
        ],
        axis=0,
    )


def project_kernel(
    emb, low, low_other, high, high_other, gain, query, key, value, decay, beta,
    mixed, own, send,
):
    half_key = query.shape[1] // 2
    half_value = value.shape[1] // 2
    first = lax.axis_index("outer") % 2 == 0
    total = emb[...].astype(F32) + whole(low, low_other, high, high_other)
    mixed[...] = total
    mean = jnp.mean(total * total, axis=-1, keepdims=True)
    taken = (total * lax.rsqrt(mean + 1e-06) * gain[...]).astype(BF16)

    def put(at, low, high):
        size = low.shape[1]
        own[:, at : at + size] = jnp.where(first, low, high).astype(BF16)
        send[:, at : at + size] = jnp.where(first, high, low).astype(BF16)

    gates = (dot(taken, decay[...], True), dot(taken, beta[...], True))
    heads = decay.shape[0] // 2
    lanes = lax.broadcasted_iota(jnp.int32, (taken.shape[0], 128), 1)
    packed = []
    for side in range(2):
        lane, pack = 0, jnp.zeros((taken.shape[0], 128), F32)
        for values in gates:
            for head in range(side * heads, (side + 1) * heads):
                column = values[:, head : head + 1]
                top = column.astype(BF16).astype(F32)
                pack = jnp.where(lanes == lane, top, pack)
                pack = jnp.where(lanes == lane + 1, column - top, pack)
                lane += 2
        packed.append(pack)
    out = dot(taken, query[...])
    put(0, out[:, :half_key], out[:, half_key:])
    out = dot(taken, key[...])
    put(half_key, out[:, :half_key], out[:, half_key:])
    low = dot(taken, value[:, :half_value])
    put(2 * half_key, low, dot(taken, value[:, half_value:]))
    put(2 * half_key + half_value, *packed)


def both_blocks(own, other, target):
    core = lax.axis_index("outer") % 2
    size = own.shape[0]
    target[pl.ds(pl.multiple_of(core * size, size), size), :] = own[...]
    target[pl.ds(pl.multiple_of((1 - core) * size, size), size), :] = other[...]


def cumulate(chosen, column):
    top = column.astype(BF16)
    rest = column - top.astype(F32)
    middle = rest.astype(BF16)
    low = (rest - middle.astype(F32)).astype(BF16)
    picked = jnp.where(chosen, 1.0, 0.0).astype(BF16)

    def part(values):
        return dot(picked, jnp.broadcast_to(values, (values.shape[0], 128)))

    return part(top) + (part(middle) + part(low))


def unit_inverses(systems):
    size = systems[0].shape[0]
    row_ids, col_ids = grid_ids(size)
    apart = row_ids - col_ids
    near = row_ids // BASE == col_ids // BASE

    def diagonal(which):
        picked = near & (apart == which)
        rows = [jnp.sum(jnp.where(picked, a, 0.0), axis=0, keepdims=True) for a in systems]
        return jnp.concatenate(rows, axis=0)

    def ahead(rows, by):
        return rows if by == 0 else pltpu.roll(rows, size - by, 1)

    given = [None] + [diagonal(which) for which in range(1, BASE)]
    found = [jnp.ones((len(systems), size), F32)]
    for which in range(1, BASE):
        terms = [ahead(given[j], which - j) * found[which - j] for j in range(1, which + 1)]
        while len(terms) > 1:
            pairs = [a + b for a, b in zip(terms[::2], terms[1::2])]
            terms = pairs + terms[2 * len(pairs) :]
        found.append(-terms[0])
    inverses = []
    for head, system in enumerate(systems):
        inverse = jnp.zeros((size, size), F32)
        for which in range(BASE):
            inverse = jnp.where(apart == which, found[which][head : head + 1], inverse)
        block = BASE
        while block < size:
            below = (row_ids // (2 * block) == col_ids // (2 * block)) & (
                row_ids // block != col_ids // block
            )
            inverse = inverse - mm(mm(inverse, jnp.where(below, system, 0.0)), inverse)
            block *= 2
        inverses.append(inverse)
    return inverses


def front_kernel(
    own, other, cot_own, cot_other, rate_log, decay_bias, beta_bias,
    packs, cots, sent, sent_map, kept_offset, kept_map,
    decay_mats, grams, inverses, scores, maps, fresh, pulled, columns,
):
    both_blocks(own, other, packs)
    both_blocks(cot_own, cot_other, cots)
    heads, length, _ = decay_mats.shape
    key_dim, value_dim = maps.shape[2], fresh.shape[2]
    place = lax.axis_index("outer")
    even = (place // 2) % 2 == 0
    first_head = (place % 2) * heads
    row_ids, col_ids = grid_ids(length)
    lower, strictly = row_ids >= col_ids, row_ids > col_ids
    lanes = lax.broadcasted_iota(jnp.int32, (length, 128), 1)
    gate_at = heads * (2 * key_dim + value_dim)
    gates = packs[:, gate_at : gate_at + 128].astype(F32)
    ready = []
    for head in range(heads):
        at = head * key_dim
        query_rows = packs[:, at : at + key_dim].astype(F32)
        at += heads * key_dim
        key_rows = packs[:, at : at + key_dim].astype(F32)
        at = 2 * heads * key_dim + head * value_dim
        values = packs[:, at : at + value_dim].astype(F32)
        cot = cots[:, head * value_dim : (head + 1) * value_dim]
        lane = 2 * head
        decay_in = gates[:, lane : lane + 1] + gates[:, lane + 1 : lane + 2]
        decay_in = decay_in + decay_bias[first_head + head]
        lane += 2 * heads
        beta_in = gates[:, lane : lane + 1] + gates[:, lane + 1 : lane + 2]
        beta_in = beta_in + beta_bias[first_head + head]
        rate = jnp.exp(jnp.full((length, 1), rate_log[first_head + head], F32))
        query_scale = lax.rsqrt(row_sum(query_rows * query_rows) + 1e-06) * key_dim ** (-0.5)
        key_scale = lax.rsqrt(row_sum(key_rows * key_rows) + 1e-06)
        queries, keys_unit = query_rows * query_scale, key_rows * key_scale
        log_decay = -rate * (jnp.maximum(decay_in, 0.0) + jnp.log1p(jnp.exp(-jnp.abs(decay_in))))
        betas = 1.0 / (1.0 + jnp.exp(-beta_in))
        cum = cumulate(lower, log_decay)
        decay_mat = jnp.where(
            lower, jnp.exp(jnp.where(lower, cum - jnp.transpose(cum), 0.0)), 0.0
        )
        total = cum[:, :1]
        start_scale = jnp.exp(total)
        tail_scale = jnp.exp(total[length - 1 :] - total)
        gram = jnp.where(strictly, decay_mat * mm(keys_unit, keys_unit, True), 0.0)
        ready.append(
            (
                queries, keys_unit, values, cot, decay_mat, gram, start_scale, tail_scale,
                betas, query_scale, key_scale, decay_in, rate,
            )
        )
    inverse_list = unit_inverses([item[8] * item[5] for item in ready])
    for head, inverse in enumerate(inverse_list):
        (
            queries, keys_unit, values, cot, decay_mat, gram, start_scale, tail_scale,
            betas, query_scale, key_scale, decay_in, rate,
        ) = ready[head]
        score = decay_mat * mm(queries, keys_unit, True)
        state_map = mm(inverse, (betas * start_scale) * keys_unit)
        fresh_vals = mm(inverse, betas * values)
        tail_t = jnp.transpose(tail_scale * keys_unit)
        transition = jnp.where(row_ids == col_ids, start_scale[length - 1 :], 0.0) - mm(
            tail_t, state_map
        )
        offset = mm(tail_t, fresh_vals)
        score_pull = mm(jnp.transpose(score), cot)
        grad_local = mm(jnp.transpose(start_scale * queries), cot) - mm(
            jnp.transpose(state_map), score_pull
        )
        flipped = jnp.transpose(transition)
        sent[head] = jnp.where(even, offset, grad_local).astype(BF16)
        sent_map[head] = jnp.where(even, transition, flipped).astype(BF16)
        kept_offset[head] = jnp.where(even, grad_local, offset)
        kept_map[head] = jnp.where(even, flipped, transition).astype(BF16)
        decay_mats[head] = decay_mat
        grams[head] = gram
        inverses[head] = jnp.transpose(inverse).astype(BF16)
        scores[head] = score
        maps[head] = state_map.astype(BF16)
        fresh[head] = fresh_vals
        pulled[head] = score_pull
        pack = jnp.zeros((length, 128), F32)
        for lane, column in enumerate(
            (query_scale, key_scale, betas, start_scale, tail_scale, decay_in, rate)
        ):
            pack = jnp.where(lanes == lane, column, pack)
        columns[head] = pack


def combine_kernel(kept_map, kept_offset, got, after, out):
    for head in range(out.shape[0]):
        joined = dot(kept_map[head], got[head]) + kept_offset[head]
        out[head] = joined.astype(BF16)


def back_kernel(
    near, near_map, far_one, far_two, packs, cots,
    decay_mats, grams, inverses, scores, maps, fresh, pulled, columns, after,
    own, send, grads,
):
    heads, length, _ = decay_mats.shape
    key_dim, value_dim = maps.shape[2], fresh.shape[2]
    place = lax.axis_index("outer")
    core, chip = place % 2, place // 2
    outer_chip = (chip == 0) | (chip == 3)
    odd = chip % 2 == 1
    row_ids, col_ids = grid_ids(length)
    strictly, upper = row_ids > col_ids, row_ids <= col_ids
    lanes = lax.broadcasted_iota(jnp.int32, (length, 128), 1)
    gate_at = heads * (2 * key_dim + value_dim)
    gate_grads = jnp.zeros((length, 128), F32)
    for head in range(heads):
        at = head * key_dim
        query_rows = packs[:, at : at + key_dim].astype(F32)
        key_at = at + heads * key_dim
        key_rows = packs[:, key_at : key_at + key_dim].astype(F32)
        value_at = 2 * heads * key_dim + head * value_dim
        values = packs[:, value_at : value_at + value_dim].astype(F32)
        cot = cots[:, head * value_dim : (head + 1) * value_dim]
        pack = columns[head]
        query_scale, key_scale, betas = pack[:, 0:1], pack[:, 1:2], pack[:, 2:3]
        start_scale, tail_scale = pack[:, 3:4], pack[:, 4:5]
        decay_in, rate = pack[:, 5:6], pack[:, 6:7]
        end_scale = start_scale[length - 1 :]
        queries, keys_unit = query_rows * query_scale, key_rows * key_scale
        decay_mat, gram, score = decay_mats[head], grams[head], scores[head]
        far = jnp.where(outer_chip, far_two[head], far_one[head])
        close = near[head].astype(F32)
        reached = dot(near_map[head], far) + close
        first = jnp.where(outer_chip, reached, close)
        second = jnp.where(outer_chip, 0.0, far.astype(F32))
        state = jnp.where(odd, first, second)
        state_grad = jnp.where(odd, second, first)
        state_half, state_grad_half = state.astype(BF16), state_grad.astype(BF16)
        new_vals = fresh[head] - dot(maps[head], state_half)
        new_half = new_vals.astype(BF16)
        grad_new = pulled[head] + mm(tail_scale * keys_unit, state_grad_half)
        grad_target = mm(inverses[head], grad_new)
        target_half = grad_target.astype(BF16)
        grad_score = dot(cot, new_half, True)
        grad_sys = jnp.where(strictly, -dot(target_half, new_half, True), 0.0)
        cot_state = dot(cot, state_half, True)
        target_state = dot(target_half, state_half, True)
        new_state = dot(new_half, state_grad_half, True)
        weighted = decay_mat * grad_score
        grad_gram = grad_sys * decay_mat * betas
        grad_query = mm(weighted, keys_unit) + start_scale * cot_state
        grad_key = (
            mm(jnp.transpose(weighted), queries)
            + mm(grad_gram + jnp.transpose(grad_gram), keys_unit)
            + tail_scale * new_state
            - (betas * start_scale) * target_state
        )
        key_target = row_sum(keys_unit * target_state)
        sys_gram = grad_sys * gram
        grad_beta = row_sum(grad_target * values) - start_scale * key_target + row_sum(sys_gram)
        both = score * grad_score + betas * sys_gram
        tails = tail_scale * row_sum(keys_unit * new_state)
        grad_cum = (
            row_sum(both - jnp.transpose(both))
            + start_scale * row_sum(queries * cot_state)
            - (betas * start_scale) * key_target
            - tails
        )
        ending = jnp.sum(tails, axis=0, keepdims=True) + end_scale * jnp.sum(
            row_sum(state * state_grad), axis=0, keepdims=True
        )
        grad_log = cumulate(upper, grad_cum)[:, :1] + ending
        grad_decay = grad_log * -rate / (1.0 + jnp.exp(-decay_in))
        grad_beta = grad_beta * betas * (1.0 - betas)
        units = queries * key_dim**0.5
        grad_query = query_scale * (grad_query - units * row_sum(units * grad_query))
        grad_key = key_scale * (grad_key - keys_unit * row_sum(keys_unit * grad_key))
        grads[:, at : at + key_dim] = grad_query.astype(BF16)
        grads[:, key_at : key_at + key_dim] = grad_key.astype(BF16)
        grads[:, value_at : value_at + value_dim] = (betas * grad_target).astype(BF16)
        gate_grads = jnp.where(lanes == head, grad_decay, gate_grads)
        gate_grads = jnp.where(lanes == heads + head, grad_beta, gate_grads)
    grads[:, gate_at : gate_at + 128] = gate_grads.astype(BF16)
    size = own.shape[0]
    own[...] = grads[pl.ds(pl.multiple_of(core * size, size), size), :]
    send[...] = grads[pl.ds(pl.multiple_of((1 - core) * size, size), size), :]


def return_kernel(own, other, query, key, value, decay, beta, part_low, part_high):
    half_key = query.shape[0] // 2
    half_value = value.shape[0] // 2
    first = lax.axis_index("outer") % 2 == 0

    def sides(at, size):
        mine, yours = own[:, at : at + size], other[:, at : at + size]
        return jnp.concatenate(
            [jnp.where(first, mine, yours), jnp.where(first, yours, mine)], axis=1
        )

    gate_at = 2 * half_key + half_value
    heads = decay.shape[0] // 2
    sums = dot(sides(0, half_key), query[...])
    sums = sums + dot(sides(half_key, half_key), key[...])
    sums = sums + dot(sides(2 * half_key, half_value), value[...])
    sums = sums + dot(sides(gate_at, heads), decay[...])
    sums = sums + dot(sides(gate_at + heads, heads), beta[...])
    half = part_low.shape[0]
    part_low[...] = sums[:half].astype(BF16)
    part_high[...] = sums[half:].astype(BF16)


def final_kernel(low, low_other, high, high_other, mixed, gain, hidden, down, out):
    total = whole(low, low_other, high, high_other)
    rows = mixed[...]
    scale = lax.rsqrt(jnp.mean(rows * rows, axis=-1, keepdims=True) + 1e-06)
    gained = total * gain[...]
    along = jnp.mean(rows * gained, axis=-1, keepdims=True)
    taken = (scale * gained - rows * (scale * scale * scale * along)).astype(BF16)
    for at, size in spans(down.shape[1], 512):
        product = dot(taken, down[:, at : at + size])
        out[:, at : at + size] = hidden[:, at : at + size] * product


def swap(array, axis, bit):
    return lax.ppermute(array, axis, [(i, i ^ bit) for i in range(lax.axis_size(axis))])


def swap_inner(arrays):
    return [swap(array, "inner", which + 1) for which, array in enumerate(arrays)]


def four_chips(
    tokens, step_index, embed_table, gain_one, gate_weight, up_weight, down_weight, gain_two,
    query_weight, key_weight, value_weight, decay_weight, beta_weight,
    rate_log, decay_bias, beta_bias, cotangent,
):
    count, model = tokens.shape[0], gain_one.shape[0]
    width = gate_weight.shape[1]
    head_count = rate_log.shape[0]
    heads = head_count // 2
    key_dim = query_weight.shape[1] // head_count
    value_dim = value_weight.shape[1] // head_count
    pack_width = heads * (2 * key_dim + value_dim) + 128
    length = 2 * count
    half_shape = like((count // 2, model), BF16)
    rows_shape = like((count, model), BF16)
    dma = pltpu.SemaphoreType.DMA
    cot_half = heads * value_dim
    columns, cot_own, cot_send = call(
        embed_kernel,
        [like((count, embed_table.shape[1]), BF16)]
        + [like((count, cot_half), BF16)] * 2,
        [HBM] * 3,
        [
            pltpu.SMEM((1, count), jnp.int32),
            pltpu.VMEM((1, count), jnp.int32),
            pltpu.VMEM((16 * count, embed_table.shape[1]), BF16),
            dma((2,)),
            dma,
            dma((2,)),
        ],
    )(pinned(tokens.reshape(1, count)), pinned(embed_table), pinned(cotangent))
    cot_other = swap(cot_send, "outer", 1)
    pieces = [columns] + swap_inner([columns] * 3)
    (down_kept,) = fetch(columns, [down_weight], [gate_weight, up_weight])
    hidden, emb, part_low, part_high = call(
        feed_kernel,
        [like((count, width), F32), rows_shape] + [half_shape] * 2,
        [SMEM] + [VMEM] * 8,
        [
            pltpu.VMEM((count, width), BF16),
        ],
    )(
        step_index, *pieces, gain_one.reshape(1, model), gate_weight, up_weight, down_kept
    )
    weights = fetch(part_low, [query_weight, key_weight])
    sums = pair_sums(part_low, part_high, [weights[0], cot_other])
    weights += fetch(sums[0], [value_weight])
    weights = (*weights, decay_weight.T, beta_weight.T)
    mixed, own, send = call(
        project_kernel,
        [like((count, model), F32)] + [like((count, pack_width), BF16)] * 2,
        [VMEM] * 11,
    )(emb, *sums, gain_two.reshape(1, model), *weights)
    other = swap(send, "outer", 1)
    square = (heads, length, length)
    valued = (heads, length, value_dim)
    packs, cots, sent, sent_map, kept_offset, kept_map, *saved = call(
        front_kernel,
        [
            like((length, pack_width), BF16),
            like((length, cot_half), BF16),
            like((heads, key_dim, value_dim), BF16),
            like((heads, key_dim, key_dim), BF16),
            like((heads, key_dim, value_dim), F32),
            like((heads, key_dim, key_dim), BF16),
            like(square, F32),
            like(square, F32),
            like(square, BF16),
            like(square, F32),
            like((heads, length, key_dim), BF16),
            like(valued, F32),
            like(valued, F32),
            like((heads, length, 128), F32),
        ],
        [VMEM] * 4 + [SMEM] * 3,
    )(own, other, cot_own, cot_other, rate_log, decay_bias, beta_bias)
    near = swap(sent, "outer", 2)
    query_turned, key_turned = turned(sent, weights[:2])
    near_map = swap(sent_map, "outer", 2)
    joined = call(combine_kernel, like((heads, key_dim, value_dim), BF16), [VMEM] * 3 + [HBM])(
        kept_map, kept_offset, near, query_turned
    )
    (value_turned,) = turned(joined, weights[2:3])
    cycle = {1: 3, 3: 2, 2: 0, 0: 1}
    far_two = lax.ppermute(
        joined, "outer", [(2 * a + core, 2 * b + core) for a, b in cycle.items() for core in (0, 1)]
    )
    far_one = lax.ppermute(joined, "outer", [(2, 4), (3, 5), (4, 2), (5, 3)])
    own, send = call(
        back_kernel,
        [like((count, pack_width), BF16)] * 2,
        [VMEM] * 14 + [HBM],
        [pltpu.VMEM((length, pack_width), BF16)],
    )(near, near_map, far_one, far_two, packs, cots, *saved, value_turned)
    other = swap(send, "outer", 1)
    part_low, part_high = call(return_kernel, [half_shape] * 2, [VMEM] * 7)(
        own, other, query_turned, key_turned, value_turned, *weights[3:]
    )
    (down_turned,) = turned(part_low, [down_kept])
    sums = pair_sums(part_low, part_high, [down_turned])
    return call(final_kernel, jax.ShapeDtypeStruct((count, width), F32), [VMEM] * 8)(
        *sums, mixed, gain_two.reshape(1, model), hidden, down_turned
    )


def local_part(*args):
    fits = (
        lax.axis_size("inner") == 4
        and lax.axis_size("outer") == 8
        and args[0].shape[0] == 64
        and args[13].shape[0] % 2 == 0
    )
    return four_chips(*args) if fits else shards(*args)


def solution(mesh):
    placed = (
        P("outer"),
        P(),
        P(None, "inner"),
        P(),
        P(None, "inner"),
        P(None, "inner"),
        P("inner", None),
        P(),
        P(None, "inner"),
        P(None, "inner"),
        P(None, "inner"),
        P(None, "inner"),
        P(None, "inner"),
        P("inner"),
        P("inner"),
        P("inner"),
        P("outer", "inner"),
    )
    return jax.shard_map(
        local_part, mesh=mesh, in_specs=placed, out_specs=P("outer", "inner"), check_vma=False
    )
```

```python
import functools
import math

import jax
import jax.numpy as jnp
from jax import lax
from jax.experimental import pallas as pl
from jax.experimental.pallas import tpu as pltpu
from jax.sharding import PartitionSpec as P

STEPS = 32


def from_behind(array, axis, by):
    devices = lax.axis_size(axis)
    pairs = [(i, i + by) for i in range(devices) if 0 <= i + by < devices]
    return lax.ppermute(array, axis, pairs)


def unit_rows(values):
    return values * lax.rsqrt(jnp.sum(values * values, axis=-1, keepdims=True) + 1e-06)


def head_inputs(query_rows, key_rows, decay_rows, beta_rows, log_rate, rate_shift, beta_shift):
    queries = unit_rows(query_rows) * query_rows.shape[-1] ** (-0.5)
    keys_unit = unit_rows(key_rows)
    log_decay = -jnp.exp(log_rate) * jax.nn.softplus(decay_rows + rate_shift)
    betas = jax.nn.sigmoid(beta_rows + beta_shift)
    return (queries, keys_unit, log_decay, betas)


def block_step(with_out, state, pieces):
    queries, keys_unit, values, log_decay, betas = pieces
    block_len = keys_unit.shape[0]
    highest = lax.Precision.HIGHEST
    cum_decay = jnp.cumsum(log_decay)
    row_ids = jnp.arange(block_len)[:, None]
    col_ids = jnp.arange(block_len)[None, :]
    lower_mask = row_ids >= col_ids
    decay_mat = jnp.where(
        lower_mask,
        jnp.exp(jnp.where(lower_mask, cum_decay[:, None] - cum_decay[None, :], 0.0)),
        0.0,
    )
    key_gram = jnp.dot(keys_unit, keys_unit.T, precision=highest)
    strict = jnp.where(row_ids > col_ids, betas[:, None] * decay_mat * key_gram, 0.0)
    system = strict + jnp.eye(block_len, dtype=jnp.float32)
    start_scale = jnp.exp(cum_decay)[:, None]
    target = betas[:, None] * (values - start_scale * jnp.dot(keys_unit, state, precision=highest))
    fresh_vals = lax.linalg.triangular_solve(
        system, target, left_side=True, lower=True, unit_diagonal=True
    )
    tail_keys = jnp.exp(cum_decay[-1] - cum_decay)[:, None] * keys_unit
    new_state = jnp.exp(cum_decay[-1]) * state + jnp.dot(tail_keys.T, fresh_vals, precision=highest)
    if with_out:
        scores = decay_mat * jnp.dot(queries, keys_unit.T, precision=highest)
        output = start_scale * jnp.dot(queries, state, precision=highest) + jnp.dot(
            scores, fresh_vals, precision=highest
        )
        return (new_state, output)
    return (new_state, None)


def run_blocks(queries, keys_unit, values, log_decay, betas, state, with_out):
    length = keys_unit.shape[0]
    block_len = math.gcd(64, length)
    block_count = length // block_len

    def blocked(array):
        return array.reshape((block_count, block_len) + array.shape[1:])

    step_fn = functools.partial(block_step, with_out)
    final_state, outputs = lax.scan(
        step_fn,
        state,
        (blocked(queries), blocked(keys_unit), blocked(values), blocked(log_decay), blocked(betas)),
    )
    if with_out:
        outputs = outputs.reshape((length,) + outputs.shape[2:])
    return (final_state, outputs)


def rms_scaled(values, gain):
    return values * lax.rsqrt(jnp.mean(values * values, axis=-1, keepdims=True) + 1e-06) * gain


def apply_map(matrix, state):
    return jnp.einsum("hij,hjv->hiv", matrix, state, precision=lax.Precision.HIGHEST)


def shards(
    tokens,
    step_index,
    embed_table,
    gain_one,
    gate_weight,
    up_weight,
    down_weight,
    gain_two,
    query_weight,
    key_weight,
    value_weight,
    decay_weight,
    beta_weight,
    rate_log,
    decay_bias,
    beta_bias,
    cotangent,
):
    columns = jnp.take(embed_table, tokens, axis=0)
    embedded = lax.all_gather(columns, "inner", axis=1, tiled=True)
    emb_float = embedded.astype(jnp.float32)
    normed_one = rms_scaled(emb_float, gain_one).astype(jnp.bfloat16)
    gate_rows = jnp.dot(normed_one, gate_weight, preferred_element_type=jnp.float32)
    up_rows = jnp.dot(normed_one, up_weight, preferred_element_type=jnp.float32)
    hidden = jax.nn.silu(gate_rows) * up_rows
    path_scale = (step_index[0].astype(jnp.float32) + 0.5) / STEPS
    scaled = (path_scale * hidden).astype(jnp.bfloat16)
    group_rows = tokens.shape[0]
    row_share = group_rows // lax.axis_size("inner")
    head_count = rate_log.shape[0]
    key_dim = query_weight.shape[1] // head_count
    value_dim = value_weight.shape[1] // head_count
    main_weight = jnp.concatenate([query_weight, key_weight, value_weight], axis=1)
    gate_pair = jnp.concatenate([decay_weight, beta_weight], axis=1)

    def normalize(values):
        return rms_scaled(values, gain_two)

    mixed_share = lax.psum_scatter(
        jnp.dot(scaled, down_weight, preferred_element_type=jnp.float32).astype(jnp.bfloat16),
        "inner",
        scatter_dimension=0,
        tiled=True,
    ).astype(jnp.float32)
    own_rows = lax.dynamic_slice_in_dim(
        emb_float, lax.axis_index("inner") * row_share, row_share, 0
    )
    normed_float, norm_pull = jax.vjp(normalize, own_rows + mixed_share)
    block_piece = lax.all_gather(normed_float.astype(jnp.bfloat16), "inner", axis=0, tiled=True)
    main_part = jnp.dot(block_piece, main_weight, preferred_element_type=jnp.float32)
    gate_part = jnp.dot(block_piece, gate_pair, preferred_element_type=jnp.float32)
    projected = jnp.concatenate([main_part, gate_part], axis=1)
    key_span = head_count * key_dim
    value_span = head_count * value_dim

    def by_head(columns_block, width):
        return columns_block.reshape(group_rows, head_count, width).transpose(1, 0, 2)

    query_pre = by_head(projected[:, :key_span], key_dim)
    key_pre = by_head(projected[:, key_span : 2 * key_span], key_dim)
    value_pre = by_head(projected[:, 2 * key_span : 2 * key_span + value_span], value_dim)
    gate_start = 2 * key_span + value_span
    decay_pre = projected[:, gate_start : gate_start + head_count].T
    beta_pre = projected[:, gate_start + head_count : gate_start + 2 * head_count].T
    cot_heads = by_head(cotangent.astype(jnp.float32), value_dim)

    def carry_map(key_rows, value_rows, decay_rows, beta_rows, log_rate, rate_shift, beta_shift):
        unused_query, keys_unit, log_decay, betas = head_inputs(
            key_rows, key_rows, decay_rows, beta_rows, log_rate, rate_shift, beta_shift
        )
        padded_vals = jnp.concatenate(
            [value_rows, jnp.zeros((key_rows.shape[0], key_dim), jnp.float32)], axis=1
        )
        start_state = jnp.concatenate(
            [jnp.zeros((key_dim, value_dim), jnp.float32), jnp.eye(key_dim, dtype=jnp.float32)],
            axis=1,
        )
        final_state, unused_out = run_blocks(
            keys_unit, keys_unit, padded_vals, log_decay, betas, start_state, False
        )
        return final_state

    joined_state = jax.vmap(carry_map)(
        key_pre, value_pre, decay_pre, beta_pre, rate_log, decay_bias, beta_bias
    )
    offset_state = joined_state[:, :, :value_dim]
    transition = joined_state[:, :, value_dim:]

    def forward_step(turn_index, carried):
        incoming = from_behind(carried[1].astype(jnp.bfloat16), "outer", 1).astype(jnp.float32)
        return (incoming, apply_map(transition, incoming) + offset_state)

    state_in, unused_end = lax.fori_loop(
        0, lax.axis_size("outer") - 1, forward_step, (jnp.zeros_like(offset_state), offset_state)
    )

    def local_score(query_in, key_in, value_in, decay_in, beta_in, start_in):

        def one_head(
            query_rows,
            key_rows,
            value_rows,
            decay_rows,
            beta_rows,
            start_state,
            cot_rows,
            log_rate,
            rate_shift,
            beta_shift,
        ):
            queries, keys_unit, log_decay, betas = head_inputs(
                query_rows, key_rows, decay_rows, beta_rows, log_rate, rate_shift, beta_shift
            )
            final_state, outputs = run_blocks(
                queries, keys_unit, value_rows, log_decay, betas, start_state, True
            )
            return (jnp.sum(outputs * cot_rows), final_state)

        head_scores, final_states = jax.vmap(one_head)(
            query_in,
            key_in,
            value_in,
            decay_in,
            beta_in,
            start_in,
            cot_heads,
            rate_log,
            decay_bias,
            beta_bias,
        )
        return (jnp.sum(head_scores), final_states)

    score_pair, pull_back = jax.vjp(
        local_score, query_pre, key_pre, value_pre, decay_pre, beta_pre, state_in
    )
    first_pull = pull_back((jnp.ones_like(score_pair[0]), jnp.zeros_like(score_pair[1])))
    grad_local = first_pull[5]
    grad_trans = jnp.swapaxes(transition, 1, 2)

    def backward_step(turn_index, carried):
        incoming = from_behind(carried[1].astype(jnp.bfloat16), "outer", -1).astype(jnp.float32)
        return (incoming, apply_map(grad_trans, incoming) + grad_local)

    state_grad, unused_start = lax.fori_loop(
        0, lax.axis_size("outer") - 1, backward_step, (jnp.zeros_like(grad_local), grad_local)
    )
    second_pull = pull_back((jnp.zeros_like(score_pair[0]), state_grad))
    summed = [first_pull[which] + second_pull[which] for which in range(5)]

    def by_rows(head_block):
        return head_block.transpose(1, 0, 2).reshape(group_rows, -1).astype(jnp.bfloat16)

    grad_main = jnp.concatenate(
        [by_rows(summed[0]), by_rows(summed[1]), by_rows(summed[2])], axis=1
    )
    grad_gates = jnp.concatenate(
        [summed[3].T.astype(jnp.bfloat16), summed[4].T.astype(jnp.bfloat16)], axis=1
    )
    main_part = jnp.dot(grad_main, main_weight.T, preferred_element_type=jnp.float32)
    back_share = lax.psum_scatter(
        (main_part + jnp.dot(grad_gates, gate_pair.T, preferred_element_type=jnp.float32)).astype(
            jnp.bfloat16
        ),
        "inner",
        scatter_dimension=0,
        tiled=True,
    ).astype(jnp.float32)
    grad_mixed = norm_pull(back_share)[0].astype(jnp.bfloat16)
    return hidden * jnp.dot(
        lax.all_gather(grad_mixed, "inner", axis=0, tiled=True),
        down_weight.T,
        preferred_element_type=jnp.float32,
    )


BF16 = jnp.bfloat16
F32 = jnp.float32
MIB = 1 << 20
FETCH_PARTS = 4
TURN_ROWS = 128
BASE = 16
VMEM = pl.BlockSpec(memory_space=pltpu.VMEM)
SMEM = pl.BlockSpec(memory_space=pltpu.SMEM)
HBM = pl.BlockSpec(memory_space=pl.ANY)


def pinned(array):
    return pltpu.with_memory_space_constraint(array, pltpu.HBM)


def call(kernel, out_shape, in_specs, scratch=(), limit=16 * MIB, out=VMEM):
    return pl.pallas_call(
        kernel,
        out_shape=out_shape,
        in_specs=in_specs,
        out_specs=jax.tree.map(lambda _: out, out_shape),
        scratch_shapes=list(scratch),
        compiler_params=pltpu.CompilerParams(vmem_limit_bytes=limit),
        cost_estimate=pl.CostEstimate(flops=0, bytes_accessed=0, transcendentals=0),
    )


def like(shape, dtype):
    return jax.ShapeDtypeStruct(shape, dtype)


def dot(a, b, transposed=False):
    dims = (((1,), (1 if transposed else 0,)), ((), ()))
    return lax.dot_general(a, b, dims, preferred_element_type=F32)


def mm(a, b, transposed=False):
    return dot(a.astype(BF16), b.astype(BF16), transposed)


def row_sum(values):
    return jnp.sum(values, axis=-1, keepdims=True)


def spans(total, step):
    return [(at, min(step, total - at)) for at in range(0, total, step)]


def stream(pairs, sems):
    copies = [
        pltpu.make_async_copy(source, target, sems.at[which])
        for which, (source, target) in enumerate(pairs)
    ]
    for copy in copies:
        copy.start()
    return copies


def grid_ids(size):
    shape = (size, size)
    return lax.broadcasted_iota(jnp.int32, shape, 0), lax.broadcasted_iota(jnp.int32, shape, 1)


def quarters(source, target):
    cuts = spans(source.shape[0], source.shape[0] // FETCH_PARTS)
    return [(source.at[pl.ds(at, size)], target.at[pl.ds(at, size)]) for at, size in cuts]


def embed_kernel(
    ids_in, table, cot, out, cot_own, cot_send,
    ids, id_row, blocks, id_sems, sem, cot_sems,
):
    count = out.shape[0]
    copies = stream([(ids_in, ids), (ids_in, id_row)], id_sems)
    copies[0].wait()
    for which in range(count):
        base = pl.multiple_of((ids[0, which] // 16) * 16, 16)
        pltpu.make_async_copy(
            table.at[pl.ds(base, 16)], blocks.at[pl.ds(which * 16, 16)], sem
        ).start()
    core, half = lax.axis_index("outer") % 2, cot_own.shape[1]
    mine = pl.ds(pl.multiple_of(core * half, half), half)
    yours = pl.ds(pl.multiple_of((1 - core) * half, half), half)
    halves = stream([(cot.at[:, mine], cot_own), (cot.at[:, yours], cot_send)], cot_sems)
    copies[1].wait()
    row_ids, col_ids = grid_ids(count)
    low_bits = jnp.broadcast_to(id_row[...] & 15, (count, count))
    inside = row_sum(jnp.where(row_ids == col_ids, low_bits, 0).astype(F32)).astype(jnp.int32)
    wide = (count, 16 * count)
    wanted = lax.broadcasted_iota(jnp.int32, wide, 0) * 16 + inside
    pick = jnp.where(lax.broadcasted_iota(jnp.int32, wide, 1) == wanted, 1.0, 0.0).astype(BF16)
    pltpu.make_async_copy(table.at[pl.ds(0, 16 * count)], blocks, sem).wait()
    out[...] = dot(pick, blocks[...]).astype(BF16)
    for copy in halves:
        copy.wait()


def fetch_kernel(count, *refs):
    sources, targets, sems = refs[-1 - 2 * count : -1 - count], refs[-1 - count : -1], refs[-1]
    pairs = []
    for source, target in zip(sources, targets):
        pairs += quarters(source, target)
    for copy in stream(pairs, sems):
        copy.wait()


def fetch(after, arrays, beside=()):
    return call(
        functools.partial(fetch_kernel, len(arrays)),
        [like(array.shape, BF16) for array in arrays],
        [HBM] * (1 + len(beside) + len(arrays)),
        [pltpu.SemaphoreType.DMA((FETCH_PARTS * len(arrays),))],
        limit=MIB,
    )(after, *beside, *[pinned(array) for array in arrays])


def turn(source, target):
    for at, size in spans(source.shape[0], TURN_ROWS):
        target[:, at : at + size] = jnp.transpose(source[at : at + size, :])


def turn_kernel(count, *refs):
    for source, target in zip(refs[1 : 1 + count], refs[1 + count :]):
        turn(source, target)


def turned(after, arrays):
    return call(
        functools.partial(turn_kernel, len(arrays)),
        [like(array.shape[::-1], BF16) for array in arrays],
        [HBM] + [VMEM] * len(arrays),
        limit=4 * MIB,
    )(after, *arrays)


def feed_own_kernel(
    piece, gain, gate, up, down, gate_part, up_part, square, down_kept, sems
):
    copies = stream(quarters(down, down_kept), sems)
    share = piece.shape[1]
    at = pl.multiple_of(lax.axis_index("inner") * share, share)
    rows = piece[...].astype(F32)
    square[...] = jnp.broadcast_to(row_sum(rows * rows), square.shape)
    taken = (rows * gain[:, pl.ds(at, share)]).astype(BF16)
    for start, size in spans(gate.shape[1], 512):
        span = slice(start, start + size)
        gate_part[:, span] = dot(taken, gate[pl.ds(at, share), span])
        up_part[:, span] = dot(taken, up[pl.ds(at, share), span])
    for copy in copies:
        copy.wait()


def feed_kernel(
    step, piece0, piece1, piece2, piece3, gain, gate, up, down, gate_part, up_part, square,
    hidden, emb, scaled, part_low,
):
    width = hidden.shape[1]
    me = lax.axis_index("inner")
    share = piece0.shape[1]
    squares = square[:, :1]
    taken = []
    for which, piece in enumerate((piece0, piece1, piece2, piece3)):
        at = pl.multiple_of((me ^ which) * share, share)
        emb[:, pl.ds(at, share)] = piece[...]
        if which > 0:
            rows = piece[...].astype(F32)
            squares = squares + row_sum(rows * rows)
            taken.append((at, (rows * gain[:, pl.ds(at, share)]).astype(BF16)))
    scale = lax.rsqrt(squares / emb.shape[1] + 1e-06)
    path_scale = (step[0].astype(F32) + 0.5) / STEPS
    for start, size in spans(width, 512):
        span = slice(start, start + size)
        gate_rows, up_rows = gate_part[:, span], up_part[:, span]
        for at, rows in taken:
            gate_rows = gate_rows + dot(rows, gate[pl.ds(at, share), span])
            up_rows = up_rows + dot(rows, up[pl.ds(at, share), span])
        gate_rows = scale * gate_rows
        units = gate_rows / (1.0 + jnp.exp(-gate_rows)) * (scale * up_rows)
        hidden[:, span] = units
        scaled[:, span] = (path_scale * units).astype(BF16)
    down_kernel(0, scaled, down, part_low)


def down_kernel(begin, scaled, down, part):
    for start, size in spans(part.shape[1], 512):
        sums = dot(scaled[...], down[:, begin + start : begin + start + size])
        part[:, start : start + size] = sums.astype(BF16)


def pair_kernel(mine, other, *refs):
    refs[-1][...] = (mine[...].astype(F32) + other[...].astype(F32)).astype(BF16)


def pair_sums(low, high, before):
    shape = like(low.shape, BF16)
    low_other, high_other = swap(low, "inner", 1), swap(high, "inner", 2)
    low = call(pair_kernel, shape, [VMEM] * 2 + [HBM] * len(before))(low, low_other, *before)
    low_other = swap(low, "inner", 2)
    high = call(pair_kernel, shape, [VMEM] * 2)(high, high_other)
    return low, low_other, high, swap(high, "inner", 1)


def added(mine, other):
    return mine[...].astype(F32) + other[...].astype(F32)


def half_product(begin, emb, mine, other, gain, mixed, weights, gate_weights):
    half = mixed.shape[1]
    span = slice(begin, begin + half)
    total = emb[:, span].astype(F32) + added(mine, other)
    mixed[...] = total
    taken = (total * gain[:, span]).astype(BF16)
    raw = [dot(taken, weight[span, :]) for weight in weights]
    gates = [dot(taken, weight[:, span], True) for weight in gate_weights]
    return raw, gates, row_sum(total * total)


def project_low_kernel(
    emb, low, low_other, gain, query, key, value, decay, beta,
    mixed, query_raw, key_raw, value_raw, gate_raw, square,
):
    raw, gates, squares = half_product(
        0, emb, low, low_other, gain, mixed, (query, key, value), (decay, beta)
    )
    query_raw[...], key_raw[...], value_raw[...] = raw
    heads = decay.shape[0]
    gate_raw[:, :heads], gate_raw[:, heads : 2 * heads] = gates
    square[...] = jnp.broadcast_to(squares, square.shape)


def project_kernel(
    emb, high, high_other, gain, query, key, value, decay, beta,
    query_raw, key_raw, value_raw, gate_raw, square,
    mixed, own, send, scales,
):
    half_key = query.shape[1] // 2
    half_value = value.shape[1] // 2
    all_heads = decay.shape[0]
    first = lax.axis_index("outer") % 2 == 0
    raw, gates, squares = half_product(
        mixed.shape[1], emb, high, high_other, gain, mixed, (query, key, value), (decay, beta)
    )
    scale = lax.rsqrt((squares + square[:, :1]) / emb.shape[1] + 1e-06)
    scales[...] = jnp.broadcast_to(scale, scales.shape)
    query_rows, key_rows, value_rows = [
        scale * (part + rest[...]) for part, rest in zip(raw, (query_raw, key_raw, value_raw))
    ]
    gates = [
        scale * (gates[0] + gate_raw[:, :all_heads]),
        scale * (gates[1] + gate_raw[:, all_heads : 2 * all_heads]),
    ]

    def put(at, low, high):
        size = low.shape[1]
        own[:, at : at + size] = jnp.where(first, low, high).astype(BF16)
        send[:, at : at + size] = jnp.where(first, high, low).astype(BF16)

    heads = decay.shape[0] // 2
    lanes = lax.broadcasted_iota(jnp.int32, scales.shape, 1)
    packed = []
    for side in range(2):
        lane, pack = 0, jnp.zeros(scales.shape, F32)
        for values in gates:
            for head in range(side * heads, (side + 1) * heads):
                column = values[:, head : head + 1]
                top = column.astype(BF16).astype(F32)
                pack = jnp.where(lanes == lane, top, pack)
                pack = jnp.where(lanes == lane + 1, column - top, pack)
                lane += 2
        packed.append(pack)
    put(0, query_rows[:, :half_key], query_rows[:, half_key:])
    put(half_key, key_rows[:, :half_key], key_rows[:, half_key:])
    put(2 * half_key, value_rows[:, :half_value], value_rows[:, half_value:])
    put(2 * half_key + half_value, *packed)


def both_blocks(own, other, target):
    core = lax.axis_index("outer") % 2
    size = own.shape[0]
    target[pl.ds(pl.multiple_of(core * size, size), size), :] = own[...]
    target[pl.ds(pl.multiple_of((1 - core) * size, size), size), :] = other[...]


def cumulate(chosen, column):
    top = column.astype(BF16)
    rest = column - top.astype(F32)
    middle = rest.astype(BF16)
    low = (rest - middle.astype(F32)).astype(BF16)
    picked = jnp.where(chosen, 1.0, 0.0).astype(BF16)

    def part(values):
        return dot(picked, jnp.broadcast_to(values, (values.shape[0], 128)))

    return part(top) + (part(middle) + part(low))


def unit_inverses(systems):
    size = systems[0].shape[0]
    row_ids, col_ids = grid_ids(size)
    apart = row_ids - col_ids
    near = row_ids // BASE == col_ids // BASE

    def diagonal(which):
        picked = near & (apart == which)
        rows = [jnp.sum(jnp.where(picked, a, 0.0), axis=0, keepdims=True) for a in systems]
        return jnp.concatenate(rows, axis=0)

    def ahead(rows, by):
        return rows if by == 0 else pltpu.roll(rows, size - by, 1)

    given = [None] + [diagonal(which) for which in range(1, BASE)]
    found = [jnp.ones((len(systems), size), F32)]
    for which in range(1, BASE):
        terms = [ahead(given[j], which - j) * found[which - j] for j in range(1, which + 1)]
        while len(terms) > 1:
            pairs = [a + b for a, b in zip(terms[::2], terms[1::2])]
            terms = pairs + terms[2 * len(pairs) :]
        found.append(-terms[0])
    inverses = []
    for head, system in enumerate(systems):
        inverse = jnp.zeros((size, size), F32)
        for which in range(BASE):
            inverse = jnp.where(apart == which, found[which][head : head + 1], inverse)
        block = BASE
        while block < size:
            below = (row_ids // (2 * block) == col_ids // (2 * block)) & (
                row_ids // block != col_ids // block
            )
            inverse = inverse - mm(mm(inverse, jnp.where(below, system, 0.0)), inverse)
            block *= 2
        inverses.append(inverse)
    return inverses


def front_kernel(
    own, other, cot_own, cot_other, rate_log, decay_bias, beta_bias,
    packs, cots, sent, kept_offset, tails,
    decay_mats, grams, inverses, scores, maps, fresh, pulled, columns,
):
    both_blocks(own, other, packs)
    both_blocks(cot_own, cot_other, cots)
    heads, length, _ = decay_mats.shape
    key_dim, value_dim = maps.shape[2], fresh.shape[2]
    place = lax.axis_index("outer")
    even = (place // 2) % 2 == 0
    first_head = (place % 2) * heads
    row_ids, col_ids = grid_ids(length)
    lower, strictly = row_ids >= col_ids, row_ids > col_ids
    lanes = lax.broadcasted_iota(jnp.int32, (length, 128), 1)
    gate_at = heads * (2 * key_dim + value_dim)
    gates = packs[:, gate_at : gate_at + 128].astype(F32)
    ready = []
    for head in range(heads):
        at = head * key_dim
        query_rows = packs[:, at : at + key_dim].astype(F32)
        at += heads * key_dim
        key_rows = packs[:, at : at + key_dim].astype(F32)
        at = 2 * heads * key_dim + head * value_dim
        values = packs[:, at : at + value_dim].astype(F32)
        cot = cots[:, head * value_dim : (head + 1) * value_dim]
        lane = 2 * head
        decay_in = gates[:, lane : lane + 1] + gates[:, lane + 1 : lane + 2]
        decay_in = decay_in + decay_bias[first_head + head]
        lane += 2 * heads
        beta_in = gates[:, lane : lane + 1] + gates[:, lane + 1 : lane + 2]
        beta_in = beta_in + beta_bias[first_head + head]
        rate = jnp.exp(jnp.full((length, 1), rate_log[first_head + head], F32))
        query_scale = lax.rsqrt(row_sum(query_rows * query_rows) + 1e-06) * key_dim ** (-0.5)
        key_scale = lax.rsqrt(row_sum(key_rows * key_rows) + 1e-06)
        queries, keys_unit = query_rows * query_scale, key_rows * key_scale
        log_decay = -rate * (jnp.maximum(decay_in, 0.0) + jnp.log1p(jnp.exp(-jnp.abs(decay_in))))
        betas = 1.0 / (1.0 + jnp.exp(-beta_in))
        cum = cumulate(lower, log_decay)
        decay_mat = jnp.where(
            lower, jnp.exp(jnp.where(lower, cum - jnp.transpose(cum), 0.0)), 0.0
        )
        total = cum[:, :1]
        start_scale = jnp.exp(total)
        tail_scale = jnp.exp(total[length - 1 :] - total)
        gram = jnp.where(strictly, decay_mat * mm(keys_unit, keys_unit, True), 0.0)
        ready.append(
            (
                queries, keys_unit, values, cot, decay_mat, gram, start_scale, tail_scale,
                betas, query_scale, key_scale, decay_in, rate,
            )
        )
    inverse_list = unit_inverses([item[8] * item[5] for item in ready])
    for head, inverse in enumerate(inverse_list):
        (
            queries, keys_unit, values, cot, decay_mat, gram, start_scale, tail_scale,
            betas, query_scale, key_scale, decay_in, rate,
        ) = ready[head]
        score = decay_mat * mm(queries, keys_unit, True)
        state_map = mm(inverse, (betas * start_scale) * keys_unit)
        fresh_vals = mm(inverse, betas * values)
        tail_t = jnp.transpose(tail_scale * keys_unit)
        offset = mm(tail_t, fresh_vals)
        score_pull = mm(jnp.transpose(score), cot)
        grad_local = mm(jnp.transpose(start_scale * queries), cot) - mm(
            jnp.transpose(state_map), score_pull
        )
        sent[head] = jnp.where(even, offset, grad_local).astype(BF16)
        kept_offset[head] = jnp.where(even, grad_local, offset)
        tails[head] = tail_t.astype(BF16)
        decay_mats[head] = decay_mat
        grams[head] = gram
        inverses[head] = inverse
        scores[head] = score
        maps[head] = state_map.astype(BF16)
        fresh[head] = fresh_vals
        pulled[head] = score_pull
        pack = jnp.zeros((length, 128), F32)
        for lane, column in enumerate(
            (query_scale, key_scale, betas, start_scale, tail_scale, decay_in, rate)
        ):
            pack = jnp.where(lanes == lane, column, pack)
        columns[head] = pack


def maps_kernel(
    tails, inverses, maps, pulled, columns, after, sent_map, kept_map, target_local, target_map
):
    heads, length, _ = inverses.shape
    even = (lax.axis_index("outer") // 2) % 2 == 0
    row_ids, col_ids = grid_ids(length)
    for head in range(heads):
        end_scale = columns[head, length - 1 :, 3:4]
        inverse, tail_t = inverses[head], tails[head]
        transition = jnp.where(row_ids == col_ids, end_scale, 0.0) - dot(tail_t, maps[head])
        flipped = jnp.transpose(transition)
        sent_map[head] = jnp.where(even, transition, flipped).astype(BF16)
        kept_map[head] = jnp.where(even, flipped, transition).astype(BF16)
        target_local[head] = mm(jnp.transpose(inverse), pulled[head])
        target_map[head] = jnp.transpose(mm(tail_t, inverse)).astype(BF16)


def combine_kernel(kept_map, kept_offset, got, after, out):
    for head in range(out.shape[0]):
        joined = dot(kept_map[head], got[head]) + kept_offset[head]
        out[head] = joined.astype(BF16)


def back_kernel(
    near, near_map, far_one, far_two, packs, cots,
    decay_mats, grams, scores, maps, fresh, columns, target_local, target_map, after,
    own, send, grads,
):
    heads, length, _ = decay_mats.shape
    key_dim, value_dim = maps.shape[2], fresh.shape[2]
    place = lax.axis_index("outer")
    core, chip = place % 2, place // 2
    outer_chip = (chip == 0) | (chip == 3)
    odd = chip % 2 == 1
    row_ids, col_ids = grid_ids(length)
    strictly, upper = row_ids > col_ids, row_ids <= col_ids
    lanes = lax.broadcasted_iota(jnp.int32, (length, 128), 1)
    gate_at = heads * (2 * key_dim + value_dim)
    gate_grads = jnp.zeros((length, 128), F32)
    for head in range(heads):
        at = head * key_dim
        query_rows = packs[:, at : at + key_dim].astype(F32)
        key_at = at + heads * key_dim
        key_rows = packs[:, key_at : key_at + key_dim].astype(F32)
        value_at = 2 * heads * key_dim + head * value_dim
        values = packs[:, value_at : value_at + value_dim].astype(F32)
        cot = cots[:, head * value_dim : (head + 1) * value_dim]
        pack = columns[head]
        query_scale, key_scale, betas = pack[:, 0:1], pack[:, 1:2], pack[:, 2:3]
        start_scale, tail_scale = pack[:, 3:4], pack[:, 4:5]
        decay_in, rate = pack[:, 5:6], pack[:, 6:7]
        end_scale = start_scale[length - 1 :]
        queries, keys_unit = query_rows * query_scale, key_rows * key_scale
        decay_mat, gram, score = decay_mats[head], grams[head], scores[head]
        far = jnp.where(outer_chip, far_two[head], far_one[head])
        close = near[head].astype(F32)
        reached = dot(near_map[head], far) + close
        first = jnp.where(outer_chip, reached, close)
        second = jnp.where(outer_chip, 0.0, far.astype(F32))
        state = jnp.where(odd, first, second)
        state_grad = jnp.where(odd, second, first)
        state_half, state_grad_half = state.astype(BF16), state_grad.astype(BF16)
        new_vals = fresh[head] - dot(maps[head], state_half)
        new_half = new_vals.astype(BF16)
        grad_target = target_local[head] + dot(target_map[head], state_grad_half)
        target_half = grad_target.astype(BF16)
        grad_score = dot(cot, new_half, True)
        grad_sys = jnp.where(strictly, -dot(target_half, new_half, True), 0.0)
        cot_state = dot(cot, state_half, True)
        target_state = dot(target_half, state_half, True)
        new_state = dot(new_half, state_grad_half, True)
        weighted = decay_mat * grad_score
        grad_gram = grad_sys * decay_mat * betas
        grad_query = mm(weighted, keys_unit) + start_scale * cot_state
        grad_key = (
            mm(jnp.transpose(weighted), queries)
            + mm(grad_gram + jnp.transpose(grad_gram), keys_unit)
            + tail_scale * new_state
            - (betas * start_scale) * target_state
        )
        key_target = start_scale * keys_unit * target_state
        sys_gram = grad_sys * gram
        weights = grad_target * values
        grad_beta = row_sum(
            sum(weights[:, at : at + length] for at in range(0, value_dim, length))
            - key_target
            + sys_gram
        )
        both = score * grad_score + betas * sys_gram
        tails = tail_scale * keys_unit * new_state
        grad_cum = row_sum(
            both
            - jnp.transpose(both)
            + start_scale * queries * cot_state
            - betas * key_target
            - tails
        )
        ending = row_sum(jnp.sum(tails, axis=0, keepdims=True)) + end_scale * row_sum(
            jnp.sum(state * state_grad, axis=0, keepdims=True)
        )
        grad_log = cumulate(upper, grad_cum)[:, :1] + ending
        grad_decay = grad_log * -rate / (1.0 + jnp.exp(-decay_in))
        grad_beta = grad_beta * betas * (1.0 - betas)
        units = queries * key_dim**0.5
        grad_query = query_scale * (grad_query - units * row_sum(units * grad_query))
        grad_key = key_scale * (grad_key - keys_unit * row_sum(keys_unit * grad_key))
        grads[:, at : at + key_dim] = grad_query.astype(BF16)
        grads[:, key_at : key_at + key_dim] = grad_key.astype(BF16)
        grads[:, value_at : value_at + value_dim] = (betas * grad_target).astype(BF16)
        gate_grads = jnp.where(lanes == head, grad_decay, gate_grads)
        gate_grads = jnp.where(lanes == heads + head, grad_beta, gate_grads)
    grads[:, gate_at : gate_at + 128] = gate_grads.astype(BF16)
    size = own.shape[0]
    own[...] = grads[pl.ds(pl.multiple_of(core * size, size), size), :]
    send[...] = grads[pl.ds(pl.multiple_of((1 - core) * size, size), size), :]


def return_own_kernel(own, query, key, value, sums):
    half_key = query.shape[0] // 2
    half_value = value.shape[0] // 2
    core = lax.axis_index("outer") % 2
    keys = pl.ds(pl.multiple_of(core * half_key, half_key), half_key)
    values = pl.ds(pl.multiple_of(core * half_value, half_value), half_value)
    for start, size in spans(sums.shape[1], 512):
        span = slice(start, start + size)
        sums[:, span] = (
            dot(own[:, :half_key], query[keys, span])
            + dot(own[:, half_key : 2 * half_key], key[keys, span])
            + dot(own[:, 2 * half_key : 2 * half_key + half_value], value[values, span])
        )


def return_kernel(begin, own, other, query, key, value, decay, beta, sums, part):
    half_key = query.shape[0] // 2
    half_value = value.shape[0] // 2
    core = lax.axis_index("outer") % 2
    first = core == 0
    keys = pl.ds(pl.multiple_of((1 - core) * half_key, half_key), half_key)
    values = pl.ds(pl.multiple_of((1 - core) * half_value, half_value), half_value)

    def sides(at, size):
        mine, yours = own[:, at : at + size], other[:, at : at + size]
        return jnp.concatenate(
            [jnp.where(first, mine, yours), jnp.where(first, yours, mine)], axis=1
        )

    gate_at = 2 * half_key + half_value
    heads = decay.shape[0] // 2
    decays, betas = sides(gate_at, heads), sides(gate_at + heads, heads)
    for start, size in spans(part.shape[1], 512):
        span = slice(begin + start, begin + start + size)
        total = (
            sums[:, span]
            + dot(other[:, :half_key], query[keys, span])
            + dot(other[:, half_key : 2 * half_key], key[keys, span])
            + dot(other[:, 2 * half_key : gate_at], value[values, span])
            + dot(decays, decay[:, span])
            + dot(betas, beta[:, span])
        )
        part[:, start : start + size] = total.astype(BF16)


def along_kernel(mixed_low, mixed_high, down, out):
    half = mixed_low.shape[1]
    out[...] = mm(mixed_low[...], down[:half, :]) + mm(mixed_high[...], down[half:, :])


def final_low_kernel(low, low_other, mixed, gain, down, along, product, dots):
    half = mixed.shape[1]
    gained = added(low, low_other) * gain[:, :half]
    dots[...] = jnp.broadcast_to(row_sum(mixed[...] * gained), dots.shape)
    product[...] = mm(gained, down[:half, :])


def final_kernel(
    high, high_other, mixed, gain, down, product, dots, along, scales, hidden, out, held, sems
):
    half = mixed.shape[1]
    gained = added(high, high_other) * gain[:, half:]
    scale = scales[:, :1]
    mean = (dots[:, :1] + row_sum(mixed[...] * gained)) / (2 * half)
    gained = gained.astype(BF16)
    backward = scale * scale * mean
    copies = []
    for which, (start, size) in enumerate(spans(held.shape[1], 512)):
        span = slice(start, start + size)
        total = product[:, span] + dot(gained, down[half:, span]) - backward * along[:, span]
        held[:, span] = hidden[:, span] * (scale * total)
        columns = pl.ds(start, size)
        copy = pltpu.make_async_copy(held.at[:, columns], out.at[:, columns], sems.at[which])
        copy.start()
        copies.append(copy)
    for copy in copies:
        copy.wait()


def swap(array, axis, bit):
    return lax.ppermute(array, axis, [(i, i ^ bit) for i in range(lax.axis_size(axis))])


def four_chips(
    tokens, step_index, embed_table, gain_one, gate_weight, up_weight, down_weight, gain_two,
    query_weight, key_weight, value_weight, decay_weight, beta_weight,
    rate_log, decay_bias, beta_bias, cotangent,
):
    count, model = tokens.shape[0], gain_one.shape[0]
    width = gate_weight.shape[1]
    head_count = rate_log.shape[0]
    heads = head_count // 2
    key_dim = query_weight.shape[1] // head_count
    value_dim = value_weight.shape[1] // head_count
    pack_width = heads * (2 * key_dim + value_dim) + 128
    length = 2 * count
    half_shape = like((count // 2, model), BF16)
    rows_shape = like((count, model), BF16)
    half_shape = like((count, model // 2), BF16)
    dma = pltpu.SemaphoreType.DMA
    cot_half = heads * value_dim
    columns, cot_own, cot_send = call(
        embed_kernel,
        [like((count, embed_table.shape[1]), BF16)]
        + [like((count, cot_half), BF16)] * 2,
        [HBM] * 3,
        [
            pltpu.SMEM((1, count), jnp.int32),
            pltpu.VMEM((1, count), jnp.int32),
            pltpu.VMEM((16 * count, embed_table.shape[1]), BF16),
            dma((2,)),
            dma,
            dma((2,)),
        ],
    )(pinned(tokens.reshape(1, count)), pinned(embed_table), pinned(cotangent))
    cot_other = swap(cot_send, "outer", 1)
    pieces = [columns] + [swap(columns, "inner", bit) for bit in (1, 2, 3)]
    wide = like((count, width), F32)
    one_lane = like((count, 128), F32)
    gain = gain_one.reshape(1, model)
    gate_part, up_part, squares, down_kept = call(
        feed_own_kernel,
        [wide, wide, one_lane, like((width, model), BF16)],
        [VMEM] * 4 + [HBM],
        [dma((FETCH_PARTS,))],
    )(columns, gain, gate_weight, up_weight, pinned(down_weight))
    hidden, emb, scaled, part_low = call(
        feed_kernel,
        [wide, rows_shape, like((count, width), BF16), half_shape],
        [SMEM] + [VMEM] * 11,
    )(
        step_index, *pieces, gain, gate_weight, up_weight, down_kept, gate_part, up_part, squares
    )
    part_high = call(functools.partial(down_kernel, model // 2), half_shape, [VMEM] * 2)(
        scaled, down_kept
    )
    weights = (query_weight, key_weight, value_weight, decay_weight.T, beta_weight.T)
    low, low_other, high, high_other = pair_sums(part_low, part_high, [*weights[:3], cot_other])
    gain = gain_two.reshape(1, model)
    mixed_low, *raw = call(
        project_low_kernel,
        [like((count, model // 2), F32)]
        + [like((count, weight.shape[1]), F32) for weight in weights[:3]]
        + [one_lane] * 2,
        [VMEM] * 9,
    )(emb, low, low_other, gain, *weights)
    mixed_high, own, send, scales = call(
        project_kernel,
        [like((count, model // 2), F32)] + [like((count, pack_width), BF16)] * 2 + [one_lane],
        [VMEM] * 14,
    )(emb, high, high_other, gain, *weights, *raw)
    other = swap(send, "outer", 1)
    square = (heads, length, length)
    valued = (heads, length, value_dim)
    packs, cots, sent, kept_offset, tails, *saved = call(
        front_kernel,
        [
            like((length, pack_width), BF16),
            like((length, cot_half), BF16),
            like((heads, key_dim, value_dim), BF16),
            like((heads, key_dim, value_dim), F32),
            like((heads, key_dim, length), BF16),
            like(square, F32),
            like(square, F32),
            like(square, F32),
            like(square, F32),
            like((heads, length, key_dim), BF16),
            like(valued, F32),
            like(valued, F32),
            like((heads, length, 128), F32),
        ],
        [VMEM] * 4 + [SMEM] * 3,
    )(own, other, cot_own, cot_other, rate_log, decay_bias, beta_bias)
    near = swap(sent, "outer", 2)
    query_turned, key_turned = turned(sent, weights[:2])
    decay_mats, grams, inverses, scores, maps, fresh, pulled, columns = saved
    sent_map, kept_map, target_local, target_map = call(
        maps_kernel,
        [like((heads, key_dim, key_dim), BF16)] * 2
        + [like(valued, F32), like((heads, length, key_dim), BF16)],
        [VMEM] * 5 + [HBM],
    )(tails, inverses, maps, pulled, columns, sent)
    near_map = swap(sent_map, "outer", 2)
    joined = call(combine_kernel, like((heads, key_dim, value_dim), BF16), [VMEM] * 3 + [HBM])(
        kept_map, kept_offset, near, query_turned
    )
    (value_turned,) = turned(joined, weights[2:3])
    cycle = {1: 3, 3: 2, 2: 0, 0: 1}
    far_two = lax.ppermute(
        joined, "outer", [(2 * a + core, 2 * b + core) for a, b in cycle.items() for core in (0, 1)]
    )
    far_one = lax.ppermute(joined, "outer", [(2, 4), (3, 5), (4, 2), (5, 3)])
    own, send = call(
        back_kernel,
        [like((count, pack_width), BF16)] * 2,
        [VMEM] * 14 + [HBM],
        [pltpu.VMEM((length, pack_width), BF16)],
    )(
        near, near_map, far_one, far_two, packs, cots, decay_mats, grams, scores, maps, fresh, columns,
        target_local, target_map, value_turned,
    )
    other = swap(send, "outer", 1)
    back_weights = (query_turned, key_turned, value_turned)
    sums = call(return_own_kernel, like((count, model), F32), [VMEM] * 4)(own, *back_weights)
    part_low, part_high = [
        call(functools.partial(return_kernel, begin), half_shape, [VMEM] * 8)(
            own, other, *back_weights, *weights[3:], sums
        )
        for begin in (0, model // 2)
    ]
    (down_turned,) = turned(part_low, [down_kept])
    low, low_other, high, high_other = pair_sums(part_low, part_high, [down_turned])
    along = call(along_kernel, wide, [VMEM] * 3)(mixed_low, mixed_high, down_turned)
    product, dots = call(final_low_kernel, [wide, one_lane], [VMEM] * 5 + [HBM])(
        low, low_other, mixed_low, gain, down_turned, along
    )
    return call(
        final_kernel,
        wide,
        [VMEM] * 10,
        [pltpu.VMEM((count, width), F32), dma((len(spans(width, 512)),))],
        out=HBM,
    )(
        high, high_other, mixed_high, gain, down_turned, product, dots, along, scales, hidden
    )


def local_part(*args):
    fits = (
        lax.axis_size("inner") == 4
        and lax.axis_size("outer") == 8
        and args[0].shape[0] == 64
        and args[13].shape[0] % 2 == 0
    )
    return four_chips(*args) if fits else shards(*args)


def solution(mesh):
    placed = (
        P("outer"),
        P(),
        P(None, "inner"),
        P(),
        P(None, "inner"),
        P(None, "inner"),
        P("inner", None),
        P(),
        P(None, "inner"),
        P(None, "inner"),
        P(None, "inner"),
        P(None, "inner"),
        P(None, "inner"),
        P("inner"),
        P("inner"),
        P("inner"),
        P("outer", "inner"),
    )
    return jax.shard_map(
        local_part, mesh=mesh, in_specs=placed, out_specs=P("outer", "inner"), check_vma=False
    )
```

```python
import functools
import math

import jax
import jax.numpy as jnp
from jax import lax
from jax.experimental import pallas as pl
from jax.experimental.pallas import tpu as pltpu
from jax.sharding import PartitionSpec as P

STEPS = 32


def from_behind(array, axis, by):
    devices = lax.axis_size(axis)
    pairs = [(i, i + by) for i in range(devices) if 0 <= i + by < devices]
    return lax.ppermute(array, axis, pairs)


def unit_rows(values):
    return values * lax.rsqrt(jnp.sum(values * values, axis=-1, keepdims=True) + 1e-06)


def head_inputs(query_rows, key_rows, decay_rows, beta_rows, log_rate, rate_shift, beta_shift):
    queries = unit_rows(query_rows) * query_rows.shape[-1] ** (-0.5)
    keys_unit = unit_rows(key_rows)
    log_decay = -jnp.exp(log_rate) * jax.nn.softplus(decay_rows + rate_shift)
    betas = jax.nn.sigmoid(beta_rows + beta_shift)
    return (queries, keys_unit, log_decay, betas)


def block_step(with_out, state, pieces):
    queries, keys_unit, values, log_decay, betas = pieces
    block_len = keys_unit.shape[0]
    highest = lax.Precision.HIGHEST
    cum_decay = jnp.cumsum(log_decay)
    row_ids = jnp.arange(block_len)[:, None]
    col_ids = jnp.arange(block_len)[None, :]
    lower_mask = row_ids >= col_ids
    decay_mat = jnp.where(
        lower_mask,
        jnp.exp(jnp.where(lower_mask, cum_decay[:, None] - cum_decay[None, :], 0.0)),
        0.0,
    )
    key_gram = jnp.dot(keys_unit, keys_unit.T, precision=highest)
    strict = jnp.where(row_ids > col_ids, betas[:, None] * decay_mat * key_gram, 0.0)
    system = strict + jnp.eye(block_len, dtype=jnp.float32)
    start_scale = jnp.exp(cum_decay)[:, None]
    target = betas[:, None] * (values - start_scale * jnp.dot(keys_unit, state, precision=highest))
    fresh_vals = lax.linalg.triangular_solve(
        system, target, left_side=True, lower=True, unit_diagonal=True
    )
    tail_keys = jnp.exp(cum_decay[-1] - cum_decay)[:, None] * keys_unit
    new_state = jnp.exp(cum_decay[-1]) * state + jnp.dot(tail_keys.T, fresh_vals, precision=highest)
    if with_out:
        scores = decay_mat * jnp.dot(queries, keys_unit.T, precision=highest)
        output = start_scale * jnp.dot(queries, state, precision=highest) + jnp.dot(
            scores, fresh_vals, precision=highest
        )
        return (new_state, output)
    return (new_state, None)


def run_blocks(queries, keys_unit, values, log_decay, betas, state, with_out):
    length = keys_unit.shape[0]
    block_len = math.gcd(64, length)
    block_count = length // block_len

    def blocked(array):
        return array.reshape((block_count, block_len) + array.shape[1:])

    step_fn = functools.partial(block_step, with_out)
    final_state, outputs = lax.scan(
        step_fn,
        state,
        (blocked(queries), blocked(keys_unit), blocked(values), blocked(log_decay), blocked(betas)),
    )
    if with_out:
        outputs = outputs.reshape((length,) + outputs.shape[2:])
    return (final_state, outputs)


def rms_scaled(values, gain):
    return values * lax.rsqrt(jnp.mean(values * values, axis=-1, keepdims=True) + 1e-06) * gain


def apply_map(matrix, state):
    return jnp.einsum("hij,hjv->hiv", matrix, state, precision=lax.Precision.HIGHEST)


def shards(
    tokens,
    step_index,
    embed_table,
    gain_one,
    gate_weight,
    up_weight,
    down_weight,
    gain_two,
    query_weight,
    key_weight,
    value_weight,
    decay_weight,
    beta_weight,
    rate_log,
    decay_bias,
    beta_bias,
    cotangent,
):
    columns = jnp.take(embed_table, tokens, axis=0)
    embedded = lax.all_gather(columns, "inner", axis=1, tiled=True)
    emb_float = embedded.astype(jnp.float32)
    normed_one = rms_scaled(emb_float, gain_one).astype(jnp.bfloat16)
    gate_rows = jnp.dot(normed_one, gate_weight, preferred_element_type=jnp.float32)
    up_rows = jnp.dot(normed_one, up_weight, preferred_element_type=jnp.float32)
    hidden = jax.nn.silu(gate_rows) * up_rows
    path_scale = (step_index[0].astype(jnp.float32) + 0.5) / STEPS
    scaled = (path_scale * hidden).astype(jnp.bfloat16)
    group_rows = tokens.shape[0]
    row_share = group_rows // lax.axis_size("inner")
    head_count = rate_log.shape[0]
    key_dim = query_weight.shape[1] // head_count
    value_dim = value_weight.shape[1] // head_count
    main_weight = jnp.concatenate([query_weight, key_weight, value_weight], axis=1)
    gate_pair = jnp.concatenate([decay_weight, beta_weight], axis=1)

    def normalize(values):
        return rms_scaled(values, gain_two)

    mixed_share = lax.psum_scatter(
        jnp.dot(scaled, down_weight, preferred_element_type=jnp.float32).astype(jnp.bfloat16),
        "inner",
        scatter_dimension=0,
        tiled=True,
    ).astype(jnp.float32)
    own_rows = lax.dynamic_slice_in_dim(
        emb_float, lax.axis_index("inner") * row_share, row_share, 0
    )
    normed_float, norm_pull = jax.vjp(normalize, own_rows + mixed_share)
    block_piece = lax.all_gather(normed_float.astype(jnp.bfloat16), "inner", axis=0, tiled=True)
    main_part = jnp.dot(block_piece, main_weight, preferred_element_type=jnp.float32)
    gate_part = jnp.dot(block_piece, gate_pair, preferred_element_type=jnp.float32)
    projected = jnp.concatenate([main_part, gate_part], axis=1)
    key_span = head_count * key_dim
    value_span = head_count * value_dim

    def by_head(columns_block, width):
        return columns_block.reshape(group_rows, head_count, width).transpose(1, 0, 2)

    query_pre = by_head(projected[:, :key_span], key_dim)
    key_pre = by_head(projected[:, key_span : 2 * key_span], key_dim)
    value_pre = by_head(projected[:, 2 * key_span : 2 * key_span + value_span], value_dim)
    gate_start = 2 * key_span + value_span
    decay_pre = projected[:, gate_start : gate_start + head_count].T
    beta_pre = projected[:, gate_start + head_count : gate_start + 2 * head_count].T
    cot_heads = by_head(cotangent.astype(jnp.float32), value_dim)

    def carry_map(key_rows, value_rows, decay_rows, beta_rows, log_rate, rate_shift, beta_shift):
        unused_query, keys_unit, log_decay, betas = head_inputs(
            key_rows, key_rows, decay_rows, beta_rows, log_rate, rate_shift, beta_shift
        )
        padded_vals = jnp.concatenate(
            [value_rows, jnp.zeros((key_rows.shape[0], key_dim), jnp.float32)], axis=1
        )
        start_state = jnp.concatenate(
            [jnp.zeros((key_dim, value_dim), jnp.float32), jnp.eye(key_dim, dtype=jnp.float32)],
            axis=1,
        )
        final_state, unused_out = run_blocks(
            keys_unit, keys_unit, padded_vals, log_decay, betas, start_state, False
        )
        return final_state

    joined_state = jax.vmap(carry_map)(
        key_pre, value_pre, decay_pre, beta_pre, rate_log, decay_bias, beta_bias
    )
    offset_state = joined_state[:, :, :value_dim]
    transition = joined_state[:, :, value_dim:]

    def forward_step(turn_index, carried):
        incoming = from_behind(carried[1].astype(jnp.bfloat16), "outer", 1).astype(jnp.float32)
        return (incoming, apply_map(transition, incoming) + offset_state)

    state_in, unused_end = lax.fori_loop(
        0, lax.axis_size("outer") - 1, forward_step, (jnp.zeros_like(offset_state), offset_state)
    )

    def local_score(query_in, key_in, value_in, decay_in, beta_in, start_in):

        def one_head(
            query_rows,
            key_rows,
            value_rows,
            decay_rows,
            beta_rows,
            start_state,
            cot_rows,
            log_rate,
            rate_shift,
            beta_shift,
        ):
            queries, keys_unit, log_decay, betas = head_inputs(
                query_rows, key_rows, decay_rows, beta_rows, log_rate, rate_shift, beta_shift
            )
            final_state, outputs = run_blocks(
                queries, keys_unit, value_rows, log_decay, betas, start_state, True
            )
            return (jnp.sum(outputs * cot_rows), final_state)

        head_scores, final_states = jax.vmap(one_head)(
            query_in,
            key_in,
            value_in,
            decay_in,
            beta_in,
            start_in,
            cot_heads,
            rate_log,
            decay_bias,
            beta_bias,
        )
        return (jnp.sum(head_scores), final_states)

    score_pair, pull_back = jax.vjp(
        local_score, query_pre, key_pre, value_pre, decay_pre, beta_pre, state_in
    )
    first_pull = pull_back((jnp.ones_like(score_pair[0]), jnp.zeros_like(score_pair[1])))
    grad_local = first_pull[5]
    grad_trans = jnp.swapaxes(transition, 1, 2)

    def backward_step(turn_index, carried):
        incoming = from_behind(carried[1].astype(jnp.bfloat16), "outer", -1).astype(jnp.float32)
        return (incoming, apply_map(grad_trans, incoming) + grad_local)

    state_grad, unused_start = lax.fori_loop(
        0, lax.axis_size("outer") - 1, backward_step, (jnp.zeros_like(grad_local), grad_local)
    )
    second_pull = pull_back((jnp.zeros_like(score_pair[0]), state_grad))
    summed = [first_pull[which] + second_pull[which] for which in range(5)]

    def by_rows(head_block):
        return head_block.transpose(1, 0, 2).reshape(group_rows, -1).astype(jnp.bfloat16)

    grad_main = jnp.concatenate(
        [by_rows(summed[0]), by_rows(summed[1]), by_rows(summed[2])], axis=1
    )
    grad_gates = jnp.concatenate(
        [summed[3].T.astype(jnp.bfloat16), summed[4].T.astype(jnp.bfloat16)], axis=1
    )
    main_part = jnp.dot(grad_main, main_weight.T, preferred_element_type=jnp.float32)
    back_share = lax.psum_scatter(
        (main_part + jnp.dot(grad_gates, gate_pair.T, preferred_element_type=jnp.float32)).astype(
            jnp.bfloat16
        ),
        "inner",
        scatter_dimension=0,
        tiled=True,
    ).astype(jnp.float32)
    grad_mixed = norm_pull(back_share)[0].astype(jnp.bfloat16)
    return hidden * jnp.dot(
        lax.all_gather(grad_mixed, "inner", axis=0, tiled=True),
        down_weight.T,
        preferred_element_type=jnp.float32,
    )


BF16 = jnp.bfloat16
F32 = jnp.float32
MIB = 1 << 20
FETCH_PARTS = 4
TURN_ROWS = 128
BASE = 16
VMEM = pl.BlockSpec(memory_space=pltpu.VMEM)
SMEM = pl.BlockSpec(memory_space=pltpu.SMEM)
HBM = pl.BlockSpec(memory_space=pl.ANY)


def pinned(array):
    return pltpu.with_memory_space_constraint(array, pltpu.HBM)


def call(kernel, out_shape, in_specs, scratch=(), limit=16 * MIB, out=VMEM):
    return pl.pallas_call(
        kernel,
        out_shape=out_shape,
        in_specs=in_specs,
        out_specs=jax.tree.map(lambda _: out, out_shape),
        scratch_shapes=list(scratch),
        compiler_params=pltpu.CompilerParams(vmem_limit_bytes=limit),
        cost_estimate=pl.CostEstimate(flops=0, bytes_accessed=0, transcendentals=0),
    )


def like(shape, dtype):
    return jax.ShapeDtypeStruct(shape, dtype)


def dot(a, b, transposed=False):
    dims = (((1,), (1 if transposed else 0,)), ((), ()))
    return lax.dot_general(a, b, dims, preferred_element_type=F32)


def mm(a, b, transposed=False):
    return dot(a.astype(BF16), b.astype(BF16), transposed)


def row_sum(values):
    return jnp.sum(values, axis=-1, keepdims=True)


def spans(total, step):
    return [(at, min(step, total - at)) for at in range(0, total, step)]


def stream(pairs, sems):
    copies = [
        pltpu.make_async_copy(source, target, sems.at[which])
        for which, (source, target) in enumerate(pairs)
    ]
    for copy in copies:
        copy.start()
    return copies


def grid_ids(size):
    shape = (size, size)
    return lax.broadcasted_iota(jnp.int32, shape, 0), lax.broadcasted_iota(jnp.int32, shape, 1)


def quarters(source, target):
    cuts = spans(source.shape[0], source.shape[0] // FETCH_PARTS)
    return [(source.at[pl.ds(at, size)], target.at[pl.ds(at, size)]) for at, size in cuts]


def embed_kernel(
    ids_in, table, cot, out, cot_own, cot_send,
    ids, id_row, blocks, id_sems, sem, cot_sems,
):
    count = out.shape[0]
    copies = stream([(ids_in, ids), (ids_in, id_row)], id_sems)
    copies[0].wait()
    for which in range(count):
        base = pl.multiple_of((ids[0, which] // 16) * 16, 16)
        pltpu.make_async_copy(
            table.at[pl.ds(base, 16)], blocks.at[pl.ds(which * 16, 16)], sem
        ).start()
    core, half = lax.axis_index("outer") % 2, cot_own.shape[1]
    mine = pl.ds(pl.multiple_of(core * half, half), half)
    yours = pl.ds(pl.multiple_of((1 - core) * half, half), half)
    halves = stream([(cot.at[:, mine], cot_own), (cot.at[:, yours], cot_send)], cot_sems)
    copies[1].wait()
    row_ids, col_ids = grid_ids(count)
    low_bits = jnp.broadcast_to(id_row[...] & 15, (count, count))
    inside = row_sum(jnp.where(row_ids == col_ids, low_bits, 0).astype(F32)).astype(jnp.int32)
    wide = (count, 16 * count)
    wanted = lax.broadcasted_iota(jnp.int32, wide, 0) * 16 + inside
    pick = jnp.where(lax.broadcasted_iota(jnp.int32, wide, 1) == wanted, 1.0, 0.0).astype(BF16)
    pltpu.make_async_copy(table.at[pl.ds(0, 16 * count)], blocks, sem).wait()
    out[...] = dot(pick, blocks[...]).astype(BF16)
    for copy in halves:
        copy.wait()


def fetch_kernel(count, *refs):
    sources, targets, sems = refs[-1 - 2 * count : -1 - count], refs[-1 - count : -1], refs[-1]
    pairs = []
    for source, target in zip(sources, targets):
        pairs += quarters(source, target)
    for copy in stream(pairs, sems):
        copy.wait()


def fetch(after, arrays, beside=()):
    return call(
        functools.partial(fetch_kernel, len(arrays)),
        [like(array.shape, BF16) for array in arrays],
        [HBM] * (1 + len(beside) + len(arrays)),
        [pltpu.SemaphoreType.DMA((FETCH_PARTS * len(arrays),))],
        limit=MIB,
    )(after, *beside, *[pinned(array) for array in arrays])


def turn(source, target):
    for at, size in spans(source.shape[0], TURN_ROWS):
        target[:, at : at + size] = jnp.transpose(source[at : at + size, :])


def turn_kernel(count, *refs):
    for source, target in zip(refs[1 : 1 + count], refs[1 + count :]):
        turn(source, target)


def turned(after, arrays):
    return call(
        functools.partial(turn_kernel, len(arrays)),
        [like(array.shape[::-1], BF16) for array in arrays],
        [HBM] + [VMEM] * len(arrays),
        limit=4 * MIB,
    )(after, *arrays)


def feed_own_kernel(
    piece, gain, gate, up, down, gate_part, up_part, square, down_kept, sems
):
    copies = stream(quarters(down, down_kept), sems)
    share = piece.shape[1]
    at = pl.multiple_of(lax.axis_index("inner") * share, share)
    rows = piece[...].astype(F32)
    square[...] = jnp.broadcast_to(row_sum(rows * rows), square.shape)
    taken = (rows * gain[:, pl.ds(at, share)]).astype(BF16)
    for start, size in spans(gate.shape[1], 512):
        span = slice(start, start + size)
        gate_part[:, span] = dot(taken, gate[pl.ds(at, share), span])
        up_part[:, span] = dot(taken, up[pl.ds(at, share), span])
    for copy in copies:
        copy.wait()


def feed_kernel(
    step, piece0, piece1, piece2, piece3, gain, gate, up, down, gate_part, up_part, square,
    hidden, emb, scaled, part_low,
):
    width = hidden.shape[1]
    me = lax.axis_index("inner")
    share = piece0.shape[1]
    squares = square[:, :1]
    taken = []
    for which, piece in enumerate((piece0, piece1, piece2, piece3)):
        at = pl.multiple_of((me ^ which) * share, share)
        emb[:, pl.ds(at, share)] = piece[...]
        if which > 0:
            rows = piece[...].astype(F32)
            squares = squares + row_sum(rows * rows)
            taken.append((at, (rows * gain[:, pl.ds(at, share)]).astype(BF16)))
    scale = lax.rsqrt(squares / emb.shape[1] + 1e-06)
    path_scale = (step[0].astype(F32) + 0.5) / STEPS
    for start, size in spans(width, 512):
        span = slice(start, start + size)
        gate_rows, up_rows = gate_part[:, span], up_part[:, span]
        for at, rows in taken:
            gate_rows = gate_rows + dot(rows, gate[pl.ds(at, share), span])
            up_rows = up_rows + dot(rows, up[pl.ds(at, share), span])
        gate_rows = scale * gate_rows
        units = gate_rows / (1.0 + jnp.exp(-gate_rows)) * (scale * up_rows)
        hidden[:, span] = units
        scaled[:, span] = (path_scale * units).astype(BF16)
    down_kernel(0, scaled, down, part_low)


def down_kernel(begin, scaled, down, part):
    for start, size in spans(part.shape[1], 512):
        sums = dot(scaled[...], down[:, begin + start : begin + start + size])
        part[:, start : start + size] = sums.astype(BF16)


def pair_kernel(mine, other, *refs):
    refs[-1][...] = (mine[...].astype(F32) + other[...].astype(F32)).astype(BF16)


def pair_sums(low, high, before):
    low_other, high_other = swap(low, "inner", 1), swap(high, "inner", 2)
    low = call(pair_kernel, like(low.shape, BF16), [VMEM] * 2 + [HBM] * len(before))(
        low, low_other, *before
    )
    low_other = swap(low, "inner", 2)
    high = call(pair_kernel, like(high.shape, BF16), [VMEM] * 2)(high, high_other)
    return low, low_other, high, swap(high, "inner", 1)


def added(mine, other):
    return mine[...].astype(F32) + other[...].astype(F32)


def half_product(begin, emb, mine, other, gain, mixed, weights, gate_weights):
    half = mixed.shape[1]
    span = slice(begin, begin + half)
    total = emb[:, span].astype(F32) + added(mine, other)
    mixed[...] = total
    taken = (total * gain[:, span]).astype(BF16)
    raw = [dot(taken, weight[span, :]) for weight in weights]
    gates = [dot(taken, weight[:, span], True) for weight in gate_weights]
    return raw, gates, row_sum(total * total)


def project_low_kernel(
    emb, low, low_other, gain, query, key, value, decay, beta,
    mixed, query_raw, key_raw, value_raw, gate_raw, square,
):
    raw, gates, squares = half_product(
        0, emb, low, low_other, gain, mixed, (query, key, value), (decay, beta)
    )
    query_raw[...], key_raw[...], value_raw[...] = raw
    heads = decay.shape[0]
    gate_raw[:, :heads], gate_raw[:, heads : 2 * heads] = gates
    square[...] = jnp.broadcast_to(squares, square.shape)


def project_kernel(
    emb, high, high_other, gain, query, key, value, decay, beta,
    query_raw, key_raw, value_raw, gate_raw, square,
    mixed, own, send, scales,
):
    half_key = query.shape[1] // 2
    half_value = value.shape[1] // 2
    all_heads = decay.shape[0]
    first = lax.axis_index("outer") % 2 == 0
    raw, gates, squares = half_product(
        emb.shape[1] - mixed.shape[1], emb, high, high_other, gain, mixed, (query, key, value), (decay, beta)
    )
    scale = lax.rsqrt((squares + square[:, :1]) / emb.shape[1] + 1e-06)
    scales[...] = jnp.broadcast_to(scale, scales.shape)
    query_rows, key_rows, value_rows = [
        scale * (part + rest[...]) for part, rest in zip(raw, (query_raw, key_raw, value_raw))
    ]
    gates = [
        scale * (gates[0] + gate_raw[:, :all_heads]),
        scale * (gates[1] + gate_raw[:, all_heads : 2 * all_heads]),
    ]

    def put(at, low, high):
        size = low.shape[1]
        own[:, at : at + size] = jnp.where(first, low, high).astype(BF16)
        send[:, at : at + size] = jnp.where(first, high, low).astype(BF16)

    heads = decay.shape[0] // 2
    lanes = lax.broadcasted_iota(jnp.int32, scales.shape, 1)
    packed = []
    for side in range(2):
        lane, pack = 0, jnp.zeros(scales.shape, F32)
        for values in gates:
            for head in range(side * heads, (side + 1) * heads):
                column = values[:, head : head + 1]
                top = column.astype(BF16).astype(F32)
                pack = jnp.where(lanes == lane, top, pack)
                pack = jnp.where(lanes == lane + 1, column - top, pack)
                lane += 2
        packed.append(pack)
    put(0, query_rows[:, :half_key], query_rows[:, half_key:])
    put(half_key, key_rows[:, :half_key], key_rows[:, half_key:])
    put(2 * half_key, value_rows[:, :half_value], value_rows[:, half_value:])
    put(2 * half_key + half_value, *packed)


def both_blocks(own, other, target):
    core = lax.axis_index("outer") % 2
    size = own.shape[0]
    target[pl.ds(pl.multiple_of(core * size, size), size), :] = own[...]
    target[pl.ds(pl.multiple_of((1 - core) * size, size), size), :] = other[...]


def cumulate(chosen, column):
    top = column.astype(BF16)
    rest = column - top.astype(F32)
    middle = rest.astype(BF16)
    low = (rest - middle.astype(F32)).astype(BF16)
    picked = jnp.where(chosen, 1.0, 0.0).astype(BF16)

    def part(values):
        return dot(picked, jnp.broadcast_to(values, (values.shape[0], 128)))

    return part(top) + (part(middle) + part(low))


def base_inverses(systems):
    size = systems[0].shape[0]
    row_ids, col_ids = grid_ids(size)
    apart = row_ids - col_ids
    near = row_ids // BASE == col_ids // BASE

    def diagonal(which):
        picked = near & (apart == which)
        rows = [jnp.sum(jnp.where(picked, a, 0.0), axis=0, keepdims=True) for a in systems]
        return jnp.concatenate(rows, axis=0)

    def ahead(rows, by):
        return rows if by == 0 else pltpu.roll(rows, size - by, 1)

    given = [None] + [diagonal(which) for which in range(1, BASE)]
    found = [jnp.ones((len(systems), size), F32)]
    for which in range(1, BASE):
        terms = [ahead(given[j], which - j) * found[which - j] for j in range(1, which + 1)]
        while len(terms) > 1:
            pairs = [a + b for a, b in zip(terms[::2], terms[1::2])]
            terms = pairs + terms[2 * len(pairs) :]
        found.append(-terms[0])
    inverses = []
    for head, system in enumerate(systems):
        inverse = jnp.zeros((size, size), F32)
        for which in range(BASE):
            inverse = jnp.where(apart == which, found[which][head : head + 1], inverse)
        inverses.append(inverse)
    return inverses


def doublings(size):
    blocks = []
    while BASE << len(blocks) < size:
        blocks.append(BASE << len(blocks))
    return blocks


def solved(base, system, *sides):
    size = system.shape[0]
    row_ids, col_ids = grid_ids(size)
    parts = []
    for block in doublings(size):
        below = (row_ids // (2 * block) == col_ids // (2 * block)) & (
            row_ids // block != col_ids // block
        )
        parts.append(jnp.where(below, system, 0.0))
    rest = mm(base, jnp.concatenate([*parts, *sides], axis=1))
    turns = []
    for _ in parts:
        turns.append(rest[:, :size].astype(BF16))
        rest = rest[:, size:]
        rest = rest - dot(turns[-1], rest.astype(BF16))
    return turns, rest


def front_kernel(
    own, other, cot_own, cot_other, rate_log, decay_bias, beta_bias,
    packs, cots, sent, kept_offset, tails,
    decay_mats, grams, bases, turn_mats, scores, maps, fresh, pulled, columns,
):
    both_blocks(own, other, packs)
    both_blocks(cot_own, cot_other, cots)
    heads, length, _ = decay_mats.shape
    key_dim, value_dim = maps.shape[2], fresh.shape[2]
    place = lax.axis_index("outer")
    even = (place // 2) % 2 == 0
    first = place % 2 == 0

    def of_head(values, head):
        return jnp.where(
            first, values[:, head : head + 1], values[:, heads + head : heads + head + 1]
        )

    row_ids, col_ids = grid_ids(length)
    lower, strictly = row_ids >= col_ids, row_ids > col_ids
    lanes = lax.broadcasted_iota(jnp.int32, (length, 128), 1)
    gate_at = heads * (2 * key_dim + value_dim)
    gates = packs[:, gate_at : gate_at + 128].astype(F32)
    ready = []
    for head in range(heads):
        at = head * key_dim
        query_rows = packs[:, at : at + key_dim].astype(F32)
        at += heads * key_dim
        key_rows = packs[:, at : at + key_dim].astype(F32)
        at = 2 * heads * key_dim + head * value_dim
        values = packs[:, at : at + value_dim].astype(F32)
        cot = cots[:, head * value_dim : (head + 1) * value_dim]
        lane = 2 * head
        decay_in = gates[:, lane : lane + 1] + gates[:, lane + 1 : lane + 2]
        decay_in = decay_in + of_head(decay_bias, head)
        lane += 2 * heads
        beta_in = gates[:, lane : lane + 1] + gates[:, lane + 1 : lane + 2]
        beta_in = beta_in + of_head(beta_bias, head)
        rate = jnp.broadcast_to(jnp.exp(of_head(rate_log, head)), (length, 1))
        query_scale = lax.rsqrt(row_sum(query_rows * query_rows) + 1e-06) * key_dim ** (-0.5)
        key_at = (heads + head) * key_dim
        key_half = packs[:, key_at : key_at + key_dim]
        raw = dot(key_half, key_half, True)
        squares = jnp.where(row_ids == col_ids, raw, 0.0)
        key_scale = lax.rsqrt(row_sum(squares) + 1e-06)
        key_scale_row = lax.rsqrt(jnp.sum(squares, axis=0, keepdims=True) + 1e-06)
        queries, keys_unit = query_rows * query_scale, key_rows * key_scale
        log_decay = -rate * (jnp.maximum(decay_in, 0.0) + jnp.log1p(jnp.exp(-jnp.abs(decay_in))))
        betas = 1.0 / (1.0 + jnp.exp(-beta_in))
        cum = cumulate(lower, log_decay)
        decay_mat = jnp.where(
            lower, jnp.exp(jnp.where(lower, cum - jnp.transpose(cum), 0.0)), 0.0
        )
        total = cum[:, :1]
        start_scale = jnp.exp(total)
        tail_scale = jnp.exp(total[length - 1 :] - total)
        gram = jnp.where(strictly, decay_mat * (key_scale * raw * key_scale_row), 0.0)
        ready.append(
            (
                queries, keys_unit, values, cot, decay_mat, gram, start_scale, tail_scale,
                betas, query_scale, key_scale, decay_in, rate,
            )
        )
    systems = [item[8] * item[5] for item in ready]
    base_list = base_inverses(systems)
    for head, base in enumerate(base_list):
        (
            queries, keys_unit, values, cot, decay_mat, gram, start_scale, tail_scale,
            betas, query_scale, key_scale, decay_in, rate,
        ) = ready[head]
        score = decay_mat * mm(queries, keys_unit, True)
        turns, both = solved(
            base, systems[head], (betas * start_scale) * keys_unit, betas * values
        )
        state_map, fresh_vals = both[:, :key_dim], both[:, key_dim:]
        tail_t = jnp.transpose(tail_scale * keys_unit)
        offset = mm(tail_t, fresh_vals)
        score_pull = mm(jnp.transpose(score), cot)
        grad_local = mm(jnp.transpose(start_scale * queries), cot) - mm(
            jnp.transpose(state_map), score_pull
        )
        sent[head] = jnp.where(even, offset, grad_local).astype(BF16)
        kept_offset[head] = jnp.where(even, grad_local, offset)
        tails[head] = tail_t.astype(BF16)
        decay_mats[head] = decay_mat
        grams[head] = gram
        bases[head] = base.astype(BF16)
        for which, turn in enumerate(turns):
            turn_mats[head, which] = turn
        scores[head] = score
        maps[head] = state_map.astype(BF16)
        fresh[head] = fresh_vals
        pulled[head] = score_pull
        pack = jnp.zeros((length, 128), F32)
        for lane, column in enumerate(
            (query_scale, key_scale, betas, start_scale, tail_scale, decay_in, rate)
        ):
            pack = jnp.where(lanes == lane, column, pack)
        columns[head] = pack


def maps_kernel(
    tails, bases, turn_mats, maps, pulled, columns, after, sent_map, kept_map, target_local, target_map
):
    heads, length, _ = bases.shape
    even = (lax.axis_index("outer") // 2) % 2 == 0
    row_ids, col_ids = grid_ids(length)
    for head in range(heads):
        end_scale = columns[head, length - 1 :, 3:4]
        tail_t, inverse = tails[head], bases[head].astype(F32)
        for which in range(turn_mats.shape[1]):
            inverse = inverse - dot(turn_mats[head, which], inverse.astype(BF16))
        transition = jnp.where(row_ids == col_ids, end_scale, 0.0) - dot(tail_t, maps[head])
        flipped = jnp.transpose(transition)
        sent_map[head] = jnp.where(even, transition, flipped).astype(BF16)
        kept_map[head] = jnp.where(even, flipped, transition).astype(BF16)
        target_local[head] = mm(jnp.transpose(inverse), pulled[head])
        target_map[head] = jnp.transpose(mm(tail_t, inverse)).astype(BF16)


def combine_kernel(kept_map, kept_offset, got, after, also, out):
    for head in range(out.shape[0]):
        joined = dot(kept_map[head], got[head]) + kept_offset[head]
        out[head] = joined.astype(BF16)


def back_kernel(
    near, near_map, far_one, far_two, packs, cots,
    decay_mats, grams, scores, maps, fresh, columns, target_local, target_map, after, also,
    own, send, grads,
):
    heads, length, _ = decay_mats.shape
    key_dim, value_dim = maps.shape[2], fresh.shape[2]
    place = lax.axis_index("outer")
    core, chip = place % 2, place // 2
    outer_chip = (chip == 0) | (chip == 3)
    odd = chip % 2 == 1
    row_ids, col_ids = grid_ids(length)
    strictly, upper = row_ids > col_ids, row_ids <= col_ids
    lanes = lax.broadcasted_iota(jnp.int32, (length, 128), 1)
    gate_at = heads * (2 * key_dim + value_dim)
    gate_grads = jnp.zeros((length, 128), F32)
    for head in range(heads):
        at = head * key_dim
        query_rows = packs[:, at : at + key_dim].astype(F32)
        key_at = at + heads * key_dim
        key_rows = packs[:, key_at : key_at + key_dim].astype(F32)
        value_at = 2 * heads * key_dim + head * value_dim
        values = packs[:, value_at : value_at + value_dim].astype(F32)
        cot = cots[:, head * value_dim : (head + 1) * value_dim]
        pack = columns[head]
        query_scale, key_scale, betas = pack[:, 0:1], pack[:, 1:2], pack[:, 2:3]
        start_scale, tail_scale = pack[:, 3:4], pack[:, 4:5]
        decay_in, rate = pack[:, 5:6], pack[:, 6:7]
        end_scale = start_scale[length - 1 :]
        queries, keys_unit = query_rows * query_scale, key_rows * key_scale
        decay_mat, gram, score = decay_mats[head], grams[head], scores[head]
        far = jnp.where(outer_chip, far_two[head], far_one[head])
        close = near[head].astype(F32)
        reached = dot(near_map[head], far) + close
        first = jnp.where(outer_chip, reached, close)
        second = jnp.where(outer_chip, 0.0, far.astype(F32))
        state = jnp.where(odd, first, second)
        state_grad = jnp.where(odd, second, first)
        state_half, state_grad_half = state.astype(BF16), state_grad.astype(BF16)
        new_vals = fresh[head] - dot(maps[head], state_half)
        new_half = new_vals.astype(BF16)
        grad_target = target_local[head] + dot(target_map[head], state_grad_half)
        target_half = grad_target.astype(BF16)
        grad_score = dot(cot, new_half, True)
        grad_sys = jnp.where(strictly, -dot(target_half, new_half, True), 0.0)
        cot_state = dot(cot, state_half, True)
        target_state = dot(target_half, state_half, True)
        new_state = dot(new_half, state_grad_half, True)
        weighted = decay_mat * grad_score
        grad_gram = grad_sys * decay_mat * betas
        grad_query = mm(weighted, keys_unit) + start_scale * cot_state
        grad_key = (
            mm(jnp.transpose(weighted), queries)
            + mm(grad_gram + jnp.transpose(grad_gram), keys_unit)
            + tail_scale * new_state
            - (betas * start_scale) * target_state
        )
        key_target = start_scale * keys_unit * target_state
        sys_gram = grad_sys * gram
        weights = grad_target * values
        grad_beta = row_sum(
            sum(weights[:, at : at + length] for at in range(0, value_dim, length))
            - key_target
            + sys_gram
        )
        both = score * grad_score + betas * sys_gram
        tails = tail_scale * keys_unit * new_state
        grad_cum = row_sum(
            both
            - jnp.transpose(both)
            + start_scale * queries * cot_state
            - betas * key_target
            - tails
        )
        ending = row_sum(jnp.sum(tails, axis=0, keepdims=True)) + end_scale * row_sum(
            jnp.sum(state * state_grad, axis=0, keepdims=True)
        )
        grad_log = cumulate(upper, grad_cum)[:, :1] + ending
        grad_decay = grad_log * -rate / (1.0 + jnp.exp(-decay_in))
        grad_beta = grad_beta * betas * (1.0 - betas)
        units = queries * key_dim**0.5
        grad_query = query_scale * (grad_query - units * row_sum(units * grad_query))
        grad_key = key_scale * (grad_key - keys_unit * row_sum(keys_unit * grad_key))
        grads[:, at : at + key_dim] = grad_query.astype(BF16)
        grads[:, key_at : key_at + key_dim] = grad_key.astype(BF16)
        grads[:, value_at : value_at + value_dim] = (betas * grad_target).astype(BF16)
        gate_grads = jnp.where(lanes == head, grad_decay, gate_grads)
        gate_grads = jnp.where(lanes == heads + head, grad_beta, gate_grads)
    grads[:, gate_at : gate_at + 128] = gate_grads.astype(BF16)
    size = own.shape[0]
    own[...] = grads[pl.ds(pl.multiple_of(core * size, size), size), :]
    send[...] = grads[pl.ds(pl.multiple_of((1 - core) * size, size), size), :]


def return_own_kernel(own, query, key, value, sums):
    half_key = query.shape[0] // 2
    half_value = value.shape[0] // 2
    core = lax.axis_index("outer") % 2
    keys = pl.ds(pl.multiple_of(core * half_key, half_key), half_key)
    values = pl.ds(pl.multiple_of(core * half_value, half_value), half_value)
    for start, size in spans(sums.shape[1], 512):
        span = slice(start, start + size)
        sums[:, span] = (
            dot(own[:, :half_key], query[keys, span])
            + dot(own[:, half_key : 2 * half_key], key[keys, span])
            + dot(own[:, 2 * half_key : 2 * half_key + half_value], value[values, span])
        )


def return_kernel(begin, own, other, query, key, value, decay, beta, sums, part):
    half_key = query.shape[0] // 2
    half_value = value.shape[0] // 2
    core = lax.axis_index("outer") % 2
    first = core == 0
    keys = pl.ds(pl.multiple_of((1 - core) * half_key, half_key), half_key)
    values = pl.ds(pl.multiple_of((1 - core) * half_value, half_value), half_value)

    def sides(at, size):
        mine, yours = own[:, at : at + size], other[:, at : at + size]
        return jnp.concatenate(
            [jnp.where(first, mine, yours), jnp.where(first, yours, mine)], axis=1
        )

    gate_at = 2 * half_key + half_value
    heads = decay.shape[0] // 2
    decays, betas = sides(gate_at, heads), sides(gate_at + heads, heads)
    for start, size in spans(part.shape[1], 512):
        span = slice(begin + start, begin + start + size)
        total = (
            sums[:, span]
            + dot(other[:, :half_key], query[keys, span])
            + dot(other[:, half_key : 2 * half_key], key[keys, span])
            + dot(other[:, 2 * half_key : gate_at], value[values, span])
            + dot(decays, decay[:, span])
            + dot(betas, beta[:, span])
        )
        part[:, start : start + size] = total.astype(BF16)


def along_kernel(mixed_low, mixed_high, down, after, out):
    half = mixed_low.shape[1]
    out[...] = mm(mixed_low[...], down[:half, :]) + mm(mixed_high[...], down[half:, :])


def final_low_kernel(low, low_other, mixed, gain, down, along, product, dots):
    half = mixed.shape[1]
    gained = added(low, low_other) * gain[:, :half]
    dots[...] = jnp.broadcast_to(row_sum(mixed[...] * gained), dots.shape)
    product[...] = mm(gained, down[:half, :])


def final_kernel(
    high, high_other, mixed, gain, down, product, dots, along, scales, hidden, out, held, sems
):
    begin = down.shape[0] - mixed.shape[1]
    gained = added(high, high_other) * gain[:, begin:]
    scale = scales[:, :1]
    mean = (dots[:, :1] + row_sum(mixed[...] * gained)) / down.shape[0]
    gained = gained.astype(BF16)
    backward = scale * scale * mean
    copies = []
    for which, (start, size) in enumerate(spans(held.shape[1], 512)):
        span = slice(start, start + size)
        total = product[:, span] + dot(gained, down[begin:, span]) - backward * along[:, span]
        held[:, span] = hidden[:, span] * (scale * total)
        columns = pl.ds(start, size)
        copy = pltpu.make_async_copy(held.at[:, columns], out.at[:, columns], sems.at[which])
        copy.start()
        copies.append(copy)
    for copy in copies:
        copy.wait()


def swap(array, axis, bit):
    return lax.ppermute(array, axis, [(i, i ^ bit) for i in range(lax.axis_size(axis))])


def four_chips(
    tokens, step_index, embed_table, gain_one, gate_weight, up_weight, down_weight, gain_two,
    query_weight, key_weight, value_weight, decay_weight, beta_weight,
    rate_log, decay_bias, beta_bias, cotangent,
):
    count, model = tokens.shape[0], gain_one.shape[0]
    width = gate_weight.shape[1]
    head_count = rate_log.shape[0]
    heads = head_count // 2
    key_dim = query_weight.shape[1] // head_count
    value_dim = value_weight.shape[1] // head_count
    pack_width = heads * (2 * key_dim + value_dim) + 128
    length = 2 * count
    rows_shape = like((count, model), BF16)
    low_width = model * 9 // 16
    widths = (low_width, model - low_width)
    part_shapes = [like((count, size), BF16) for size in widths]
    dma = pltpu.SemaphoreType.DMA
    cot_half = heads * value_dim
    columns, cot_own, cot_send = call(
        embed_kernel,
        [like((count, embed_table.shape[1]), BF16)]
        + [like((count, cot_half), BF16)] * 2,
        [HBM] * 3,
        [
            pltpu.SMEM((1, count), jnp.int32),
            pltpu.VMEM((1, count), jnp.int32),
            pltpu.VMEM((16 * count, embed_table.shape[1]), BF16),
            dma((2,)),
            dma,
            dma((2,)),
        ],
    )(pinned(tokens.reshape(1, count)), pinned(embed_table), pinned(cotangent))
    cot_other = swap(cot_send, "outer", 1)
    pieces = [columns] + [swap(columns, "inner", bit) for bit in (1, 2, 3)]
    wide = like((count, width), F32)
    one_lane = like((count, 128), F32)
    gain = gain_one.reshape(1, model)
    gate_part, up_part, squares, down_kept = call(
        feed_own_kernel,
        [wide, wide, one_lane, like((width, model), BF16)],
        [VMEM] * 4 + [HBM],
        [dma((FETCH_PARTS,))],
    )(columns, gain, gate_weight, up_weight, pinned(down_weight))
    hidden, emb, scaled, part_low = call(
        feed_kernel,
        [wide, rows_shape, like((count, width), BF16), part_shapes[0]],
        [SMEM] + [VMEM] * 11,
    )(
        step_index, *pieces, gain, gate_weight, up_weight, down_kept, gate_part, up_part, squares
    )
    part_high = call(functools.partial(down_kernel, low_width), part_shapes[1], [VMEM] * 2)(
        scaled, down_kept
    )
    weights = (query_weight, key_weight, value_weight, decay_weight.T, beta_weight.T)
    low, low_other, high, high_other = pair_sums(part_low, part_high, [*weights[:3], cot_other])
    gain = gain_two.reshape(1, model)
    mixed_low, *raw = call(
        project_low_kernel,
        [like((count, widths[0]), F32)]
        + [like((count, weight.shape[1]), F32) for weight in weights[:3]]
        + [one_lane] * 2,
        [VMEM] * 9,
    )(emb, low, low_other, gain, *weights)
    mixed_high, own, send, scales = call(
        project_kernel,
        [like((count, widths[1]), F32)] + [like((count, pack_width), BF16)] * 2 + [one_lane],
        [VMEM] * 14,
    )(emb, high, high_other, gain, *weights, *raw)
    other = swap(send, "outer", 1)
    square = (heads, length, length)
    valued = (heads, length, value_dim)
    packs, cots, sent, kept_offset, tails, *saved = call(
        front_kernel,
        [
            like((length, pack_width), BF16),
            like((length, cot_half), BF16),
            like((heads, key_dim, value_dim), BF16),
            like((heads, key_dim, value_dim), F32),
            like((heads, key_dim, length), BF16),
            like(square, F32),
            like(square, F32),
            like(square, BF16),
            like((heads, len(doublings(length)), length, length), BF16),
            like(square, F32),
            like((heads, length, key_dim), BF16),
            like(valued, F32),
            like(valued, F32),
            like((heads, length, 128), F32),
        ],
        [VMEM] * 7,
    )(
        own, other, cot_own, cot_other,
        *[array.reshape(1, head_count) for array in (rate_log, decay_bias, beta_bias)],
    )
    near = swap(sent, "outer", 2)
    query_turned, key_turned = turned(sent, weights[:2])
    (down_turned,) = turned(sent, [down_kept])
    decay_mats, grams, bases, turn_mats, scores, maps, fresh, pulled, columns = saved
    sent_map, kept_map, target_local, target_map = call(
        maps_kernel,
        [like((heads, key_dim, key_dim), BF16)] * 2
        + [like(valued, F32), like((heads, length, key_dim), BF16)],
        [VMEM] * 6 + [HBM],
    )(tails, bases, turn_mats, maps, pulled, columns, sent)
    near_map = swap(sent_map, "outer", 2)
    joined = call(combine_kernel, like((heads, key_dim, value_dim), BF16), [VMEM] * 3 + [HBM] * 2)(
        kept_map, kept_offset, near, query_turned, down_turned
    )
    (value_turned,) = turned(joined, weights[2:3])
    along = call(along_kernel, wide, [VMEM] * 3 + [HBM])(mixed_low, mixed_high, down_turned, joined)
    cycle = {1: 3, 3: 2, 2: 0, 0: 1}
    far_two = lax.ppermute(
        joined, "outer", [(2 * a + core, 2 * b + core) for a, b in cycle.items() for core in (0, 1)]
    )
    far_one = lax.ppermute(joined, "outer", [(2, 4), (3, 5), (4, 2), (5, 3)])
    own, send = call(
        back_kernel,
        [like((count, pack_width), BF16)] * 2,
        [VMEM] * 14 + [HBM] * 2,
        [pltpu.VMEM((length, pack_width), BF16)],
    )(
        near, near_map, far_one, far_two, packs, cots, decay_mats, grams, scores, maps, fresh, columns,
        target_local, target_map, value_turned, along,
    )
    other = swap(send, "outer", 1)
    back_weights = (query_turned, key_turned, value_turned)
    sums = call(return_own_kernel, like((count, model), F32), [VMEM] * 4)(own, *back_weights)
    part_low, part_high = [
        call(functools.partial(return_kernel, begin), shape, [VMEM] * 8)(
            own, other, *back_weights, *weights[3:], sums
        )
        for begin, shape in zip((0, low_width), part_shapes)
    ]
    low, low_other, high, high_other = pair_sums(part_low, part_high, [])
    product, dots = call(final_low_kernel, [wide, one_lane], [VMEM] * 5 + [HBM])(
        low, low_other, mixed_low, gain, down_turned, along
    )
    return call(
        final_kernel,
        wide,
        [VMEM] * 10,
        [pltpu.VMEM((count, width), F32), dma((len(spans(width, 512)),))],
        out=HBM,
    )(
        high, high_other, mixed_high, gain, down_turned, product, dots, along, scales, hidden
    )


def local_part(*args):
    fits = (
        lax.axis_size("inner") == 4
        and lax.axis_size("outer") == 8
        and args[0].shape[0] == 64
        and args[13].shape[0] % 2 == 0
    )
    return four_chips(*args) if fits else shards(*args)


def solution(mesh):
    placed = (
        P("outer"),
        P(),
        P(None, "inner"),
        P(),
        P(None, "inner"),
        P(None, "inner"),
        P("inner", None),
        P(),
        P(None, "inner"),
        P(None, "inner"),
        P(None, "inner"),
        P(None, "inner"),
        P(None, "inner"),
        P("inner"),
        P("inner"),
        P("inner"),
        P("outer", "inner"),
    )
    return jax.shard_map(
        local_part, mesh=mesh, in_specs=placed, out_specs=P("outer", "inner"), check_vma=False
    )
```

```python
import functools
import math

import jax
import jax.numpy as jnp
from jax import lax
from jax.experimental import pallas as pl
from jax.experimental.pallas import tpu as pltpu
from jax.sharding import PartitionSpec as P

STEPS = 32


def from_behind(array, axis, by):
    devices = lax.axis_size(axis)
    pairs = [(i, i + by) for i in range(devices) if 0 <= i + by < devices]
    return lax.ppermute(array, axis, pairs)


def unit_rows(values):
    return values * lax.rsqrt(jnp.sum(values * values, axis=-1, keepdims=True) + 1e-06)


def head_inputs(query_rows, key_rows, decay_rows, beta_rows, log_rate, rate_shift, beta_shift):
    queries = unit_rows(query_rows) * query_rows.shape[-1] ** (-0.5)
    keys_unit = unit_rows(key_rows)
    log_decay = -jnp.exp(log_rate) * jax.nn.softplus(decay_rows + rate_shift)
    betas = jax.nn.sigmoid(beta_rows + beta_shift)
    return (queries, keys_unit, log_decay, betas)


def block_step(with_out, state, pieces):
    queries, keys_unit, values, log_decay, betas = pieces
    block_len = keys_unit.shape[0]
    highest = lax.Precision.HIGHEST
    cum_decay = jnp.cumsum(log_decay)
    row_ids = jnp.arange(block_len)[:, None]
    col_ids = jnp.arange(block_len)[None, :]
    lower_mask = row_ids >= col_ids
    decay_mat = jnp.where(
        lower_mask,
        jnp.exp(jnp.where(lower_mask, cum_decay[:, None] - cum_decay[None, :], 0.0)),
        0.0,
    )
    key_gram = jnp.dot(keys_unit, keys_unit.T, precision=highest)
    strict = jnp.where(row_ids > col_ids, betas[:, None] * decay_mat * key_gram, 0.0)
    system = strict + jnp.eye(block_len, dtype=jnp.float32)
    start_scale = jnp.exp(cum_decay)[:, None]
    target = betas[:, None] * (values - start_scale * jnp.dot(keys_unit, state, precision=highest))
    fresh_vals = lax.linalg.triangular_solve(
        system, target, left_side=True, lower=True, unit_diagonal=True
    )
    tail_keys = jnp.exp(cum_decay[-1] - cum_decay)[:, None] * keys_unit
    new_state = jnp.exp(cum_decay[-1]) * state + jnp.dot(tail_keys.T, fresh_vals, precision=highest)
    if with_out:
        scores = decay_mat * jnp.dot(queries, keys_unit.T, precision=highest)
        output = start_scale * jnp.dot(queries, state, precision=highest) + jnp.dot(
            scores, fresh_vals, precision=highest
        )
        return (new_state, output)
    return (new_state, None)


def run_blocks(queries, keys_unit, values, log_decay, betas, state, with_out):
    length = keys_unit.shape[0]
    block_len = math.gcd(64, length)
    block_count = length // block_len

    def blocked(array):
        return array.reshape((block_count, block_len) + array.shape[1:])

    step_fn = functools.partial(block_step, with_out)
    final_state, outputs = lax.scan(
        step_fn,
        state,
        (blocked(queries), blocked(keys_unit), blocked(values), blocked(log_decay), blocked(betas)),
    )
    if with_out:
        outputs = outputs.reshape((length,) + outputs.shape[2:])
    return (final_state, outputs)


def rms_scaled(values, gain):
    return values * lax.rsqrt(jnp.mean(values * values, axis=-1, keepdims=True) + 1e-06) * gain


def apply_map(matrix, state):
    return jnp.einsum("hij,hjv->hiv", matrix, state, precision=lax.Precision.HIGHEST)


def shards(
    tokens,
    step_index,
    embed_table,
    gain_one,
    gate_weight,
    up_weight,
    down_weight,
    gain_two,
    query_weight,
    key_weight,
    value_weight,
    decay_weight,
    beta_weight,
    rate_log,
    decay_bias,
    beta_bias,
    cotangent,
):
    columns = jnp.take(embed_table, tokens, axis=0)
    embedded = lax.all_gather(columns, "inner", axis=1, tiled=True)
    emb_float = embedded.astype(jnp.float32)
    normed_one = rms_scaled(emb_float, gain_one).astype(jnp.bfloat16)
    gate_rows = jnp.dot(normed_one, gate_weight, preferred_element_type=jnp.float32)
    up_rows = jnp.dot(normed_one, up_weight, preferred_element_type=jnp.float32)
    hidden = jax.nn.silu(gate_rows) * up_rows
    path_scale = (step_index[0].astype(jnp.float32) + 0.5) / STEPS
    scaled = (path_scale * hidden).astype(jnp.bfloat16)
    group_rows = tokens.shape[0]
    row_share = group_rows // lax.axis_size("inner")
    head_count = rate_log.shape[0]
    key_dim = query_weight.shape[1] // head_count
    value_dim = value_weight.shape[1] // head_count
    main_weight = jnp.concatenate([query_weight, key_weight, value_weight], axis=1)
    gate_pair = jnp.concatenate([decay_weight, beta_weight], axis=1)

    def normalize(values):
        return rms_scaled(values, gain_two)

    mixed_share = lax.psum_scatter(
        jnp.dot(scaled, down_weight, preferred_element_type=jnp.float32).astype(jnp.bfloat16),
        "inner",
        scatter_dimension=0,
        tiled=True,
    ).astype(jnp.float32)
    own_rows = lax.dynamic_slice_in_dim(
        emb_float, lax.axis_index("inner") * row_share, row_share, 0
    )
    normed_float, norm_pull = jax.vjp(normalize, own_rows + mixed_share)
    block_piece = lax.all_gather(normed_float.astype(jnp.bfloat16), "inner", axis=0, tiled=True)
    main_part = jnp.dot(block_piece, main_weight, preferred_element_type=jnp.float32)
    gate_part = jnp.dot(block_piece, gate_pair, preferred_element_type=jnp.float32)
    projected = jnp.concatenate([main_part, gate_part], axis=1)
    key_span = head_count * key_dim
    value_span = head_count * value_dim

    def by_head(columns_block, width):
        return columns_block.reshape(group_rows, head_count, width).transpose(1, 0, 2)

    query_pre = by_head(projected[:, :key_span], key_dim)
    key_pre = by_head(projected[:, key_span : 2 * key_span], key_dim)
    value_pre = by_head(projected[:, 2 * key_span : 2 * key_span + value_span], value_dim)
    gate_start = 2 * key_span + value_span
    decay_pre = projected[:, gate_start : gate_start + head_count].T
    beta_pre = projected[:, gate_start + head_count : gate_start + 2 * head_count].T
    cot_heads = by_head(cotangent.astype(jnp.float32), value_dim)

    def carry_map(key_rows, value_rows, decay_rows, beta_rows, log_rate, rate_shift, beta_shift):
        unused_query, keys_unit, log_decay, betas = head_inputs(
            key_rows, key_rows, decay_rows, beta_rows, log_rate, rate_shift, beta_shift
        )
        padded_vals = jnp.concatenate(
            [value_rows, jnp.zeros((key_rows.shape[0], key_dim), jnp.float32)], axis=1
        )
        start_state = jnp.concatenate(
            [jnp.zeros((key_dim, value_dim), jnp.float32), jnp.eye(key_dim, dtype=jnp.float32)],
            axis=1,
        )
        final_state, unused_out = run_blocks(
            keys_unit, keys_unit, padded_vals, log_decay, betas, start_state, False
        )
        return final_state

    joined_state = jax.vmap(carry_map)(
        key_pre, value_pre, decay_pre, beta_pre, rate_log, decay_bias, beta_bias
    )
    offset_state = joined_state[:, :, :value_dim]
    transition = joined_state[:, :, value_dim:]

    def forward_step(turn_index, carried):
        incoming = from_behind(carried[1].astype(jnp.bfloat16), "outer", 1).astype(jnp.float32)
        return (incoming, apply_map(transition, incoming) + offset_state)

    state_in, unused_end = lax.fori_loop(
        0, lax.axis_size("outer") - 1, forward_step, (jnp.zeros_like(offset_state), offset_state)
    )

    def local_score(query_in, key_in, value_in, decay_in, beta_in, start_in):

        def one_head(
            query_rows,
            key_rows,
            value_rows,
            decay_rows,
            beta_rows,
            start_state,
            cot_rows,
            log_rate,
            rate_shift,
            beta_shift,
        ):
            queries, keys_unit, log_decay, betas = head_inputs(
                query_rows, key_rows, decay_rows, beta_rows, log_rate, rate_shift, beta_shift
            )
            final_state, outputs = run_blocks(
                queries, keys_unit, value_rows, log_decay, betas, start_state, True
            )
            return (jnp.sum(outputs * cot_rows), final_state)

        head_scores, final_states = jax.vmap(one_head)(
            query_in,
            key_in,
            value_in,
            decay_in,
            beta_in,
            start_in,
            cot_heads,
            rate_log,
            decay_bias,
            beta_bias,
        )
        return (jnp.sum(head_scores), final_states)

    score_pair, pull_back = jax.vjp(
        local_score, query_pre, key_pre, value_pre, decay_pre, beta_pre, state_in
    )
    first_pull = pull_back((jnp.ones_like(score_pair[0]), jnp.zeros_like(score_pair[1])))
    grad_local = first_pull[5]
    grad_trans = jnp.swapaxes(transition, 1, 2)

    def backward_step(turn_index, carried):
        incoming = from_behind(carried[1].astype(jnp.bfloat16), "outer", -1).astype(jnp.float32)
        return (incoming, apply_map(grad_trans, incoming) + grad_local)

    state_grad, unused_start = lax.fori_loop(
        0, lax.axis_size("outer") - 1, backward_step, (jnp.zeros_like(grad_local), grad_local)
    )
    second_pull = pull_back((jnp.zeros_like(score_pair[0]), state_grad))
    summed = [first_pull[which] + second_pull[which] for which in range(5)]

    def by_rows(head_block):
        return head_block.transpose(1, 0, 2).reshape(group_rows, -1).astype(jnp.bfloat16)

    grad_main = jnp.concatenate(
        [by_rows(summed[0]), by_rows(summed[1]), by_rows(summed[2])], axis=1
    )
    grad_gates = jnp.concatenate(
        [summed[3].T.astype(jnp.bfloat16), summed[4].T.astype(jnp.bfloat16)], axis=1
    )
    main_part = jnp.dot(grad_main, main_weight.T, preferred_element_type=jnp.float32)
    back_share = lax.psum_scatter(
        (main_part + jnp.dot(grad_gates, gate_pair.T, preferred_element_type=jnp.float32)).astype(
            jnp.bfloat16
        ),
        "inner",
        scatter_dimension=0,
        tiled=True,
    ).astype(jnp.float32)
    grad_mixed = norm_pull(back_share)[0].astype(jnp.bfloat16)
    return hidden * jnp.dot(
        lax.all_gather(grad_mixed, "inner", axis=0, tiled=True),
        down_weight.T,
        preferred_element_type=jnp.float32,
    )


BF16 = jnp.bfloat16
F32 = jnp.float32
MIB = 1 << 20
FETCH_PARTS = 4
TURN_ROWS = 128
BASE = 16
VMEM = pl.BlockSpec(memory_space=pltpu.VMEM)
SMEM = pl.BlockSpec(memory_space=pltpu.SMEM)
HBM = pl.BlockSpec(memory_space=pl.ANY)


def pinned(array):
    return pltpu.with_memory_space_constraint(array, pltpu.HBM)


def call(kernel, out_shape, in_specs, scratch=(), limit=16 * MIB, out=VMEM):
    return pl.pallas_call(
        kernel,
        out_shape=out_shape,
        in_specs=in_specs,
        out_specs=jax.tree.map(lambda _: out, out_shape),
        scratch_shapes=list(scratch),
        compiler_params=pltpu.CompilerParams(vmem_limit_bytes=limit),
        cost_estimate=pl.CostEstimate(flops=0, bytes_accessed=0, transcendentals=0),
    )


def like(shape, dtype):
    return jax.ShapeDtypeStruct(shape, dtype)


def dot(a, b, transposed=False):
    dims = (((1,), (1 if transposed else 0,)), ((), ()))
    return lax.dot_general(a, b, dims, preferred_element_type=F32)


def mm(a, b, transposed=False):
    return dot(a.astype(BF16), b.astype(BF16), transposed)


def row_sum(values):
    return jnp.sum(values, axis=-1, keepdims=True)


def spans(total, step):
    return [(at, min(step, total - at)) for at in range(0, total, step)]


def stream(pairs, sems):
    copies = [
        pltpu.make_async_copy(source, target, sems.at[which])
        for which, (source, target) in enumerate(pairs)
    ]
    for copy in copies:
        copy.start()
    return copies


def grid_ids(size):
    shape = (size, size)
    return lax.broadcasted_iota(jnp.int32, shape, 0), lax.broadcasted_iota(jnp.int32, shape, 1)


def quarters(source, target):
    cuts = spans(source.shape[0], source.shape[0] // FETCH_PARTS)
    return [(source.at[pl.ds(at, size)], target.at[pl.ds(at, size)]) for at, size in cuts]


def embed_kernel(
    ids_in, table, cot, out, cot_own, cot_send,
    ids, id_row, blocks, id_sems, sem, cot_sems,
):
    count = out.shape[0]
    copies = stream([(ids_in, ids), (ids_in, id_row)], id_sems)
    copies[0].wait()
    for which in range(count):
        base = pl.multiple_of((ids[0, which] // 16) * 16, 16)
        pltpu.make_async_copy(
            table.at[pl.ds(base, 16)], blocks.at[pl.ds(which * 16, 16)], sem
        ).start()
    core, half = lax.axis_index("outer") % 2, cot_own.shape[1]
    mine = pl.ds(pl.multiple_of(core * half, half), half)
    yours = pl.ds(pl.multiple_of((1 - core) * half, half), half)
    halves = stream([(cot.at[:, mine], cot_own), (cot.at[:, yours], cot_send)], cot_sems)
    copies[1].wait()
    row_ids, col_ids = grid_ids(count)
    low_bits = jnp.broadcast_to(id_row[...] & 15, (count, count))
    inside = row_sum(jnp.where(row_ids == col_ids, low_bits, 0).astype(F32)).astype(jnp.int32)
    wide = (count, 16 * count)
    wanted = lax.broadcasted_iota(jnp.int32, wide, 0) * 16 + inside
    pick = jnp.where(lax.broadcasted_iota(jnp.int32, wide, 1) == wanted, 1.0, 0.0).astype(BF16)
    pltpu.make_async_copy(table.at[pl.ds(0, 16 * count)], blocks, sem).wait()
    out[...] = dot(pick, blocks[...]).astype(BF16)
    for copy in halves:
        copy.wait()


def fetch_kernel(count, *refs):
    sources, targets, sems = refs[-1 - 2 * count : -1 - count], refs[-1 - count : -1], refs[-1]
    pairs = []
    for source, target in zip(sources, targets):
        pairs += quarters(source, target)
    for copy in stream(pairs, sems):
        copy.wait()


def fetch(after, arrays, beside=()):
    return call(
        functools.partial(fetch_kernel, len(arrays)),
        [like(array.shape, BF16) for array in arrays],
        [HBM] * (1 + len(beside) + len(arrays)),
        [pltpu.SemaphoreType.DMA((FETCH_PARTS * len(arrays),))],
        limit=MIB,
    )(after, *beside, *[pinned(array) for array in arrays])


def turn(source, target):
    for at, size in spans(source.shape[0], TURN_ROWS):
        target[:, at : at + size] = jnp.transpose(source[at : at + size, :])


def turn_kernel(count, *refs):
    for source, target in zip(refs[1 : 1 + count], refs[1 + count :]):
        turn(source, target)


def turned(after, arrays):
    return call(
        functools.partial(turn_kernel, len(arrays)),
        [like(array.shape[::-1], BF16) for array in arrays],
        [HBM] + [VMEM] * len(arrays),
        limit=4 * MIB,
    )(after, *arrays)


def feed_own_kernel(
    piece, gain, gate, up, down, gate_part, up_part, square, down_kept, sems
):
    copies = stream(quarters(down, down_kept), sems)
    share = piece.shape[1]
    at = pl.multiple_of(lax.axis_index("inner") * share, share)
    rows = piece[...].astype(F32)
    square[...] = jnp.broadcast_to(row_sum(rows * rows), square.shape)
    taken = (rows * gain[:, pl.ds(at, share)]).astype(BF16)
    for start, size in spans(gate.shape[1], 512):
        span = slice(start, start + size)
        gate_part[:, span] = dot(taken, gate[pl.ds(at, share), span])
        up_part[:, span] = dot(taken, up[pl.ds(at, share), span])
    for copy in copies:
        copy.wait()


def feed_kernel(
    step, piece0, piece1, piece2, piece3, gain, gate, up, down, gate_part, up_part, square,
    hidden, emb, scaled, part_low,
):
    width = hidden.shape[1]
    me = lax.axis_index("inner")
    share = piece0.shape[1]
    squares = square[:, :1]
    taken = []
    for which, piece in enumerate((piece0, piece1, piece2, piece3)):
        at = pl.multiple_of((me ^ which) * share, share)
        emb[:, pl.ds(at, share)] = piece[...]
        if which > 0:
            rows = piece[...].astype(F32)
            squares = squares + row_sum(rows * rows)
            taken.append((at, (rows * gain[:, pl.ds(at, share)]).astype(BF16)))
    scale = lax.rsqrt(squares / emb.shape[1] + 1e-06)
    path_scale = (step[0].astype(F32) + 0.5) / STEPS
    for start, size in spans(width, 512):
        span = slice(start, start + size)
        gate_rows, up_rows = gate_part[:, span], up_part[:, span]
        for at, rows in taken:
            gate_rows = gate_rows + dot(rows, gate[pl.ds(at, share), span])
            up_rows = up_rows + dot(rows, up[pl.ds(at, share), span])
        gate_rows = scale * gate_rows
        units = gate_rows / (1.0 + jnp.exp(-gate_rows)) * (scale * up_rows)
        hidden[:, span] = units
        scaled[:, span] = (path_scale * units).astype(BF16)
    down_kernel(0, scaled, down, part_low)


def down_kernel(begin, scaled, down, part):
    for start, size in spans(part.shape[1], 512):
        sums = dot(scaled[...], down[:, begin + start : begin + start + size])
        part[:, start : start + size] = sums.astype(BF16)


def pair_kernel(mine, other, *refs):
    refs[-1][...] = (mine[...].astype(F32) + other[...].astype(F32)).astype(BF16)


def pair_sums(low, high, before):
    low_other, high_other = swap(low, "inner", 1), swap(high, "inner", 2)
    low = call(pair_kernel, like(low.shape, BF16), [VMEM] * 2 + [HBM] * len(before))(
        low, low_other, *before
    )
    low_other = swap(low, "inner", 2)
    high = call(pair_kernel, like(high.shape, BF16), [VMEM] * 2)(high, high_other)
    return low, low_other, high, swap(high, "inner", 1)


def added(mine, other):
    return mine[...].astype(F32) + other[...].astype(F32)


def half_product(begin, emb, mine, other, gain, mixed, weights, gate_weights):
    half = mixed.shape[1]
    span = slice(begin, begin + half)
    total = emb[:, span].astype(F32) + added(mine, other)
    mixed[...] = total
    taken = (total * gain[:, span]).astype(BF16)
    raw = [dot(taken, weight[span, :]) for weight in weights]
    gates = [dot(taken, weight[:, span], True) for weight in gate_weights]
    return raw, gates, row_sum(total * total)


def project_low_kernel(
    emb, low, low_other, gain, query, key, value, decay, beta,
    mixed, query_raw, key_raw, value_raw, gate_raw, square,
):
    raw, gates, squares = half_product(
        0, emb, low, low_other, gain, mixed, (query, key, value), (decay, beta)
    )
    query_raw[...], key_raw[...], value_raw[...] = raw
    heads = decay.shape[0]
    gate_raw[:, :heads], gate_raw[:, heads : 2 * heads] = gates
    square[...] = jnp.broadcast_to(squares, square.shape)


def project_kernel(
    emb, high, high_other, gain, query, key, value, decay, beta,
    query_raw, key_raw, value_raw, gate_raw, square,
    mixed, own, send, scales,
):
    half_key = query.shape[1] // 2
    half_value = value.shape[1] // 2
    all_heads = decay.shape[0]
    first = lax.axis_index("outer") % 2 == 0
    raw, gates, squares = half_product(
        emb.shape[1] - mixed.shape[1], emb, high, high_other, gain, mixed, (query, key, value), (decay, beta)
    )
    scale = lax.rsqrt((squares + square[:, :1]) / emb.shape[1] + 1e-06)
    scales[...] = jnp.broadcast_to(scale, scales.shape)
    query_rows, key_rows, value_rows = [
        scale * (part + rest[...]) for part, rest in zip(raw, (query_raw, key_raw, value_raw))
    ]
    gates = [
        scale * (gates[0] + gate_raw[:, :all_heads]),
        scale * (gates[1] + gate_raw[:, all_heads : 2 * all_heads]),
    ]

    def put(at, low, high):
        size = low.shape[1]
        own[:, at : at + size] = jnp.where(first, low, high).astype(BF16)
        send[:, at : at + size] = jnp.where(first, high, low).astype(BF16)

    heads = decay.shape[0] // 2
    lanes = lax.broadcasted_iota(jnp.int32, scales.shape, 1)
    packed = []
    for side in range(2):
        lane, pack = 0, jnp.zeros(scales.shape, F32)
        for values in gates:
            for head in range(side * heads, (side + 1) * heads):
                column = values[:, head : head + 1]
                top = column.astype(BF16).astype(F32)
                pack = jnp.where(lanes == lane, top, pack)
                pack = jnp.where(lanes == lane + 1, column - top, pack)
                lane += 2
        packed.append(pack)
    put(0, query_rows[:, :half_key], query_rows[:, half_key:])
    put(half_key, key_rows[:, :half_key], key_rows[:, half_key:])
    put(2 * half_key, value_rows[:, :half_value], value_rows[:, half_value:])
    put(2 * half_key + half_value, *packed)


def both_blocks(own, other, target):
    core = lax.axis_index("outer") % 2
    size = own.shape[0]
    target[pl.ds(pl.multiple_of(core * size, size), size), :] = own[...]
    target[pl.ds(pl.multiple_of((1 - core) * size, size), size), :] = other[...]


def cumulate(chosen, column):
    top = column.astype(BF16)
    rest = column - top.astype(F32)
    middle = rest.astype(BF16)
    low = (rest - middle.astype(F32)).astype(BF16)
    picked = jnp.where(chosen, 1.0, 0.0).astype(BF16)

    def part(values):
        return dot(picked, jnp.broadcast_to(values, (values.shape[0], 128)))

    return part(top) + (part(middle) + part(low))


def base_inverses(systems):
    size = systems[0].shape[0]
    row_ids, col_ids = grid_ids(size)
    apart = row_ids - col_ids
    near = row_ids // BASE == col_ids // BASE

    def diagonal(which):
        picked = near & (apart == which)
        rows = [jnp.sum(jnp.where(picked, a, 0.0), axis=0, keepdims=True) for a in systems]
        return jnp.concatenate(rows, axis=0)

    def ahead(rows, by):
        return rows if by == 0 else pltpu.roll(rows, size - by, 1)

    given = [None] + [diagonal(which) for which in range(1, BASE)]
    found = [jnp.ones((len(systems), size), F32)]
    for which in range(1, BASE):
        terms = [ahead(given[j], which - j) * found[which - j] for j in range(1, which + 1)]
        while len(terms) > 1:
            pairs = [a + b for a, b in zip(terms[::2], terms[1::2])]
            terms = pairs + terms[2 * len(pairs) :]
        found.append(-terms[0])
    inverses = []
    for head, system in enumerate(systems):
        inverse = jnp.zeros((size, size), F32)
        for which in range(BASE):
            inverse = jnp.where(apart == which, found[which][head : head + 1], inverse)
        inverses.append(inverse)
    return inverses


def doublings(size):
    blocks = []
    while BASE << len(blocks) < size:
        blocks.append(BASE << len(blocks))
    return blocks


def solved(base, system, *sides):
    size = system.shape[0]
    row_ids, col_ids = grid_ids(size)
    parts = []
    for block in doublings(size):
        below = (row_ids // (2 * block) == col_ids // (2 * block)) & (
            row_ids // block != col_ids // block
        )
        parts.append(jnp.where(below, system, 0.0))
    rest = mm(base, jnp.concatenate([*parts, *sides], axis=1))
    turns = []
    for _ in parts:
        turns.append(rest[:, :size].astype(BF16))
        rest = rest[:, size:]
        rest = rest - dot(turns[-1], rest.astype(BF16))
    return turns, rest


def front_kernel(
    own, other, cot_own, cot_other, rate_log, decay_bias, beta_bias,
    packs, cots, sent, kept_offset, tails,
    decay_mats, grams, bases, turn_mats, scores, maps, fresh, pulled, columns,
):
    both_blocks(own, other, packs)
    both_blocks(cot_own, cot_other, cots)
    heads, length, _ = decay_mats.shape
    key_dim, value_dim = maps.shape[2], fresh.shape[2]
    place = lax.axis_index("outer")
    even = (place // 2) % 2 == 0
    first = place % 2 == 0

    def of_head(values, head):
        return jnp.where(
            first, values[:, head : head + 1], values[:, heads + head : heads + head + 1]
        )

    row_ids, col_ids = grid_ids(length)
    lower, strictly = row_ids >= col_ids, row_ids > col_ids
    lanes = lax.broadcasted_iota(jnp.int32, (length, 128), 1)
    gate_at = heads * (2 * key_dim + value_dim)
    gates = packs[:, gate_at : gate_at + 128].astype(F32)
    ready = []
    for head in range(heads):
        at = head * key_dim
        query_rows = packs[:, at : at + key_dim].astype(F32)
        at += heads * key_dim
        key_rows = packs[:, at : at + key_dim].astype(F32)
        at = 2 * heads * key_dim + head * value_dim
        values = packs[:, at : at + value_dim].astype(F32)
        cot = cots[:, head * value_dim : (head + 1) * value_dim]
        lane = 2 * head
        decay_in = gates[:, lane : lane + 1] + gates[:, lane + 1 : lane + 2]
        decay_in = decay_in + of_head(decay_bias, head)
        lane += 2 * heads
        beta_in = gates[:, lane : lane + 1] + gates[:, lane + 1 : lane + 2]
        beta_in = beta_in + of_head(beta_bias, head)
        rate = jnp.broadcast_to(jnp.exp(of_head(rate_log, head)), (length, 1))
        query_scale = lax.rsqrt(row_sum(query_rows * query_rows) + 1e-06) * key_dim ** (-0.5)
        key_at = (heads + head) * key_dim
        key_half = packs[:, key_at : key_at + key_dim]
        raw = dot(key_half, key_half, True)
        squares = jnp.where(row_ids == col_ids, raw, 0.0)
        key_scale = lax.rsqrt(row_sum(squares) + 1e-06)
        key_scale_row = lax.rsqrt(jnp.sum(squares, axis=0, keepdims=True) + 1e-06)
        queries, keys_unit = query_rows * query_scale, key_rows * key_scale
        log_decay = -rate * (jnp.maximum(decay_in, 0.0) + jnp.log1p(jnp.exp(-jnp.abs(decay_in))))
        betas = 1.0 / (1.0 + jnp.exp(-beta_in))
        cum = cumulate(lower, log_decay)
        decay_mat = jnp.where(
            lower, jnp.exp(jnp.where(lower, cum - jnp.transpose(cum), 0.0)), 0.0
        )
        total = cum[:, :1]
        start_scale = jnp.exp(total)
        tail_scale = jnp.exp(total[length - 1 :] - total)
        gram = jnp.where(strictly, decay_mat * (key_scale * raw * key_scale_row), 0.0)
        ready.append(
            (
                queries, keys_unit, values, cot, decay_mat, gram, start_scale, tail_scale,
                betas, query_scale, key_scale, decay_in, rate,
            )
        )
    systems = [item[8] * item[5] for item in ready]
    base_list = base_inverses(systems)
    for head, base in enumerate(base_list):
        (
            queries, keys_unit, values, cot, decay_mat, gram, start_scale, tail_scale,
            betas, query_scale, key_scale, decay_in, rate,
        ) = ready[head]
        score = decay_mat * mm(queries, keys_unit, True)
        turns, both = solved(
            base, systems[head], (betas * start_scale) * keys_unit, betas * values
        )
        state_map, fresh_vals = both[:, :key_dim], both[:, key_dim:]
        tail_t = jnp.transpose(tail_scale * keys_unit)
        offset = mm(tail_t, fresh_vals)
        score_pull = mm(jnp.transpose(score), cot)
        grad_local = mm(jnp.transpose(start_scale * queries), cot) - mm(
            jnp.transpose(state_map), score_pull
        )
        sent[head] = jnp.where(even, offset, grad_local).astype(BF16)
        kept_offset[head] = jnp.where(even, grad_local, offset)
        tails[head] = tail_t.astype(BF16)
        decay_mats[head] = decay_mat
        grams[head] = gram
        bases[head] = base.astype(BF16)
        for which, turn in enumerate(turns):
            turn_mats[head, which] = turn
        scores[head] = score
        maps[head] = state_map.astype(BF16)
        fresh[head] = fresh_vals
        pulled[head] = score_pull
        pack = jnp.zeros((length, 128), F32)
        for lane, column in enumerate(
            (query_scale, key_scale, betas, start_scale, tail_scale, decay_in, rate)
        ):
            pack = jnp.where(lanes == lane, column, pack)
        columns[head] = pack


def maps_kernel(
    tails, bases, turn_mats, maps, pulled, columns, after, sent_map, kept_map, target_local, target_map
):
    heads, length, _ = bases.shape
    even = (lax.axis_index("outer") // 2) % 2 == 0
    row_ids, col_ids = grid_ids(length)
    for head in range(heads):
        end_scale = columns[head, length - 1 :, 3:4]
        tail_t, inverse = tails[head], bases[head].astype(F32)
        for which in range(turn_mats.shape[1]):
            inverse = inverse - dot(turn_mats[head, which], inverse.astype(BF16))
        transition = jnp.where(row_ids == col_ids, end_scale, 0.0) - dot(tail_t, maps[head])
        flipped = jnp.transpose(transition)
        sent_map[head] = jnp.where(even, transition, flipped)
        kept_map[head] = jnp.where(even, flipped, transition).astype(BF16)
        target_local[head] = mm(jnp.transpose(inverse), pulled[head])
        target_map[head] = jnp.transpose(mm(tail_t, inverse)).astype(BF16)


def combine_kernel(kept_map, kept_offset, got, out):
    for head in range(out.shape[0]):
        joined = dot(kept_map[head], got[head]) + kept_offset[head]
        out[head] = joined.astype(BF16)


def back_kernel(
    near, near_map, far_one, far_two, packs, cots,
    decay_mats, grams, scores, maps, fresh, columns, target_local, target_map, after,
    own, send, grads,
):
    heads, length, _ = decay_mats.shape
    key_dim, value_dim = maps.shape[2], fresh.shape[2]
    place = lax.axis_index("outer")
    core, chip = place % 2, place // 2
    outer_chip = (chip == 0) | (chip == 3)
    odd = chip % 2 == 1
    row_ids, col_ids = grid_ids(length)
    strictly, upper = row_ids > col_ids, row_ids <= col_ids
    lanes = lax.broadcasted_iota(jnp.int32, (length, 128), 1)
    gate_at = heads * (2 * key_dim + value_dim)
    gate_grads = jnp.zeros((length, 128), F32)
    for head in range(heads):
        at = head * key_dim
        query_rows = packs[:, at : at + key_dim].astype(F32)
        key_at = at + heads * key_dim
        key_rows = packs[:, key_at : key_at + key_dim].astype(F32)
        value_at = 2 * heads * key_dim + head * value_dim
        values = packs[:, value_at : value_at + value_dim].astype(F32)
        cot = cots[:, head * value_dim : (head + 1) * value_dim]
        pack = columns[head]
        query_scale, key_scale, betas = pack[:, 0:1], pack[:, 1:2], pack[:, 2:3]
        start_scale, tail_scale = pack[:, 3:4], pack[:, 4:5]
        decay_in, rate = pack[:, 5:6], pack[:, 6:7]
        end_scale = start_scale[length - 1 :]
        queries, keys_unit = query_rows * query_scale, key_rows * key_scale
        decay_mat, gram, score = decay_mats[head], grams[head], scores[head]
        far = jnp.where(outer_chip, far_two[head], far_one[head])
        close = near[head].astype(F32)
        reached = mm(near_map[head], far) + close
        first = jnp.where(outer_chip, reached, close)
        second = jnp.where(outer_chip, 0.0, far.astype(F32))
        state = jnp.where(odd, first, second)
        state_grad = jnp.where(odd, second, first)
        state_half, state_grad_half = state.astype(BF16), state_grad.astype(BF16)
        new_vals = fresh[head] - dot(maps[head], state_half)
        new_half = new_vals.astype(BF16)
        grad_target = target_local[head] + dot(target_map[head], state_grad_half)
        target_half = grad_target.astype(BF16)
        grad_score = dot(cot, new_half, True)
        grad_sys = jnp.where(strictly, -dot(target_half, new_half, True), 0.0)
        cot_state = dot(cot, state_half, True)
        target_state = dot(target_half, state_half, True)
        new_state = dot(new_half, state_grad_half, True)
        weighted = decay_mat * grad_score
        grad_gram = grad_sys * decay_mat * betas
        grad_query = mm(weighted, keys_unit) + start_scale * cot_state
        grad_key = (
            mm(jnp.transpose(weighted), queries)
            + mm(grad_gram + jnp.transpose(grad_gram), keys_unit)
            + tail_scale * new_state
            - (betas * start_scale) * target_state
        )
        key_target = start_scale * keys_unit * target_state
        sys_gram = grad_sys * gram
        weights = grad_target * values
        grad_beta = row_sum(
            sum(weights[:, at : at + length] for at in range(0, value_dim, length))
            - key_target
            + sys_gram
        )
        both = score * grad_score + betas * sys_gram
        tails = tail_scale * keys_unit * new_state
        grad_cum = row_sum(
            both
            - jnp.transpose(both)
            + start_scale * queries * cot_state
            - betas * key_target
            - tails
        )
        ending = row_sum(jnp.sum(tails, axis=0, keepdims=True)) + end_scale * row_sum(
            jnp.sum(state * state_grad, axis=0, keepdims=True)
        )
        grad_log = cumulate(upper, grad_cum)[:, :1] + ending
        grad_decay = grad_log * -rate / (1.0 + jnp.exp(-decay_in))
        grad_beta = grad_beta * betas * (1.0 - betas)
        units = queries * key_dim**0.5
        grad_query = query_scale * (grad_query - units * row_sum(units * grad_query))
        grad_key = key_scale * (grad_key - keys_unit * row_sum(keys_unit * grad_key))
        grads[:, at : at + key_dim] = grad_query.astype(BF16)
        grads[:, key_at : key_at + key_dim] = grad_key.astype(BF16)
        grads[:, value_at : value_at + value_dim] = (betas * grad_target).astype(BF16)
        gate_grads = jnp.where(lanes == head, grad_decay, gate_grads)
        gate_grads = jnp.where(lanes == heads + head, grad_beta, gate_grads)
    grads[:, gate_at : gate_at + 128] = gate_grads.astype(BF16)
    size = own.shape[0]
    own[...] = grads[pl.ds(pl.multiple_of(core * size, size), size), :]
    send[...] = grads[pl.ds(pl.multiple_of((1 - core) * size, size), size), :]


def return_own_kernel(own, query, key, value, sums):
    half_key = query.shape[0] // 2
    half_value = value.shape[0] // 2
    core = lax.axis_index("outer") % 2
    keys = pl.ds(pl.multiple_of(core * half_key, half_key), half_key)
    values = pl.ds(pl.multiple_of(core * half_value, half_value), half_value)
    for start, size in spans(sums.shape[1], 512):
        span = slice(start, start + size)
        sums[:, span] = (
            dot(own[:, :half_key], query[keys, span])
            + dot(own[:, half_key : 2 * half_key], key[keys, span])
            + dot(own[:, 2 * half_key : 2 * half_key + half_value], value[values, span])
        )


def return_kernel(begin, own, other, query, key, value, decay, beta, sums, part):
    half_key = query.shape[0] // 2
    half_value = value.shape[0] // 2
    core = lax.axis_index("outer") % 2
    first = core == 0
    keys = pl.ds(pl.multiple_of((1 - core) * half_key, half_key), half_key)
    values = pl.ds(pl.multiple_of((1 - core) * half_value, half_value), half_value)

    def sides(at, size):
        mine, yours = own[:, at : at + size], other[:, at : at + size]
        return jnp.concatenate(
            [jnp.where(first, mine, yours), jnp.where(first, yours, mine)], axis=1
        )

    gate_at = 2 * half_key + half_value
    heads = decay.shape[0] // 2
    decays, betas = sides(gate_at, heads), sides(gate_at + heads, heads)
    for start, size in spans(part.shape[1], 512):
        span = slice(begin + start, begin + start + size)
        total = (
            sums[:, span]
            + dot(other[:, :half_key], query[keys, span])
            + dot(other[:, half_key : 2 * half_key], key[keys, span])
            + dot(other[:, 2 * half_key : gate_at], value[values, span])
            + dot(decays, decay[:, span])
            + dot(betas, beta[:, span])
        )
        part[:, start : start + size] = total.astype(BF16)


def along_kernel(mixed_low, mixed_high, down, after, out):
    half = mixed_low.shape[1]
    out[...] = mm(mixed_low[...], down[:half, :]) + mm(mixed_high[...], down[half:, :])


def final_low_kernel(low, low_other, mixed, gain, down, along, product, dots):
    half = mixed.shape[1]
    gained = added(low, low_other) * gain[:, :half]
    dots[...] = jnp.broadcast_to(row_sum(mixed[...] * gained), dots.shape)
    product[...] = mm(gained, down[:half, :])


def final_kernel(
    high, high_other, mixed, gain, down, product, dots, along, scales, hidden, out, held, sems
):
    begin = down.shape[0] - mixed.shape[1]
    gained = added(high, high_other) * gain[:, begin:]
    scale = scales[:, :1]
    mean = (dots[:, :1] + row_sum(mixed[...] * gained)) / down.shape[0]
    gained = gained.astype(BF16)
    backward = scale * scale * mean
    copies = []
    for which, (start, size) in enumerate(spans(held.shape[1], 512)):
        span = slice(start, start + size)
        total = product[:, span] + dot(gained, down[begin:, span]) - backward * along[:, span]
        held[:, span] = hidden[:, span] * (scale * total)
        columns = pl.ds(start, size)
        copy = pltpu.make_async_copy(held.at[:, columns], out.at[:, columns], sems.at[which])
        copy.start()
        copies.append(copy)
    for copy in copies:
        copy.wait()


def swap(array, axis, bit):
    return lax.ppermute(array, axis, [(i, i ^ bit) for i in range(lax.axis_size(axis))])


def four_chips(
    tokens, step_index, embed_table, gain_one, gate_weight, up_weight, down_weight, gain_two,
    query_weight, key_weight, value_weight, decay_weight, beta_weight,
    rate_log, decay_bias, beta_bias, cotangent,
):
    count, model = tokens.shape[0], gain_one.shape[0]
    width = gate_weight.shape[1]
    head_count = rate_log.shape[0]
    heads = head_count // 2
    key_dim = query_weight.shape[1] // head_count
    value_dim = value_weight.shape[1] // head_count
    pack_width = heads * (2 * key_dim + value_dim) + 128
    length = 2 * count
    rows_shape = like((count, model), BF16)
    low_width = model * 9 // 16
    widths = (low_width, model - low_width)
    part_shapes = [like((count, size), BF16) for size in widths]
    dma = pltpu.SemaphoreType.DMA
    cot_half = heads * value_dim
    columns, cot_own, cot_send = call(
        embed_kernel,
        [like((count, embed_table.shape[1]), BF16)]
        + [like((count, cot_half), BF16)] * 2,
        [HBM] * 3,
        [
            pltpu.SMEM((1, count), jnp.int32),
            pltpu.VMEM((1, count), jnp.int32),
            pltpu.VMEM((16 * count, embed_table.shape[1]), BF16),
            dma((2,)),
            dma,
            dma((2,)),
        ],
    )(pinned(tokens.reshape(1, count)), pinned(embed_table), pinned(cotangent))
    cot_other = swap(cot_send, "outer", 1)
    pieces = [columns] + [swap(columns, "inner", bit) for bit in (1, 2, 3)]
    wide = like((count, width), F32)
    one_lane = like((count, 128), F32)
    gain = gain_one.reshape(1, model)
    gate_part, up_part, squares, down_kept = call(
        feed_own_kernel,
        [wide, wide, one_lane, like((width, model), BF16)],
        [VMEM] * 4 + [HBM],
        [dma((FETCH_PARTS,))],
    )(columns, gain, gate_weight, up_weight, pinned(down_weight))
    hidden, emb, scaled, part_low = call(
        feed_kernel,
        [wide, rows_shape, like((count, width), BF16), part_shapes[0]],
        [SMEM] + [VMEM] * 11,
    )(
        step_index, *pieces, gain, gate_weight, up_weight, down_kept, gate_part, up_part, squares
    )
    part_high = call(functools.partial(down_kernel, low_width), part_shapes[1], [VMEM] * 2)(
        scaled, down_kept
    )
    weights = (query_weight, key_weight, value_weight, decay_weight.T, beta_weight.T)
    low, low_other, high, high_other = pair_sums(part_low, part_high, [*weights[:3], cot_other])
    gain = gain_two.reshape(1, model)
    mixed_low, *raw = call(
        project_low_kernel,
        [like((count, widths[0]), F32)]
        + [like((count, weight.shape[1]), F32) for weight in weights[:3]]
        + [one_lane] * 2,
        [VMEM] * 9,
    )(emb, low, low_other, gain, *weights)
    mixed_high, own, send, scales = call(
        project_kernel,
        [like((count, widths[1]), F32)] + [like((count, pack_width), BF16)] * 2 + [one_lane],
        [VMEM] * 14,
    )(emb, high, high_other, gain, *weights, *raw)
    other = swap(send, "outer", 1)
    square = (heads, length, length)
    valued = (heads, length, value_dim)
    packs, cots, sent, kept_offset, tails, *saved = call(
        front_kernel,
        [
            like((length, pack_width), BF16),
            like((length, cot_half), BF16),
            like((heads, key_dim, value_dim), BF16),
            like((heads, key_dim, value_dim), F32),
            like((heads, key_dim, length), BF16),
            like(square, F32),
            like(square, F32),
            like(square, BF16),
            like((heads, len(doublings(length)), length, length), BF16),
            like(square, F32),
            like((heads, length, key_dim), BF16),
            like(valued, F32),
            like(valued, F32),
            like((heads, length, 128), F32),
        ],
        [VMEM] * 7,
    )(
        own, other, cot_own, cot_other,
        *[array.reshape(1, head_count) for array in (rate_log, decay_bias, beta_bias)],
    )
    near = swap(sent, "outer", 2)
    decay_mats, grams, bases, turn_mats, scores, maps, fresh, pulled, columns = saved
    sent_map, kept_map, target_local, target_map = call(
        maps_kernel,
        [like((heads, key_dim, key_dim), F32), like((heads, key_dim, key_dim), BF16)]
        + [like(valued, F32), like((heads, length, key_dim), BF16)],
        [VMEM] * 6 + [HBM],
    )(tails, bases, turn_mats, maps, pulled, columns, sent)
    near_map = lax.ppermute(sent_map, "outer", [(2, 0), (3, 1), (4, 6), (5, 7)])
    joined = call(combine_kernel, like((heads, key_dim, value_dim), BF16), [VMEM] * 3)(
        kept_map, kept_offset, near
    )
    query_turned, key_turned, value_turned = turned(joined, weights[:3])
    cycle = {1: 3, 3: 2, 2: 0, 0: 1}
    far_two = lax.ppermute(
        joined, "outer", [(2 * a + core, 2 * b + core) for a, b in cycle.items() for core in (0, 1)]
    )
    far_one = lax.ppermute(joined, "outer", [(2, 4), (3, 5), (4, 2), (5, 3)])
    own, send = call(
        back_kernel,
        [like((count, pack_width), BF16)] * 2,
        [VMEM] * 14 + [HBM],
        [pltpu.VMEM((length, pack_width), BF16)],
    )(
        near, near_map, far_one, far_two, packs, cots, decay_mats, grams, scores, maps, fresh, columns,
        target_local, target_map, value_turned,
    )
    other = swap(send, "outer", 1)
    back_weights = (query_turned, key_turned, value_turned)
    sums = call(return_own_kernel, like((count, model), F32), [VMEM] * 4)(own, *back_weights)
    part_low, part_high = [
        call(functools.partial(return_kernel, begin), shape, [VMEM] * 8)(
            own, other, *back_weights, *weights[3:], sums
        )
        for begin, shape in zip((0, low_width), part_shapes)
    ]
    (down_turned,) = turned(part_low, [down_kept])
    low, low_other, high, high_other = pair_sums(part_low, part_high, [down_turned])
    along = call(along_kernel, wide, [VMEM] * 3 + [HBM])(
        mixed_low, mixed_high, down_turned, part_low
    )
    product, dots = call(final_low_kernel, [wide, one_lane], [VMEM] * 5 + [HBM])(
        low, low_other, mixed_low, gain, down_turned, along
    )
    return call(
        final_kernel,
        wide,
        [VMEM] * 10,
        [pltpu.VMEM((count, width), F32), dma((len(spans(width, 512)),))],
        out=HBM,
    )(
        high, high_other, mixed_high, gain, down_turned, product, dots, along, scales, hidden
    )


def local_part(*args):
    fits = (
        lax.axis_size("inner") == 4
        and lax.axis_size("outer") == 8
        and args[0].shape[0] == 64
        and args[13].shape[0] % 2 == 0
    )
    return four_chips(*args) if fits else shards(*args)


def solution(mesh):
    placed = (
        P("outer"),
        P(),
        P(None, "inner"),
        P(),
        P(None, "inner"),
        P(None, "inner"),
        P("inner", None),
        P(),
        P(None, "inner"),
        P(None, "inner"),
        P(None, "inner"),
        P(None, "inner"),
        P(None, "inner"),
        P("inner"),
        P("inner"),
        P("inner"),
        P("outer", "inner"),
    )
    return jax.shard_map(
        local_part, mesh=mesh, in_specs=placed, out_specs=P("outer", "inner"), check_vma=False
    )
```

```python
import functools
import math

import jax
import jax.numpy as jnp
from jax import lax
from jax.experimental import pallas as pl
from jax.experimental.pallas import tpu as pltpu
from jax.sharding import PartitionSpec as P

STEPS = 32


def from_behind(array, axis, by):
    devices = lax.axis_size(axis)
    pairs = [(i, i + by) for i in range(devices) if 0 <= i + by < devices]
    return lax.ppermute(array, axis, pairs)


def unit_rows(values):
    return values * lax.rsqrt(jnp.sum(values * values, axis=-1, keepdims=True) + 1e-06)


def head_inputs(query_rows, key_rows, decay_rows, beta_rows, log_rate, rate_shift, beta_shift):
    queries = unit_rows(query_rows) * query_rows.shape[-1] ** (-0.5)
    keys_unit = unit_rows(key_rows)
    log_decay = -jnp.exp(log_rate) * jax.nn.softplus(decay_rows + rate_shift)
    betas = jax.nn.sigmoid(beta_rows + beta_shift)
    return (queries, keys_unit, log_decay, betas)


def block_step(with_out, state, pieces):
    queries, keys_unit, values, log_decay, betas = pieces
    block_len = keys_unit.shape[0]
    highest = lax.Precision.HIGHEST
    cum_decay = jnp.cumsum(log_decay)
    row_ids = jnp.arange(block_len)[:, None]
    col_ids = jnp.arange(block_len)[None, :]
    lower_mask = row_ids >= col_ids
    decay_mat = jnp.where(
        lower_mask,
        jnp.exp(jnp.where(lower_mask, cum_decay[:, None] - cum_decay[None, :], 0.0)),
        0.0,
    )
    key_gram = jnp.dot(keys_unit, keys_unit.T, precision=highest)
    strict = jnp.where(row_ids > col_ids, betas[:, None] * decay_mat * key_gram, 0.0)
    system = strict + jnp.eye(block_len, dtype=jnp.float32)
    start_scale = jnp.exp(cum_decay)[:, None]
    target = betas[:, None] * (values - start_scale * jnp.dot(keys_unit, state, precision=highest))
    fresh_vals = lax.linalg.triangular_solve(
        system, target, left_side=True, lower=True, unit_diagonal=True
    )
    tail_keys = jnp.exp(cum_decay[-1] - cum_decay)[:, None] * keys_unit
    new_state = jnp.exp(cum_decay[-1]) * state + jnp.dot(tail_keys.T, fresh_vals, precision=highest)
    if with_out:
        scores = decay_mat * jnp.dot(queries, keys_unit.T, precision=highest)
        output = start_scale * jnp.dot(queries, state, precision=highest) + jnp.dot(
            scores, fresh_vals, precision=highest
        )
        return (new_state, output)
    return (new_state, None)


def run_blocks(queries, keys_unit, values, log_decay, betas, state, with_out):
    length = keys_unit.shape[0]
    block_len = math.gcd(64, length)
    block_count = length // block_len

    def blocked(array):
        return array.reshape((block_count, block_len) + array.shape[1:])

    step_fn = functools.partial(block_step, with_out)
    final_state, outputs = lax.scan(
        step_fn,
        state,
        (blocked(queries), blocked(keys_unit), blocked(values), blocked(log_decay), blocked(betas)),
    )
    if with_out:
        outputs = outputs.reshape((length,) + outputs.shape[2:])
    return (final_state, outputs)


def rms_scaled(values, gain):
    return values * lax.rsqrt(jnp.mean(values * values, axis=-1, keepdims=True) + 1e-06) * gain


def apply_map(matrix, state):
    return jnp.einsum("hij,hjv->hiv", matrix, state, precision=lax.Precision.HIGHEST)


def shards(
    tokens,
    step_index,
    embed_table,
    gain_one,
    gate_weight,
    up_weight,
    down_weight,
    gain_two,
    query_weight,
    key_weight,
    value_weight,
    decay_weight,
    beta_weight,
    rate_log,
    decay_bias,
    beta_bias,
    cotangent,
):
    columns = jnp.take(embed_table, tokens, axis=0)
    embedded = lax.all_gather(columns, "inner", axis=1, tiled=True)
    emb_float = embedded.astype(jnp.float32)
    normed_one = rms_scaled(emb_float, gain_one).astype(jnp.bfloat16)
    gate_rows = jnp.dot(normed_one, gate_weight, preferred_element_type=jnp.float32)
    up_rows = jnp.dot(normed_one, up_weight, preferred_element_type=jnp.float32)
    hidden = jax.nn.silu(gate_rows) * up_rows
    path_scale = (step_index[0].astype(jnp.float32) + 0.5) / STEPS
    scaled = (path_scale * hidden).astype(jnp.bfloat16)
    group_rows = tokens.shape[0]
    row_share = group_rows // lax.axis_size("inner")
    head_count = rate_log.shape[0]
    key_dim = query_weight.shape[1] // head_count
    value_dim = value_weight.shape[1] // head_count
    main_weight = jnp.concatenate([query_weight, key_weight, value_weight], axis=1)
    gate_pair = jnp.concatenate([decay_weight, beta_weight], axis=1)

    def normalize(values):
        return rms_scaled(values, gain_two)

    mixed_share = lax.psum_scatter(
        jnp.dot(scaled, down_weight, preferred_element_type=jnp.float32).astype(jnp.bfloat16),
        "inner",
        scatter_dimension=0,
        tiled=True,
    ).astype(jnp.float32)
    own_rows = lax.dynamic_slice_in_dim(
        emb_float, lax.axis_index("inner") * row_share, row_share, 0
    )
    normed_float, norm_pull = jax.vjp(normalize, own_rows + mixed_share)
    block_piece = lax.all_gather(normed_float.astype(jnp.bfloat16), "inner", axis=0, tiled=True)
    main_part = jnp.dot(block_piece, main_weight, preferred_element_type=jnp.float32)
    gate_part = jnp.dot(block_piece, gate_pair, preferred_element_type=jnp.float32)
    projected = jnp.concatenate([main_part, gate_part], axis=1)
    key_span = head_count * key_dim
    value_span = head_count * value_dim

    def by_head(columns_block, width):
        return columns_block.reshape(group_rows, head_count, width).transpose(1, 0, 2)

    query_pre = by_head(projected[:, :key_span], key_dim)
    key_pre = by_head(projected[:, key_span : 2 * key_span], key_dim)
    value_pre = by_head(projected[:, 2 * key_span : 2 * key_span + value_span], value_dim)
    gate_start = 2 * key_span + value_span
    decay_pre = projected[:, gate_start : gate_start + head_count].T
    beta_pre = projected[:, gate_start + head_count : gate_start + 2 * head_count].T
    cot_heads = by_head(cotangent.astype(jnp.float32), value_dim)

    def carry_map(key_rows, value_rows, decay_rows, beta_rows, log_rate, rate_shift, beta_shift):
        unused_query, keys_unit, log_decay, betas = head_inputs(
            key_rows, key_rows, decay_rows, beta_rows, log_rate, rate_shift, beta_shift
        )
        padded_vals = jnp.concatenate(
            [value_rows, jnp.zeros((key_rows.shape[0], key_dim), jnp.float32)], axis=1
        )
        start_state = jnp.concatenate(
            [jnp.zeros((key_dim, value_dim), jnp.float32), jnp.eye(key_dim, dtype=jnp.float32)],
            axis=1,
        )
        final_state, unused_out = run_blocks(
            keys_unit, keys_unit, padded_vals, log_decay, betas, start_state, False
        )
        return final_state

    joined_state = jax.vmap(carry_map)(
        key_pre, value_pre, decay_pre, beta_pre, rate_log, decay_bias, beta_bias
    )
    offset_state = joined_state[:, :, :value_dim]
    transition = joined_state[:, :, value_dim:]

    def forward_step(turn_index, carried):
        incoming = from_behind(carried[1].astype(jnp.bfloat16), "outer", 1).astype(jnp.float32)
        return (incoming, apply_map(transition, incoming) + offset_state)

    state_in, unused_end = lax.fori_loop(
        0, lax.axis_size("outer") - 1, forward_step, (jnp.zeros_like(offset_state), offset_state)
    )

    def local_score(query_in, key_in, value_in, decay_in, beta_in, start_in):

        def one_head(
            query_rows,
            key_rows,
            value_rows,
            decay_rows,
            beta_rows,
            start_state,
            cot_rows,
            log_rate,
            rate_shift,
            beta_shift,
        ):
            queries, keys_unit, log_decay, betas = head_inputs(
                query_rows, key_rows, decay_rows, beta_rows, log_rate, rate_shift, beta_shift
            )
            final_state, outputs = run_blocks(
                queries, keys_unit, value_rows, log_decay, betas, start_state, True
            )
            return (jnp.sum(outputs * cot_rows), final_state)

        head_scores, final_states = jax.vmap(one_head)(
            query_in,
            key_in,
            value_in,
            decay_in,
            beta_in,
            start_in,
            cot_heads,
            rate_log,
            decay_bias,
            beta_bias,
        )
        return (jnp.sum(head_scores), final_states)

    score_pair, pull_back = jax.vjp(
        local_score, query_pre, key_pre, value_pre, decay_pre, beta_pre, state_in
    )
    first_pull = pull_back((jnp.ones_like(score_pair[0]), jnp.zeros_like(score_pair[1])))
    grad_local = first_pull[5]
    grad_trans = jnp.swapaxes(transition, 1, 2)

    def backward_step(turn_index, carried):
        incoming = from_behind(carried[1].astype(jnp.bfloat16), "outer", -1).astype(jnp.float32)
        return (incoming, apply_map(grad_trans, incoming) + grad_local)

    state_grad, unused_start = lax.fori_loop(
        0, lax.axis_size("outer") - 1, backward_step, (jnp.zeros_like(grad_local), grad_local)
    )
    second_pull = pull_back((jnp.zeros_like(score_pair[0]), state_grad))
    summed = [first_pull[which] + second_pull[which] for which in range(5)]

    def by_rows(head_block):
        return head_block.transpose(1, 0, 2).reshape(group_rows, -1).astype(jnp.bfloat16)

    grad_main = jnp.concatenate(
        [by_rows(summed[0]), by_rows(summed[1]), by_rows(summed[2])], axis=1
    )
    grad_gates = jnp.concatenate(
        [summed[3].T.astype(jnp.bfloat16), summed[4].T.astype(jnp.bfloat16)], axis=1
    )
    main_part = jnp.dot(grad_main, main_weight.T, preferred_element_type=jnp.float32)
    back_share = lax.psum_scatter(
        (main_part + jnp.dot(grad_gates, gate_pair.T, preferred_element_type=jnp.float32)).astype(
            jnp.bfloat16
        ),
        "inner",
        scatter_dimension=0,
        tiled=True,
    ).astype(jnp.float32)
    grad_mixed = norm_pull(back_share)[0].astype(jnp.bfloat16)
    return hidden * jnp.dot(
        lax.all_gather(grad_mixed, "inner", axis=0, tiled=True),
        down_weight.T,
        preferred_element_type=jnp.float32,
    )


BF16 = jnp.bfloat16
F32 = jnp.float32
MIB = 1 << 20
FETCH_PARTS = 4
TURN_ROWS = 128
BASE = 16
VMEM = pl.BlockSpec(memory_space=pltpu.VMEM)
SMEM = pl.BlockSpec(memory_space=pltpu.SMEM)
HBM = pl.BlockSpec(memory_space=pl.ANY)


def pinned(array):
    return pltpu.with_memory_space_constraint(array, pltpu.HBM)


def call(kernel, out_shape, in_specs, scratch=(), limit=16 * MIB, out=VMEM):
    return pl.pallas_call(
        kernel,
        out_shape=out_shape,
        in_specs=in_specs,
        out_specs=jax.tree.map(lambda _: out, out_shape),
        scratch_shapes=list(scratch),
        compiler_params=pltpu.CompilerParams(vmem_limit_bytes=limit),
        cost_estimate=pl.CostEstimate(flops=0, bytes_accessed=0, transcendentals=0),
    )


def like(shape, dtype):
    return jax.ShapeDtypeStruct(shape, dtype)


def dot(a, b, transposed=False):
    dims = (((1,), (1 if transposed else 0,)), ((), ()))
    return lax.dot_general(a, b, dims, preferred_element_type=F32)


def mm(a, b, transposed=False):
    return dot(a.astype(BF16), b.astype(BF16), transposed)


def row_sum(values):
    return jnp.sum(values, axis=-1, keepdims=True)


def spans(total, step):
    return [(at, min(step, total - at)) for at in range(0, total, step)]


def stream(pairs, sems):
    copies = [
        pltpu.make_async_copy(source, target, sems.at[which])
        for which, (source, target) in enumerate(pairs)
    ]
    for copy in copies:
        copy.start()
    return copies


def grid_ids(size):
    shape = (size, size)
    return lax.broadcasted_iota(jnp.int32, shape, 0), lax.broadcasted_iota(jnp.int32, shape, 1)


def quarters(source, target):
    cuts = spans(source.shape[0], source.shape[0] // FETCH_PARTS)
    return [(source.at[pl.ds(at, size)], target.at[pl.ds(at, size)]) for at, size in cuts]


def embed_kernel(
    ids_in, table, cot, out, cot_own, cot_send,
    ids, id_row, blocks, id_sems, sem, cot_sems,
):
    count = out.shape[0]
    copies = stream([(ids_in, ids), (ids_in, id_row)], id_sems)
    copies[0].wait()
    for which in range(count):
        base = pl.multiple_of((ids[0, which] // 16) * 16, 16)
        pltpu.make_async_copy(
            table.at[pl.ds(base, 16)], blocks.at[pl.ds(which * 16, 16)], sem
        ).start()
    core, half = lax.axis_index("outer") % 2, cot_own.shape[1]
    mine = pl.ds(pl.multiple_of(core * half, half), half)
    yours = pl.ds(pl.multiple_of((1 - core) * half, half), half)
    halves = stream([(cot.at[:, mine], cot_own), (cot.at[:, yours], cot_send)], cot_sems)
    copies[1].wait()
    row_ids, col_ids = grid_ids(count)
    low_bits = jnp.broadcast_to(id_row[...] & 15, (count, count))
    inside = row_sum(jnp.where(row_ids == col_ids, low_bits, 0).astype(F32)).astype(jnp.int32)
    wide = (count, 16 * count)
    wanted = lax.broadcasted_iota(jnp.int32, wide, 0) * 16 + inside
    pick = jnp.where(lax.broadcasted_iota(jnp.int32, wide, 1) == wanted, 1.0, 0.0).astype(BF16)
    pltpu.make_async_copy(table.at[pl.ds(0, 16 * count)], blocks, sem).wait()
    out[...] = dot(pick, blocks[...]).astype(BF16)
    for copy in halves:
        copy.wait()


def fetch_kernel(count, *refs):
    sources, targets, sems = refs[-1 - 2 * count : -1 - count], refs[-1 - count : -1], refs[-1]
    pairs = []
    for source, target in zip(sources, targets):
        pairs += quarters(source, target)
    for copy in stream(pairs, sems):
        copy.wait()


def fetch(after, arrays, beside=()):
    return call(
        functools.partial(fetch_kernel, len(arrays)),
        [like(array.shape, BF16) for array in arrays],
        [HBM] * (1 + len(beside) + len(arrays)),
        [pltpu.SemaphoreType.DMA((FETCH_PARTS * len(arrays),))],
        limit=MIB,
    )(after, *beside, *[pinned(array) for array in arrays])


def turn(source, target):
    for at, size in spans(source.shape[0], TURN_ROWS):
        target[:, at : at + size] = jnp.transpose(source[at : at + size, :])


def turn_kernel(count, *refs):
    for source, target in zip(refs[1 : 1 + count], refs[1 + count :]):
        turn(source, target)


def turned(after, arrays):
    return call(
        functools.partial(turn_kernel, len(arrays)),
        [like(array.shape[::-1], BF16) for array in arrays],
        [HBM] + [VMEM] * len(arrays),
        limit=4 * MIB,
    )(after, *arrays)


def feed_own_kernel(
    piece, gain, gate, up, down, gate_part, up_part, square, down_kept, sems
):
    copies = stream(quarters(down, down_kept), sems)
    share = piece.shape[1]
    at = pl.multiple_of(lax.axis_index("inner") * share, share)
    rows = piece[...].astype(F32)
    square[...] = jnp.broadcast_to(row_sum(rows * rows), square.shape)
    taken = (rows * gain[:, pl.ds(at, share)]).astype(BF16)
    for start, size in spans(gate.shape[1], 512):
        span = slice(start, start + size)
        gate_part[:, span] = dot(taken, gate[pl.ds(at, share), span])
        up_part[:, span] = dot(taken, up[pl.ds(at, share), span])
    for copy in copies:
        copy.wait()


def feed_kernel(
    step, piece0, piece1, piece2, piece3, gain, gate, up, down, gate_part, up_part, square,
    hidden, emb, scaled, part_low,
):
    width = hidden.shape[1]
    me = lax.axis_index("inner")
    share = piece0.shape[1]
    squares = square[:, :1]
    taken = []
    for which, piece in enumerate((piece0, piece1, piece2, piece3)):
        at = pl.multiple_of((me ^ which) * share, share)
        emb[:, pl.ds(at, share)] = piece[...]
        if which > 0:
            rows = piece[...].astype(F32)
            squares = squares + row_sum(rows * rows)
            taken.append((at, (rows * gain[:, pl.ds(at, share)]).astype(BF16)))
    scale = lax.rsqrt(squares / emb.shape[1] + 1e-06)
    path_scale = (step[0].astype(F32) + 0.5) / STEPS
    for start, size in spans(width, 512):
        span = slice(start, start + size)
        gate_rows, up_rows = gate_part[:, span], up_part[:, span]
        for at, rows in taken:
            gate_rows = gate_rows + dot(rows, gate[pl.ds(at, share), span])
            up_rows = up_rows + dot(rows, up[pl.ds(at, share), span])
        gate_rows = scale * gate_rows
        units = gate_rows / (1.0 + jnp.exp(-gate_rows)) * (scale * up_rows)
        hidden[:, span] = units
        scaled[:, span] = (path_scale * units).astype(BF16)
    down_kernel(0, scaled, down, part_low)


def down_kernel(begin, scaled, down, part):
    for start, size in spans(part.shape[1], 512):
        sums = dot(scaled[...], down[:, begin + start : begin + start + size])
        part[:, start : start + size] = sums.astype(BF16)


def pair_kernel(mine, other, *refs):
    refs[-1][...] = (mine[...].astype(F32) + other[...].astype(F32)).astype(BF16)


def pair_sums(low, high, before):
    low_other, high_other = swap(low, "inner", 1), swap(high, "inner", 2)
    low = call(pair_kernel, like(low.shape, BF16), [VMEM] * 2 + [HBM] * len(before))(
        low, low_other, *before
    )
    low_other = swap(low, "inner", 2)
    high = call(pair_kernel, like(high.shape, BF16), [VMEM] * 2)(high, high_other)
    return low, low_other, high, swap(high, "inner", 1)


def added(mine, other):
    return mine[...].astype(F32) + other[...].astype(F32)


def half_product(begin, emb, mine, other, gain, mixed, weights, gate_weights):
    half = mixed.shape[1]
    span = slice(begin, begin + half)
    total = emb[:, span].astype(F32) + added(mine, other)
    mixed[...] = total
    taken = (total * gain[:, span]).astype(BF16)
    raw = [dot(taken, weight[span, :]) for weight in weights]
    gates = [dot(taken, weight[:, span], True) for weight in gate_weights]
    return raw, gates, row_sum(total * total)


def project_low_kernel(
    emb, low, low_other, gain, query, key, value, decay, beta,
    mixed, query_raw, key_raw, value_raw, gate_raw, square,
):
    raw, gates, squares = half_product(
        0, emb, low, low_other, gain, mixed, (query, key, value), (decay, beta)
    )
    query_raw[...], key_raw[...], value_raw[...] = raw
    heads = decay.shape[0]
    gate_raw[:, :heads], gate_raw[:, heads : 2 * heads] = gates
    square[...] = jnp.broadcast_to(squares, square.shape)


def project_kernel(
    emb, high, high_other, gain, query, key, value, decay, beta,
    query_raw, key_raw, value_raw, gate_raw, square,
    mixed, own, send, scales,
):
    half_key = query.shape[1] // 2
    half_value = value.shape[1] // 2
    all_heads = decay.shape[0]
    first = lax.axis_index("outer") % 2 == 0
    raw, gates, squares = half_product(
        emb.shape[1] - mixed.shape[1], emb, high, high_other, gain, mixed, (query, key, value), (decay, beta)
    )
    scale = lax.rsqrt((squares + square[:, :1]) / emb.shape[1] + 1e-06)
    scales[...] = jnp.broadcast_to(scale, scales.shape)
    query_rows, key_rows, value_rows = [
        scale * (part + rest[...]) for part, rest in zip(raw, (query_raw, key_raw, value_raw))
    ]
    gates = [
        scale * (gates[0] + gate_raw[:, :all_heads]),
        scale * (gates[1] + gate_raw[:, all_heads : 2 * all_heads]),
    ]

    def put(at, low, high):
        size = low.shape[1]
        own[:, at : at + size] = jnp.where(first, low, high).astype(BF16)
        send[:, at : at + size] = jnp.where(first, high, low).astype(BF16)

    heads = decay.shape[0] // 2
    lanes = lax.broadcasted_iota(jnp.int32, scales.shape, 1)
    packed = []
    for side in range(2):
        lane, pack = 0, jnp.zeros(scales.shape, F32)
        for values in gates:
            for head in range(side * heads, (side + 1) * heads):
                column = values[:, head : head + 1]
                top = column.astype(BF16).astype(F32)
                pack = jnp.where(lanes == lane, top, pack)
                pack = jnp.where(lanes == lane + 1, column - top, pack)
                lane += 2
        packed.append(pack)
    put(0, query_rows[:, :half_key], query_rows[:, half_key:])
    put(half_key, key_rows[:, :half_key], key_rows[:, half_key:])
    put(2 * half_key, value_rows[:, :half_value], value_rows[:, half_value:])
    put(2 * half_key + half_value, *packed)


def both_blocks(own, other, target):
    core = lax.axis_index("outer") % 2
    size = own.shape[0]
    target[pl.ds(pl.multiple_of(core * size, size), size), :] = own[...]
    target[pl.ds(pl.multiple_of((1 - core) * size, size), size), :] = other[...]


def cumulate(chosen, column):
    top = column.astype(BF16)
    rest = column - top.astype(F32)
    middle = rest.astype(BF16)
    low = (rest - middle.astype(F32)).astype(BF16)
    picked = jnp.where(chosen, 1.0, 0.0).astype(BF16)

    def part(values):
        return dot(picked, jnp.broadcast_to(values, (values.shape[0], 128)))

    return part(top) + (part(middle) + part(low))


def base_inverses(systems):
    size = systems[0].shape[0]
    row_ids, col_ids = grid_ids(size)
    apart = row_ids - col_ids
    near = row_ids // BASE == col_ids // BASE

    def diagonal(which):
        picked = near & (apart == which)
        rows = [jnp.sum(jnp.where(picked, a, 0.0), axis=0, keepdims=True) for a in systems]
        return jnp.concatenate(rows, axis=0)

    def ahead(rows, by):
        return rows if by == 0 else pltpu.roll(rows, size - by, 1)

    given = [None] + [diagonal(which) for which in range(1, BASE)]
    found = [jnp.ones((len(systems), size), F32)]
    for which in range(1, BASE):
        terms = [ahead(given[j], which - j) * found[which - j] for j in range(1, which + 1)]
        while len(terms) > 1:
            pairs = [a + b for a, b in zip(terms[::2], terms[1::2])]
            terms = pairs + terms[2 * len(pairs) :]
        found.append(-terms[0])
    inverses = []
    for head, system in enumerate(systems):
        inverse = jnp.zeros((size, size), F32)
        for which in range(BASE):
            inverse = jnp.where(apart == which, found[which][head : head + 1], inverse)
        inverses.append(inverse)
    return inverses


def doublings(size):
    blocks = []
    while BASE << len(blocks) < size:
        blocks.append(BASE << len(blocks))
    return blocks


def solved(base, system, *sides):
    size = system.shape[0]
    row_ids, col_ids = grid_ids(size)
    parts = []
    for block in doublings(size):
        below = (row_ids // (2 * block) == col_ids // (2 * block)) & (
            row_ids // block != col_ids // block
        )
        parts.append(jnp.where(below, system, 0.0))
    rest = mm(base, jnp.concatenate([*parts, *sides], axis=1))
    turns = []
    for _ in parts:
        turns.append(rest[:, :size].astype(BF16))
        rest = rest[:, size:]
        rest = rest - dot(turns[-1], rest.astype(BF16))
    return turns, rest


def front_kernel(
    own, other, cot_own, cot_other, rate_log, decay_bias, beta_bias,
    packs, cots, sent, kept_offset, tails,
    decay_mats, grams, bases, turn_mats, scores, maps, fresh, pulled, columns,
):
    both_blocks(own, other, packs)
    both_blocks(cot_own, cot_other, cots)
    heads, length, _ = decay_mats.shape
    key_dim, value_dim = maps.shape[2], fresh.shape[2]
    place = lax.axis_index("outer")
    even = (place // 2) % 2 == 0
    first = place % 2 == 0

    def of_head(values, head):
        return jnp.where(
            first, values[:, head : head + 1], values[:, heads + head : heads + head + 1]
        )

    row_ids, col_ids = grid_ids(length)
    lower, strictly = row_ids >= col_ids, row_ids > col_ids
    lanes = lax.broadcasted_iota(jnp.int32, (length, 128), 1)
    gate_at = heads * (2 * key_dim + value_dim)
    gates = packs[:, gate_at : gate_at + 128].astype(F32)
    ready = []
    for head in range(heads):
        at = head * key_dim
        query_rows = packs[:, at : at + key_dim].astype(F32)
        at += heads * key_dim
        key_rows = packs[:, at : at + key_dim].astype(F32)
        at = 2 * heads * key_dim + head * value_dim
        values = packs[:, at : at + value_dim].astype(F32)
        cot = cots[:, head * value_dim : (head + 1) * value_dim]
        lane = 2 * head
        decay_in = gates[:, lane : lane + 1] + gates[:, lane + 1 : lane + 2]
        decay_in = decay_in + of_head(decay_bias, head)
        lane += 2 * heads
        beta_in = gates[:, lane : lane + 1] + gates[:, lane + 1 : lane + 2]
        beta_in = beta_in + of_head(beta_bias, head)
        rate = jnp.broadcast_to(jnp.exp(of_head(rate_log, head)), (length, 1))
        query_scale = lax.rsqrt(row_sum(query_rows * query_rows) + 1e-06) * key_dim ** (-0.5)
        key_at = (heads + head) * key_dim
        key_half = packs[:, key_at : key_at + key_dim]
        raw = dot(key_half, key_half, True)
        squares = jnp.where(row_ids == col_ids, raw, 0.0)
        key_scale = lax.rsqrt(row_sum(squares) + 1e-06)
        key_scale_row = lax.rsqrt(jnp.sum(squares, axis=0, keepdims=True) + 1e-06)
        queries, keys_unit = query_rows * query_scale, key_rows * key_scale
        log_decay = -rate * (jnp.maximum(decay_in, 0.0) + jnp.log1p(jnp.exp(-jnp.abs(decay_in))))
        betas = 1.0 / (1.0 + jnp.exp(-beta_in))
        cum = cumulate(lower, log_decay)
        decay_mat = jnp.where(
            lower, jnp.exp(jnp.where(lower, cum - jnp.transpose(cum), 0.0)), 0.0
        )
        total = cum[:, :1]
        start_scale = jnp.exp(total)
        tail_scale = jnp.exp(total[length - 1 :] - total)
        gram = jnp.where(strictly, decay_mat * (key_scale * raw * key_scale_row), 0.0)
        ready.append(
            (
                queries, keys_unit, values, cot, decay_mat, gram, start_scale, tail_scale,
                betas, query_scale, key_scale, decay_in, rate,
            )
        )
    systems = [item[8] * item[5] for item in ready]
    base_list = base_inverses(systems)
    for head, base in enumerate(base_list):
        (
            queries, keys_unit, values, cot, decay_mat, gram, start_scale, tail_scale,
            betas, query_scale, key_scale, decay_in, rate,
        ) = ready[head]
        score = decay_mat * mm(queries, keys_unit, True)
        turns, both = solved(
            base, systems[head], (betas * start_scale) * keys_unit, betas * values
        )
        state_map, fresh_vals = both[:, :key_dim], both[:, key_dim:]
        tail_t = jnp.transpose(tail_scale * keys_unit)
        offset = mm(tail_t, fresh_vals)
        score_pull = mm(jnp.transpose(score), cot)
        grad_local = mm(jnp.transpose(start_scale * queries), cot) - mm(
            jnp.transpose(state_map), score_pull
        )
        sent[head] = jnp.where(even, offset, grad_local).astype(BF16)
        kept_offset[head] = jnp.where(even, grad_local, offset)
        tails[head] = tail_t.astype(BF16)
        decay_mats[head] = decay_mat
        grams[head] = gram
        bases[head] = base.astype(BF16)
        for which, turn in enumerate(turns):
            turn_mats[head, which] = turn
        scores[head] = score
        maps[head] = state_map.astype(BF16)
        fresh[head] = fresh_vals
        pulled[head] = score_pull
        pack = jnp.zeros((length, 128), F32)
        for lane, column in enumerate(
            (query_scale, key_scale, betas, start_scale, tail_scale, decay_in, rate)
        ):
            pack = jnp.where(lanes == lane, column, pack)
        columns[head] = pack


def maps_kernel(
    tails, bases, turn_mats, maps, pulled, columns, after, sent_map, kept_map, target_local, target_map
):
    heads, length, _ = bases.shape
    even = (lax.axis_index("outer") // 2) % 2 == 0
    row_ids, col_ids = grid_ids(length)
    for head in range(heads):
        end_scale = columns[head, length - 1 :, 3:4]
        tail_t, inverse = tails[head], bases[head].astype(F32)
        for which in range(turn_mats.shape[1]):
            inverse = inverse - dot(turn_mats[head, which], inverse.astype(BF16))
        transition = jnp.where(row_ids == col_ids, end_scale, 0.0) - dot(tail_t, maps[head])
        flipped = jnp.transpose(transition)
        sent_map[head] = jnp.where(even, transition, flipped)
        kept_map[head] = jnp.where(even, flipped, transition).astype(BF16)
        target_local[head] = mm(jnp.transpose(inverse), pulled[head])
        target_map[head] = jnp.transpose(mm(tail_t, inverse)).astype(BF16)


def combine_kernel(kept_map, kept_offset, got, out):
    for head in range(out.shape[0]):
        joined = dot(kept_map[head], got[head]) + kept_offset[head]
        out[head] = joined.astype(BF16)


def back_kernel(
    near, near_map, far_one, far_two, packs, cots,
    decay_mats, grams, scores, maps, fresh, columns, target_local, target_map, after,
    own, send, grads,
):
    heads, length, _ = decay_mats.shape
    key_dim, value_dim = maps.shape[2], fresh.shape[2]
    place = lax.axis_index("outer")
    core, chip = place % 2, place // 2
    outer_chip = (chip == 0) | (chip == 3)
    odd = chip % 2 == 1
    row_ids, col_ids = grid_ids(length)
    strictly, upper = row_ids > col_ids, row_ids <= col_ids
    lanes = lax.broadcasted_iota(jnp.int32, (length, 128), 1)
    gate_at = heads * (2 * key_dim + value_dim)
    gate_grads = jnp.zeros((length, 128), F32)
    for head in range(heads):
        at = head * key_dim
        query_rows = packs[:, at : at + key_dim].astype(F32)
        key_at = at + heads * key_dim
        key_rows = packs[:, key_at : key_at + key_dim].astype(F32)
        value_at = 2 * heads * key_dim + head * value_dim
        values = packs[:, value_at : value_at + value_dim].astype(F32)
        cot = cots[:, head * value_dim : (head + 1) * value_dim]
        pack = columns[head]
        query_scale, key_scale, betas = pack[:, 0:1], pack[:, 1:2], pack[:, 2:3]
        start_scale, tail_scale = pack[:, 3:4], pack[:, 4:5]
        decay_in, rate = pack[:, 5:6], pack[:, 6:7]
        end_scale = start_scale[length - 1 :]
        queries, keys_unit = query_rows * query_scale, key_rows * key_scale
        decay_mat, gram, score = decay_mats[head], grams[head], scores[head]
        far = jnp.where(outer_chip, far_two[head], far_one[head])
        close = near[head].astype(F32)
        reached = mm(near_map[head], far) + close
        first = jnp.where(outer_chip, reached, close)
        second = jnp.where(outer_chip, 0.0, far.astype(F32))
        state = jnp.where(odd, first, second)
        state_grad = jnp.where(odd, second, first)
        state_half, state_grad_half = state.astype(BF16), state_grad.astype(BF16)
        new_vals = fresh[head] - dot(maps[head], state_half)
        new_half = new_vals.astype(BF16)
        grad_target = target_local[head] + dot(target_map[head], state_grad_half)
        target_half = grad_target.astype(BF16)
        grad_score = dot(cot, new_half, True)
        grad_sys = jnp.where(strictly, -dot(target_half, new_half, True), 0.0)
        cot_state = dot(cot, state_half, True)
        target_state = dot(target_half, state_half, True)
        new_state = dot(new_half, state_grad_half, True)
        weighted = decay_mat * grad_score
        grad_gram = grad_sys * decay_mat * betas
        grad_query = mm(weighted, keys_unit) + start_scale * cot_state
        grad_key = (
            mm(jnp.transpose(weighted), queries)
            + mm(grad_gram + jnp.transpose(grad_gram), keys_unit)
            + tail_scale * new_state
            - (betas * start_scale) * target_state
        )
        key_target = start_scale * keys_unit * target_state
        sys_gram = grad_sys * gram
        weights = grad_target * values
        grad_beta = row_sum(
            sum(weights[:, at : at + length] for at in range(0, value_dim, length))
            - key_target
            + sys_gram
        )
        both = score * grad_score + betas * sys_gram
        tails = tail_scale * keys_unit * new_state
        grad_cum = row_sum(
            both
            - jnp.transpose(both)
            + start_scale * queries * cot_state
            - betas * key_target
            - tails
        )
        ending = row_sum(jnp.sum(tails, axis=0, keepdims=True)) + end_scale * row_sum(
            jnp.sum(state * state_grad, axis=0, keepdims=True)
        )
        grad_log = cumulate(upper, grad_cum)[:, :1] + ending
        grad_decay = grad_log * -rate / (1.0 + jnp.exp(-decay_in))
        grad_beta = grad_beta * betas * (1.0 - betas)
        units = queries * key_dim**0.5
        grad_query = query_scale * (grad_query - units * row_sum(units * grad_query))
        grad_key = key_scale * (grad_key - keys_unit * row_sum(keys_unit * grad_key))
        grads[:, at : at + key_dim] = grad_query.astype(BF16)
        grads[:, key_at : key_at + key_dim] = grad_key.astype(BF16)
        grads[:, value_at : value_at + value_dim] = (betas * grad_target).astype(BF16)
        gate_grads = jnp.where(lanes == head, grad_decay, gate_grads)
        gate_grads = jnp.where(lanes == heads + head, grad_beta, gate_grads)
    grads[:, gate_at : gate_at + 128] = gate_grads.astype(BF16)
    size = own.shape[0]
    own[...] = grads[pl.ds(pl.multiple_of(core * size, size), size), :]
    send[...] = grads[pl.ds(pl.multiple_of((1 - core) * size, size), size), :]


def return_own_kernel(own, query, key, value, sums):
    half_key = query.shape[0] // 2
    half_value = value.shape[0] // 2
    core = lax.axis_index("outer") % 2
    keys = pl.ds(pl.multiple_of(core * half_key, half_key), half_key)
    values = pl.ds(pl.multiple_of(core * half_value, half_value), half_value)
    for start, size in spans(sums.shape[1], 512):
        span = slice(start, start + size)
        sums[:, span] = (
            dot(own[:, :half_key], query[keys, span])
            + dot(own[:, half_key : 2 * half_key], key[keys, span])
            + dot(own[:, 2 * half_key : 2 * half_key + half_value], value[values, span])
        )


def return_kernel(begin, own, other, query, key, value, decay, beta, sums, part):
    half_key = query.shape[0] // 2
    half_value = value.shape[0] // 2
    core = lax.axis_index("outer") % 2
    first = core == 0
    keys = pl.ds(pl.multiple_of((1 - core) * half_key, half_key), half_key)
    values = pl.ds(pl.multiple_of((1 - core) * half_value, half_value), half_value)

    def sides(at, size):
        mine, yours = own[:, at : at + size], other[:, at : at + size]
        return jnp.concatenate(
            [jnp.where(first, mine, yours), jnp.where(first, yours, mine)], axis=1
        )

    gate_at = 2 * half_key + half_value
    heads = decay.shape[0] // 2
    decays, betas = sides(gate_at, heads), sides(gate_at + heads, heads)
    for start, size in spans(part.shape[1], 512):
        span = slice(begin + start, begin + start + size)
        total = (
            sums[:, span]
            + dot(other[:, :half_key], query[keys, span])
            + dot(other[:, half_key : 2 * half_key], key[keys, span])
            + dot(other[:, 2 * half_key : gate_at], value[values, span])
            + dot(decays, decay[:, span])
            + dot(betas, beta[:, span])
        )
        part[:, start : start + size] = total.astype(BF16)


def along_kernel(mixed_low, mixed_high, down, after, out):
    half = mixed_low.shape[1]
    out[...] = mm(mixed_low[...], down[:half, :]) + mm(mixed_high[...], down[half:, :])


def final_low_kernel(low, low_other, mixed, gain, down, along, product, dots):
    half = mixed.shape[1]
    gained = added(low, low_other) * gain[:, :half]
    dots[...] = jnp.broadcast_to(row_sum(mixed[...] * gained), dots.shape)
    product[...] = mm(gained, down[:half, :])


def final_kernel(
    high, high_other, mixed, gain, down, product, dots, along, scales, hidden, out, held, sems
):
    begin = down.shape[0] - mixed.shape[1]
    gained = added(high, high_other) * gain[:, begin:]
    scale = scales[:, :1]
    mean = (dots[:, :1] + row_sum(mixed[...] * gained)) / down.shape[0]
    gained = gained.astype(BF16)
    backward = scale * scale * mean
    copies = []
    for which, (start, size) in enumerate(spans(held.shape[1], 512)):
        span = slice(start, start + size)
        total = product[:, span] + dot(gained, down[begin:, span]) - backward * along[:, span]
        held[:, span] = hidden[:, span] * (scale * total)
        columns = pl.ds(start, size)
        copy = pltpu.make_async_copy(held.at[:, columns], out.at[:, columns], sems.at[which])
        copy.start()
        copies.append(copy)
    for copy in copies:
        copy.wait()


def swap(array, axis, bit):
    return lax.ppermute(array, axis, [(i, i ^ bit) for i in range(lax.axis_size(axis))])


def four_chips(
    tokens, step_index, embed_table, gain_one, gate_weight, up_weight, down_weight, gain_two,
    query_weight, key_weight, value_weight, decay_weight, beta_weight,
    rate_log, decay_bias, beta_bias, cotangent,
):
    count, model = tokens.shape[0], gain_one.shape[0]
    width = gate_weight.shape[1]
    head_count = rate_log.shape[0]
    heads = head_count // 2
    key_dim = query_weight.shape[1] // head_count
    value_dim = value_weight.shape[1] // head_count
    pack_width = heads * (2 * key_dim + value_dim) + 128
    length = 2 * count
    rows_shape = like((count, model), BF16)
    low_width = model * 9 // 16
    widths = (low_width, model - low_width)
    part_shapes = [like((count, size), BF16) for size in widths]
    dma = pltpu.SemaphoreType.DMA
    cot_half = heads * value_dim
    columns, cot_own, cot_send = call(
        embed_kernel,
        [like((count, embed_table.shape[1]), BF16)]
        + [like((count, cot_half), BF16)] * 2,
        [HBM] * 3,
        [
            pltpu.SMEM((1, count), jnp.int32),
            pltpu.VMEM((1, count), jnp.int32),
            pltpu.VMEM((16 * count, embed_table.shape[1]), BF16),
            dma((2,)),
            dma,
            dma((2,)),
        ],
    )(pinned(tokens.reshape(1, count)), pinned(embed_table), pinned(cotangent))
    cot_other = swap(cot_send, "outer", 1)
    pieces = [columns] + [swap(columns, "inner", bit) for bit in (1, 2, 3)]
    wide = like((count, width), F32)
    one_lane = like((count, 128), F32)
    gain = gain_one.reshape(1, model)
    gate_part, up_part, squares, down_kept = call(
        feed_own_kernel,
        [wide, wide, one_lane, like((width, model), BF16)],
        [VMEM] * 4 + [HBM],
        [dma((FETCH_PARTS,))],
    )(columns, gain, gate_weight, up_weight, pinned(down_weight))
    hidden, emb, scaled, part_low = call(
        feed_kernel,
        [wide, rows_shape, like((count, width), BF16), part_shapes[0]],
        [SMEM] + [VMEM] * 11,
    )(
        step_index, *pieces, gain, gate_weight, up_weight, down_kept, gate_part, up_part, squares
    )
    part_high = call(functools.partial(down_kernel, low_width), part_shapes[1], [VMEM] * 2)(
        scaled, down_kept
    )
    weights = (query_weight, key_weight, value_weight, decay_weight.T, beta_weight.T)
    low, low_other, high, high_other = pair_sums(part_low, part_high, [*weights[:3], cot_other])
    gain = gain_two.reshape(1, model)
    mixed_low, *raw = call(
        project_low_kernel,
        [like((count, widths[0]), F32)]
        + [like((count, weight.shape[1]), F32) for weight in weights[:3]]
        + [one_lane] * 2,
        [VMEM] * 9,
    )(emb, low, low_other, gain, *weights)
    mixed_high, own, send, scales = call(
        project_kernel,
        [like((count, widths[1]), F32)] + [like((count, pack_width), BF16)] * 2 + [one_lane],
        [VMEM] * 14,
    )(emb, high, high_other, gain, *weights, *raw)
    other = swap(send, "outer", 1)
    square = (heads, length, length)
    valued = (heads, length, value_dim)
    packs, cots, sent, kept_offset, tails, *saved = call(
        front_kernel,
        [
            like((length, pack_width), BF16),
            like((length, cot_half), BF16),
            like((heads, key_dim, value_dim), BF16),
            like((heads, key_dim, value_dim), F32),
            like((heads, key_dim, length), BF16),
            like(square, F32),
            like(square, F32),
            like(square, BF16),
            like((heads, len(doublings(length)), length, length), BF16),
            like(square, F32),
            like((heads, length, key_dim), BF16),
            like(valued, F32),
            like(valued, F32),
            like((heads, length, 128), F32),
        ],
        [VMEM] * 7,
    )(
        own, other, cot_own, cot_other,
        *[array.reshape(1, head_count) for array in (rate_log, decay_bias, beta_bias)],
    )
    near = swap(sent, "outer", 2)
    decay_mats, grams, bases, turn_mats, scores, maps, fresh, pulled, columns = saved
    sent_map, kept_map, target_local, target_map = call(
        maps_kernel,
        [like((heads, key_dim, key_dim), F32), like((heads, key_dim, key_dim), BF16)]
        + [like(valued, F32), like((heads, length, key_dim), BF16)],
        [VMEM] * 6 + [HBM],
    )(tails, bases, turn_mats, maps, pulled, columns, sent)
    near_map = lax.ppermute(sent_map, "outer", [(2, 0), (3, 1), (4, 6), (5, 7)])
    joined = call(combine_kernel, like((heads, key_dim, value_dim), BF16), [VMEM] * 3)(
        kept_map, kept_offset, near
    )
    query_turned, key_turned, value_turned = turned(joined, weights[:3])
    cycle = {1: 3, 3: 2, 2: 0, 0: 1}
    far_two = lax.ppermute(
        joined, "outer", [(2 * a + core, 2 * b + core) for a, b in cycle.items() for core in (0, 1)]
    )
    far_one = lax.ppermute(
        joined, "outer", [(2, 4), (3, 5), (4, 2), (5, 3), (0, 1), (1, 0), (6, 7), (7, 6)]
    )
    own, send = call(
        back_kernel,
        [like((count, pack_width), BF16)] * 2,
        [VMEM] * 14 + [HBM],
        [pltpu.VMEM((length, pack_width), BF16)],
    )(
        near, near_map, far_one, far_two, packs, cots, decay_mats, grams, scores, maps, fresh, columns,
        target_local, target_map, value_turned,
    )
    other = swap(send, "outer", 1)
    back_weights = (query_turned, key_turned, value_turned)
    sums = call(return_own_kernel, like((count, model), F32), [VMEM] * 4)(own, *back_weights)
    part_low, part_high = [
        call(functools.partial(return_kernel, begin), shape, [VMEM] * 8)(
            own, other, *back_weights, *weights[3:], sums
        )
        for begin, shape in zip((0, low_width), part_shapes)
    ]
    (down_turned,) = turned(part_low, [down_kept])
    low, low_other, high, high_other = pair_sums(part_low, part_high, [down_turned])
    along = call(along_kernel, wide, [VMEM] * 3 + [HBM])(
        mixed_low, mixed_high, down_turned, part_low
    )
    product, dots = call(final_low_kernel, [wide, one_lane], [VMEM] * 5 + [HBM])(
        low, low_other, mixed_low, gain, down_turned, along
    )
    return call(
        final_kernel,
        wide,
        [VMEM] * 10,
        [pltpu.VMEM((count, width), F32), dma((len(spans(width, 512)),))],
        out=HBM,
    )(
        high, high_other, mixed_high, gain, down_turned, product, dots, along, scales, hidden
    )


def local_part(*args):
    fits = (
        lax.axis_size("inner") == 4
        and lax.axis_size("outer") == 8
        and args[0].shape[0] == 64
        and args[13].shape[0] % 2 == 0
    )
    return four_chips(*args) if fits else shards(*args)


def solution(mesh):
    placed = (
        P("outer"),
        P(),
        P(None, "inner"),
        P(),
        P(None, "inner"),
        P(None, "inner"),
        P("inner", None),
        P(),
        P(None, "inner"),
        P(None, "inner"),
        P(None, "inner"),
        P(None, "inner"),
        P(None, "inner"),
        P("inner"),
        P("inner"),
        P("inner"),
        P("outer", "inner"),
    )
    return jax.shard_map(
        local_part, mesh=mesh, in_specs=placed, out_specs=P("outer", "inner"), check_vma=False
    )
```

```python
import functools
import math

import jax
import jax.numpy as jnp
from jax import lax
from jax.experimental import pallas as pl
from jax.experimental.pallas import tpu as pltpu
from jax.sharding import PartitionSpec as P

STEPS = 32


def from_behind(array, axis, by):
    devices = lax.axis_size(axis)
    pairs = [(i, i + by) for i in range(devices) if 0 <= i + by < devices]
    return lax.ppermute(array, axis, pairs)


def unit_rows(values):
    return values * lax.rsqrt(jnp.sum(values * values, axis=-1, keepdims=True) + 1e-06)


def head_inputs(query_rows, key_rows, decay_rows, beta_rows, log_rate, rate_shift, beta_shift):
    queries = unit_rows(query_rows) * query_rows.shape[-1] ** (-0.5)
    keys_unit = unit_rows(key_rows)
    log_decay = -jnp.exp(log_rate) * jax.nn.softplus(decay_rows + rate_shift)
    betas = jax.nn.sigmoid(beta_rows + beta_shift)
    return (queries, keys_unit, log_decay, betas)


def block_step(with_out, state, pieces):
    queries, keys_unit, values, log_decay, betas = pieces
    block_len = keys_unit.shape[0]
    highest = lax.Precision.HIGHEST
    cum_decay = jnp.cumsum(log_decay)
    row_ids = jnp.arange(block_len)[:, None]
    col_ids = jnp.arange(block_len)[None, :]
    lower_mask = row_ids >= col_ids
    decay_mat = jnp.where(
        lower_mask,
        jnp.exp(jnp.where(lower_mask, cum_decay[:, None] - cum_decay[None, :], 0.0)),
        0.0,
    )
    key_gram = jnp.dot(keys_unit, keys_unit.T, precision=highest)
    strict = jnp.where(row_ids > col_ids, betas[:, None] * decay_mat * key_gram, 0.0)
    system = strict + jnp.eye(block_len, dtype=jnp.float32)
    start_scale = jnp.exp(cum_decay)[:, None]
    target = betas[:, None] * (values - start_scale * jnp.dot(keys_unit, state, precision=highest))
    fresh_vals = lax.linalg.triangular_solve(
        system, target, left_side=True, lower=True, unit_diagonal=True
    )
    tail_keys = jnp.exp(cum_decay[-1] - cum_decay)[:, None] * keys_unit
    new_state = jnp.exp(cum_decay[-1]) * state + jnp.dot(tail_keys.T, fresh_vals, precision=highest)
    if with_out:
        scores = decay_mat * jnp.dot(queries, keys_unit.T, precision=highest)
        output = start_scale * jnp.dot(queries, state, precision=highest) + jnp.dot(
            scores, fresh_vals, precision=highest
        )
        return (new_state, output)
    return (new_state, None)


def run_blocks(queries, keys_unit, values, log_decay, betas, state, with_out):
    length = keys_unit.shape[0]
    block_len = math.gcd(64, length)
    block_count = length // block_len

    def blocked(array):
        return array.reshape((block_count, block_len) + array.shape[1:])

    step_fn = functools.partial(block_step, with_out)
    final_state, outputs = lax.scan(
        step_fn,
        state,
        (blocked(queries), blocked(keys_unit), blocked(values), blocked(log_decay), blocked(betas)),
    )
    if with_out:
        outputs = outputs.reshape((length,) + outputs.shape[2:])
    return (final_state, outputs)


def rms_scaled(values, gain):
    return values * lax.rsqrt(jnp.mean(values * values, axis=-1, keepdims=True) + 1e-06) * gain


def apply_map(matrix, state):
    return jnp.einsum("hij,hjv->hiv", matrix, state, precision=lax.Precision.HIGHEST)


def shards(
    tokens,
    step_index,
    embed_table,
    gain_one,
    gate_weight,
    up_weight,
    down_weight,
    gain_two,
    query_weight,
    key_weight,
    value_weight,
    decay_weight,
    beta_weight,
    rate_log,
    decay_bias,
    beta_bias,
    cotangent,
):
    columns = jnp.take(embed_table, tokens, axis=0)
    embedded = lax.all_gather(columns, "inner", axis=1, tiled=True)
    emb_float = embedded.astype(jnp.float32)
    normed_one = rms_scaled(emb_float, gain_one).astype(jnp.bfloat16)
    gate_rows = jnp.dot(normed_one, gate_weight, preferred_element_type=jnp.float32)
    up_rows = jnp.dot(normed_one, up_weight, preferred_element_type=jnp.float32)
    hidden = jax.nn.silu(gate_rows) * up_rows
    path_scale = (step_index[0].astype(jnp.float32) + 0.5) / STEPS
    scaled = (path_scale * hidden).astype(jnp.bfloat16)
    group_rows = tokens.shape[0]
    row_share = group_rows // lax.axis_size("inner")
    head_count = rate_log.shape[0]
    key_dim = query_weight.shape[1] // head_count
    value_dim = value_weight.shape[1] // head_count
    main_weight = jnp.concatenate([query_weight, key_weight, value_weight], axis=1)
    gate_pair = jnp.concatenate([decay_weight, beta_weight], axis=1)

    def normalize(values):
        return rms_scaled(values, gain_two)

    mixed_share = lax.psum_scatter(
        jnp.dot(scaled, down_weight, preferred_element_type=jnp.float32).astype(jnp.bfloat16),
        "inner",
        scatter_dimension=0,
        tiled=True,
    ).astype(jnp.float32)
    own_rows = lax.dynamic_slice_in_dim(
        emb_float, lax.axis_index("inner") * row_share, row_share, 0
    )
    normed_float, norm_pull = jax.vjp(normalize, own_rows + mixed_share)
    block_piece = lax.all_gather(normed_float.astype(jnp.bfloat16), "inner", axis=0, tiled=True)
    main_part = jnp.dot(block_piece, main_weight, preferred_element_type=jnp.float32)
    gate_part = jnp.dot(block_piece, gate_pair, preferred_element_type=jnp.float32)
    projected = jnp.concatenate([main_part, gate_part], axis=1)
    key_span = head_count * key_dim
    value_span = head_count * value_dim

    def by_head(columns_block, width):
        return columns_block.reshape(group_rows, head_count, width).transpose(1, 0, 2)

    query_pre = by_head(projected[:, :key_span], key_dim)
    key_pre = by_head(projected[:, key_span : 2 * key_span], key_dim)
    value_pre = by_head(projected[:, 2 * key_span : 2 * key_span + value_span], value_dim)
    gate_start = 2 * key_span + value_span
    decay_pre = projected[:, gate_start : gate_start + head_count].T
    beta_pre = projected[:, gate_start + head_count : gate_start + 2 * head_count].T
    cot_heads = by_head(cotangent.astype(jnp.float32), value_dim)

    def carry_map(key_rows, value_rows, decay_rows, beta_rows, log_rate, rate_shift, beta_shift):
        unused_query, keys_unit, log_decay, betas = head_inputs(
            key_rows, key_rows, decay_rows, beta_rows, log_rate, rate_shift, beta_shift
        )
        padded_vals = jnp.concatenate(
            [value_rows, jnp.zeros((key_rows.shape[0], key_dim), jnp.float32)], axis=1
        )
        start_state = jnp.concatenate(
            [jnp.zeros((key_dim, value_dim), jnp.float32), jnp.eye(key_dim, dtype=jnp.float32)],
            axis=1,
        )
        final_state, unused_out = run_blocks(
            keys_unit, keys_unit, padded_vals, log_decay, betas, start_state, False
        )
        return final_state

    joined_state = jax.vmap(carry_map)(
        key_pre, value_pre, decay_pre, beta_pre, rate_log, decay_bias, beta_bias
    )
    offset_state = joined_state[:, :, :value_dim]
    transition = joined_state[:, :, value_dim:]

    def forward_step(turn_index, carried):
        incoming = from_behind(carried[1].astype(jnp.bfloat16), "outer", 1).astype(jnp.float32)
        return (incoming, apply_map(transition, incoming) + offset_state)

    state_in, unused_end = lax.fori_loop(
        0, lax.axis_size("outer") - 1, forward_step, (jnp.zeros_like(offset_state), offset_state)
    )

    def local_score(query_in, key_in, value_in, decay_in, beta_in, start_in):

        def one_head(
            query_rows,
            key_rows,
            value_rows,
            decay_rows,
            beta_rows,
            start_state,
            cot_rows,
            log_rate,
            rate_shift,
            beta_shift,
        ):
            queries, keys_unit, log_decay, betas = head_inputs(
                query_rows, key_rows, decay_rows, beta_rows, log_rate, rate_shift, beta_shift
            )
            final_state, outputs = run_blocks(
                queries, keys_unit, value_rows, log_decay, betas, start_state, True
            )
            return (jnp.sum(outputs * cot_rows), final_state)

        head_scores, final_states = jax.vmap(one_head)(
            query_in,
            key_in,
            value_in,
            decay_in,
            beta_in,
            start_in,
            cot_heads,
            rate_log,
            decay_bias,
            beta_bias,
        )
        return (jnp.sum(head_scores), final_states)

    score_pair, pull_back = jax.vjp(
        local_score, query_pre, key_pre, value_pre, decay_pre, beta_pre, state_in
    )
    first_pull = pull_back((jnp.ones_like(score_pair[0]), jnp.zeros_like(score_pair[1])))
    grad_local = first_pull[5]
    grad_trans = jnp.swapaxes(transition, 1, 2)

    def backward_step(turn_index, carried):
        incoming = from_behind(carried[1].astype(jnp.bfloat16), "outer", -1).astype(jnp.float32)
        return (incoming, apply_map(grad_trans, incoming) + grad_local)

    state_grad, unused_start = lax.fori_loop(
        0, lax.axis_size("outer") - 1, backward_step, (jnp.zeros_like(grad_local), grad_local)
    )
    second_pull = pull_back((jnp.zeros_like(score_pair[0]), state_grad))
    summed = [first_pull[which] + second_pull[which] for which in range(5)]

    def by_rows(head_block):
        return head_block.transpose(1, 0, 2).reshape(group_rows, -1).astype(jnp.bfloat16)

    grad_main = jnp.concatenate(
        [by_rows(summed[0]), by_rows(summed[1]), by_rows(summed[2])], axis=1
    )
    grad_gates = jnp.concatenate(
        [summed[3].T.astype(jnp.bfloat16), summed[4].T.astype(jnp.bfloat16)], axis=1
    )
    main_part = jnp.dot(grad_main, main_weight.T, preferred_element_type=jnp.float32)
    back_share = lax.psum_scatter(
        (main_part + jnp.dot(grad_gates, gate_pair.T, preferred_element_type=jnp.float32)).astype(
            jnp.bfloat16
        ),
        "inner",
        scatter_dimension=0,
        tiled=True,
    ).astype(jnp.float32)
    grad_mixed = norm_pull(back_share)[0].astype(jnp.bfloat16)
    return hidden * jnp.dot(
        lax.all_gather(grad_mixed, "inner", axis=0, tiled=True),
        down_weight.T,
        preferred_element_type=jnp.float32,
    )


BF16 = jnp.bfloat16
F32 = jnp.float32
MIB = 1 << 20
FETCH_PARTS = 4
TURN_ROWS = 128
BASE = 16
VMEM = pl.BlockSpec(memory_space=pltpu.VMEM)
SMEM = pl.BlockSpec(memory_space=pltpu.SMEM)
HBM = pl.BlockSpec(memory_space=pl.ANY)


def pinned(array):
    return pltpu.with_memory_space_constraint(array, pltpu.HBM)


def call(kernel, out_shape, in_specs, scratch=(), limit=16 * MIB, out=VMEM):
    return pl.pallas_call(
        kernel,
        out_shape=out_shape,
        in_specs=in_specs,
        out_specs=jax.tree.map(lambda _: out, out_shape),
        scratch_shapes=list(scratch),
        compiler_params=pltpu.CompilerParams(vmem_limit_bytes=limit),
        cost_estimate=pl.CostEstimate(flops=0, bytes_accessed=0, transcendentals=0),
    )


def like(shape, dtype):
    return jax.ShapeDtypeStruct(shape, dtype)


def dot(a, b, transposed=False):
    dims = (((1,), (1 if transposed else 0,)), ((), ()))
    return lax.dot_general(a, b, dims, preferred_element_type=F32)


def mm(a, b, transposed=False):
    return dot(a.astype(BF16), b.astype(BF16), transposed)


def row_sum(values):
    return jnp.sum(values, axis=-1, keepdims=True)


def spans(total, step):
    return [(at, min(step, total - at)) for at in range(0, total, step)]


def stream(pairs, sems):
    copies = [
        pltpu.make_async_copy(source, target, sems.at[which])
        for which, (source, target) in enumerate(pairs)
    ]
    for copy in copies:
        copy.start()
    return copies


def grid_ids(size):
    shape = (size, size)
    return lax.broadcasted_iota(jnp.int32, shape, 0), lax.broadcasted_iota(jnp.int32, shape, 1)


def quarters(source, target):
    cuts = spans(source.shape[0], source.shape[0] // FETCH_PARTS)
    return [(source.at[pl.ds(at, size)], target.at[pl.ds(at, size)]) for at, size in cuts]


def embed_kernel(
    ids_in, table, cot, out, cot_own, cot_send,
    ids, id_row, blocks, id_sems, sem, cot_sems,
):
    count = out.shape[0]
    copies = stream([(ids_in, ids), (ids_in, id_row)], id_sems)
    copies[0].wait()
    for which in range(count):
        base = pl.multiple_of((ids[0, which] // 16) * 16, 16)
        pltpu.make_async_copy(
            table.at[pl.ds(base, 16)], blocks.at[pl.ds(which * 16, 16)], sem
        ).start()
    core, half = lax.axis_index("outer") % 2, cot_own.shape[1]
    mine = pl.ds(pl.multiple_of(core * half, half), half)
    yours = pl.ds(pl.multiple_of((1 - core) * half, half), half)
    halves = stream([(cot.at[:, mine], cot_own), (cot.at[:, yours], cot_send)], cot_sems)
    copies[1].wait()
    row_ids, col_ids = grid_ids(count)
    low_bits = jnp.broadcast_to(id_row[...] & 15, (count, count))
    inside = row_sum(jnp.where(row_ids == col_ids, low_bits, 0).astype(F32)).astype(jnp.int32)
    wide = (count, 16 * count)
    wanted = lax.broadcasted_iota(jnp.int32, wide, 0) * 16 + inside
    pick = jnp.where(lax.broadcasted_iota(jnp.int32, wide, 1) == wanted, 1.0, 0.0).astype(BF16)
    pltpu.make_async_copy(table.at[pl.ds(0, 16 * count)], blocks, sem).wait()
    out[...] = dot(pick, blocks[...]).astype(BF16)
    for copy in halves:
        copy.wait()


def fetch_kernel(count, *refs):
    sources, targets, sems = refs[-1 - 2 * count : -1 - count], refs[-1 - count : -1], refs[-1]
    pairs = []
    for source, target in zip(sources, targets):
        pairs += quarters(source, target)
    for copy in stream(pairs, sems):
        copy.wait()


def fetch(after, arrays, beside=()):
    return call(
        functools.partial(fetch_kernel, len(arrays)),
        [like(array.shape, BF16) for array in arrays],
        [HBM] * (1 + len(beside) + len(arrays)),
        [pltpu.SemaphoreType.DMA((FETCH_PARTS * len(arrays),))],
        limit=MIB,
    )(after, *beside, *[pinned(array) for array in arrays])


def turn(source, target):
    for at, size in spans(source.shape[0], TURN_ROWS):
        target[:, at : at + size] = jnp.transpose(source[at : at + size, :])


def turn_kernel(count, *refs):
    for source, target in zip(refs[1 : 1 + count], refs[1 + count :]):
        turn(source, target)


def turned(after, arrays):
    return call(
        functools.partial(turn_kernel, len(arrays)),
        [like(array.shape[::-1], BF16) for array in arrays],
        [HBM] + [VMEM] * len(arrays),
        limit=4 * MIB,
    )(after, *arrays)


def feed_own_kernel(
    piece, gain, gate, up, down, gate_part, up_part, square, down_kept, sems
):
    copies = stream(quarters(down, down_kept), sems)
    share = piece.shape[1]
    at = pl.multiple_of(lax.axis_index("inner") * share, share)
    rows = piece[...].astype(F32)
    square[...] = jnp.broadcast_to(row_sum(rows * rows), square.shape)
    taken = (rows * gain[:, pl.ds(at, share)]).astype(BF16)
    for start, size in spans(gate.shape[1], 512):
        span = slice(start, start + size)
        gate_part[:, span] = dot(taken, gate[pl.ds(at, share), span])
        up_part[:, span] = dot(taken, up[pl.ds(at, share), span])
    for copy in copies:
        copy.wait()


def feed_kernel(
    step, piece0, piece1, piece2, piece3, gain, gate, up, down, gate_part, up_part, square,
    hidden, emb, scaled, part_low,
):
    width = hidden.shape[1]
    me = lax.axis_index("inner")
    share = piece0.shape[1]
    squares = square[:, :1]
    taken = []
    for which, piece in enumerate((piece0, piece1, piece2, piece3)):
        at = pl.multiple_of((me ^ which) * share, share)
        emb[:, pl.ds(at, share)] = piece[...]
        if which > 0:
            rows = piece[...].astype(F32)
            squares = squares + row_sum(rows * rows)
            taken.append((at, (rows * gain[:, pl.ds(at, share)]).astype(BF16)))
    scale = lax.rsqrt(squares / emb.shape[1] + 1e-06)
    path_scale = (step[0].astype(F32) + 0.5) / STEPS
    for start, size in spans(width, 512):
        span = slice(start, start + size)
        gate_rows, up_rows = gate_part[:, span], up_part[:, span]
        for at, rows in taken:
            gate_rows = gate_rows + dot(rows, gate[pl.ds(at, share), span])
            up_rows = up_rows + dot(rows, up[pl.ds(at, share), span])
        gate_rows = scale * gate_rows
        units = gate_rows / (1.0 + jnp.exp(-gate_rows)) * (scale * up_rows)
        hidden[:, span] = units
        scaled[:, span] = (path_scale * units).astype(BF16)
    down_kernel(0, scaled, down, part_low)


def down_kernel(begin, scaled, down, part):
    for start, size in spans(part.shape[1], 512):
        sums = dot(scaled[...], down[:, begin + start : begin + start + size])
        part[:, start : start + size] = sums.astype(BF16)


def pair_kernel(mine, other, *refs):
    refs[-1][...] = (mine[...].astype(F32) + other[...].astype(F32)).astype(BF16)


def pair_sums(low, high, before):
    low_other, high_other = swap(low, "inner", 1), swap(high, "inner", 2)
    low = call(pair_kernel, like(low.shape, BF16), [VMEM] * 2 + [HBM] * len(before))(
        low, low_other, *before
    )
    low_other = swap(low, "inner", 2)
    high = call(pair_kernel, like(high.shape, BF16), [VMEM] * 2)(high, high_other)
    return low, low_other, high, swap(high, "inner", 1)


def added(mine, other):
    return mine[...].astype(F32) + other[...].astype(F32)


def half_product(begin, emb, mine, other, gain, mixed, weights, gate_weights):
    half = mixed.shape[1]
    span = slice(begin, begin + half)
    total = emb[:, span].astype(F32) + added(mine, other)
    mixed[...] = total
    taken = (total * gain[:, span]).astype(BF16)
    raw = [dot(taken, weight[span, :]) for weight in weights]
    gates = [dot(taken, weight[:, span], True) for weight in gate_weights]
    return raw, gates, row_sum(total * total)


def project_low_kernel(
    emb, low, low_other, gain, query, key, value, decay, beta,
    mixed, query_raw, key_raw, value_raw, gate_raw, square,
):
    raw, gates, squares = half_product(
        0, emb, low, low_other, gain, mixed, (query, key, value), (decay, beta)
    )
    query_raw[...], key_raw[...], value_raw[...] = raw
    heads = decay.shape[0]
    gate_raw[:, :heads], gate_raw[:, heads : 2 * heads] = gates
    square[...] = jnp.broadcast_to(squares, square.shape)


def project_kernel(
    emb, high, high_other, gain, query, key, value, decay, beta,
    query_raw, key_raw, value_raw, gate_raw, square, rate_log, decay_bias, beta_bias,
    mixed, own, send, scales,
):
    half_key = query.shape[1] // 2
    half_value = value.shape[1] // 2
    all_heads = decay.shape[0]
    first = lax.axis_index("outer") % 2 == 0
    raw, gates, squares = half_product(
        emb.shape[1] - mixed.shape[1], emb, high, high_other, gain, mixed, (query, key, value), (decay, beta)
    )
    scale = lax.rsqrt((squares + square[:, :1]) / emb.shape[1] + 1e-06)
    scales[...] = jnp.broadcast_to(scale, scales.shape)
    query_rows, key_rows, value_rows = [
        scale * (part + rest[...]) for part, rest in zip(raw, (query_raw, key_raw, value_raw))
    ]
    decay_in = scale * (gates[0] + gate_raw[:, :all_heads]) + decay_bias[...]
    beta_in = scale * (gates[1] + gate_raw[:, all_heads : 2 * all_heads]) + beta_bias[...]
    rate = jnp.exp(rate_log[...])
    gates = [
        -rate * (jnp.maximum(decay_in, 0.0) + jnp.log1p(jnp.exp(-jnp.abs(decay_in)))),
        1.0 / (1.0 + jnp.exp(-beta_in)),
        -rate / (1.0 + jnp.exp(-decay_in)),
    ]

    def put(at, low, high):
        size = low.shape[1]
        own[:, at : at + size] = jnp.where(first, low, high).astype(BF16)
        send[:, at : at + size] = jnp.where(first, high, low).astype(BF16)

    heads = decay.shape[0] // 2
    lanes = lax.broadcasted_iota(jnp.int32, scales.shape, 1)
    packed = []
    for side in range(2):
        lane, pack = 0, jnp.zeros(scales.shape, F32)
        for values in gates:
            for head in range(side * heads, (side + 1) * heads):
                column = values[:, head : head + 1]
                top = column.astype(BF16).astype(F32)
                pack = jnp.where(lanes == lane, top, pack)
                pack = jnp.where(lanes == lane + 1, column - top, pack)
                lane += 2
        packed.append(pack)
    put(0, query_rows[:, :half_key], query_rows[:, half_key:])
    put(half_key, key_rows[:, :half_key], key_rows[:, half_key:])
    put(2 * half_key, value_rows[:, :half_value], value_rows[:, half_value:])
    put(2 * half_key + half_value, *packed)


def both_blocks(own, other, target):
    core = lax.axis_index("outer") % 2
    size = own.shape[0]
    target[pl.ds(pl.multiple_of(core * size, size), size), :] = own[...]
    target[pl.ds(pl.multiple_of((1 - core) * size, size), size), :] = other[...]


def cumulate(chosen, column):
    top = column.astype(BF16)
    rest = column - top.astype(F32)
    middle = rest.astype(BF16)
    low = (rest - middle.astype(F32)).astype(BF16)
    picked = jnp.where(chosen, 1.0, 0.0).astype(BF16)

    def part(values):
        return dot(picked, jnp.broadcast_to(values, (values.shape[0], 128)))

    return part(top) + (part(middle) + part(low))


def base_inverses(systems):
    size = systems[0].shape[0]
    row_ids, col_ids = grid_ids(size)
    apart = row_ids - col_ids
    near = row_ids // BASE == col_ids // BASE

    def diagonal(which):
        picked = near & (apart == which)
        rows = [jnp.sum(jnp.where(picked, a, 0.0), axis=0, keepdims=True) for a in systems]
        return jnp.concatenate(rows, axis=0)

    def ahead(rows, by):
        return rows if by == 0 else pltpu.roll(rows, size - by, 1)

    given = [None] + [diagonal(which) for which in range(1, BASE)]
    found = [jnp.ones((len(systems), size), F32)]
    for which in range(1, BASE):
        terms = [ahead(given[j], which - j) * found[which - j] for j in range(1, which + 1)]
        while len(terms) > 1:
            pairs = [a + b for a, b in zip(terms[::2], terms[1::2])]
            terms = pairs + terms[2 * len(pairs) :]
        found.append(-terms[0])
    inverses = []
    for head, system in enumerate(systems):
        inverse = jnp.zeros((size, size), F32)
        for which in range(BASE):
            inverse = jnp.where(apart == which, found[which][head : head + 1], inverse)
        inverses.append(inverse)
    return inverses


def doublings(size):
    blocks = []
    while BASE << len(blocks) < size:
        blocks.append(BASE << len(blocks))
    return blocks


def solved(base, system, *sides):
    size = system.shape[0]
    row_ids, col_ids = grid_ids(size)
    parts = []
    for block in doublings(size):
        below = (row_ids // (2 * block) == col_ids // (2 * block)) & (
            row_ids // block != col_ids // block
        )
        parts.append(jnp.where(below, system, 0.0))
    rest = mm(base, jnp.concatenate([*parts, *sides], axis=1))
    turns = []
    for _ in parts:
        turns.append(rest[:, :size].astype(BF16))
        rest = rest[:, size:]
        rest = rest - dot(turns[-1], rest.astype(BF16))
    return turns, rest


def front_kernel(
    own, other, cot_own, cot_other,
    packs, cots, sent, kept_offset, tails,
    decay_mats, grams, bases, turn_mats, scores, maps, fresh, pulled, columns,
):
    both_blocks(own, other, packs)
    both_blocks(cot_own, cot_other, cots)
    heads, length, _ = decay_mats.shape
    key_dim, value_dim = maps.shape[2], fresh.shape[2]
    place = lax.axis_index("outer")
    even = (place // 2) % 2 == 0
    row_ids, col_ids = grid_ids(length)
    lower, strictly = row_ids >= col_ids, row_ids > col_ids
    lanes = lax.broadcasted_iota(jnp.int32, (length, 128), 1)
    gate_at = heads * (2 * key_dim + value_dim)
    gates = packs[:, gate_at : gate_at + 128].astype(F32)
    ready = []
    for head in range(heads):
        at = head * key_dim
        query_rows = packs[:, at : at + key_dim].astype(F32)
        at += heads * key_dim
        key_rows = packs[:, at : at + key_dim].astype(F32)
        at = 2 * heads * key_dim + head * value_dim
        values = packs[:, at : at + value_dim].astype(F32)
        cot = cots[:, head * value_dim : (head + 1) * value_dim]
        lane = 2 * head
        log_decay = gates[:, lane : lane + 1] + gates[:, lane + 1 : lane + 2]
        lane += 2 * heads
        betas = gates[:, lane : lane + 1] + gates[:, lane + 1 : lane + 2]
        lane += 2 * heads
        slope = gates[:, lane : lane + 1] + gates[:, lane + 1 : lane + 2]
        query_scale = lax.rsqrt(row_sum(query_rows * query_rows) + 1e-06) * key_dim ** (-0.5)
        key_at = (heads + head) * key_dim
        key_half = packs[:, key_at : key_at + key_dim]
        raw = dot(key_half, key_half, True)
        squares = jnp.where(row_ids == col_ids, raw, 0.0)
        key_scale = lax.rsqrt(row_sum(squares) + 1e-06)
        key_scale_row = lax.rsqrt(jnp.sum(squares, axis=0, keepdims=True) + 1e-06)
        queries, keys_unit = query_rows * query_scale, key_rows * key_scale
        cum = cumulate(lower, log_decay)
        decay_mat = jnp.where(
            lower, jnp.exp(jnp.where(lower, cum - jnp.transpose(cum), 0.0)), 0.0
        )
        total = cum[:, :1]
        start_scale = jnp.exp(total)
        tail_scale = jnp.exp(total[length - 1 :] - total)
        gram = jnp.where(strictly, decay_mat * (key_scale * raw * key_scale_row), 0.0)
        ready.append(
            (
                queries, keys_unit, values, cot, decay_mat, gram, start_scale, tail_scale,
                betas, query_scale, key_scale, slope,
            )
        )
    systems = [item[8] * item[5] for item in ready]
    base_list = base_inverses(systems)
    for head, base in enumerate(base_list):
        (
            queries, keys_unit, values, cot, decay_mat, gram, start_scale, tail_scale,
            betas, query_scale, key_scale, slope,
        ) = ready[head]
        score = decay_mat * mm(queries, keys_unit, True)
        turns, both = solved(
            base, systems[head], (betas * start_scale) * keys_unit, betas * values
        )
        state_map, fresh_vals = both[:, :key_dim], both[:, key_dim:]
        tail_t = jnp.transpose(tail_scale * keys_unit)
        offset = mm(tail_t, fresh_vals)
        score_pull = mm(jnp.transpose(score), cot)
        grad_local = mm(jnp.transpose(start_scale * queries), cot) - mm(
            jnp.transpose(state_map), score_pull
        )
        sent[head] = jnp.where(even, offset, grad_local).astype(BF16)
        kept_offset[head] = jnp.where(even, grad_local, offset)
        tails[head] = tail_t.astype(BF16)
        decay_mats[head] = decay_mat
        grams[head] = gram
        bases[head] = base.astype(BF16)
        for which, turn in enumerate(turns):
            turn_mats[head, which] = turn
        scores[head] = score
        maps[head] = state_map.astype(BF16)
        fresh[head] = fresh_vals
        pulled[head] = score_pull
        pack = jnp.zeros((length, 128), F32)
        for lane, column in enumerate(
            (query_scale, key_scale, betas, start_scale, tail_scale, slope)
        ):
            pack = jnp.where(lanes == lane, column, pack)
        columns[head] = pack


def maps_kernel(
    tails, bases, turn_mats, maps, pulled, columns, after, sent_map, kept_map, target_local, target_map
):
    heads, length, _ = bases.shape
    even = (lax.axis_index("outer") // 2) % 2 == 0
    row_ids, col_ids = grid_ids(length)
    for head in range(heads):
        end_scale = columns[head, length - 1 :, 3:4]
        tail_t, inverse = tails[head], bases[head].astype(F32)
        for which in range(turn_mats.shape[1]):
            inverse = inverse - dot(turn_mats[head, which], inverse.astype(BF16))
        transition = jnp.where(row_ids == col_ids, end_scale, 0.0) - dot(tail_t, maps[head])
        flipped = jnp.transpose(transition)
        sent_map[head] = jnp.where(even, transition, flipped)
        kept_map[head] = jnp.where(even, flipped, transition).astype(BF16)
        target_local[head] = mm(jnp.transpose(inverse), pulled[head])
        target_map[head] = jnp.transpose(mm(tail_t, inverse)).astype(BF16)


def combine_kernel(kept_map, kept_offset, got, out):
    for head in range(out.shape[0]):
        joined = dot(kept_map[head], got[head]) + kept_offset[head]
        out[head] = joined.astype(BF16)


def back_kernel(
    near, near_map, far_one, far_two, packs, cots,
    decay_mats, grams, scores, maps, fresh, columns, target_local, target_map, after,
    own, send, grads,
):
    heads, length, _ = decay_mats.shape
    key_dim, value_dim = maps.shape[2], fresh.shape[2]
    place = lax.axis_index("outer")
    core, chip = place % 2, place // 2
    outer_chip = (chip == 0) | (chip == 3)
    odd = chip % 2 == 1
    row_ids, col_ids = grid_ids(length)
    strictly, upper = row_ids > col_ids, row_ids <= col_ids
    lanes = lax.broadcasted_iota(jnp.int32, (length, 128), 1)
    gate_at = heads * (2 * key_dim + value_dim)
    gate_grads = jnp.zeros((length, 128), F32)
    for head in range(heads):
        at = head * key_dim
        query_rows = packs[:, at : at + key_dim].astype(F32)
        key_at = at + heads * key_dim
        key_rows = packs[:, key_at : key_at + key_dim].astype(F32)
        value_at = 2 * heads * key_dim + head * value_dim
        values = packs[:, value_at : value_at + value_dim].astype(F32)
        cot = cots[:, head * value_dim : (head + 1) * value_dim]
        pack = columns[head]
        query_scale, key_scale, betas = pack[:, 0:1], pack[:, 1:2], pack[:, 2:3]
        start_scale, tail_scale = pack[:, 3:4], pack[:, 4:5]
        slope = pack[:, 5:6]
        end_scale = start_scale[length - 1 :]
        queries, keys_unit = query_rows * query_scale, key_rows * key_scale
        decay_mat, gram, score = decay_mats[head], grams[head], scores[head]
        far = jnp.where(outer_chip, far_two[head], far_one[head])
        close = near[head].astype(F32)
        reached = mm(near_map[head], far) + close
        first = jnp.where(outer_chip, reached, close)
        second = jnp.where(outer_chip, 0.0, far.astype(F32))
        state = jnp.where(odd, first, second)
        state_grad = jnp.where(odd, second, first)
        state_half, state_grad_half = state.astype(BF16), state_grad.astype(BF16)
        new_vals = fresh[head] - dot(maps[head], state_half)
        new_half = new_vals.astype(BF16)
        grad_target = target_local[head] + dot(target_map[head], state_grad_half)
        target_half = grad_target.astype(BF16)
        grad_score = dot(cot, new_half, True)
        grad_sys = jnp.where(strictly, -dot(target_half, new_half, True), 0.0)
        cot_state = dot(cot, state_half, True)
        target_state = dot(target_half, state_half, True)
        new_state = dot(new_half, state_grad_half, True)
        weighted = decay_mat * grad_score
        grad_gram = grad_sys * decay_mat * betas
        grad_query = mm(weighted, keys_unit) + start_scale * cot_state
        grad_key = (
            mm(jnp.transpose(weighted), queries)
            + mm(grad_gram + jnp.transpose(grad_gram), keys_unit)
            + tail_scale * new_state
            - (betas * start_scale) * target_state
        )
        key_target = start_scale * keys_unit * target_state
        sys_gram = grad_sys * gram
        weights = grad_target * values
        grad_beta = row_sum(
            sum(weights[:, at : at + length] for at in range(0, value_dim, length))
            - key_target
            + sys_gram
        )
        both = score * grad_score + betas * sys_gram
        tails = tail_scale * keys_unit * new_state
        grad_cum = row_sum(
            both
            - jnp.transpose(both)
            + start_scale * queries * cot_state
            - betas * key_target
            - tails
        )
        ending = row_sum(jnp.sum(tails, axis=0, keepdims=True)) + end_scale * row_sum(
            jnp.sum(state * state_grad, axis=0, keepdims=True)
        )
        grad_log = cumulate(upper, grad_cum)[:, :1] + ending
        grad_decay = grad_log * slope
        grad_beta = grad_beta * betas * (1.0 - betas)
        units = queries * key_dim**0.5
        grad_query = query_scale * (grad_query - units * row_sum(units * grad_query))
        grad_key = key_scale * (grad_key - keys_unit * row_sum(keys_unit * grad_key))
        grads[:, at : at + key_dim] = grad_query.astype(BF16)
        grads[:, key_at : key_at + key_dim] = grad_key.astype(BF16)
        grads[:, value_at : value_at + value_dim] = (betas * grad_target).astype(BF16)
        gate_grads = jnp.where(lanes == head, grad_decay, gate_grads)
        gate_grads = jnp.where(lanes == heads + head, grad_beta, gate_grads)
    grads[:, gate_at : gate_at + 128] = gate_grads.astype(BF16)
    size = own.shape[0]
    own[...] = grads[pl.ds(pl.multiple_of(core * size, size), size), :]
    send[...] = grads[pl.ds(pl.multiple_of((1 - core) * size, size), size), :]


def return_own_kernel(own, query, key, value, sums):
    half_key = query.shape[0] // 2
    half_value = value.shape[0] // 2
    core = lax.axis_index("outer") % 2
    keys = pl.ds(pl.multiple_of(core * half_key, half_key), half_key)
    values = pl.ds(pl.multiple_of(core * half_value, half_value), half_value)
    for start, size in spans(sums.shape[1], 512):
        span = slice(start, start + size)
        sums[:, span] = (
            dot(own[:, :half_key], query[keys, span])
            + dot(own[:, half_key : 2 * half_key], key[keys, span])
            + dot(own[:, 2 * half_key : 2 * half_key + half_value], value[values, span])
        )


def return_kernel(begin, own, other, query, key, value, decay, beta, sums, part):
    half_key = query.shape[0] // 2
    half_value = value.shape[0] // 2
    core = lax.axis_index("outer") % 2
    first = core == 0
    keys = pl.ds(pl.multiple_of((1 - core) * half_key, half_key), half_key)
    values = pl.ds(pl.multiple_of((1 - core) * half_value, half_value), half_value)

    def sides(at, size):
        mine, yours = own[:, at : at + size], other[:, at : at + size]
        return jnp.concatenate(
            [jnp.where(first, mine, yours), jnp.where(first, yours, mine)], axis=1
        )

    gate_at = 2 * half_key + half_value
    heads = decay.shape[0] // 2
    decays, betas = sides(gate_at, heads), sides(gate_at + heads, heads)
    for start, size in spans(part.shape[1], 512):
        span = slice(begin + start, begin + start + size)
        total = (
            sums[:, span]
            + dot(other[:, :half_key], query[keys, span])
            + dot(other[:, half_key : 2 * half_key], key[keys, span])
            + dot(other[:, 2 * half_key : gate_at], value[values, span])
            + dot(decays, decay[:, span])
            + dot(betas, beta[:, span])
        )
        part[:, start : start + size] = total.astype(BF16)


def along_kernel(mixed_low, mixed_high, down, after, out):
    half = mixed_low.shape[1]
    out[...] = mm(mixed_low[...], down[:half, :]) + mm(mixed_high[...], down[half:, :])


def final_low_kernel(low, low_other, mixed, gain, down, along, product, dots):
    half = mixed.shape[1]
    gained = added(low, low_other) * gain[:, :half]
    dots[...] = jnp.broadcast_to(row_sum(mixed[...] * gained), dots.shape)
    product[...] = mm(gained, down[:half, :])


def final_kernel(
    high, high_other, mixed, gain, down, product, dots, along, scales, hidden, out, held, sems
):
    begin = down.shape[0] - mixed.shape[1]
    gained = added(high, high_other) * gain[:, begin:]
    scale = scales[:, :1]
    mean = (dots[:, :1] + row_sum(mixed[...] * gained)) / down.shape[0]
    gained = gained.astype(BF16)
    backward = scale * scale * mean
    copies = []
    for which, (start, size) in enumerate(spans(held.shape[1], 512)):
        span = slice(start, start + size)
        total = product[:, span] + dot(gained, down[begin:, span]) - backward * along[:, span]
        held[:, span] = hidden[:, span] * (scale * total)
        columns = pl.ds(start, size)
        copy = pltpu.make_async_copy(held.at[:, columns], out.at[:, columns], sems.at[which])
        copy.start()
        copies.append(copy)
    for copy in copies:
        copy.wait()


def swap(array, axis, bit):
    return lax.ppermute(array, axis, [(i, i ^ bit) for i in range(lax.axis_size(axis))])


def four_chips(
    tokens, step_index, embed_table, gain_one, gate_weight, up_weight, down_weight, gain_two,
    query_weight, key_weight, value_weight, decay_weight, beta_weight,
    rate_log, decay_bias, beta_bias, cotangent,
):
    count, model = tokens.shape[0], gain_one.shape[0]
    width = gate_weight.shape[1]
    head_count = rate_log.shape[0]
    heads = head_count // 2
    key_dim = query_weight.shape[1] // head_count
    value_dim = value_weight.shape[1] // head_count
    pack_width = heads * (2 * key_dim + value_dim) + 128
    length = 2 * count
    rows_shape = like((count, model), BF16)
    low_width = model * 9 // 16
    widths = (low_width, model - low_width)
    part_shapes = [like((count, size), BF16) for size in widths]
    dma = pltpu.SemaphoreType.DMA
    cot_half = heads * value_dim
    columns, cot_own, cot_send = call(
        embed_kernel,
        [like((count, embed_table.shape[1]), BF16)]
        + [like((count, cot_half), BF16)] * 2,
        [HBM] * 3,
        [
            pltpu.SMEM((1, count), jnp.int32),
            pltpu.VMEM((1, count), jnp.int32),
            pltpu.VMEM((16 * count, embed_table.shape[1]), BF16),
            dma((2,)),
            dma,
            dma((2,)),
        ],
    )(pinned(tokens.reshape(1, count)), pinned(embed_table), pinned(cotangent))
    cot_other = swap(cot_send, "outer", 1)
    pieces = [columns] + [swap(columns, "inner", bit) for bit in (1, 2, 3)]
    wide = like((count, width), F32)
    one_lane = like((count, 128), F32)
    gain = gain_one.reshape(1, model)
    gate_part, up_part, squares, down_kept = call(
        feed_own_kernel,
        [wide, wide, one_lane, like((width, model), BF16)],
        [VMEM] * 4 + [HBM],
        [dma((FETCH_PARTS,))],
    )(columns, gain, gate_weight, up_weight, pinned(down_weight))
    hidden, emb, scaled, part_low = call(
        feed_kernel,
        [wide, rows_shape, like((count, width), BF16), part_shapes[0]],
        [SMEM] + [VMEM] * 11,
    )(
        step_index, *pieces, gain, gate_weight, up_weight, down_kept, gate_part, up_part, squares
    )
    part_high = call(functools.partial(down_kernel, low_width), part_shapes[1], [VMEM] * 2)(
        scaled, down_kept
    )
    weights = (query_weight, key_weight, value_weight, decay_weight.T, beta_weight.T)
    low, low_other, high, high_other = pair_sums(part_low, part_high, [*weights[:3], cot_other])
    gain = gain_two.reshape(1, model)
    mixed_low, *raw = call(
        project_low_kernel,
        [like((count, widths[0]), F32)]
        + [like((count, weight.shape[1]), F32) for weight in weights[:3]]
        + [one_lane] * 2,
        [VMEM] * 9,
    )(emb, low, low_other, gain, *weights)
    mixed_high, own, send, scales = call(
        project_kernel,
        [like((count, widths[1]), F32)] + [like((count, pack_width), BF16)] * 2 + [one_lane],
        [VMEM] * 17,
    )(
        emb, high, high_other, gain, *weights, *raw,
        *[array.reshape(1, head_count) for array in (rate_log, decay_bias, beta_bias)],
    )
    other = swap(send, "outer", 1)
    square = (heads, length, length)
    valued = (heads, length, value_dim)
    packs, cots, sent, kept_offset, tails, *saved = call(
        front_kernel,
        [
            like((length, pack_width), BF16),
            like((length, cot_half), BF16),
            like((heads, key_dim, value_dim), BF16),
            like((heads, key_dim, value_dim), F32),
            like((heads, key_dim, length), BF16),
            like(square, F32),
            like(square, F32),
            like(square, BF16),
            like((heads, len(doublings(length)), length, length), BF16),
            like(square, F32),
            like((heads, length, key_dim), BF16),
            like(valued, F32),
            like(valued, F32),
            like((heads, length, 128), F32),
        ],
        [VMEM] * 4,
    )(own, other, cot_own, cot_other)
    near = swap(sent, "outer", 2)
    decay_mats, grams, bases, turn_mats, scores, maps, fresh, pulled, columns = saved
    sent_map, kept_map, target_local, target_map = call(
        maps_kernel,
        [like((heads, key_dim, key_dim), F32), like((heads, key_dim, key_dim), BF16)]
        + [like(valued, F32), like((heads, length, key_dim), BF16)],
        [VMEM] * 6 + [HBM],
    )(tails, bases, turn_mats, maps, pulled, columns, sent)
    near_map = lax.ppermute(sent_map, "outer", [(2, 0), (3, 1), (4, 6), (5, 7)])
    joined = call(combine_kernel, like((heads, key_dim, value_dim), BF16), [VMEM] * 3)(
        kept_map, kept_offset, near
    )
    query_turned, key_turned, value_turned = turned(joined, weights[:3])
    cycle = {1: 3, 3: 2, 2: 0, 0: 1}
    far_two = lax.ppermute(
        joined, "outer", [(2 * a + core, 2 * b + core) for a, b in cycle.items() for core in (0, 1)]
    )
    far_one = lax.ppermute(
        joined, "outer", [(2, 4), (3, 5), (4, 2), (5, 3), (0, 1), (1, 0), (6, 7), (7, 6)]
    )
    own, send = call(
        back_kernel,
        [like((count, pack_width), BF16)] * 2,
        [VMEM] * 14 + [HBM],
        [pltpu.VMEM((length, pack_width), BF16)],
    )(
        near, near_map, far_one, far_two, packs, cots, decay_mats, grams, scores, maps, fresh, columns,
        target_local, target_map, value_turned,
    )
    other = swap(send, "outer", 1)
    back_weights = (query_turned, key_turned, value_turned)
    sums = call(return_own_kernel, like((count, model), F32), [VMEM] * 4)(own, *back_weights)
    part_low, part_high = [
        call(functools.partial(return_kernel, begin), shape, [VMEM] * 8)(
            own, other, *back_weights, *weights[3:], sums
        )
        for begin, shape in zip((0, low_width), part_shapes)
    ]
    (down_turned,) = turned(part_low, [down_kept])
    low, low_other, high, high_other = pair_sums(part_low, part_high, [down_turned])
    along = call(along_kernel, wide, [VMEM] * 3 + [HBM])(
        mixed_low, mixed_high, down_turned, part_low
    )
    product, dots = call(final_low_kernel, [wide, one_lane], [VMEM] * 5 + [HBM])(
        low, low_other, mixed_low, gain, down_turned, along
    )
    return call(
        final_kernel,
        wide,
        [VMEM] * 10,
        [pltpu.VMEM((count, width), F32), dma((len(spans(width, 512)),))],
        out=HBM,
    )(
        high, high_other, mixed_high, gain, down_turned, product, dots, along, scales, hidden
    )


def local_part(*args):
    fits = (
        lax.axis_size("inner") == 4
        and lax.axis_size("outer") == 8
        and args[0].shape[0] == 64
        and args[13].shape[0] % 2 == 0
    )
    return four_chips(*args) if fits else shards(*args)


def solution(mesh):
    placed = (
        P("outer"),
        P(),
        P(None, "inner"),
        P(),
        P(None, "inner"),
        P(None, "inner"),
        P("inner", None),
        P(),
        P(None, "inner"),
        P(None, "inner"),
        P(None, "inner"),
        P(None, "inner"),
        P(None, "inner"),
        P("inner"),
        P("inner"),
        P("inner"),
        P("outer", "inner"),
    )
    return jax.shard_map(
        local_part, mesh=mesh, in_specs=placed, out_specs=P("outer", "inner"), check_vma=False
    )
```

```python
import functools
import math

import jax
import jax.numpy as jnp
from jax import lax
from jax.experimental import pallas as pl
from jax.experimental.pallas import tpu as pltpu
from jax.sharding import PartitionSpec as P

STEPS = 32


def from_behind(array, axis, by):
    devices = lax.axis_size(axis)
    pairs = [(i, i + by) for i in range(devices) if 0 <= i + by < devices]
    return lax.ppermute(array, axis, pairs)


def unit_rows(values):
    return values * lax.rsqrt(jnp.sum(values * values, axis=-1, keepdims=True) + 1e-06)


def head_inputs(query_rows, key_rows, decay_rows, beta_rows, log_rate, rate_shift, beta_shift):
    queries = unit_rows(query_rows) * query_rows.shape[-1] ** (-0.5)
    keys_unit = unit_rows(key_rows)
    log_decay = -jnp.exp(log_rate) * jax.nn.softplus(decay_rows + rate_shift)
    betas = jax.nn.sigmoid(beta_rows + beta_shift)
    return (queries, keys_unit, log_decay, betas)


def block_step(with_out, state, pieces):
    queries, keys_unit, values, log_decay, betas = pieces
    block_len = keys_unit.shape[0]
    highest = lax.Precision.HIGHEST
    cum_decay = jnp.cumsum(log_decay)
    row_ids = jnp.arange(block_len)[:, None]
    col_ids = jnp.arange(block_len)[None, :]
    lower_mask = row_ids >= col_ids
    decay_mat = jnp.where(
        lower_mask,
        jnp.exp(jnp.where(lower_mask, cum_decay[:, None] - cum_decay[None, :], 0.0)),
        0.0,
    )
    key_gram = jnp.dot(keys_unit, keys_unit.T, precision=highest)
    strict = jnp.where(row_ids > col_ids, betas[:, None] * decay_mat * key_gram, 0.0)
    system = strict + jnp.eye(block_len, dtype=jnp.float32)
    start_scale = jnp.exp(cum_decay)[:, None]
    target = betas[:, None] * (values - start_scale * jnp.dot(keys_unit, state, precision=highest))
    fresh_vals = lax.linalg.triangular_solve(
        system, target, left_side=True, lower=True, unit_diagonal=True
    )
    tail_keys = jnp.exp(cum_decay[-1] - cum_decay)[:, None] * keys_unit
    new_state = jnp.exp(cum_decay[-1]) * state + jnp.dot(tail_keys.T, fresh_vals, precision=highest)
    if with_out:
        scores = decay_mat * jnp.dot(queries, keys_unit.T, precision=highest)
        output = start_scale * jnp.dot(queries, state, precision=highest) + jnp.dot(
            scores, fresh_vals, precision=highest
        )
        return (new_state, output)
    return (new_state, None)


def run_blocks(queries, keys_unit, values, log_decay, betas, state, with_out):
    length = keys_unit.shape[0]
    block_len = math.gcd(64, length)
    block_count = length // block_len

    def blocked(array):
        return array.reshape((block_count, block_len) + array.shape[1:])

    step_fn = functools.partial(block_step, with_out)
    final_state, outputs = lax.scan(
        step_fn,
        state,
        (blocked(queries), blocked(keys_unit), blocked(values), blocked(log_decay), blocked(betas)),
    )
    if with_out:
        outputs = outputs.reshape((length,) + outputs.shape[2:])
    return (final_state, outputs)


def rms_scaled(values, gain):
    return values * lax.rsqrt(jnp.mean(values * values, axis=-1, keepdims=True) + 1e-06) * gain


def apply_map(matrix, state):
    return jnp.einsum("hij,hjv->hiv", matrix, state, precision=lax.Precision.HIGHEST)


def shards(
    tokens,
    step_index,
    embed_table,
    gain_one,
    gate_weight,
    up_weight,
    down_weight,
    gain_two,
    query_weight,
    key_weight,
    value_weight,
    decay_weight,
    beta_weight,
    rate_log,
    decay_bias,
    beta_bias,
    cotangent,
):
    columns = jnp.take(embed_table, tokens, axis=0)
    embedded = lax.all_gather(columns, "inner", axis=1, tiled=True)
    emb_float = embedded.astype(jnp.float32)
    normed_one = rms_scaled(emb_float, gain_one).astype(jnp.bfloat16)
    gate_rows = jnp.dot(normed_one, gate_weight, preferred_element_type=jnp.float32)
    up_rows = jnp.dot(normed_one, up_weight, preferred_element_type=jnp.float32)
    hidden = jax.nn.silu(gate_rows) * up_rows
    path_scale = (step_index[0].astype(jnp.float32) + 0.5) / STEPS
    scaled = (path_scale * hidden).astype(jnp.bfloat16)
    group_rows = tokens.shape[0]
    row_share = group_rows // lax.axis_size("inner")
    head_count = rate_log.shape[0]
    key_dim = query_weight.shape[1] // head_count
    value_dim = value_weight.shape[1] // head_count
    main_weight = jnp.concatenate([query_weight, key_weight, value_weight], axis=1)
    gate_pair = jnp.concatenate([decay_weight, beta_weight], axis=1)

    def normalize(values):
        return rms_scaled(values, gain_two)

    mixed_share = lax.psum_scatter(
        jnp.dot(scaled, down_weight, preferred_element_type=jnp.float32).astype(jnp.bfloat16),
        "inner",
        scatter_dimension=0,
        tiled=True,
    ).astype(jnp.float32)
    own_rows = lax.dynamic_slice_in_dim(
        emb_float, lax.axis_index("inner") * row_share, row_share, 0
    )
    normed_float, norm_pull = jax.vjp(normalize, own_rows + mixed_share)
    block_piece = lax.all_gather(normed_float.astype(jnp.bfloat16), "inner", axis=0, tiled=True)
    main_part = jnp.dot(block_piece, main_weight, preferred_element_type=jnp.float32)
    gate_part = jnp.dot(block_piece, gate_pair, preferred_element_type=jnp.float32)
    projected = jnp.concatenate([main_part, gate_part], axis=1)
    key_span = head_count * key_dim
    value_span = head_count * value_dim

    def by_head(columns_block, width):
        return columns_block.reshape(group_rows, head_count, width).transpose(1, 0, 2)

    query_pre = by_head(projected[:, :key_span], key_dim)
    key_pre = by_head(projected[:, key_span : 2 * key_span], key_dim)
    value_pre = by_head(projected[:, 2 * key_span : 2 * key_span + value_span], value_dim)
    gate_start = 2 * key_span + value_span
    decay_pre = projected[:, gate_start : gate_start + head_count].T
    beta_pre = projected[:, gate_start + head_count : gate_start + 2 * head_count].T
    cot_heads = by_head(cotangent.astype(jnp.float32), value_dim)

    def carry_map(key_rows, value_rows, decay_rows, beta_rows, log_rate, rate_shift, beta_shift):
        unused_query, keys_unit, log_decay, betas = head_inputs(
            key_rows, key_rows, decay_rows, beta_rows, log_rate, rate_shift, beta_shift
        )
        padded_vals = jnp.concatenate(
            [value_rows, jnp.zeros((key_rows.shape[0], key_dim), jnp.float32)], axis=1
        )
        start_state = jnp.concatenate(
            [jnp.zeros((key_dim, value_dim), jnp.float32), jnp.eye(key_dim, dtype=jnp.float32)],
            axis=1,
        )
        final_state, unused_out = run_blocks(
            keys_unit, keys_unit, padded_vals, log_decay, betas, start_state, False
        )
        return final_state

    joined_state = jax.vmap(carry_map)(
        key_pre, value_pre, decay_pre, beta_pre, rate_log, decay_bias, beta_bias
    )
    offset_state = joined_state[:, :, :value_dim]
    transition = joined_state[:, :, value_dim:]

    def forward_step(turn_index, carried):
        incoming = from_behind(carried[1].astype(jnp.bfloat16), "outer", 1).astype(jnp.float32)
        return (incoming, apply_map(transition, incoming) + offset_state)

    state_in, unused_end = lax.fori_loop(
        0, lax.axis_size("outer") - 1, forward_step, (jnp.zeros_like(offset_state), offset_state)
    )

    def local_score(query_in, key_in, value_in, decay_in, beta_in, start_in):

        def one_head(
            query_rows,
            key_rows,
            value_rows,
            decay_rows,
            beta_rows,
            start_state,
            cot_rows,
            log_rate,
            rate_shift,
            beta_shift,
        ):
            queries, keys_unit, log_decay, betas = head_inputs(
                query_rows, key_rows, decay_rows, beta_rows, log_rate, rate_shift, beta_shift
            )
            final_state, outputs = run_blocks(
                queries, keys_unit, value_rows, log_decay, betas, start_state, True
            )
            return (jnp.sum(outputs * cot_rows), final_state)

        head_scores, final_states = jax.vmap(one_head)(
            query_in,
            key_in,
            value_in,
            decay_in,
            beta_in,
            start_in,
            cot_heads,
            rate_log,
            decay_bias,
            beta_bias,
        )
        return (jnp.sum(head_scores), final_states)

    score_pair, pull_back = jax.vjp(
        local_score, query_pre, key_pre, value_pre, decay_pre, beta_pre, state_in
    )
    first_pull = pull_back((jnp.ones_like(score_pair[0]), jnp.zeros_like(score_pair[1])))
    grad_local = first_pull[5]
    grad_trans = jnp.swapaxes(transition, 1, 2)

    def backward_step(turn_index, carried):
        incoming = from_behind(carried[1].astype(jnp.bfloat16), "outer", -1).astype(jnp.float32)
        return (incoming, apply_map(grad_trans, incoming) + grad_local)

    state_grad, unused_start = lax.fori_loop(
        0, lax.axis_size("outer") - 1, backward_step, (jnp.zeros_like(grad_local), grad_local)
    )
    second_pull = pull_back((jnp.zeros_like(score_pair[0]), state_grad))
    summed = [first_pull[which] + second_pull[which] for which in range(5)]

    def by_rows(head_block):
        return head_block.transpose(1, 0, 2).reshape(group_rows, -1).astype(jnp.bfloat16)

    grad_main = jnp.concatenate(
        [by_rows(summed[0]), by_rows(summed[1]), by_rows(summed[2])], axis=1
    )
    grad_gates = jnp.concatenate(
        [summed[3].T.astype(jnp.bfloat16), summed[4].T.astype(jnp.bfloat16)], axis=1
    )
    main_part = jnp.dot(grad_main, main_weight.T, preferred_element_type=jnp.float32)
    back_share = lax.psum_scatter(
        (main_part + jnp.dot(grad_gates, gate_pair.T, preferred_element_type=jnp.float32)).astype(
            jnp.bfloat16
        ),
        "inner",
        scatter_dimension=0,
        tiled=True,
    ).astype(jnp.float32)
    grad_mixed = norm_pull(back_share)[0].astype(jnp.bfloat16)
    return hidden * jnp.dot(
        lax.all_gather(grad_mixed, "inner", axis=0, tiled=True),
        down_weight.T,
        preferred_element_type=jnp.float32,
    )


BF16 = jnp.bfloat16
F32 = jnp.float32
MIB = 1 << 20
FETCH_PARTS = 4
TURN_ROWS = 128
BASE = 16
VMEM = pl.BlockSpec(memory_space=pltpu.VMEM)
SMEM = pl.BlockSpec(memory_space=pltpu.SMEM)
HBM = pl.BlockSpec(memory_space=pl.ANY)


def pinned(array):
    return pltpu.with_memory_space_constraint(array, pltpu.HBM)


def call(kernel, out_shape, in_specs, scratch=(), limit=16 * MIB, out=VMEM):
    return pl.pallas_call(
        kernel,
        out_shape=out_shape,
        in_specs=in_specs,
        out_specs=jax.tree.map(lambda _: out, out_shape),
        scratch_shapes=list(scratch),
        compiler_params=pltpu.CompilerParams(vmem_limit_bytes=limit),
        cost_estimate=pl.CostEstimate(flops=0, bytes_accessed=0, transcendentals=0),
    )


def like(shape, dtype):
    return jax.ShapeDtypeStruct(shape, dtype)


def dot(a, b, transposed=False):
    dims = (((1,), (1 if transposed else 0,)), ((), ()))
    return lax.dot_general(a, b, dims, preferred_element_type=F32)


def mm(a, b, transposed=False):
    return dot(a.astype(BF16), b.astype(BF16), transposed)


def row_sum(values):
    return jnp.sum(values, axis=-1, keepdims=True)


def spans(total, step):
    return [(at, min(step, total - at)) for at in range(0, total, step)]


def stream(pairs, sems):
    copies = [
        pltpu.make_async_copy(source, target, sems.at[which])
        for which, (source, target) in enumerate(pairs)
    ]
    for copy in copies:
        copy.start()
    return copies


def grid_ids(size):
    shape = (size, size)
    return lax.broadcasted_iota(jnp.int32, shape, 0), lax.broadcasted_iota(jnp.int32, shape, 1)


def quarters(source, target):
    cuts = spans(source.shape[0], source.shape[0] // FETCH_PARTS)
    return [(source.at[pl.ds(at, size)], target.at[pl.ds(at, size)]) for at, size in cuts]


def embed_kernel(
    ids_in, table, cot, out, cot_own, cot_send,
    ids, id_row, blocks, id_sems, sem, cot_sems,
):
    count = out.shape[0]
    copies = stream([(ids_in, ids), (ids_in, id_row)], id_sems)
    copies[0].wait()
    for which in range(count):
        base = pl.multiple_of((ids[0, which] // 16) * 16, 16)
        pltpu.make_async_copy(
            table.at[pl.ds(base, 16)], blocks.at[pl.ds(which * 16, 16)], sem
        ).start()
    core, half = lax.axis_index("outer") % 2, cot_own.shape[1]
    mine = pl.ds(pl.multiple_of(core * half, half), half)
    yours = pl.ds(pl.multiple_of((1 - core) * half, half), half)
    halves = stream([(cot.at[:, mine], cot_own), (cot.at[:, yours], cot_send)], cot_sems)
    copies[1].wait()
    row_ids, col_ids = grid_ids(count)
    low_bits = jnp.broadcast_to(id_row[...] & 15, (count, count))
    inside = row_sum(jnp.where(row_ids == col_ids, low_bits, 0).astype(F32)).astype(jnp.int32)
    wide = (count, 16 * count)
    wanted = lax.broadcasted_iota(jnp.int32, wide, 0) * 16 + inside
    pick = jnp.where(lax.broadcasted_iota(jnp.int32, wide, 1) == wanted, 1.0, 0.0).astype(BF16)
    pltpu.make_async_copy(table.at[pl.ds(0, 16 * count)], blocks, sem).wait()
    out[...] = dot(pick, blocks[...]).astype(BF16)
    for copy in halves:
        copy.wait()


def fetch_kernel(count, *refs):
    sources, targets, sems = refs[-1 - 2 * count : -1 - count], refs[-1 - count : -1], refs[-1]
    pairs = []
    for source, target in zip(sources, targets):
        pairs += quarters(source, target)
    for copy in stream(pairs, sems):
        copy.wait()


def fetch(after, arrays, beside=()):
    return call(
        functools.partial(fetch_kernel, len(arrays)),
        [like(array.shape, BF16) for array in arrays],
        [HBM] * (1 + len(beside) + len(arrays)),
        [pltpu.SemaphoreType.DMA((FETCH_PARTS * len(arrays),))],
        limit=MIB,
    )(after, *beside, *[pinned(array) for array in arrays])


def turn(source, target):
    for at, size in spans(source.shape[0], TURN_ROWS):
        target[:, at : at + size] = jnp.transpose(source[at : at + size, :])


def turn_kernel(count, *refs):
    for source, target in zip(refs[1 : 1 + count], refs[1 + count :]):
        turn(source, target)


def turned(after, arrays):
    return call(
        functools.partial(turn_kernel, len(arrays)),
        [like(array.shape[::-1], BF16) for array in arrays],
        [HBM] + [VMEM] * len(arrays),
        limit=4 * MIB,
    )(after, *arrays)


def feed_own_kernel(
    piece, gain, gate, up, down, after, gate_part, up_part, square, down_kept, sems
):
    copies = stream(quarters(down, down_kept), sems)
    share = piece.shape[1]
    at = pl.multiple_of(lax.axis_index("inner") * share, share)
    rows = piece[...].astype(F32)
    square[...] = jnp.broadcast_to(row_sum(rows * rows), square.shape)
    taken = (rows * gain[:, pl.ds(at, share)]).astype(BF16)
    for start, size in spans(gate.shape[1], 512):
        span = slice(start, start + size)
        gate_part[:, span] = dot(taken, gate[pl.ds(at, share), span])
        up_part[:, span] = dot(taken, up[pl.ds(at, share), span])
    for copy in copies:
        copy.wait()


def feed_kernel(
    step, piece0, piece1, piece2, piece3, gain, gate, up, down, gate_part, up_part, square,
    hidden, emb, scaled, part_low,
):
    width = hidden.shape[1]
    me = lax.axis_index("inner")
    share = piece0.shape[1]
    squares = square[:, :1]
    taken = []
    for which, piece in enumerate((piece0, piece1, piece2, piece3)):
        at = pl.multiple_of((me ^ which) * share, share)
        emb[:, pl.ds(at, share)] = piece[...]
        if which > 0:
            rows = piece[...].astype(F32)
            squares = squares + row_sum(rows * rows)
            taken.append((at, (rows * gain[:, pl.ds(at, share)]).astype(BF16)))
    scale = lax.rsqrt(squares / emb.shape[1] + 1e-06)
    path_scale = (step[0].astype(F32) + 0.5) / STEPS
    for start, size in spans(width, 512):
        span = slice(start, start + size)
        gate_rows, up_rows = gate_part[:, span], up_part[:, span]
        for at, rows in taken:
            gate_rows = gate_rows + dot(rows, gate[pl.ds(at, share), span])
            up_rows = up_rows + dot(rows, up[pl.ds(at, share), span])
        gate_rows = scale * gate_rows
        units = gate_rows / (1.0 + jnp.exp(-gate_rows)) * (scale * up_rows)
        hidden[:, span] = units
        scaled[:, span] = (path_scale * units).astype(BF16)
    down_kernel(0, scaled, down, part_low)


def down_kernel(begin, scaled, down, part):
    for start, size in spans(part.shape[1], 512):
        sums = dot(scaled[...], down[:, begin + start : begin + start + size])
        part[:, start : start + size] = sums.astype(BF16)


def pair_kernel(mine, other, *refs):
    refs[-1][...] = (mine[...].astype(F32) + other[...].astype(F32)).astype(BF16)


def pair_sums(low, high, before):
    low_other, high_other = swap(low, "inner", 1), swap(high, "inner", 2)
    low = call(pair_kernel, like(low.shape, BF16), [VMEM] * 2 + [HBM] * len(before))(
        low, low_other, *before
    )
    low_other = swap(low, "inner", 2)
    high = call(pair_kernel, like(high.shape, BF16), [VMEM] * 2)(high, high_other)
    return low, low_other, high, swap(high, "inner", 1)


def added(mine, other):
    return mine[...].astype(F32) + other[...].astype(F32)


def half_product(begin, emb, mine, other, gain, mixed, weights, gate_weights):
    half = mixed.shape[1]
    span = slice(begin, begin + half)
    total = emb[:, span].astype(F32) + added(mine, other)
    mixed[...] = total
    taken = (total * gain[:, span]).astype(BF16)
    raw = [dot(taken, weight[span, :]) for weight in weights]
    gates = [dot(taken, weight[:, span], True) for weight in gate_weights]
    return raw, gates, row_sum(total * total)


def project_low_kernel(
    emb, low, low_other, gain, query, key, value, decay, beta,
    mixed, query_raw, key_raw, value_raw, gate_raw, square,
):
    raw, gates, squares = half_product(
        0, emb, low, low_other, gain, mixed, (query, key, value), (decay, beta)
    )
    query_raw[...], key_raw[...], value_raw[...] = raw
    heads = decay.shape[0]
    gate_raw[:, :heads], gate_raw[:, heads : 2 * heads] = gates
    square[...] = jnp.broadcast_to(squares, square.shape)


def project_kernel(
    emb, high, high_other, gain, query, key, value, decay, beta,
    query_raw, key_raw, value_raw, gate_raw, square,
    mixed, own, send, scales,
):
    half_key = query.shape[1] // 2
    half_value = value.shape[1] // 2
    all_heads = decay.shape[0]
    first = lax.axis_index("outer") % 2 == 0
    raw, gates, squares = half_product(
        emb.shape[1] - mixed.shape[1], emb, high, high_other, gain, mixed, (query, key, value), (decay, beta)
    )
    scale = lax.rsqrt((squares + square[:, :1]) / emb.shape[1] + 1e-06)
    scales[...] = jnp.broadcast_to(scale, scales.shape)
    query_rows, key_rows, value_rows = [
        scale * (part + rest[...]) for part, rest in zip(raw, (query_raw, key_raw, value_raw))
    ]
    gates = [
        scale * (gates[0] + gate_raw[:, :all_heads]),
        scale * (gates[1] + gate_raw[:, all_heads : 2 * all_heads]),
    ]

    def put(at, low, high):
        size = low.shape[1]
        own[:, at : at + size] = jnp.where(first, low, high).astype(BF16)
        send[:, at : at + size] = jnp.where(first, high, low).astype(BF16)

    heads = decay.shape[0] // 2
    lanes = lax.broadcasted_iota(jnp.int32, scales.shape, 1)
    packed = []
    for side in range(2):
        lane, pack = 0, jnp.zeros(scales.shape, F32)
        for values in gates:
            for head in range(side * heads, (side + 1) * heads):
                column = values[:, head : head + 1]
                top = column.astype(BF16).astype(F32)
                pack = jnp.where(lanes == lane, top, pack)
                pack = jnp.where(lanes == lane + 1, column - top, pack)
                lane += 2
        packed.append(pack)
    put(0, query_rows[:, :half_key], query_rows[:, half_key:])
    put(half_key, key_rows[:, :half_key], key_rows[:, half_key:])
    put(2 * half_key, value_rows[:, :half_value], value_rows[:, half_value:])
    put(2 * half_key + half_value, *packed)


def both_blocks(own, other, target):
    core = lax.axis_index("outer") % 2
    size = own.shape[0]
    target[pl.ds(pl.multiple_of(core * size, size), size), :] = own[...]
    target[pl.ds(pl.multiple_of((1 - core) * size, size), size), :] = other[...]


def cumulate(chosen, column):
    top = column.astype(BF16)
    rest = column - top.astype(F32)
    middle = rest.astype(BF16)
    low = (rest - middle.astype(F32)).astype(BF16)
    picked = jnp.where(chosen, 1.0, 0.0).astype(BF16)

    def part(values):
        return dot(picked, jnp.broadcast_to(values, (values.shape[0], 128)))

    return part(top) + (part(middle) + part(low))


def base_inverses(systems):
    size = systems[0].shape[0]
    row_ids, col_ids = grid_ids(size)
    apart = row_ids - col_ids
    near = row_ids // BASE == col_ids // BASE

    def diagonal(which):
        picked = near & (apart == which)
        rows = [jnp.sum(jnp.where(picked, a, 0.0), axis=0, keepdims=True) for a in systems]
        return jnp.concatenate(rows, axis=0)

    def ahead(rows, by):
        return rows if by == 0 else pltpu.roll(rows, size - by, 1)

    given = [None] + [diagonal(which) for which in range(1, BASE)]
    found = [jnp.ones((len(systems), size), F32)]
    for which in range(1, BASE):
        terms = [ahead(given[j], which - j) * found[which - j] for j in range(1, which + 1)]
        while len(terms) > 1:
            pairs = [a + b for a, b in zip(terms[::2], terms[1::2])]
            terms = pairs + terms[2 * len(pairs) :]
        found.append(-terms[0])
    inverses = []
    for head, system in enumerate(systems):
        inverse = jnp.zeros((size, size), F32)
        for which in range(BASE):
            inverse = jnp.where(apart == which, found[which][head : head + 1], inverse)
        inverses.append(inverse)
    return inverses


def doublings(size):
    blocks = []
    while BASE << len(blocks) < size:
        blocks.append(BASE << len(blocks))
    return blocks


def solved(base, system, *sides):
    size = system.shape[0]
    row_ids, col_ids = grid_ids(size)
    parts = []
    for block in doublings(size):
        below = (row_ids // (2 * block) == col_ids // (2 * block)) & (
            row_ids // block != col_ids // block
        )
        parts.append(jnp.where(below, system, 0.0))
    rest = mm(base, jnp.concatenate([*parts, *sides], axis=1))
    turns = []
    for _ in parts:
        turns.append(rest[:, :size].astype(BF16))
        rest = rest[:, size:]
        rest = rest - dot(turns[-1], rest.astype(BF16))
    return turns, rest


def front_kernel(
    own, other, cot_own, cot_other, rate_log, decay_bias, beta_bias,
    packs, cots, sent, kept_offset, tails,
    decay_mats, grams, bases, turn_mats, scores, maps, fresh, pulled, columns,
):
    both_blocks(own, other, packs)
    both_blocks(cot_own, cot_other, cots)
    heads, length, _ = decay_mats.shape
    key_dim, value_dim = maps.shape[2], fresh.shape[2]
    place = lax.axis_index("outer")
    even = (place // 2) % 2 == 0
    first = place % 2 == 0

    def of_head(values, head):
        return jnp.where(
            first, values[:, head : head + 1], values[:, heads + head : heads + head + 1]
        )

    row_ids, col_ids = grid_ids(length)
    lower, strictly = row_ids >= col_ids, row_ids > col_ids
    lanes = lax.broadcasted_iota(jnp.int32, (length, 128), 1)
    gate_at = heads * (2 * key_dim + value_dim)
    gates = packs[:, gate_at : gate_at + 128].astype(F32)
    ready = []
    for head in range(heads):
        at = head * key_dim
        query_rows = packs[:, at : at + key_dim].astype(F32)
        at += heads * key_dim
        key_rows = packs[:, at : at + key_dim].astype(F32)
        at = 2 * heads * key_dim + head * value_dim
        values = packs[:, at : at + value_dim].astype(F32)
        cot = cots[:, head * value_dim : (head + 1) * value_dim]
        lane = 2 * head
        decay_in = gates[:, lane : lane + 1] + gates[:, lane + 1 : lane + 2]
        decay_in = decay_in + of_head(decay_bias, head)
        lane += 2 * heads
        beta_in = gates[:, lane : lane + 1] + gates[:, lane + 1 : lane + 2]
        beta_in = beta_in + of_head(beta_bias, head)
        rate = jnp.broadcast_to(jnp.exp(of_head(rate_log, head)), (length, 1))
        query_scale = lax.rsqrt(row_sum(query_rows * query_rows) + 1e-06) * key_dim ** (-0.5)
        key_at = (heads + head) * key_dim
        key_half = packs[:, key_at : key_at + key_dim]
        raw = dot(key_half, key_half, True)
        squares = jnp.where(row_ids == col_ids, raw, 0.0)
        key_scale = lax.rsqrt(row_sum(squares) + 1e-06)
        key_scale_row = lax.rsqrt(jnp.sum(squares, axis=0, keepdims=True) + 1e-06)
        queries, keys_unit = query_rows * query_scale, key_rows * key_scale
        log_decay = -rate * (jnp.maximum(decay_in, 0.0) + jnp.log1p(jnp.exp(-jnp.abs(decay_in))))
        betas = 1.0 / (1.0 + jnp.exp(-beta_in))
        cum = cumulate(lower, log_decay)
        decay_mat = jnp.where(
            lower, jnp.exp(jnp.where(lower, cum - jnp.transpose(cum), 0.0)), 0.0
        )
        total = cum[:, :1]
        start_scale = jnp.exp(total)
        tail_scale = jnp.exp(total[length - 1 :] - total)
        gram = jnp.where(strictly, decay_mat * (key_scale * raw * key_scale_row), 0.0)
        ready.append(
            (
                queries, keys_unit, values, cot, decay_mat, gram, start_scale, tail_scale,
                betas, query_scale, key_scale, decay_in, rate,
            )
        )
    systems = [item[8] * item[5] for item in ready]
    base_list = base_inverses(systems)
    for head, base in enumerate(base_list):
        (
            queries, keys_unit, values, cot, decay_mat, gram, start_scale, tail_scale,
            betas, query_scale, key_scale, decay_in, rate,
        ) = ready[head]
        score = decay_mat * mm(queries, keys_unit, True)
        turns, both = solved(
            base, systems[head], (betas * start_scale) * keys_unit, betas * values
        )
        state_map, fresh_vals = both[:, :key_dim], both[:, key_dim:]
        tail_t = jnp.transpose(tail_scale * keys_unit)
        offset = mm(tail_t, fresh_vals)
        score_pull = mm(jnp.transpose(score), cot)
        grad_local = mm(jnp.transpose(start_scale * queries), cot) - mm(
            jnp.transpose(state_map), score_pull
        )
        sent[head] = jnp.where(even, offset, grad_local).astype(BF16)
        kept_offset[head] = jnp.where(even, grad_local, offset)
        tails[head] = tail_t.astype(BF16)
        decay_mats[head] = decay_mat
        grams[head] = gram
        bases[head] = base.astype(BF16)
        for which, turn in enumerate(turns):
            turn_mats[head, which] = turn
        scores[head] = score
        maps[head] = state_map.astype(BF16)
        fresh[head] = fresh_vals
        pulled[head] = score_pull
        pack = jnp.zeros((length, 128), F32)
        for lane, column in enumerate(
            (query_scale, key_scale, betas, start_scale, tail_scale, decay_in, rate)
        ):
            pack = jnp.where(lanes == lane, column, pack)
        columns[head] = pack


def maps_kernel(
    tails, bases, turn_mats, maps, pulled, columns, after, sent_map, kept_map, target_local, target_map
):
    heads, length, _ = bases.shape
    even = (lax.axis_index("outer") // 2) % 2 == 0
    row_ids, col_ids = grid_ids(length)
    for head in range(heads):
        end_scale = columns[head, length - 1 :, 3:4]
        tail_t, inverse = tails[head], bases[head].astype(F32)
        for which in range(turn_mats.shape[1]):
            inverse = inverse - dot(turn_mats[head, which], inverse.astype(BF16))
        transition = jnp.where(row_ids == col_ids, end_scale, 0.0) - dot(tail_t, maps[head])
        flipped = jnp.transpose(transition)
        sent_map[head] = jnp.where(even, transition, flipped)
        kept_map[head] = jnp.where(even, flipped, transition).astype(BF16)
        target_local[head] = mm(jnp.transpose(inverse), pulled[head])
        target_map[head] = jnp.transpose(mm(tail_t, inverse)).astype(BF16)


def combine_kernel(kept_map, kept_offset, got, out):
    for head in range(out.shape[0]):
        joined = dot(kept_map[head], got[head]) + kept_offset[head]
        out[head] = joined.astype(BF16)


def back_kernel(
    near, near_map, far_one, far_two, packs, cots,
    decay_mats, grams, scores, maps, fresh, columns, target_local, target_map, after,
    own, send, grads,
):
    heads, length, _ = decay_mats.shape
    key_dim, value_dim = maps.shape[2], fresh.shape[2]
    place = lax.axis_index("outer")
    core, chip = place % 2, place // 2
    outer_chip = (chip == 0) | (chip == 3)
    odd = chip % 2 == 1
    row_ids, col_ids = grid_ids(length)
    strictly, upper = row_ids > col_ids, row_ids <= col_ids
    lanes = lax.broadcasted_iota(jnp.int32, (length, 128), 1)
    gate_at = heads * (2 * key_dim + value_dim)
    gate_grads = jnp.zeros((length, 128), F32)
    for head in range(heads):
        at = head * key_dim
        query_rows = packs[:, at : at + key_dim].astype(F32)
        key_at = at + heads * key_dim
        key_rows = packs[:, key_at : key_at + key_dim].astype(F32)
        value_at = 2 * heads * key_dim + head * value_dim
        values = packs[:, value_at : value_at + value_dim].astype(F32)
        cot = cots[:, head * value_dim : (head + 1) * value_dim]
        pack = columns[head]
        query_scale, key_scale, betas = pack[:, 0:1], pack[:, 1:2], pack[:, 2:3]
        start_scale, tail_scale = pack[:, 3:4], pack[:, 4:5]
        decay_in, rate = pack[:, 5:6], pack[:, 6:7]
        end_scale = start_scale[length - 1 :]
        queries, keys_unit = query_rows * query_scale, key_rows * key_scale
        decay_mat, gram, score = decay_mats[head], grams[head], scores[head]
        far = jnp.where(outer_chip, far_two[head], far_one[head])
        close = near[head].astype(F32)
        reached = mm(near_map[head], far) + close
        first = jnp.where(outer_chip, reached, close)
        second = jnp.where(outer_chip, 0.0, far.astype(F32))
        state = jnp.where(odd, first, second)
        state_grad = jnp.where(odd, second, first)
        state_half, state_grad_half = state.astype(BF16), state_grad.astype(BF16)
        new_vals = fresh[head] - dot(maps[head], state_half)
        new_half = new_vals.astype(BF16)
        grad_target = target_local[head] + dot(target_map[head], state_grad_half)
        target_half = grad_target.astype(BF16)
        grad_score = dot(cot, new_half, True)
        grad_sys = jnp.where(strictly, -dot(target_half, new_half, True), 0.0)
        cot_state = dot(cot, state_half, True)
        target_state = dot(target_half, state_half, True)
        new_state = dot(new_half, state_grad_half, True)
        weighted = decay_mat * grad_score
        grad_gram = grad_sys * decay_mat * betas
        grad_query = mm(weighted, keys_unit) + start_scale * cot_state
        grad_key = (
            mm(jnp.transpose(weighted), queries)
            + mm(grad_gram + jnp.transpose(grad_gram), keys_unit)
            + tail_scale * new_state
            - (betas * start_scale) * target_state
        )
        key_target = start_scale * keys_unit * target_state
        sys_gram = grad_sys * gram
        weights = grad_target * values
        grad_beta = row_sum(
            sum(weights[:, at : at + length] for at in range(0, value_dim, length))
            - key_target
            + sys_gram
        )
        both = score * grad_score + betas * sys_gram
        tails = tail_scale * keys_unit * new_state
        grad_cum = row_sum(
            both
            - jnp.transpose(both)
            + start_scale * queries * cot_state
            - betas * key_target
            - tails
        )
        ending = row_sum(jnp.sum(tails, axis=0, keepdims=True)) + end_scale * row_sum(
            jnp.sum(state * state_grad, axis=0, keepdims=True)
        )
        grad_log = cumulate(upper, grad_cum)[:, :1] + ending
        grad_decay = grad_log * -rate / (1.0 + jnp.exp(-decay_in))
        grad_beta = grad_beta * betas * (1.0 - betas)
        units = queries * key_dim**0.5
        grad_query = query_scale * (grad_query - units * row_sum(units * grad_query))
        grad_key = key_scale * (grad_key - keys_unit * row_sum(keys_unit * grad_key))
        grads[:, at : at + key_dim] = grad_query.astype(BF16)
        grads[:, key_at : key_at + key_dim] = grad_key.astype(BF16)
        grads[:, value_at : value_at + value_dim] = (betas * grad_target).astype(BF16)
        gate_grads = jnp.where(lanes == head, grad_decay, gate_grads)
        gate_grads = jnp.where(lanes == heads + head, grad_beta, gate_grads)
    grads[:, gate_at : gate_at + 128] = gate_grads.astype(BF16)
    size = own.shape[0]
    own[...] = grads[pl.ds(pl.multiple_of(core * size, size), size), :]
    send[...] = grads[pl.ds(pl.multiple_of((1 - core) * size, size), size), :]


def return_own_kernel(own, query, key, value, sums):
    half_key = query.shape[0] // 2
    half_value = value.shape[0] // 2
    core = lax.axis_index("outer") % 2
    keys = pl.ds(pl.multiple_of(core * half_key, half_key), half_key)
    values = pl.ds(pl.multiple_of(core * half_value, half_value), half_value)
    for start, size in spans(sums.shape[1], 512):
        span = slice(start, start + size)
        sums[:, span] = (
            dot(own[:, :half_key], query[keys, span])
            + dot(own[:, half_key : 2 * half_key], key[keys, span])
            + dot(own[:, 2 * half_key : 2 * half_key + half_value], value[values, span])
        )


def return_kernel(begin, own, other, query, key, value, decay, beta, sums, part):
    half_key = query.shape[0] // 2
    half_value = value.shape[0] // 2
    core = lax.axis_index("outer") % 2
    first = core == 0
    keys = pl.ds(pl.multiple_of((1 - core) * half_key, half_key), half_key)
    values = pl.ds(pl.multiple_of((1 - core) * half_value, half_value), half_value)

    def sides(at, size):
        mine, yours = own[:, at : at + size], other[:, at : at + size]
        return jnp.concatenate(
            [jnp.where(first, mine, yours), jnp.where(first, yours, mine)], axis=1
        )

    gate_at = 2 * half_key + half_value
    heads = decay.shape[0] // 2
    decays, betas = sides(gate_at, heads), sides(gate_at + heads, heads)
    for start, size in spans(part.shape[1], 512):
        span = slice(begin + start, begin + start + size)
        total = (
            sums[:, span]
            + dot(other[:, :half_key], query[keys, span])
            + dot(other[:, half_key : 2 * half_key], key[keys, span])
            + dot(other[:, 2 * half_key : gate_at], value[values, span])
            + dot(decays, decay[:, span])
            + dot(betas, beta[:, span])
        )
        part[:, start : start + size] = total.astype(BF16)


def along_kernel(mixed_low, mixed_high, down, after, out):
    half = mixed_low.shape[1]
    out[...] = mm(mixed_low[...], down[:half, :]) + mm(mixed_high[...], down[half:, :])


def final_low_kernel(low, low_other, mixed, gain, down, along, product, dots):
    half = mixed.shape[1]
    gained = added(low, low_other) * gain[:, :half]
    dots[...] = jnp.broadcast_to(row_sum(mixed[...] * gained), dots.shape)
    product[...] = mm(gained, down[:half, :])


def final_kernel(
    high, high_other, mixed, gain, down, product, dots, along, scales, hidden, out, held, sems
):
    begin = down.shape[0] - mixed.shape[1]
    gained = added(high, high_other) * gain[:, begin:]
    scale = scales[:, :1]
    mean = (dots[:, :1] + row_sum(mixed[...] * gained)) / down.shape[0]
    gained = gained.astype(BF16)
    backward = scale * scale * mean
    copies = []
    for which, (start, size) in enumerate(spans(held.shape[1], 512)):
        span = slice(start, start + size)
        total = product[:, span] + dot(gained, down[begin:, span]) - backward * along[:, span]
        held[:, span] = hidden[:, span] * (scale * total)
        columns = pl.ds(start, size)
        copy = pltpu.make_async_copy(held.at[:, columns], out.at[:, columns], sems.at[which])
        copy.start()
        copies.append(copy)
    for copy in copies:
        copy.wait()


def swap(array, axis, bit):
    return lax.ppermute(array, axis, [(i, i ^ bit) for i in range(lax.axis_size(axis))])


def four_chips(
    tokens, step_index, embed_table, gain_one, gate_weight, up_weight, down_weight, gain_two,
    query_weight, key_weight, value_weight, decay_weight, beta_weight,
    rate_log, decay_bias, beta_bias, cotangent,
):
    count, model = tokens.shape[0], gain_one.shape[0]
    width = gate_weight.shape[1]
    head_count = rate_log.shape[0]
    heads = head_count // 2
    key_dim = query_weight.shape[1] // head_count
    value_dim = value_weight.shape[1] // head_count
    pack_width = heads * (2 * key_dim + value_dim) + 128
    length = 2 * count
    rows_shape = like((count, model), BF16)
    low_width = model * 9 // 16
    widths = (low_width, model - low_width)
    part_shapes = [like((count, size), BF16) for size in widths]
    dma = pltpu.SemaphoreType.DMA
    cot_half = heads * value_dim
    columns, cot_own, cot_send = call(
        embed_kernel,
        [like((count, embed_table.shape[1]), BF16)]
        + [like((count, cot_half), BF16)] * 2,
        [HBM] * 3,
        [
            pltpu.SMEM((1, count), jnp.int32),
            pltpu.VMEM((1, count), jnp.int32),
            pltpu.VMEM((16 * count, embed_table.shape[1]), BF16),
            dma((2,)),
            dma,
            dma((2,)),
        ],
    )(pinned(tokens.reshape(1, count)), pinned(embed_table), pinned(cotangent))
    cot_other = swap(cot_send, "outer", 1)
    pieces = [columns] + [swap(columns, "inner", bit) for bit in (1, 2, 3)]
    wide = like((count, width), F32)
    one_lane = like((count, 128), F32)
    gain = gain_one.reshape(1, model)
    gate_part, up_part, squares, down_kept = call(
        feed_own_kernel,
        [wide, wide, one_lane, like((width, model), BF16)],
        [VMEM] * 4 + [HBM] * 2,
        [dma((FETCH_PARTS,))],
    )(columns, gain, gate_weight, up_weight, pinned(down_weight), cot_other)
    hidden, emb, scaled, part_low = call(
        feed_kernel,
        [wide, rows_shape, like((count, width), BF16), part_shapes[0]],
        [SMEM] + [VMEM] * 11,
    )(
        step_index, *pieces, gain, gate_weight, up_weight, down_kept, gate_part, up_part, squares
    )
    part_high = call(functools.partial(down_kernel, low_width), part_shapes[1], [VMEM] * 2)(
        scaled, down_kept
    )
    weights = (query_weight, key_weight, value_weight, decay_weight.T, beta_weight.T)
    low, low_other, high, high_other = pair_sums(part_low, part_high, [*weights[:3]])
    gain = gain_two.reshape(1, model)
    mixed_low, *raw = call(
        project_low_kernel,
        [like((count, widths[0]), F32)]
        + [like((count, weight.shape[1]), F32) for weight in weights[:3]]
        + [one_lane] * 2,
        [VMEM] * 9,
    )(emb, low, low_other, gain, *weights)
    mixed_high, own, send, scales = call(
        project_kernel,
        [like((count, widths[1]), F32)] + [like((count, pack_width), BF16)] * 2 + [one_lane],
        [VMEM] * 14,
    )(emb, high, high_other, gain, *weights, *raw)
    other = swap(send, "outer", 1)
    square = (heads, length, length)
    valued = (heads, length, value_dim)
    packs, cots, sent, kept_offset, tails, *saved = call(
        front_kernel,
        [
            like((length, pack_width), BF16),
            like((length, cot_half), BF16),
            like((heads, key_dim, value_dim), BF16),
            like((heads, key_dim, value_dim), F32),
            like((heads, key_dim, length), BF16),
            like(square, F32),
            like(square, F32),
            like(square, BF16),
            like((heads, len(doublings(length)), length, length), BF16),
            like(square, F32),
            like((heads, length, key_dim), BF16),
            like(valued, F32),
            like(valued, F32),
            like((heads, length, 128), F32),
        ],
        [VMEM] * 7,
    )(
        own, other, cot_own, cot_other,
        *[array.reshape(1, head_count) for array in (rate_log, decay_bias, beta_bias)],
    )
    near = swap(sent, "outer", 2)
    decay_mats, grams, bases, turn_mats, scores, maps, fresh, pulled, columns = saved
    sent_map, kept_map, target_local, target_map = call(
        maps_kernel,
        [like((heads, key_dim, key_dim), F32), like((heads, key_dim, key_dim), BF16)]
        + [like(valued, F32), like((heads, length, key_dim), BF16)],
        [VMEM] * 6 + [HBM],
    )(tails, bases, turn_mats, maps, pulled, columns, sent)
    near_map = lax.ppermute(sent_map, "outer", [(2, 0), (3, 1), (4, 6), (5, 7)])
    joined = call(combine_kernel, like((heads, key_dim, value_dim), BF16), [VMEM] * 3)(
        kept_map, kept_offset, near
    )
    query_turned, key_turned, value_turned = turned(joined, weights[:3])
    cycle = {1: 3, 3: 2, 2: 0, 0: 1}
    far_two = lax.ppermute(
        joined, "outer", [(2 * a + core, 2 * b + core) for a, b in cycle.items() for core in (0, 1)]
    )
    far_one = lax.ppermute(
        joined, "outer", [(2, 4), (3, 5), (4, 2), (5, 3), (0, 1), (1, 0), (6, 7), (7, 6)]
    )
    own, send = call(
        back_kernel,
        [like((count, pack_width), BF16)] * 2,
        [VMEM] * 14 + [HBM],
        [pltpu.VMEM((length, pack_width), BF16)],
    )(
        near, near_map, far_one, far_two, packs, cots, decay_mats, grams, scores, maps, fresh, columns,
        target_local, target_map, value_turned,
    )
    other = swap(send, "outer", 1)
    back_weights = (query_turned, key_turned, value_turned)
    sums = call(return_own_kernel, like((count, model), F32), [VMEM] * 4)(own, *back_weights)
    part_low, part_high = [
        call(functools.partial(return_kernel, begin), shape, [VMEM] * 8)(
            own, other, *back_weights, *weights[3:], sums
        )
        for begin, shape in zip((0, low_width), part_shapes)
    ]
    (down_turned,) = turned(part_low, [down_kept])
    low, low_other, high, high_other = pair_sums(part_low, part_high, [down_turned])
    along = call(along_kernel, wide, [VMEM] * 3 + [HBM])(
        mixed_low, mixed_high, down_turned, part_low
    )
    product, dots = call(final_low_kernel, [wide, one_lane], [VMEM] * 5 + [HBM])(
        low, low_other, mixed_low, gain, down_turned, along
    )
    return call(
        final_kernel,
        wide,
        [VMEM] * 10,
        [pltpu.VMEM((count, width), F32), dma((len(spans(width, 512)),))],
        out=HBM,
    )(
        high, high_other, mixed_high, gain, down_turned, product, dots, along, scales, hidden
    )


def local_part(*args):
    fits = (
        lax.axis_size("inner") == 4
        and lax.axis_size("outer") == 8
        and args[0].shape[0] == 64
        and args[13].shape[0] % 2 == 0
    )
    return four_chips(*args) if fits else shards(*args)


def solution(mesh):
    placed = (
        P("outer"),
        P(),
        P(None, "inner"),
        P(),
        P(None, "inner"),
        P(None, "inner"),
        P("inner", None),
        P(),
        P(None, "inner"),
        P(None, "inner"),
        P(None, "inner"),
        P(None, "inner"),
        P(None, "inner"),
        P("inner"),
        P("inner"),
        P("inner"),
        P("outer", "inner"),
    )
    return jax.shard_map(
        local_part, mesh=mesh, in_specs=placed, out_specs=P("outer", "inner"), check_vma=False
    )
```
